32 devices in a mesh: fsdp: 8 (over y, x, core), tp: 4 (over z).
Axes of the slice: x: 2, y: 2, z: 4, core: 2. Of those that a mesh axis runs over, the one named last changes fastest.
Arguments:
- states: bfloat16 [16384, 2048], P(('fsdp', 'tp')), may hold values from -6 to 6
- lengths: int32 [8, 4], P('fsdp'), may hold values from 1 to 2045, as said below
- padding: int32 [8, 2048], P('fsdp'), may hold values from 0 to 1, as said below
- teacher: bfloat16 [16384, 2048], P(('fsdp', 'tp')), may hold values from -6 to 6
- norm_attn: float32 [2048], replicated, may hold values from 0.25 to 1.75
- w_query: bfloat16 [2048, 2048], P('fsdp', 'tp'), may hold values from -0.125 to 0.125
- w_key: bfloat16 [2048, 1024], P('fsdp', 'tp'), may hold values from -0.125 to 0.125
- w_value: bfloat16 [2048, 1024], P('fsdp', 'tp'), may hold values from -0.125 to 0.125
- norm_query: float32 [128], replicated, may hold values from 0.25 to 1.75
- norm_key: float32 [128], replicated, may hold values from 0.25 to 1.75
- w_out: bfloat16 [2048, 2048], P('tp', 'fsdp'), may hold values from -0.75 to 0.75
- norm_mlp: float32 [2048], replicated, may hold values from 0.25 to 1.75
- w_gate: bfloat16 [2048, 6144], P('fsdp', 'tp'), may hold values from -0.125 to 0.125
- w_up: bfloat16 [2048, 6144], P('fsdp', 'tp'), may hold values from -0.125 to 0.125
- w_down: bfloat16 [6144, 2048], P('tp', 'fsdp'), may hold values from -0.078125 to 0.078125
Outputs:
- outputs: float32 [16384, 2048], P(('fsdp', 'tp'))
- loss: float32 [], replicated
- grad_x: float32 [16384, 2048], P(('fsdp', 'tp'))
- grad_norm_attn: float32 [2048], replicated
- grad_w_query: float32 [2048, 2048], P('fsdp', 'tp')
- grad_w_key: float32 [2048, 1024], P('fsdp', 'tp')
- grad_w_value: float32 [2048, 1024], P('fsdp', 'tp')
- grad_norm_query: float32 [128], replicated
- grad_norm_key: float32 [128], replicated
- grad_w_out: float32 [2048, 2048], P('tp', 'fsdp')
- grad_norm_mlp: float32 [2048], replicated
- grad_w_gate: float32 [2048, 6144], P('fsdp', 'tp')
- grad_w_up: float32 [2048, 6144], P('fsdp', 'tp')
- grad_w_down: float32 [6144, 2048], P('tp', 'fsdp')
The draws below stay inside these ranges and needn't reach their ends.
Inputs may be any that keep to these rules, and one draw needn't show every extreme that they name: `lengths`: each row sums to 2048; each entry is at least 1, so none exceeds 2048 - 3. `padding`: each row is 1 on a leading run of 768 or more positions and 0 after it.
All inputs are finite; a program needn't handle non-finite values.
Results may differ from the reference program's by a relative error of at most 0.0085.
The reference program's roundings to bfloat16 on the way count: a program that leaves them out, or rounds other values in their place, can miss the bound.
Values may be sent and summed in bfloat16 or wider, within the bound.
A program may use at most 320 MiB of HBM per device.

```python
import jax
import jax.numpy as jnp
from jax import lax

D = 2048
HQ = 16
KV = 8
HD = 128
FF = 6144
LEN = 2048
WINDOW = 1024
DOCS = 4
SEQS = 8
TOKENS = 16384
SHORT = 128


def draw_lengths(key, part):
    key = jax.random.fold_in(key, 11)
    short_key, slot_key = jax.random.split(key)
    shorts = jax.random.randint(short_key, (SEQS, DOCS), 1, SHORT + 1)
    long_slot = jax.random.randint(slot_key, (SEQS, 1), 0, DOCS)
    is_long = jnp.arange(DOCS)[None, :] == long_slot
    remainder = LEN - jnp.sum(jnp.where(is_long, 0, shorts), axis=1, keepdims=True)
    return jnp.where(is_long, remainder, shorts).astype(jnp.int32)


def draw_padding(key, part):
    key = jax.random.fold_in(key, 23)
    ranking_key, jitter_key = jax.random.split(key)
    ranking = jax.random.permutation(ranking_key, SEQS)
    pad_count = ranking * (LEN // 2) // max(SEQS - 1, 1) + jax.random.randint(jitter_key, (SEQS,), 0, LEN // 8 + 1)
    live_count = LEN - pad_count
    return (jnp.arange(LEN)[None, :] < live_count[:, None]).astype(jnp.int32)


def block_scale(key, extent, shards, least, top_value):
    level = 1.0
    for position, shards_of in shards:
        draws = jax.random.uniform(jax.random.fold_in(jax.random.fold_in(key, 6), position), (shards_of,), jnp.float32, least / len(shards), top_value / len(shards))
        level = level * jnp.repeat(jnp.exp(draws), extent[position] // shards_of).reshape((-1,) + (1,) * (len(extent) - 1 - position))
    return level


def noise(rng, extent, spread, reach, pieces=(), kind=jnp.bfloat16):
    array = jax.random.normal(rng, extent, jnp.float32) * spread
    if len(pieces) > 0:
        array = block_scale(rng, extent, pieces, -0.22, 0.18) * array
    return jnp.clip(array, min=-reach, max=reach).astype(kind)


def setup_inputs(seed: int = 0) -> dict:
    arg_keys = jax.random.split(jax.random.key(seed), 16)
    states = noise(arg_keys[0], (TOKENS, D), 1.0, 6.0, ((0, 32),))
    lengths = draw_lengths(jax.random.fold_in(arg_keys[15], 71), 0)
    padding = draw_padding(jax.random.fold_in(arg_keys[15], 71), 0)
    teacher = noise(arg_keys[3], (TOKENS, D), 1.0, 6.0, ((0, 32),))
    norm_attn = jnp.clip(1.0 + 0.15 * jax.random.normal(arg_keys[4], (D,), jnp.float32), 0.25, 1.75)
    w_query = noise(arg_keys[5], (D, HQ * HD), D ** -0.5, 0.125, ((0, 8), (1, 4)))
    w_key = noise(arg_keys[6], (D, KV * HD), D ** -0.5, 0.125, ((0, 8), (1, 4)))
    w_value = noise(arg_keys[7], (D, KV * HD), D ** -0.5, 0.125, ((0, 8), (1, 4)))
    norm_query = jnp.clip(1.0 + 0.15 * jax.random.normal(arg_keys[8], (HD,), jnp.float32), 0.25, 1.75)
    norm_key = jnp.clip(1.0 + 0.15 * jax.random.normal(arg_keys[9], (HD,), jnp.float32), 0.25, 1.75)
    w_out = noise(arg_keys[10], (HQ * HD, D), (HQ * HD // 32) ** -0.5, 0.75, ((0, 4), (1, 8)))
    norm_mlp = jnp.clip(1.0 + 0.15 * jax.random.normal(arg_keys[11], (D,), jnp.float32), 0.25, 1.75)
    w_gate = noise(arg_keys[12], (D, FF), D ** -0.5, 0.125, ((0, 8), (1, 4)))
    w_up = noise(arg_keys[13], (D, FF), D ** -0.5, 0.125, ((0, 8), (1, 4)))
    w_down = noise(arg_keys[14], (FF, D), FF ** -0.5, 0.078125, ((0, 4), (1, 8)))
    return {"states": states, "lengths": lengths, "padding": padding, "teacher": teacher, "norm_attn": norm_attn, "w_query": w_query, "w_key": w_key, "w_value": w_value, "norm_query": norm_query, "norm_key": norm_key, "w_out": w_out, "norm_mlp": norm_mlp, "w_gate": w_gate, "w_up": w_up, "w_down": w_down}


EPS = 1e-06
THETA = 1000000.0
NEG = -1e+30

@jax.custom_vjp
def low(v):
    return lax.optimization_barrier(v.astype(jnp.bfloat16)).astype(jnp.float32)

@jax.custom_vjp
def low_back(v):
    return v

def low_keep(v):
    return (low(v), None)

def low_pass(kept, grad):
    return (grad,)

def back_keep(v):
    return (v, None)

def back_low(kept, grad):
    return (low(grad),)
low.defvjp(low_keep, low_pass)
low_back.defvjp(back_keep, back_low)

def matmul(left, right):
    return jnp.dot(left, right, precision=lax.Precision.HIGHEST, preferred_element_type=jnp.float32)

def normalize(values):
    return values * lax.rsqrt(lax.optimization_barrier(jnp.mean(values * values, axis=-1, keepdims=True)) + EPS)

def rotate(values, cosine, sine):
    half = values.shape[-1] // 2
    first, second = (values[..., :half], values[..., half:])
    return jnp.concatenate([first * cosine - second * sine, second * cosine + first * sine], axis=-1)

def doc_tables(length_row, number):
    places = jnp.arange(number, dtype=jnp.int32)
    ends = jnp.cumsum(length_row).astype(jnp.int32)
    passed = places[:, None] >= ends[None, :]
    doc_ids = lax.optimization_barrier(jnp.sum(passed.astype(jnp.int32), axis=1))
    starts = lax.optimization_barrier(jnp.sum(jnp.where(passed, length_row[None, :], 0), axis=1)).astype(jnp.int32)
    return (doc_ids, places - starts)

def rope_tables(positions):
    freqs = THETA ** (-(jnp.arange(HD // 2).astype(jnp.float32) * 2.0 / HD))
    angles = positions.astype(jnp.float32)[:, None] * freqs[None, :]
    return (jnp.cos(angles)[:, None, :], jnp.sin(angles)[:, None, :])

def allowed(first, rows, doc_ids, key_live):
    query_idx = first + jnp.arange(rows, dtype=jnp.int32)
    key_idx = jnp.arange(doc_ids.shape[0], dtype=jnp.int32)
    query_doc = lax.dynamic_slice_in_dim(doc_ids, first, rows, 0)
    causal = (key_idx[None, :] <= query_idx[:, None]) & (query_idx[:, None] - key_idx[None, :] < WINDOW)
    same_doc = query_doc[:, None] == doc_ids[None, :]
    live_keys = (key_live[None, :] == 1) | (key_idx[None, :] == query_idx[:, None])
    return causal & same_doc & live_keys

def layer(inputs, length_row, pad_row, target, params):
    norm_attn, w_query, w_key, w_value, norm_query, norm_key, w_out, norm_mlp, w_gate, w_up, w_down = params
    number = inputs.shape[0]
    doc_ids, positions = doc_tables(length_row, number)
    cosine, sine = rope_tables(positions)
    normed_in = low(normalize(inputs) * norm_attn)
    query_raw = low_back(matmul(normed_in, w_query)).reshape(number, HQ, HD)
    key_raw = low_back(matmul(normed_in, w_key)).reshape(number, KV, HD)
    value_rows = low_back(low(matmul(normed_in, w_value))).reshape(number, KV, HD)
    query_rot = low(rotate(normalize(query_raw) * norm_query, cosine, sine)).reshape(number, KV, HQ // KV, HD)
    key_rot = low(rotate(normalize(key_raw) * norm_key, cosine, sine))
    block = min(512, number)
    scale = HD ** (-0.5)

    def attend(index):
        first = index * block
        query_rows = lax.dynamic_slice_in_dim(query_rot, first, block, 0)
        scores = low_back(jnp.einsum('qkgd,tkd->kgqt', query_rows, key_rot, precision=lax.Precision.HIGHEST) * scale)
        scores = jnp.where(allowed(first, block, doc_ids, pad_row)[None, None], scores, NEG)
        row_max = lax.optimization_barrier(jnp.max(scores, axis=-1, keepdims=True))
        exp_scores = jnp.exp(scores - row_max)
        probabilities = low(exp_scores / lax.optimization_barrier(jnp.sum(exp_scores, axis=-1, keepdims=True)))
        mixed = jnp.einsum('kgqt,tkd->qkgd', probabilities, value_rows, precision=lax.Precision.HIGHEST)
        return mixed.reshape(block, HQ * HD)
    attended = lax.map(jax.checkpoint(attend), jnp.arange(number // block, dtype=jnp.int32)).reshape(number, HQ * HD)
    attn_low = low_back(low(attended))
    hidden_one = inputs + low_back(matmul(attn_low, w_out))
    normed_mid = low(normalize(hidden_one) * norm_mlp)
    gate_rows = low_back(matmul(normed_mid, w_gate))
    up_rows = low_back(matmul(normed_mid, w_up))
    product = low(jax.nn.silu(gate_rows) * up_rows)
    outputs = hidden_one + low_back(matmul(product, w_down))
    errors = (outputs - target) * pad_row.astype(jnp.float32)[:, None]
    return (outputs, jnp.sum(errors * errors))

def reference(states, lengths, padding, teacher, norm_attn, w_query, w_key, w_value, norm_query, norm_key, w_out, norm_mlp, w_gate, w_up, w_down):
    params = tuple((entry.astype(jnp.float32) for entry in (norm_attn, w_query, w_key, w_value, norm_query, norm_key, w_out, norm_mlp, w_gate, w_up, w_down)))
    count_valid = jnp.sum(padding).astype(jnp.float32)
    targets = teacher.astype(jnp.float32).reshape(SEQS, LEN, D)

    def total(inputs, weights):

        def step(carry, item):
            rows, length_row, pad_row, target = item
            outputs, squares = layer(rows, length_row, pad_row, target, weights)
            return (carry + squares, outputs)
        squares, outputs = lax.scan(jax.checkpoint(step), jnp.zeros((), jnp.float32), (inputs.reshape(SEQS, LEN, D), lengths, padding, targets))
        return (outputs.reshape(TOKENS, D), squares / (count_valid * D))
    inputs = states.astype(jnp.float32)
    (outputs, loss), pullback = jax.vjp(total, inputs, params)
    grad_in, grads = pullback((jnp.zeros_like(outputs), jnp.ones_like(loss)))
    return (outputs, loss, grad_in, grads[0], grads[1], grads[2], grads[3], grads[4], grads[5], grads[6], grads[7], grads[8], grads[9], grads[10])
```

```python
import functools

import jax
import jax.numpy as jnp
from jax import lax
from jax.experimental import pallas as pl
from jax.experimental.pallas import tpu as pltpu
from jax.sharding import PartitionSpec as P

D = 2048
HD = 128
WINDOW = 1024

EPS = 1e-06
THETA = 1000000.0
NEG = -1e30
VMEM = 56 * 1024 * 1024


def normalize_rows(values):
    factor = lax.rsqrt(jnp.mean(values * values, axis=-1, keepdims=True) + EPS)
    return (values * factor, factor)


def norm_back(grad, normed, factor, gain):
    scaled = grad * gain
    return factor * (scaled - normed * jnp.mean(scaled * normed, axis=-1, keepdims=True))


def contract_last(left, right):
    return lax.dot_general(
        left, right, (((1,), (1,)), ((), ())), preferred_element_type=jnp.float32
    )


def contract_first(left, right):
    return lax.dot_general(
        left, right, (((0,), (0,)), ((), ())), preferred_element_type=jnp.float32
    )


def dot(left, right):
    return jnp.dot(left, right, preferred_element_type=jnp.float32)


MESH = pl.DeviceIdType.MESH
PARTS = 2


def flip(index, mask):
    bit = 1
    while bit <= mask:
        if mask & bit:
            index = index + bit - 2 * bit * lax.rem(lax.div(index, bit), 2)
        bit *= 2
    return index


def chip_bits(size):
    bits = []
    bit = 2
    while bit < size:
        bits.append(bit)
        bit *= 2
    return bits


def orders(size):
    bits = chip_bits(size)
    return (bits, bits[::-1])


def mask_of(pattern, order):
    return sum(bit for i, bit in enumerate(order) if pattern >> i & 1)


def top(pattern):
    return pattern.bit_length() - 1


def greet(me, size):
    barrier = pltpu.get_barrier_semaphore()
    bits = [1] + chip_bits(size)
    for bit in bits:
        pl.semaphore_signal(
            barrier, inc=1, device_id={"fsdp": flip(me, bit)}, device_id_type=MESH
        )
    pl.semaphore_wait(barrier, len(bits))


def pick(part, pair):
    return pair[0] + part * (pair[1] - pair[0])


class Gather:
    def __init__(self, size, me, whole, sems, parts=PARTS, lane=lambda part: part):
        self.size, self.me, self.whole, self.parts, self.lane = (size, me, whole, parts, lane)
        self.chip_send, self.chip_recv, self.core_send, self.core_recv = sems
        self.steps = len(chip_bits(size))
        self.patterns = sorted(range(1 << self.steps), key=lambda m: (top(m), m))

    def order(self, part):
        return orders(self.size)[part % 2]

    def slot(self, part, pattern, sibling):
        return flip(self.me, mask_of(pattern, self.order(part)) + sibling)

    def chip_copy(self, part, step, pattern):
        block = self.whole.at[self.slot(part, pattern, 0), self.lane(part)]
        number = (1 << step) - 1 + pattern
        return pltpu.make_async_remote_copy(
            src_ref=block,
            dst_ref=block,
            send_sem=self.chip_send.at[part, number],
            recv_sem=self.chip_recv.at[part, number],
            device_id={"fsdp": flip(self.me, self.order(part)[step])},
            device_id_type=MESH,
        )

    def core_copy(self, part, pattern):
        block = self.whole.at[self.slot(part, pattern, 0), self.lane(part)]
        return pltpu.make_async_remote_copy(
            src_ref=block,
            dst_ref=block,
            send_sem=self.core_send.at[part, pattern],
            recv_sem=self.core_recv.at[part, pattern],
            device_id={"fsdp": flip(self.me, 1)},
            device_id_type=MESH,
        )

    def arrive(self, part, pattern):
        if pattern:
            step = top(pattern)
            self.chip_copy(part, step, pattern - (1 << step)).wait_recv()

    def forward(self, part, pattern):
        for step in range(top(pattern) + 1, self.steps):
            self.chip_copy(part, step, pattern).start()
        self.core_copy(part, pattern).start()

    def pairs(self, work):
        for pattern in self.patterns:
            for part in range(self.parts):
                self.arrive(part, pattern)
            for part in range(self.parts):
                self.forward(part, pattern)
            work([self.slot(part, pattern, 0) for part in range(self.parts)])
            for part in range(self.parts):
                self.core_copy(part, pattern).wait_recv()
            work([self.slot(part, pattern, 1) for part in range(self.parts)])

    def finish(self):
        for pattern in self.patterns:
            for part in range(self.parts):
                for step in range(top(pattern) + 1, self.steps):
                    self.chip_copy(part, step, pattern).wait_send()
                self.core_copy(part, pattern).wait_send()


def gather_semaphores(size, parts=PARTS):
    moves = max(1, size // 2 - 1)
    return [
        pltpu.SemaphoreType.DMA((parts, moves)),
        pltpu.SemaphoreType.DMA((parts, moves)),
        pltpu.SemaphoreType.DMA((parts, size // 2)),
        pltpu.SemaphoreType.DMA((parts, size // 2)),
    ]


def scatter_rows_in(size, me, made, held, sent, came, sems, partial, final):
    chip_send, chip_recv, core_send, core_recv = sems
    steps = len(chip_bits(size))
    order = [bits[::-1] for bits in orders(size)]
    first = lambda m: (m & -m).bit_length() - 1 if m else steps
    patterns = sorted(range(1 << steps), key=lambda m: (first(m), -bin(m).count("1"), m))
    place = {m: q for q, m in enumerate(patterns)}
    width = final.shape[-1]
    chunk = min(512, width)

    def slots(pattern, sibling):
        return [flip(me, mask_of(pattern, order[part]) + sibling) for part in range(PARTS)]

    def core_copy(part, q):
        return pltpu.make_async_remote_copy(
            src_ref=made.at[part, q],
            dst_ref=held.at[part, q],
            send_sem=core_send.at[part, q],
            recv_sem=core_recv.at[part, q],
            device_id={"fsdp": flip(me, 1)},
            device_id_type=MESH,
        )

    def chip_copy(part, q):
        return pltpu.make_async_remote_copy(
            src_ref=sent.at[part, q],
            dst_ref=came.at[part, q],
            send_sem=chip_send.at[part, q],
            recv_sem=chip_recv.at[part, q],
            device_id={"fsdp": flip(me, order[part][first(patterns[q])])},
            device_id_type=MESH,
        )

    def for_sibling(q):
        pair = slots(patterns[q], 1)

        @pl.loop(0, PARTS)
        def _(part):
            @pl.loop(0, width // chunk)
            def _(index):
                columns = pl.ds(pl.multiple_of(index * chunk, chunk), chunk)
                made[part, q, :, columns] = partial(part, pick(part, pair), columns).astype(
                    jnp.bfloat16
                )

        for part in range(PARTS):
            core_copy(part, q).start()

    def for_chips(q):
        pattern = patterns[q]
        pair = slots(pattern, 0)
        arrivals = [place[pattern | 1 << step] for step in range(first(pattern))]
        for part in range(PARTS):
            core_copy(part, q).wait_recv()
            for arrival in arrivals:
                chip_copy(part, arrival).wait_recv()

        @pl.loop(0, PARTS)
        def _(part):
            @pl.loop(0, width // chunk)
            def _(index):
                columns = pl.ds(pl.multiple_of(index * chunk, chunk), chunk)
                total = partial(part, pick(part, pair), columns)
                total = total + held[part, q, :, columns].astype(jnp.float32)
                for arrival in arrivals:
                    total = total + came[part, arrival, :, columns].astype(jnp.float32)
                if pattern:
                    sent[part, q, :, columns] = total.astype(jnp.bfloat16)
                else:
                    final[part, :, columns] = total

        if pattern:
            for part in range(PARTS):
                chip_copy(part, q).start()

    for_sibling(0)
    for q in range(len(patterns)):
        if q + 1 < len(patterns):
            for_sibling(q + 1)
        for_chips(q)
    for q in range(len(patterns)):
        for part in range(PARTS):
            core_copy(part, q).wait_send()
            if patterns[q]:
                chip_copy(part, q).wait_send()


def scatter_scratch(size, rows, width):
    held = size // 2
    moved = max(1, held - 1)
    return [
        pltpu.VMEM((PARTS, held, rows, width), jnp.bfloat16),
        pltpu.VMEM((PARTS, held, rows, width), jnp.bfloat16),
        pltpu.VMEM((PARTS, moved, rows, width), jnp.bfloat16),
        pltpu.VMEM((PARTS, moved, rows, width), jnp.bfloat16),
        pltpu.SemaphoreType.DMA((PARTS, moved)),
        pltpu.SemaphoreType.DMA((PARTS, moved)),
        pltpu.SemaphoreType.DMA((PARTS, held)),
        pltpu.SemaphoreType.DMA((PARTS, held)),
    ]


def gate_up_kernel(
    size, x_ref, wg_ref, wu_ref, x_out, gate_out, up_out, prod_out, whole, gate, up, prod, load, keep, store, *sems
):
    me = lax.axis_index("fsdp")
    hidden = wg_ref.shape[0]
    chunk = 256 if hidden % 256 == 0 else 128
    own = pltpu.make_async_copy(x_ref, whole.at[me], load)
    own.start()
    own.wait()
    greet(me, size)
    state = {"count": 0, "last": None}

    def stores(part, at):
        return [
            pltpu.make_async_copy(buffer.at[part], out.at[at, part], store.at[part, i])
            for i, (buffer, out) in enumerate(((gate, gate_out), (up, up_out), (prod, prod_out)))
        ]

    def work(pair):
        count, last = (state["count"], state["last"])
        for part in range(PARTS):
            pltpu.make_async_copy(
                whole.at[pair[part], part], x_out.at[pair[part], part], keep.at[part, count]
            ).start()

        @pl.loop(0, PARTS)
        def _(part):
            at = pick(part, pair)
            if last is not None:
                for copy in stores(part, pick(part, last)):
                    copy.wait()

            @pl.loop(0, hidden // chunk)
            def _(index):
                units = pl.ds(pl.multiple_of(index * chunk, chunk), chunk)
                rows = whole[at, part]
                gates = contract_last(rows, wg_ref[units, :])
                ups = contract_last(rows, wu_ref[units, :])
                gate[part, :, units] = gates
                up[part, :, units] = ups
                prod[part, :, units] = (gates * jax.nn.sigmoid(gates) * ups).astype(jnp.bfloat16)

            for copy in stores(part, at):
                copy.start()

        state["count"], state["last"] = (count + 1, pair)
        state.setdefault("all", []).append(pair)

    gather = Gather(size, me, whole, sems)
    gather.pairs(work)
    gather.finish()
    for part in range(PARTS):
        for copy in stores(part, state["last"][part]):
            copy.wait()
        for count, pair in enumerate(state["all"]):
            pltpu.make_async_copy(
                whole.at[pair[part], part], x_out.at[pair[part], part], keep.at[part, count]
            ).wait()


def gate_up(size, values, rows_gate, rows_up):
    own, width = values.shape
    rows, hidden = (own // PARTS, rows_gate.shape[0])
    any_space = pl.BlockSpec(memory_space=pl.ANY)
    vmem = pl.BlockSpec(memory_space=pltpu.VMEM)
    shape = lambda columns, kind: jax.ShapeDtypeStruct((size, PARTS, rows, columns), kind)
    outs = pl.pallas_call(
        functools.partial(gate_up_kernel, size),
        out_shape=(
            shape(width, jnp.bfloat16),
            shape(hidden, jnp.float32),
            shape(hidden, jnp.float32),
            shape(hidden, jnp.bfloat16),
        ),
        in_specs=[any_space, vmem, vmem],
        out_specs=(any_space,) * 4,
        scratch_shapes=[
            pltpu.VMEM((size, PARTS, rows, width), jnp.bfloat16),
            pltpu.VMEM((PARTS, rows, hidden), jnp.float32),
            pltpu.VMEM((PARTS, rows, hidden), jnp.float32),
            pltpu.VMEM((PARTS, rows, hidden), jnp.bfloat16),
            pltpu.SemaphoreType.DMA,
            pltpu.SemaphoreType.DMA((PARTS, size)),
            pltpu.SemaphoreType.DMA((PARTS, 3)),
            *gather_semaphores(size),
        ],
        compiler_params=pltpu.CompilerParams(
            collective_id=1, has_side_effects=True, vmem_limit_bytes=VMEM
        ),
        cost_estimate=pl.CostEstimate(
            flops=4 * size * own * width * hidden, bytes_accessed=200 * 1024 * 1024, transcendentals=0
        ),
        name="gate_up",
    )(values.reshape(PARTS, rows, width), rows_gate, rows_up)
    return tuple(out.reshape(size * own, -1) for out in outs)


def grad_hidden_kernel(
    size, x_ref, wd_ref, gate_in, up_in, x_out, dgate_out, dup_out, whole, gate, up, dprod, dgate, dup, load, keep, fetch, store, *sems
):
    me = lax.axis_index("fsdp")
    hidden = wd_ref.shape[0]
    chunk = 256 if hidden % 256 == 0 else 128
    own = pltpu.make_async_copy(x_ref, whole.at[me], load)
    own.start()
    own.wait()
    greet(me, size)
    state = {"count": 0, "last": None, "all": []}

    def stores(part, at):
        return [
            pltpu.make_async_copy(buffer.at[part], out.at[at, part], store.at[part, i])
            for i, (buffer, out) in enumerate(((dgate, dgate_out), (dup, dup_out)))
        ]

    def fetches(part, at):
        return [
            pltpu.make_async_copy(source.at[at, part], buffer, fetch.at[i])
            for i, (source, buffer) in enumerate(((gate_in, gate), (up_in, up)))
        ]

    def work(pair):
        count, last = (state["count"], state["last"])
        for part in range(PARTS):
            pltpu.make_async_copy(
                whole.at[pair[part], part], x_out.at[pair[part], part], keep.at[part, count]
            ).start()

        @pl.loop(0, PARTS)
        def _(part):
            at = pick(part, pair)
            for copy in fetches(part, at):
                copy.start()
            if last is not None:
                for copy in stores(part, pick(part, last)):
                    copy.wait()

            @pl.loop(0, hidden // chunk)
            def _(index):
                units = pl.ds(pl.multiple_of(index * chunk, chunk), chunk)
                dprod[:, units] = contract_last(whole[at, part], wd_ref[units, :])

            for copy in fetches(part, at):
                copy.wait()

            @pl.loop(0, hidden // chunk)
            def _(index):
                units = pl.ds(pl.multiple_of(index * chunk, chunk), chunk)
                gates, grads = (gate[:, units], dprod[:, units])
                sigmoid = jax.nn.sigmoid(gates)
                dgate[part, :, units] = (
                    grads * up[:, units] * sigmoid * (1.0 + gates * (1.0 - sigmoid))
                ).astype(jnp.bfloat16)
                dup[part, :, units] = (grads * (gates * sigmoid)).astype(jnp.bfloat16)

            for copy in stores(part, at):
                copy.start()

        state["count"], state["last"] = (count + 1, pair)
        state["all"].append(pair)

    gather = Gather(size, me, whole, sems)
    gather.pairs(work)
    gather.finish()
    for part in range(PARTS):
        for copy in stores(part, state["last"][part]):
            copy.wait()
        for count, pair in enumerate(state["all"]):
            pltpu.make_async_copy(
                whole.at[pair[part], part], x_out.at[pair[part], part], keep.at[part, count]
            ).wait()


def grad_hidden_units(size, values, rows_down, gate, up):
    own, width = values.shape
    rows, hidden = (own // PARTS, rows_down.shape[0])
    any_space = pl.BlockSpec(memory_space=pl.ANY)
    vmem = pl.BlockSpec(memory_space=pltpu.VMEM)
    shape = lambda columns, kind: jax.ShapeDtypeStruct((size, PARTS, rows, columns), kind)
    blocks = lambda array: array.reshape(size, PARTS, rows, hidden)
    outs = pl.pallas_call(
        functools.partial(grad_hidden_kernel, size),
        out_shape=(
            shape(width, jnp.bfloat16),
            shape(hidden, jnp.bfloat16),
            shape(hidden, jnp.bfloat16),
        ),
        in_specs=[any_space, vmem, any_space, any_space],
        out_specs=(any_space,) * 3,
        scratch_shapes=[
            pltpu.VMEM((size, PARTS, rows, width), jnp.bfloat16),
            pltpu.VMEM((rows, hidden), jnp.float32),
            pltpu.VMEM((rows, hidden), jnp.float32),
            pltpu.VMEM((rows, hidden), jnp.float32),
            pltpu.VMEM((PARTS, rows, hidden), jnp.bfloat16),
            pltpu.VMEM((PARTS, rows, hidden), jnp.bfloat16),
            pltpu.SemaphoreType.DMA,
            pltpu.SemaphoreType.DMA((PARTS, size)),
            pltpu.SemaphoreType.DMA((2,)),
            pltpu.SemaphoreType.DMA((PARTS, 2)),
            *gather_semaphores(size),
        ],
        compiler_params=pltpu.CompilerParams(
            collective_id=3, has_side_effects=True, vmem_limit_bytes=VMEM
        ),
        cost_estimate=pl.CostEstimate(
            flops=2 * size * own * width * hidden, bytes_accessed=200 * 1024 * 1024, transcendentals=0
        ),
        name="grad_hidden_units",
    )(values.reshape(PARTS, rows, width), rows_down, blocks(gate), blocks(up))
    return tuple(out.reshape(size * own, -1) for out in outs)


def sum_products_kernel(size, terms, *refs):
    lefts, rights, out = (refs[:terms], refs[terms : 2 * terms], refs[2 * terms])
    made, held, sent, came, *sems = refs[2 * terms + 1 :]
    me = lax.axis_index("fsdp")
    greet(me, size)

    def partial(part, slot, columns):
        return sum(
            dot(left[slot, part], right[:, columns]) for left, right in zip(lefts, rights)
        )

    scatter_rows_in(size, me, made, held, sent, came, sems, partial, out)


def sum_products(size, number, lefts, rights):
    total, hidden = lefts[0].shape
    width = rights[0].shape[1]
    rows = total // size // PARTS
    vmem = pl.BlockSpec(memory_space=pltpu.VMEM)
    terms = len(lefts)
    out = pl.pallas_call(
        functools.partial(sum_products_kernel, size, terms),
        out_shape=jax.ShapeDtypeStruct((PARTS, rows, width), jnp.float32),
        in_specs=[vmem] * (2 * terms),
        out_specs=vmem,
        scratch_shapes=scatter_scratch(size, rows, width),
        compiler_params=pltpu.CompilerParams(
            collective_id=number, has_side_effects=True, vmem_limit_bytes=VMEM
        ),
        cost_estimate=pl.CostEstimate(
            flops=2 * total * hidden * width * terms, bytes_accessed=200 * 1024 * 1024, transcendentals=0
        ),
        name="sum_products",
    )(*[left.reshape(size, PARTS, rows, hidden) for left in lefts], *rights)
    return out.reshape(PARTS * rows, width)


def enter_kernel(size, lanes, back, x_ref, w_ref, before, whole, load, z_send, z_recv, x_send, x_recv, *sems):
    me, z = (lax.axis_index("fsdp"), lax.axis_index("tp"))
    own = pltpu.make_async_copy(w_ref, whole.at[me, z], load)
    own.start()
    barrier = pltpu.get_barrier_semaphore()
    peers = [{"fsdp": flip(me, bit)} for bit in [1] + chip_bits(size)]
    peers += [{"tp": lax.rem(z + hop, lanes)} for hop in range(1, lanes)]
    for peer in peers:
        pl.semaphore_signal(barrier, inc=1, device_id=peer, device_id_type=MESH)
    pl.semaphore_wait(barrier, len(peers))
    own.wait()

    def lane(part):
        return lax.rem(z + lanes - part, lanes)

    def lane_copy(hop):
        return pltpu.make_async_remote_copy(
            src_ref=w_ref,
            dst_ref=whole.at[me, z],
            send_sem=z_send.at[hop - 1],
            recv_sem=z_recv.at[hop - 1],
            device_id={"tp": lax.rem(z + hop, lanes)},
            device_id_type=MESH,
        )

    def token_copy(hop):
        return pltpu.make_async_remote_copy(
            src_ref=x_ref,
            dst_ref=before.at[hop - 1],
            send_sem=x_send.at[hop - 1],
            recv_sem=x_recv.at[hop - 1],
            device_id={"tp": lax.rem(z + hop, lanes)},
            device_id_type=MESH,
        )

    gather = Gather(size, me, whole, sems, lanes, lane)
    for hop in range(1, lanes):
        lane_copy(hop).start()
    gather.forward(0, 0)
    for hop in range(1, back + 1):

        @pl.when(z + hop < lanes)
        def _():
            token_copy(hop).start()

    events = [(part, pattern) for part in range(lanes) for pattern in gather.patterns]
    events.sort(key=lambda event: (2 * event[0] + top(event[1]) + 1, event))
    for part, pattern in events[1:]:
        if pattern:
            gather.arrive(part, pattern)
        else:
            lane_copy(part).wait_recv()
        gather.forward(part, pattern)
    for part, pattern in events:
        gather.core_copy(part, pattern).wait_recv()
    gather.finish()
    for hop in range(1, lanes):
        lane_copy(hop).wait_send()
    for hop in range(1, back + 1):

        @pl.when(z + hop < lanes)
        def _():
            token_copy(hop).wait_send()

        @pl.when(z >= hop)
        def _():
            token_copy(hop).wait_recv()


def enter(size, lanes, back, values, weights):
    any_space = pl.BlockSpec(memory_space=pl.ANY)
    return pl.pallas_call(
        functools.partial(enter_kernel, size, lanes, back),
        out_shape=(
            jax.ShapeDtypeStruct((back, *values.shape), values.dtype),
            jax.ShapeDtypeStruct((size, lanes, *weights.shape), weights.dtype),
        ),
        in_specs=[any_space, any_space],
        out_specs=(any_space, any_space),
        scratch_shapes=[
            pltpu.SemaphoreType.DMA,
            pltpu.SemaphoreType.DMA((lanes - 1,)),
            pltpu.SemaphoreType.DMA((lanes - 1,)),
            pltpu.SemaphoreType.DMA((back,)),
            pltpu.SemaphoreType.DMA((back,)),
            *gather_semaphores(size, lanes),
        ],
        compiler_params=pltpu.CompilerParams(collective_id=5, has_side_effects=True),
        cost_estimate=pl.CostEstimate(flops=0, bytes_accessed=400 * 1024 * 1024, transcendentals=0),
        name="enter",
    )(values, weights)


def project_kernel(
    wq, wk, before_ref, x_ref, gain_ref, w_ref, n_ref, q_ref, k_ref, v_ref, normed
):
    back, own, _ = before_ref.shape
    lead = back * own
    tile = min(256, own)
    z = lax.axis_index("tp")

    @pl.when(pl.program_id(0) == 0)
    def _():
        for hop in range(back + 1):

            @pl.loop(0, own // tile)
            def _(index):
                span = pl.ds(pl.multiple_of(index * tile, tile), tile)
                values = x_ref[span, :] if hop == 0 else before_ref[hop - 1, span, :]
                values = normalize_rows(values.astype(jnp.float32))[0] * gain_ref[...]
                values = values.astype(jnp.bfloat16)
                if hop:
                    values = jnp.where(z >= hop, values, jnp.zeros_like(values))
                else:
                    n_ref[span, :] = values
                at = lead - hop * own + index * tile
                normed[pl.ds(pl.multiple_of(at, tile), tile), :] = values

    weights = lambda start, size: w_ref[:, 0, :, start : start + size].reshape(D, size)

    @pl.loop(0, (lead + own) // tile)
    def _(index):
        span = pl.ds(pl.multiple_of(index * tile, tile), tile)
        pair = dot(normed[span, :], weights(wq, 2 * wk))
        k_ref[span, :] = pair[:, :wk]
        v_ref[span, :] = pair[:, wk:].astype(jnp.bfloat16)

    @pl.loop(0, own // tile)
    def _(index):
        span = pl.ds(pl.multiple_of(index * tile, tile), tile)
        from_lead = pl.ds(pl.multiple_of(lead + index * tile, tile), tile)
        q_ref[span, :] = dot(normed[from_lead, :], weights(0, wq))


def project(before, values, gain, weights, wq, wk):
    size, parts, rows_in, columns = weights.shape
    back, own, _ = before.shape
    rows = (back + 1) * own
    whole = lambda *_: (0, 0)
    return pl.pallas_call(
        functools.partial(project_kernel, wq, wk),
        grid=(parts,),
        out_shape=(
            jax.ShapeDtypeStruct((own, D), jnp.bfloat16),
            jax.ShapeDtypeStruct((own, parts * wq), jnp.float32),
            jax.ShapeDtypeStruct((rows, parts * wk), jnp.float32),
            jax.ShapeDtypeStruct((rows, parts * wk), jnp.bfloat16),
        ),
        in_specs=[
            pl.BlockSpec((back, own, D), lambda z: (0, 0, 0)),
            pl.BlockSpec((own, D), whole),
            pl.BlockSpec((1, D), whole),
            pl.BlockSpec((size, 1, rows_in, wq + 2 * wk), lambda z: (0, z, 0, 0)),
        ],
        out_specs=(
            pl.BlockSpec((own, D), whole),
            pl.BlockSpec((own, wq), lambda z: (0, z)),
            pl.BlockSpec((rows, wk), lambda z: (0, z)),
            pl.BlockSpec((rows, wk), lambda z: (0, z)),
        ),
        scratch_shapes=[pltpu.VMEM((rows, D), jnp.bfloat16)],
        compiler_params=pltpu.CompilerParams(vmem_limit_bytes=VMEM),
        cost_estimate=pl.CostEstimate(
            flops=2 * D * parts * (own * wq + rows * 2 * wk),
            bytes_accessed=2 * D * parts * (wq + 2 * wk) + 2 * rows * D,
            transcendentals=0,
        ),
        name="project_in",
    )(before, values, gain.reshape(1, D), weights)


def out_kernel(a_ref, w_ref, x_ref, o_ref):
    parts, _, width = w_ref.shape[1:]
    total = x_ref[...].astype(jnp.float32)
    for z in range(parts):
        total += contract_last(a_ref[:, z * width : (z + 1) * width], w_ref[0, z])
    o_ref[...] = total


def project_out(attended, weights, states, wo):
    size, parts, rows, columns = weights.shape
    own = states.shape[0]
    last = columns // wo - 1
    return pl.pallas_call(
        out_kernel,
        grid=(size,),
        out_shape=jax.ShapeDtypeStruct(states.shape, jnp.float32),
        in_specs=[
            pl.BlockSpec(attended.shape, lambda f: (0, 0)),
            pl.BlockSpec((1, parts, rows, wo), lambda f: (f, 0, 0, last)),
            pl.BlockSpec((own, rows), lambda f: (0, f)),
        ],
        out_specs=pl.BlockSpec((own, rows), lambda f: (0, f)),
        compiler_params=pltpu.CompilerParams(vmem_limit_bytes=VMEM),
        cost_estimate=pl.CostEstimate(
            flops=2 * own * D * parts * wo, bytes_accessed=24 * 1024 * 1024, transcendentals=0
        ),
        name="project_out",
    )(attended, weights, states)


def back_out_kernel(g_ref, w_ref, o_ref):
    size, _, rows, width = w_ref.shape
    o_ref[...] = dot(g_ref[...], w_ref[:, 0].reshape(size * rows, width)).astype(jnp.bfloat16)


def back_out(grad, weights, wo):
    size, parts, rows, columns = weights.shape
    own = grad.shape[0]
    last = columns // wo - 1
    return pl.pallas_call(
        back_out_kernel,
        grid=(parts,),
        out_shape=jax.ShapeDtypeStruct((own, parts * wo), jnp.bfloat16),
        in_specs=[
            pl.BlockSpec(grad.shape, lambda z: (0, 0)),
            pl.BlockSpec((size, 1, rows, wo), lambda z: (0, z, 0, last)),
        ],
        out_specs=pl.BlockSpec((own, wo), lambda z: (0, z)),
        compiler_params=pltpu.CompilerParams(vmem_limit_bytes=VMEM),
        cost_estimate=pl.CostEstimate(
            flops=2 * own * D * parts * wo, bytes_accessed=16 * 1024 * 1024, transcendentals=0
        ),
        name="back_out",
    )(grad, weights)


def back_in_kernel(q_ref, k_ref, v_ref, w_ref, o_ref):
    parts = w_ref.shape[1]
    total = jnp.zeros(o_ref.shape, jnp.float32)
    for z in range(parts):
        start = 0
        for ref in (q_ref, k_ref, v_ref):
            width = ref.shape[1] // parts
            total += contract_last(
                ref[:, z * width : (z + 1) * width], w_ref[0, z, :, start : start + width]
            )
            start += width
    o_ref[...] = total


def back_in(grad_query, grad_key, grad_value, weights):
    size, parts, rows, _ = weights.shape
    own = grad_query.shape[0]
    columns = (grad_query.shape[1] + 2 * grad_key.shape[1]) // parts
    whole = lambda f: (0, 0)
    return pl.pallas_call(
        back_in_kernel,
        grid=(size,),
        out_shape=jax.ShapeDtypeStruct((own, D), jnp.float32),
        in_specs=[
            pl.BlockSpec(grad_query.shape, whole),
            pl.BlockSpec(grad_key.shape, whole),
            pl.BlockSpec(grad_value.shape, whole),
            pl.BlockSpec((1, parts, rows, columns), lambda f: (f, 0, 0, 0)),
        ],
        out_specs=pl.BlockSpec((own, rows), lambda f: (0, f)),
        compiler_params=pltpu.CompilerParams(vmem_limit_bytes=VMEM),
        cost_estimate=pl.CostEstimate(
            flops=2 * own * D * parts * columns, bytes_accessed=24 * 1024 * 1024, transcendentals=0
        ),
        name="back_in",
    )(grad_query, grad_key, grad_value, weights)


def turn(values, cosine, sine):
    return values * cosine + pltpu.roll(values, HD // 2, 1) * sine


def turn_back(grad, cosine, sine):
    return grad * cosine - pltpu.roll(grad, HD // 2, 1) * sine


def split_heads(block, group):
    return jnp.concatenate([block[:, i * HD : (i + 1) * HD] for i in range(group)], axis=0)


def join_heads(stacked, group):
    rows = stacked.shape[0] // group
    return jnp.concatenate([stacked[i * rows : (i + 1) * rows] for i in range(group)], axis=1)


def head_probs(query, keys, bias, group, scale):
    scores = contract_last(query, keys) * scale
    rows, span = scores.shape
    scores = (scores.reshape(group, rows // group, span) + bias[None]).reshape(rows, span)
    weights = jnp.exp(scores - jnp.max(scores, axis=-1, keepdims=True))
    return weights * (1.0 / jnp.sum(weights, axis=-1, keepdims=True))


def attend_kernel(
    group, step, lead, q_ref, k_ref, v_ref, bias_ref, cos_ref, sin_ref, nq_ref, nk_ref, o_ref, keys
):
    tile, span = bias_ref.shape
    scale = HD ** (-0.5)
    index = pl.program_id(1)

    @pl.when(index == 0)
    def _():
        normed = normalize_rows(k_ref[...])[0] * nk_ref[...]
        keys[...] = turn(normed, cos_ref[...], sin_ref[...]).astype(jnp.bfloat16)

    here = pl.ds(pl.multiple_of(lead + index * tile, tile), tile)
    cosine, sine = (cos_ref[here, :], sin_ref[here, :])
    normed = normalize_rows(split_heads(q_ref[...], group))[0] * nq_ref[...]
    cosine, sine = (jnp.concatenate([cosine] * group, 0), jnp.concatenate([sine] * group, 0))
    query = turn(normed, cosine, sine).astype(jnp.bfloat16)
    window = pl.ds(pl.multiple_of(index * step, tile), span)
    probs = head_probs(query, keys[window, :], bias_ref[...], group, scale)
    mixed = dot(probs.astype(jnp.bfloat16), v_ref[window, :])
    o_ref[...] = join_heads(mixed.astype(jnp.bfloat16), group)


def attend_back_kernel(
    group,
    step,
    lead,
    q_ref,
    k_ref,
    v_ref,
    bias_ref,
    cos_ref,
    sin_ref,
    nq_ref,
    nk_ref,
    do_ref,
    dq_ref,
    prev_ref,
    own_ref,
    gq_ref,
    gk_ref,
    keys,
    dk,
    dv,
):
    tile, span = bias_ref.shape
    scale = HD ** (-0.5)
    index = pl.program_id(1)

    @pl.when((pl.program_id(0) == 0) & (index == 0))
    def _():
        gq_ref[...] = jnp.zeros_like(gq_ref)
        gk_ref[...] = jnp.zeros_like(gk_ref)

    @pl.when(index == 0)
    def _():
        normed = normalize_rows(k_ref[...])[0] * nk_ref[...]
        keys[...] = turn(normed, cos_ref[...], sin_ref[...]).astype(jnp.bfloat16)
        dk[...] = jnp.zeros_like(dk)
        dv[...] = jnp.zeros_like(dv)

    here = pl.ds(pl.multiple_of(lead + index * tile, tile), tile)
    cosine, sine = (cos_ref[here, :], sin_ref[here, :])
    cosine, sine = (jnp.concatenate([cosine] * group, 0), jnp.concatenate([sine] * group, 0))
    normed, factor = normalize_rows(split_heads(q_ref[...], group))
    query = turn(normed * nq_ref[...], cosine, sine).astype(jnp.bfloat16)
    window = pl.ds(pl.multiple_of(index * step, tile), span)
    probs = head_probs(query, keys[window, :], bias_ref[...], group, scale)
    grad_out = split_heads(do_ref[...], group)
    dv[window, :] += contract_first(probs.astype(jnp.bfloat16), grad_out)
    grad_probs = contract_last(grad_out, v_ref[window, :])
    centre = jnp.sum(probs * grad_probs, axis=-1, keepdims=True)
    grad_scores = (probs * (grad_probs - centre)).astype(jnp.bfloat16)
    dk[window, :] += contract_first(grad_scores, query) * scale
    grad_query = turn_back(dot(grad_scores, keys[window, :]) * scale, cosine, sine)
    gq_ref[...] += jnp.sum(grad_query * normed, axis=0, keepdims=True)
    grad_raw = norm_back(grad_query, normed, factor, nq_ref[...])
    dq_ref[...] = join_heads(grad_raw.astype(jnp.bfloat16), group)

    @pl.when(index == pl.num_programs(1) - 1)
    def _():
        normed_key, key_factor = normalize_rows(k_ref[...])
        grad_key = turn_back(dk[...], cos_ref[...], sin_ref[...])
        gk_ref[...] += jnp.sum(grad_key * normed_key, axis=0, keepdims=True)
        grad_key = norm_back(grad_key, normed_key, key_factor, nk_ref[...])
        if lead:
            prev_ref[0] = grad_key[:lead].astype(jnp.bfloat16)
            prev_ref[1] = dv[:lead, :].astype(jnp.bfloat16)
        own_ref[0] = grad_key[lead:]
        own_ref[1] = dv[lead:, :]


def attention_specs(own, rows, group, tile, span):
    whole = lambda g, t: (0, 0)
    return [
        pl.BlockSpec((tile, group * HD), lambda g, t: (t, g)),
        pl.BlockSpec((rows, HD), lambda g, t: (0, g)),
        pl.BlockSpec((rows, HD), lambda g, t: (0, g)),
        pl.BlockSpec((tile, span), lambda g, t: (t, 0)),
        pl.BlockSpec((rows, HD), whole),
        pl.BlockSpec((rows, HD), whole),
        pl.BlockSpec((1, HD), whole),
        pl.BlockSpec((1, HD), whole),
    ]


def attend(queries, keys, values, bias, cosine, sine, norm_query, norm_key, tile, step):
    own, rows = (queries.shape[0], keys.shape[0])
    heads = keys.shape[1] // HD
    group = queries.shape[1] // keys.shape[1]
    span = bias.shape[1]
    return pl.pallas_call(
        functools.partial(attend_kernel, group, step, rows - own),
        grid=(heads, own // tile),
        out_shape=jax.ShapeDtypeStruct(queries.shape, jnp.bfloat16),
        in_specs=attention_specs(own, rows, group, tile, span),
        out_specs=pl.BlockSpec((tile, group * HD), lambda g, t: (t, g)),
        scratch_shapes=[pltpu.VMEM((rows, HD), jnp.bfloat16)],
        compiler_params=pltpu.CompilerParams(vmem_limit_bytes=VMEM),
        cost_estimate=pl.CostEstimate(
            flops=16 * own * span * queries.shape[1],
            bytes_accessed=4 * queries.size + 6 * keys.size,
            transcendentals=own * span * heads * group,
        ),
        name="attend",
    )(queries, keys, values, bias, cosine, sine, norm_query, norm_key)


def attend_back(
    queries, keys, values, bias, cosine, sine, norm_query, norm_key, grad, tile, step
):
    own, rows = (queries.shape[0], keys.shape[0])
    heads = keys.shape[1] // HD
    group = queries.shape[1] // keys.shape[1]
    span = bias.shape[1]
    lead = rows - own
    whole = lambda g, t: (0, 0)
    return pl.pallas_call(
        functools.partial(attend_back_kernel, group, step, lead),
        grid=(heads, own // tile),
        out_shape=(
            jax.ShapeDtypeStruct(queries.shape, jnp.bfloat16),
            jax.ShapeDtypeStruct((2, lead, heads * HD), jnp.bfloat16),
            jax.ShapeDtypeStruct((2, own, heads * HD), jnp.float32),
            jax.ShapeDtypeStruct((1, HD), jnp.float32),
            jax.ShapeDtypeStruct((1, HD), jnp.float32),
        ),
        in_specs=attention_specs(own, rows, group, tile, span)
        + [pl.BlockSpec((tile, group * HD), lambda g, t: (t, g))],
        out_specs=(
            pl.BlockSpec((tile, group * HD), lambda g, t: (t, g)),
            pl.BlockSpec((2, lead, HD), lambda g, t: (0, 0, g)),
            pl.BlockSpec((2, own, HD), lambda g, t: (0, 0, g)),
            pl.BlockSpec((1, HD), whole),
            pl.BlockSpec((1, HD), whole),
        ),
        scratch_shapes=[
            pltpu.VMEM((rows, HD), jnp.bfloat16),
            pltpu.VMEM((rows, HD), jnp.float32),
            pltpu.VMEM((rows, HD), jnp.float32),
        ],
        compiler_params=pltpu.CompilerParams(vmem_limit_bytes=VMEM),
        cost_estimate=pl.CostEstimate(
            flops=40 * own * span * queries.shape[1],
            bytes_accessed=8 * queries.size + 16 * keys.size,
            transcendentals=own * span * heads * group,
        ),
        name="attend_back",
    )(queries, keys, values, bias, cosine, sine, norm_query, norm_key, grad)


def window_tables(length_row, pad_row, first, own, lead, tile, span):
    places = first - lead + jnp.arange(lead + own, dtype=jnp.int32)
    ends = jnp.cumsum(length_row)
    passed = places[:, None] >= ends[None, :]
    docs = jnp.sum(passed.astype(jnp.int32), axis=1)
    starts = jnp.sum(jnp.where(passed, length_row[None, :], 0), axis=1)
    freqs = THETA ** (-(jnp.arange(HD // 2).astype(jnp.float32) * 2.0 / HD))
    angles = (places - starts).astype(jnp.float32)[:, None] * freqs[None, :]
    cosine, sine = (jnp.cos(angles), jnp.sin(angles))
    padded = jnp.concatenate((jnp.zeros((lead,), pad_row.dtype), pad_row))
    live = lax.dynamic_slice_in_dim(padded, first, lead + own, 0)
    step = tile if lead + own > span else 0
    masks = []
    for index in range(own // tile):
        at = lead + index * tile
        query, key = (places[at : at + tile, None], places[None, index * step : index * step + span])
        same = docs[at : at + tile, None] == docs[None, index * step : index * step + span]
        seen = (live[None, index * step : index * step + span] == 1) | (key == query)
        masks.append((key >= 0) & (key <= query) & (query - key < WINDOW) & same & seen)
    bias = jnp.where(jnp.concatenate(masks, axis=0), 0.0, NEG).astype(jnp.float32)
    cosine = jnp.concatenate((cosine, cosine), axis=1)
    sine = jnp.concatenate((-sine, sine), axis=1)
    return (bias, cosine, sine, step, live[lead:].astype(jnp.float32))


def hidden_rows(weight_t):
    mine = lax.all_to_all(weight_t, "fsdp", 0, 1, tiled=True)
    return lax.all_gather(mine, "tp", axis=0, tiled=True)


def hidden_rows_grad(grad):
    mine = lax.psum_scatter(grad.astype(jnp.bfloat16), "tp", scatter_dimension=0, tiled=True)
    return lax.all_to_all(mine, "fsdp", 1, 0, tiled=True).astype(jnp.float32)


def scatter_grad(grad):
    rows = lax.psum_scatter(
        grad.astype(jnp.bfloat16), "fsdp", scatter_dimension=0, tiled=True
    )
    return lax.psum_scatter(rows, "tp", scatter_dimension=1, tiled=True).astype(jnp.float32)


def shards(
    states,
    lengths,
    padding,
    teacher,
    norm_attn,
    w_query,
    w_key,
    w_value,
    norm_query,
    norm_key,
    w_out,
    norm_mlp,
    w_gate,
    w_up,
    w_down,
):
    own = states.shape[0]
    n_tp, n_fsdp = (lax.axis_size("tp"), lax.axis_size("fsdp"))
    first = lax.axis_index("tp") * own
    back = min(n_tp - 1, -(-WINDOW // own))
    lead = back * own
    tile = min(256, own)
    span = WINDOW + tile if lead >= WINDOW else lead + own
    wq, wk = (w_query.shape[1], w_key.shape[1])
    count = lax.psum(jnp.sum(padding).astype(jnp.float32), "fsdp")
    bias, cosine, sine, step, live = window_tables(
        lengths[0], padding[0], first, own, lead, tile, span
    )
    joined = jnp.concatenate((w_query, w_key, w_value, w_out.T), axis=1)
    wo = w_out.shape[0]
    before, weights_attn = enter(n_fsdp, n_tp, back, states, joined)
    rows_gate = hidden_rows(w_gate.T)
    rows_up = hidden_rows(w_up.T)
    rows_down = hidden_rows(w_down)

    normed_in, query_raw, key_raw, value = project(
        before, states, norm_attn, weights_attn, wq, wk
    )
    gains = (norm_query.reshape(1, HD), norm_key.reshape(1, HD))
    attended = attend(query_raw, key_raw, value, bias, cosine, sine, *gains, tile, step)
    inputs = states.astype(jnp.float32)
    hidden_one = project_out(attended, weights_attn, states, wo)
    normed_two, factor_two = normalize_rows(hidden_one)
    whole_two, gate, up, product = gate_up(
        n_fsdp, (normed_two * norm_mlp).astype(jnp.bfloat16), rows_gate, rows_up
    )
    outputs = hidden_one + sum_products(n_fsdp, 2, (product,), (rows_down,))
    errors = (outputs - teacher.astype(jnp.float32)) * live[:, None]
    squares = jnp.sum(errors * errors)
    grad_out = errors * (2.0 / (count * D))

    grad_whole, grad_gate, grad_up = grad_hidden_units(
        n_fsdp, grad_out.astype(jnp.bfloat16), rows_down, gate, up
    )
    grad_mid = sum_products(n_fsdp, 4, (grad_gate, grad_up), (rows_gate, rows_up))
    grad_w_down = hidden_rows_grad(contract_first(product, grad_whole))
    grad_w_gate = hidden_rows_grad(contract_first(grad_gate, whole_two)).T
    grad_w_up = hidden_rows_grad(contract_first(grad_up, whole_two)).T
    grad_norm_mlp = jnp.sum(grad_mid * normed_two, axis=0)
    grad_hidden = grad_out + norm_back(grad_mid, normed_two, factor_two, norm_mlp)

    grad_low_out = grad_hidden.astype(jnp.bfloat16)
    grad_w_out = scatter_grad(contract_first(grad_low_out, attended)).T
    grad_attended = back_out(grad_low_out, weights_attn, wo)
    grad_query, grad_before, grad_own, grad_norm_query, grad_norm_key = attend_back(
        query_raw, key_raw, value, bias, cosine, sine, *gains, grad_attended, tile, step
    )
    for j in range(1, back + 1):
        block = grad_before[:, lead - j * own : lead - (j - 1) * own]
        block = lax.ppermute(block, "tp", [(i + j, i) for i in range(n_tp - j)])
        grad_own = grad_own + block.astype(jnp.float32)
    grad_key, grad_value = (grad_own[0].astype(jnp.bfloat16), grad_own[1].astype(jnp.bfloat16))
    grad_joined = jnp.concatenate(
        [
            part.reshape(own, n_tp, -1)
            for part in (grad_query, grad_key, grad_value)
        ],
        axis=2,
    )
    grad_low = back_in(grad_query, grad_key, grad_value, weights_attn)
    grad_weights = scatter_grad(
        contract_first(normed_in, grad_joined.reshape(own, n_tp * (wq + 2 * wk)))
    )
    normed_one, factor_one = normalize_rows(inputs)
    grad_norm_attn = jnp.sum(grad_low * normed_one, axis=0)
    grad_input = grad_hidden + norm_back(grad_low, normed_one, factor_one, norm_attn)
    squares, grad_norm_attn, grad_norm_query, grad_norm_key, grad_norm_mlp = lax.psum(
        (squares, grad_norm_attn, grad_norm_query[0], grad_norm_key[0], grad_norm_mlp),
        ("fsdp", "tp"),
    )
    return (
        outputs,
        squares / (count * D),
        grad_input,
        grad_norm_attn,
        grad_weights[:, :wq],
        grad_weights[:, wq : wq + wk],
        grad_weights[:, wq + wk :],
        grad_norm_query,
        grad_norm_key,
        grad_w_out,
        grad_norm_mlp,
        grad_w_gate,
        grad_w_up,
        grad_w_down,
    )


def solution(mesh):
    tokens = P(("fsdp", "tp"), None)
    rows, columns, sequences = (P("fsdp", "tp"), P("tp", "fsdp"), P("fsdp", None))
    in_specs = (
        tokens,
        sequences,
        sequences,
        tokens,
        P(),
        rows,
        rows,
        rows,
        P(),
        P(),
        columns,
        P(),
        rows,
        rows,
        columns,
    )
    out_specs = (
        tokens,
        P(),
        tokens,
        P(),
        rows,
        rows,
        rows,
        P(),
        P(),
        columns,
        P(),
        rows,
        rows,
        columns,
    )
    return jax.shard_map(shards, mesh=mesh, in_specs=in_specs, out_specs=out_specs, check_vma=False)
```

```python
import functools

import jax
import jax.numpy as jnp
from jax import lax
from jax.experimental import pallas as pl
from jax.experimental.pallas import tpu as pltpu
from jax.sharding import PartitionSpec as P

D = 2048
HD = 128
WINDOW = 1024

EPS = 1e-06
THETA = 1000000.0
NEG = -1e30
VMEM = 56 * 1024 * 1024


def normalize_rows(values):
    factor = lax.rsqrt(jnp.mean(values * values, axis=-1, keepdims=True) + EPS)
    return (values * factor, factor)


def norm_back(grad, normed, factor, gain):
    scaled = grad * gain
    return factor * (scaled - normed * jnp.mean(scaled * normed, axis=-1, keepdims=True))


def contract_last(left, right):
    return lax.dot_general(
        left, right, (((1,), (1,)), ((), ())), preferred_element_type=jnp.float32
    )


def contract_first(left, right):
    return lax.dot_general(
        left, right, (((0,), (0,)), ((), ())), preferred_element_type=jnp.float32
    )


def dot(left, right):
    return jnp.dot(left, right, preferred_element_type=jnp.float32)


MESH = pl.DeviceIdType.MESH
PARTS = 2


def flip(index, mask):
    bit = 1
    while bit <= mask:
        if mask & bit:
            index = index + bit - 2 * bit * lax.rem(lax.div(index, bit), 2)
        bit *= 2
    return index


def chip_bits(size):
    bits = []
    bit = 2
    while bit < size:
        bits.append(bit)
        bit *= 2
    return bits


def orders(size):
    bits = chip_bits(size)
    return (bits, bits[::-1])


def mask_of(pattern, order):
    return sum(bit for i, bit in enumerate(order) if pattern >> i & 1)


def top(pattern):
    return pattern.bit_length() - 1


def greet(me, size):
    barrier = pltpu.get_barrier_semaphore()
    bits = [1] + chip_bits(size)
    for bit in bits:
        pl.semaphore_signal(
            barrier, inc=1, device_id={"fsdp": flip(me, bit)}, device_id_type=MESH
        )
    pl.semaphore_wait(barrier, len(bits))


def pick(part, pair):
    return pair[0] + part * (pair[1] - pair[0])


class Gather:
    def __init__(self, size, me, whole, sems, parts=PARTS, lane=lambda part: part):
        self.size, self.me, self.whole, self.parts, self.lane = (size, me, whole, parts, lane)
        self.chip_send, self.chip_recv, self.core_send, self.core_recv = sems
        self.steps = len(chip_bits(size))
        self.patterns = sorted(range(1 << self.steps), key=lambda m: (top(m), m))

    def order(self, part):
        return orders(self.size)[part % 2]

    def slot(self, part, pattern, sibling):
        return flip(self.me, mask_of(pattern, self.order(part)) + sibling)

    def chip_copy(self, part, step, pattern):
        block = self.whole.at[self.slot(part, pattern, 0), self.lane(part)]
        number = (1 << step) - 1 + pattern
        return pltpu.make_async_remote_copy(
            src_ref=block,
            dst_ref=block,
            send_sem=self.chip_send.at[part, number],
            recv_sem=self.chip_recv.at[part, number],
            device_id={"fsdp": flip(self.me, self.order(part)[step])},
            device_id_type=MESH,
        )

    def core_copy(self, part, pattern):
        block = self.whole.at[self.slot(part, pattern, 0), self.lane(part)]
        return pltpu.make_async_remote_copy(
            src_ref=block,
            dst_ref=block,
            send_sem=self.core_send.at[part, pattern],
            recv_sem=self.core_recv.at[part, pattern],
            device_id={"fsdp": flip(self.me, 1)},
            device_id_type=MESH,
        )

    def arrive(self, part, pattern):
        if pattern:
            step = top(pattern)
            self.chip_copy(part, step, pattern - (1 << step)).wait_recv()

    def forward(self, part, pattern):
        for step in range(top(pattern) + 1, self.steps):
            self.chip_copy(part, step, pattern).start()
        self.core_copy(part, pattern).start()

    def pairs(self, work):
        for pattern in self.patterns:
            for part in range(self.parts):
                self.arrive(part, pattern)
            for part in range(self.parts):
                self.forward(part, pattern)
            work([self.slot(part, pattern, 0) for part in range(self.parts)])
            for part in range(self.parts):
                self.core_copy(part, pattern).wait_recv()
            work([self.slot(part, pattern, 1) for part in range(self.parts)])

    def finish(self):
        for pattern in self.patterns:
            for part in range(self.parts):
                for step in range(top(pattern) + 1, self.steps):
                    self.chip_copy(part, step, pattern).wait_send()
                self.core_copy(part, pattern).wait_send()


def gather_semaphores(size, parts=PARTS):
    moves = max(1, size // 2 - 1)
    return [
        pltpu.SemaphoreType.DMA((parts, moves)),
        pltpu.SemaphoreType.DMA((parts, moves)),
        pltpu.SemaphoreType.DMA((parts, size // 2)),
        pltpu.SemaphoreType.DMA((parts, size // 2)),
    ]


def scatter_rows_in(size, me, made, held, sent, came, sems, partial, final, between=None):
    chip_send, chip_recv, core_send, core_recv = sems
    steps = len(chip_bits(size))
    order = [bits[::-1] for bits in orders(size)]
    first = lambda m: (m & -m).bit_length() - 1 if m else steps
    patterns = sorted(range(1 << steps), key=lambda m: (first(m), -bin(m).count("1"), m))
    place = {m: q for q, m in enumerate(patterns)}
    width = final.shape[-1]
    chunk = min(512, width)

    def slots(pattern, sibling):
        return [flip(me, mask_of(pattern, order[part]) + sibling) for part in range(PARTS)]

    def core_copy(part, q):
        return pltpu.make_async_remote_copy(
            src_ref=made.at[part, q],
            dst_ref=held.at[part, q],
            send_sem=core_send.at[part, q],
            recv_sem=core_recv.at[part, q],
            device_id={"fsdp": flip(me, 1)},
            device_id_type=MESH,
        )

    def chip_copy(part, q):
        return pltpu.make_async_remote_copy(
            src_ref=sent.at[part, q],
            dst_ref=came.at[part, q],
            send_sem=chip_send.at[part, q],
            recv_sem=chip_recv.at[part, q],
            device_id={"fsdp": flip(me, order[part][first(patterns[q])])},
            device_id_type=MESH,
        )

    def for_sibling(q):
        pair = slots(patterns[q], 1)

        @pl.loop(0, PARTS)
        def _(part):
            @pl.loop(0, width // chunk)
            def _(index):
                columns = pl.ds(pl.multiple_of(index * chunk, chunk), chunk)
                made[part, q, :, columns] = partial(part, pick(part, pair), columns).astype(
                    jnp.bfloat16
                )

        for part in range(PARTS):
            core_copy(part, q).start()

    def for_chips(q):
        pattern = patterns[q]
        pair = slots(pattern, 0)
        arrivals = [place[pattern | 1 << step] for step in range(first(pattern))]
        for part in range(PARTS):
            core_copy(part, q).wait_recv()
            for arrival in arrivals:
                chip_copy(part, arrival).wait_recv()

        @pl.loop(0, PARTS)
        def _(part):
            @pl.loop(0, width // chunk)
            def _(index):
                columns = pl.ds(pl.multiple_of(index * chunk, chunk), chunk)
                total = partial(part, pick(part, pair), columns)
                total = total + held[part, q, :, columns].astype(jnp.float32)
                for arrival in arrivals:
                    total = total + came[part, arrival, :, columns].astype(jnp.float32)
                if pattern:
                    sent[part, q, :, columns] = total.astype(jnp.bfloat16)
                else:
                    final[part, :, columns] = total

        if pattern:
            for part in range(PARTS):
                chip_copy(part, q).start()

    for_sibling(0)
    for q in range(len(patterns)):
        if q + 1 < len(patterns):
            for_sibling(q + 1)
        for_chips(q)
        if between:
            between(q + 1, len(patterns))
    for q in range(len(patterns)):
        for part in range(PARTS):
            core_copy(part, q).wait_send()
            if patterns[q]:
                chip_copy(part, q).wait_send()


def scatter_scratch(size, rows, width):
    held = size // 2
    moved = max(1, held - 1)
    return [
        pltpu.VMEM((PARTS, held, rows, width), jnp.bfloat16),
        pltpu.VMEM((PARTS, held, rows, width), jnp.bfloat16),
        pltpu.VMEM((PARTS, moved, rows, width), jnp.bfloat16),
        pltpu.VMEM((PARTS, moved, rows, width), jnp.bfloat16),
        pltpu.SemaphoreType.DMA((PARTS, moved)),
        pltpu.SemaphoreType.DMA((PARTS, moved)),
        pltpu.SemaphoreType.DMA((PARTS, held)),
        pltpu.SemaphoreType.DMA((PARTS, held)),
    ]


def gate_up_kernel(
    size, x_ref, wg_ref, wu_ref, x_out, gate_out, up_out, prod_out, whole, gate, up, prod, load, keep, store, *sems
):
    me = lax.axis_index("fsdp")
    hidden = wg_ref.shape[0]
    chunk = 256 if hidden % 256 == 0 else 128
    own = pltpu.make_async_copy(x_ref, whole.at[me], load)
    own.start()
    own.wait()
    greet(me, size)
    state = {"count": 0, "last": None}

    def stores(part, at):
        return [
            pltpu.make_async_copy(buffer.at[part], out.at[at, part], store.at[part, i])
            for i, (buffer, out) in enumerate(((gate, gate_out), (up, up_out), (prod, prod_out)))
        ]

    def work(pair):
        count, last = (state["count"], state["last"])
        for part in range(PARTS):
            pltpu.make_async_copy(
                whole.at[pair[part], part], x_out.at[pair[part], part], keep.at[part, count]
            ).start()

        @pl.loop(0, PARTS)
        def _(part):
            at = pick(part, pair)
            if last is not None:
                for copy in stores(part, pick(part, last)):
                    copy.wait()

            @pl.loop(0, hidden // chunk)
            def _(index):
                units = pl.ds(pl.multiple_of(index * chunk, chunk), chunk)
                rows = whole[at, part]
                gates = contract_last(rows, wg_ref[units, :])
                ups = contract_last(rows, wu_ref[units, :])
                gate[part, :, units] = gates
                up[part, :, units] = ups
                prod[part, :, units] = (gates * jax.nn.sigmoid(gates) * ups).astype(jnp.bfloat16)

            for copy in stores(part, at):
                copy.start()

        state["count"], state["last"] = (count + 1, pair)
        state.setdefault("all", []).append(pair)

    gather = Gather(size, me, whole, sems)
    gather.pairs(work)
    gather.finish()
    for part in range(PARTS):
        for copy in stores(part, state["last"][part]):
            copy.wait()
        for count, pair in enumerate(state["all"]):
            pltpu.make_async_copy(
                whole.at[pair[part], part], x_out.at[pair[part], part], keep.at[part, count]
            ).wait()


def gate_up(size, values, rows_gate, rows_up):
    own, width = values.shape
    rows, hidden = (own // PARTS, rows_gate.shape[0])
    any_space = pl.BlockSpec(memory_space=pl.ANY)
    vmem = pl.BlockSpec(memory_space=pltpu.VMEM)
    shape = lambda columns, kind: jax.ShapeDtypeStruct((size, PARTS, rows, columns), kind)
    outs = pl.pallas_call(
        functools.partial(gate_up_kernel, size),
        out_shape=(
            shape(width, jnp.bfloat16),
            shape(hidden, jnp.float32),
            shape(hidden, jnp.float32),
            shape(hidden, jnp.bfloat16),
        ),
        in_specs=[any_space, vmem, vmem],
        out_specs=(any_space,) * 4,
        scratch_shapes=[
            pltpu.VMEM((size, PARTS, rows, width), jnp.bfloat16),
            pltpu.VMEM((PARTS, rows, hidden), jnp.float32),
            pltpu.VMEM((PARTS, rows, hidden), jnp.float32),
            pltpu.VMEM((PARTS, rows, hidden), jnp.bfloat16),
            pltpu.SemaphoreType.DMA,
            pltpu.SemaphoreType.DMA((PARTS, size)),
            pltpu.SemaphoreType.DMA((PARTS, 3)),
            *gather_semaphores(size),
        ],
        compiler_params=pltpu.CompilerParams(
            collective_id=1, has_side_effects=True, vmem_limit_bytes=VMEM
        ),
        cost_estimate=pl.CostEstimate(
            flops=4 * size * own * width * hidden, bytes_accessed=200 * 1024 * 1024, transcendentals=0
        ),
        name="gate_up",
    )(values.reshape(PARTS, rows, width), rows_gate, rows_up)
    return tuple(out.reshape(size * own, -1) for out in outs)


def grad_hidden_kernel(
    size, x_ref, wd_ref, gate_in, up_in, x_out, dgate_out, dup_out, whole, gate, up, dprod, dgate, dup, load, keep, fetch, store, *sems
):
    me = lax.axis_index("fsdp")
    hidden = wd_ref.shape[0]
    chunk = 256 if hidden % 256 == 0 else 128
    own = pltpu.make_async_copy(x_ref, whole.at[me], load)
    own.start()
    own.wait()
    greet(me, size)
    state = {"count": 0, "last": None, "all": []}

    def stores(part, at):
        return [
            pltpu.make_async_copy(buffer.at[part], out.at[at, part], store.at[part, i])
            for i, (buffer, out) in enumerate(((dgate, dgate_out), (dup, dup_out)))
        ]

    def fetches(part, at):
        return [
            pltpu.make_async_copy(source.at[at, part], buffer, fetch.at[i])
            for i, (source, buffer) in enumerate(((gate_in, gate), (up_in, up)))
        ]

    def work(pair):
        count, last = (state["count"], state["last"])
        for part in range(PARTS):
            pltpu.make_async_copy(
                whole.at[pair[part], part], x_out.at[pair[part], part], keep.at[part, count]
            ).start()

        @pl.loop(0, PARTS)
        def _(part):
            at = pick(part, pair)
            for copy in fetches(part, at):
                copy.start()
            if last is not None:
                for copy in stores(part, pick(part, last)):
                    copy.wait()

            @pl.loop(0, hidden // chunk)
            def _(index):
                units = pl.ds(pl.multiple_of(index * chunk, chunk), chunk)
                dprod[:, units] = contract_last(whole[at, part], wd_ref[units, :])

            for copy in fetches(part, at):
                copy.wait()

            @pl.loop(0, hidden // chunk)
            def _(index):
                units = pl.ds(pl.multiple_of(index * chunk, chunk), chunk)
                gates, grads = (gate[:, units], dprod[:, units])
                sigmoid = jax.nn.sigmoid(gates)
                dgate[part, :, units] = (
                    grads * up[:, units] * sigmoid * (1.0 + gates * (1.0 - sigmoid))
                ).astype(jnp.bfloat16)
                dup[part, :, units] = (grads * (gates * sigmoid)).astype(jnp.bfloat16)

            for copy in stores(part, at):
                copy.start()

        state["count"], state["last"] = (count + 1, pair)
        state["all"].append(pair)

    gather = Gather(size, me, whole, sems)
    gather.pairs(work)
    gather.finish()
    for part in range(PARTS):
        for copy in stores(part, state["last"][part]):
            copy.wait()
        for count, pair in enumerate(state["all"]):
            pltpu.make_async_copy(
                whole.at[pair[part], part], x_out.at[pair[part], part], keep.at[part, count]
            ).wait()


def grad_hidden_units(size, values, rows_down, gate, up):
    own, width = values.shape
    rows, hidden = (own // PARTS, rows_down.shape[0])
    any_space = pl.BlockSpec(memory_space=pl.ANY)
    vmem = pl.BlockSpec(memory_space=pltpu.VMEM)
    shape = lambda columns, kind: jax.ShapeDtypeStruct((size, PARTS, rows, columns), kind)
    blocks = lambda array: array.reshape(size, PARTS, rows, hidden)
    outs = pl.pallas_call(
        functools.partial(grad_hidden_kernel, size),
        out_shape=(
            shape(width, jnp.bfloat16),
            shape(hidden, jnp.bfloat16),
            shape(hidden, jnp.bfloat16),
        ),
        in_specs=[any_space, vmem, any_space, any_space],
        out_specs=(any_space,) * 3,
        scratch_shapes=[
            pltpu.VMEM((size, PARTS, rows, width), jnp.bfloat16),
            pltpu.VMEM((rows, hidden), jnp.float32),
            pltpu.VMEM((rows, hidden), jnp.float32),
            pltpu.VMEM((rows, hidden), jnp.float32),
            pltpu.VMEM((PARTS, rows, hidden), jnp.bfloat16),
            pltpu.VMEM((PARTS, rows, hidden), jnp.bfloat16),
            pltpu.SemaphoreType.DMA,
            pltpu.SemaphoreType.DMA((PARTS, size)),
            pltpu.SemaphoreType.DMA((2,)),
            pltpu.SemaphoreType.DMA((PARTS, 2)),
            *gather_semaphores(size),
        ],
        compiler_params=pltpu.CompilerParams(
            collective_id=3, has_side_effects=True, vmem_limit_bytes=VMEM
        ),
        cost_estimate=pl.CostEstimate(
            flops=2 * size * own * width * hidden, bytes_accessed=200 * 1024 * 1024, transcendentals=0
        ),
        name="grad_hidden_units",
    )(values.reshape(PARTS, rows, width), rows_down, blocks(gate), blocks(up))
    return tuple(out.reshape(size * own, -1) for out in outs)


def sum_products_kernel(size, terms, *refs):
    lefts, rights, out = (refs[:terms], refs[terms : 2 * terms], refs[2 * terms])
    made, held, sent, came, *sems = refs[2 * terms + 1 :]
    me = lax.axis_index("fsdp")
    greet(me, size)

    def partial(part, slot, columns):
        return sum(
            dot(left[slot, part], right[:, columns]) for left, right in zip(lefts, rights)
        )

    scatter_rows_in(size, me, made, held, sent, came, sems, partial, out)


def sum_products(size, number, lefts, rights):
    total, hidden = lefts[0].shape
    width = rights[0].shape[1]
    rows = total // size // PARTS
    vmem = pl.BlockSpec(memory_space=pltpu.VMEM)
    terms = len(lefts)
    out = pl.pallas_call(
        functools.partial(sum_products_kernel, size, terms),
        out_shape=jax.ShapeDtypeStruct((PARTS, rows, width), jnp.float32),
        in_specs=[vmem] * (2 * terms),
        out_specs=vmem,
        scratch_shapes=scatter_scratch(size, rows, width),
        compiler_params=pltpu.CompilerParams(
            collective_id=number, has_side_effects=True, vmem_limit_bytes=VMEM
        ),
        cost_estimate=pl.CostEstimate(
            flops=2 * total * hidden * width * terms, bytes_accessed=200 * 1024 * 1024, transcendentals=0
        ),
        name="sum_products",
    )(*[left.reshape(size, PARTS, rows, hidden) for left in lefts], *rights)
    return out.reshape(PARTS * rows, width)


def enter_kernel(
    size, lanes, back, x_ref, w_ref, m_ref, c_ref,
    before, whole, mine, count, counts, loads, z_send, z_recv, x_send, x_recv, m_send, m_recv, c_send, c_recv, *sems
):
    me, z = (lax.axis_index("fsdp"), lax.axis_index("tp"))
    part_of = lambda device: pl.ds(
        pl.multiple_of(device * m_ref.shape[-1], m_ref.shape[-1]), m_ref.shape[-1]
    )
    local = [
        pltpu.make_async_copy(w_ref, whole.at[me, z], loads.at[0]),
        pltpu.make_async_copy(m_ref.at[me], mine.at[:, :, part_of(me)], loads.at[1]),
    ]
    for copy in local:
        copy.start()
    counts[me] = c_ref[...]
    barrier = pltpu.get_barrier_semaphore()
    peers = [{"fsdp": flip(me, other)} for other in range(1, size)]
    peers += [{"tp": lax.rem(z + hop, lanes)} for hop in range(1, lanes)]
    for peer in peers:
        pl.semaphore_signal(barrier, inc=1, device_id=peer, device_id_type=MESH)
    pl.semaphore_wait(barrier, len(peers))
    for copy in local:
        copy.wait()

    def lane(part):
        return lax.rem(z + lanes - part, lanes)

    def lane_copy(hop):
        return pltpu.make_async_remote_copy(
            src_ref=w_ref,
            dst_ref=whole.at[me, z],
            send_sem=z_send.at[hop - 1],
            recv_sem=z_recv.at[hop - 1],
            device_id={"tp": lax.rem(z + hop, lanes)},
            device_id_type=MESH,
        )

    def token_copy(hop):
        return pltpu.make_async_remote_copy(
            src_ref=x_ref if hop == 1 else before.at[hop - 2],
            dst_ref=before.at[hop - 1],
            send_sem=x_send.at[hop - 1],
            recv_sem=x_recv.at[hop - 1],
            device_id={"tp": lax.rem(z + 1, lanes)},
            device_id_type=MESH,
        )

    def unit_copy(other):
        peer = flip(me, other)
        return pltpu.make_async_remote_copy(
            src_ref=m_ref.at[peer],
            dst_ref=mine.at[:, :, part_of(me)],
            send_sem=m_send.at[other - 1],
            recv_sem=m_recv.at[other - 1],
            device_id={"fsdp": peer},
            device_id_type=MESH,
        )

    def count_copy(other):
        return pltpu.make_async_remote_copy(
            src_ref=c_ref,
            dst_ref=counts.at[me],
            send_sem=c_send.at[other - 1],
            recv_sem=c_recv.at[other - 1],
            device_id={"fsdp": flip(me, other)},
            device_id_type=MESH,
        )

    def send_tokens(hop):
        @pl.when((z >= hop - 1) & (z + 1 < lanes))
        def _():
            token_copy(hop).start()

    def take_tokens(hop):
        @pl.when(z >= hop)
        def _():
            token_copy(hop).wait_recv()

    gather = Gather(size, me, whole, sems, lanes, lane)
    gather.forward(0, 0)
    for hop in range(1, lanes):
        lane_copy(hop).start()
    send_tokens(1)
    for other in range(1, size):
        count_copy(other).start()
    events = [(part, pattern) for part in range(lanes) for pattern in gather.patterns]
    events.sort(key=lambda event: (2 * event[0] + top(event[1]) + 1, event))
    for part, pattern in events:
        if (part, pattern) != (0, 0):
            if pattern:
                gather.arrive(part, pattern)
            else:
                lane_copy(part).wait_recv()
            gather.forward(part, pattern)
        if (part, pattern) == (lanes - 1, 0):
            for hop in range(1, back):
                take_tokens(hop)
                send_tokens(hop + 1)
    for other in range(1, size):
        unit_copy(other).start()
    for other in range(1, size):
        count_copy(other).wait_recv()
    count[...] = sum(counts[other] for other in range(size))
    for part, pattern in events:
        gather.core_copy(part, pattern).wait_recv()
    for other in range(1, size):
        unit_copy(other).wait_recv()
    take_tokens(back)
    gather.finish()
    for hop in range(1, lanes):
        lane_copy(hop).wait_send()
    for other in range(1, size):
        unit_copy(other).wait_send()
        count_copy(other).wait_send()
    for hop in range(1, back + 1):

        @pl.when((z >= hop - 1) & (z + 1 < lanes))
        def _():
            token_copy(hop).wait_send()


def enter(size, lanes, back, values, weights, units, count):
    any_space = pl.BlockSpec(memory_space=pl.ANY)
    vmem = pl.BlockSpec(memory_space=pltpu.VMEM)
    _, kinds, rows, columns = units.shape
    others = pltpu.SemaphoreType.DMA((size - 1,))
    lane = pltpu.SemaphoreType.DMA((lanes - 1,))
    hop = pltpu.SemaphoreType.DMA((back,))
    return pl.pallas_call(
        functools.partial(enter_kernel, size, lanes, back),
        out_shape=(
            jax.ShapeDtypeStruct((back, *values.shape), values.dtype),
            jax.ShapeDtypeStruct((size, lanes, *weights.shape), weights.dtype),
            jax.ShapeDtypeStruct((kinds, rows, size * columns), units.dtype),
            jax.ShapeDtypeStruct(count.shape, count.dtype),
        ),
        in_specs=[any_space, any_space, any_space, vmem],
        out_specs=(any_space, any_space, any_space, vmem),
        scratch_shapes=[
            pltpu.VMEM((size, *count.shape), count.dtype),
            pltpu.SemaphoreType.DMA((2,)),
            lane,
            lane,
            hop,
            hop,
            others,
            others,
            others,
            others,
            *gather_semaphores(size, lanes),
        ],
        compiler_params=pltpu.CompilerParams(collective_id=5, has_side_effects=True),
        cost_estimate=pl.CostEstimate(flops=0, bytes_accessed=400 * 1024 * 1024, transcendentals=0),
        name="enter",
    )(values, weights, units, count)


def flow_kernel(size, lanes, terms, hops, *refs):
    lefts, rights = (refs[:terms], refs[terms : 2 * terms])
    at = 2 * terms + (1 if hops else 0)
    parts_in = refs[2 * terms] if hops else None
    out = refs[at]
    arrived = refs[at + 1] if hops else None
    at += 2 if hops else 1
    left, right, loads, made, held, sent, came, *rest = refs[at:]
    sems = rest[:4]
    me, z = (lax.axis_index("fsdp"), lax.axis_index("tp"))
    copies = [
        pltpu.make_async_copy(source, target.at[i], loads.at[j, i])
        for j, (sources, target) in enumerate(((lefts, left), (rights, right)))
        for i, source in enumerate(sources)
        if j or i < left.shape[0]
    ]
    for copy in copies:
        copy.start()
    barrier = pltpu.get_barrier_semaphore()
    peers = [{"fsdp": flip(me, bit)} for bit in [1] + chip_bits(size)]
    if hops:
        peers += [{"tp": lax.rem(z + 1, lanes)}, {"tp": lax.rem(z + lanes - 1, lanes)}]
    for peer in peers:
        pl.semaphore_signal(barrier, inc=1, device_id=peer, device_id_type=MESH)
    pl.semaphore_wait(barrier, len(peers))
    rows = left.shape[2] // size

    if hops:
        mixed, got, mix_sem, hop_send, hop_recv = rest[4:]

        def hop_copy(number):
            return pltpu.make_async_remote_copy(
                src_ref=mixed.at[number],
                dst_ref=got.at[number],
                send_sem=hop_send.at[number],
                recv_sem=hop_recv.at[number],
                device_id={"tp": lax.rem(z + lanes - 1, lanes)},
                device_id_type=MESH,
            )

        def hop(number):
            load = pltpu.make_async_copy(
                parts_in.at[hops - 1 - number], mixed.at[number], mix_sem.at[number]
            )
            load.start()
            load.wait()
            if number:

                @pl.when(z + 1 < lanes)
                def _():
                    hop_copy(number - 1).wait_recv()

                    @pl.loop(0, 2)
                    def _(kind):
                        total = mixed[number, kind].astype(jnp.float32)
                        total = total + got[number - 1, kind].astype(jnp.float32)
                        mixed[number, kind] = total.astype(jnp.bfloat16)

            @pl.when(z > 0)
            def _():
                hop_copy(number).start()

        hop(0)
    for copy in copies:
        copy.wait()

    def partial(part, slot, columns):
        block = left[part if left.shape[0] > 1 else 0, :, pl.ds(pl.multiple_of(slot * rows, rows), rows)]
        return contract_first(block, right[part, :, columns])

    def between(q, count):
        if hops:
            for number in range(1, hops):
                if q == number * count // hops:
                    hop(number)

    scatter_rows_in(size, me, made, held, sent, came, sems, partial, out, between)
    if hops:

        @pl.when(z + 1 < lanes)
        def _():
            hop_copy(hops - 1).wait_recv()
            arrived[...] = got[hops - 1]

        @pl.when(z + 1 == lanes)
        def _():
            arrived[...] = jnp.zeros_like(arrived)

        @pl.when(z > 0)
        def _():
            for number in range(hops):
                hop_copy(number).wait_send()


def flow(size, lanes, number, lefts, rights, parts_in=None):
    tokens, depth = lefts[0].shape
    width = rights[0].shape[1]
    any_space = pl.BlockSpec(memory_space=pl.ANY)
    vmem = pl.BlockSpec(memory_space=pltpu.VMEM)
    rows = depth // size
    hops = parts_in.shape[0] if parts_in is not None else 0
    distinct = 1 if lefts[0] is lefts[1] else PARTS
    out_shape = [jax.ShapeDtypeStruct((PARTS, rows, width), jnp.float32)]
    scratch = [
        pltpu.VMEM((distinct, tokens, depth), jnp.bfloat16),
        pltpu.VMEM((PARTS, tokens, width), jnp.bfloat16),
        pltpu.SemaphoreType.DMA((2, PARTS)),
        *scatter_scratch(size, rows, width),
    ]
    operands = [*lefts, *rights]
    if hops:
        out_shape.append(jax.ShapeDtypeStruct(parts_in.shape[1:], jnp.bfloat16))
        scratch += [
            pltpu.VMEM(parts_in.shape, jnp.bfloat16),
            pltpu.VMEM(parts_in.shape, jnp.bfloat16),
            pltpu.SemaphoreType.DMA((hops,)),
            pltpu.SemaphoreType.DMA((hops,)),
            pltpu.SemaphoreType.DMA((hops,)),
        ]
        operands.append(parts_in)
    return pl.pallas_call(
        functools.partial(flow_kernel, size, lanes, PARTS, hops),
        out_shape=tuple(out_shape),
        in_specs=[any_space] * len(operands),
        out_specs=(vmem,) * len(out_shape),
        scratch_shapes=scratch,
        compiler_params=pltpu.CompilerParams(
            collective_id=number, has_side_effects=True, vmem_limit_bytes=VMEM
        ),
        cost_estimate=pl.CostEstimate(
            flops=4 * tokens * depth * width, bytes_accessed=200 * 1024 * 1024, transcendentals=0
        ),
        name="flow",
    )(*operands)


def sum_small_kernel(size, lanes, x_ref, o_ref, came, send, recv):
    me, z = (lax.axis_index("fsdp"), lax.axis_index("tp"))
    peers = []
    for name, index, count in (("fsdp", me, size), ("tp", z, lanes)):
        bit = 1
        while bit < count:
            peers.append({name: flip(index, bit)})
            bit *= 2
    barrier = pltpu.get_barrier_semaphore()
    for peer in peers:
        pl.semaphore_signal(barrier, inc=1, device_id=peer, device_id_type=MESH)
    pl.semaphore_wait(barrier, len(peers))
    sent = came.shape[0] // 2
    came[sent] = x_ref[...]
    for step, peer in enumerate(peers):
        copy = pltpu.make_async_remote_copy(
            src_ref=came.at[sent + step],
            dst_ref=came.at[step],
            send_sem=send.at[step],
            recv_sem=recv.at[step],
            device_id=peer,
            device_id_type=MESH,
        )
        copy.start()
        copy.wait()
        came[sent + step + 1] = came[sent + step] + came[step]
    o_ref[...] = came[sent + len(peers)]


def sum_small(size, lanes, values):
    steps = (size * lanes).bit_length() - 1
    vmem = pl.BlockSpec(memory_space=pltpu.VMEM)
    return pl.pallas_call(
        functools.partial(sum_small_kernel, size, lanes),
        out_shape=jax.ShapeDtypeStruct(values.shape, values.dtype),
        in_specs=[vmem],
        out_specs=vmem,
        scratch_shapes=[
            pltpu.VMEM((2 * (steps + 1), *values.shape), values.dtype),
            pltpu.SemaphoreType.DMA((steps,)),
            pltpu.SemaphoreType.DMA((steps,)),
        ],
        compiler_params=pltpu.CompilerParams(collective_id=8, has_side_effects=True),
        name="sum_small",
    )(values)


def project_kernel(
    wq, wk, before_ref, x_ref, gain_ref, w_ref, n_ref, q_ref, k_ref, v_ref, normed
):
    back, own, _ = before_ref.shape
    lead = back * own
    tile = min(256, own)
    z = lax.axis_index("tp")

    @pl.when(pl.program_id(0) == 0)
    def _():
        for hop in range(back + 1):

            @pl.loop(0, own // tile)
            def _(index):
                span = pl.ds(pl.multiple_of(index * tile, tile), tile)
                values = x_ref[span, :] if hop == 0 else before_ref[hop - 1, span, :]
                values = normalize_rows(values.astype(jnp.float32))[0] * gain_ref[...]
                values = values.astype(jnp.bfloat16)
                if hop:
                    values = jnp.where(z >= hop, values, jnp.zeros_like(values))
                else:
                    n_ref[span, :] = values
                at = lead - hop * own + index * tile
                normed[pl.ds(pl.multiple_of(at, tile), tile), :] = values

    weights = lambda start, size: w_ref[:, 0, :, start : start + size].reshape(D, size)

    @pl.loop(0, (lead + own) // tile)
    def _(index):
        span = pl.ds(pl.multiple_of(index * tile, tile), tile)
        pair = dot(normed[span, :], weights(wq, 2 * wk))
        k_ref[span, :] = pair[:, :wk]
        v_ref[span, :] = pair[:, wk:].astype(jnp.bfloat16)

    @pl.loop(0, own // tile)
    def _(index):
        span = pl.ds(pl.multiple_of(index * tile, tile), tile)
        from_lead = pl.ds(pl.multiple_of(lead + index * tile, tile), tile)
        q_ref[span, :] = dot(normed[from_lead, :], weights(0, wq))


def project(before, values, gain, weights, wq, wk):
    size, parts, rows_in, columns = weights.shape
    back, own, _ = before.shape
    rows = (back + 1) * own
    whole = lambda *_: (0, 0)
    return pl.pallas_call(
        functools.partial(project_kernel, wq, wk),
        grid=(parts,),
        out_shape=(
            jax.ShapeDtypeStruct((own, D), jnp.bfloat16),
            jax.ShapeDtypeStruct((own, parts * wq), jnp.float32),
            jax.ShapeDtypeStruct((rows, parts * wk), jnp.float32),
            jax.ShapeDtypeStruct((rows, parts * wk), jnp.bfloat16),
        ),
        in_specs=[
            pl.BlockSpec((back, own, D), lambda z: (0, 0, 0)),
            pl.BlockSpec((own, D), whole),
            pl.BlockSpec((1, D), whole),
            pl.BlockSpec((size, 1, rows_in, wq + 2 * wk), lambda z: (0, z, 0, 0)),
        ],
        out_specs=(
            pl.BlockSpec((own, D), whole),
            pl.BlockSpec((own, wq), lambda z: (0, z)),
            pl.BlockSpec((rows, wk), lambda z: (0, z)),
            pl.BlockSpec((rows, wk), lambda z: (0, z)),
        ),
        scratch_shapes=[pltpu.VMEM((rows, D), jnp.bfloat16)],
        compiler_params=pltpu.CompilerParams(vmem_limit_bytes=VMEM),
        cost_estimate=pl.CostEstimate(
            flops=2 * D * parts * (own * wq + rows * 2 * wk),
            bytes_accessed=2 * D * parts * (wq + 2 * wk) + 2 * rows * D,
            transcendentals=0,
        ),
        name="project_in",
    )(before, values, gain.reshape(1, D), weights)


def out_kernel(a_ref, w_ref, x_ref, o_ref):
    parts, _, width = w_ref.shape[1:]
    total = x_ref[...].astype(jnp.float32)
    for z in range(parts):
        total += contract_last(a_ref[:, z * width : (z + 1) * width], w_ref[0, z])
    o_ref[...] = total


def project_out(attended, weights, states, wo):
    size, parts, rows, columns = weights.shape
    own = states.shape[0]
    last = columns // wo - 1
    return pl.pallas_call(
        out_kernel,
        grid=(size,),
        out_shape=jax.ShapeDtypeStruct(states.shape, jnp.float32),
        in_specs=[
            pl.BlockSpec(attended.shape, lambda f: (0, 0)),
            pl.BlockSpec((1, parts, rows, wo), lambda f: (f, 0, 0, last)),
            pl.BlockSpec((own, rows), lambda f: (0, f)),
        ],
        out_specs=pl.BlockSpec((own, rows), lambda f: (0, f)),
        compiler_params=pltpu.CompilerParams(vmem_limit_bytes=VMEM),
        cost_estimate=pl.CostEstimate(
            flops=2 * own * D * parts * wo, bytes_accessed=24 * 1024 * 1024, transcendentals=0
        ),
        name="project_out",
    )(attended, weights, states)


def back_out_kernel(g_ref, w_ref, o_ref):
    size, _, rows, width = w_ref.shape
    o_ref[...] = dot(g_ref[...], w_ref[:, 0].reshape(size * rows, width)).astype(jnp.bfloat16)


def back_out(grad, weights, wo):
    size, parts, rows, columns = weights.shape
    own = grad.shape[0]
    last = columns // wo - 1
    return pl.pallas_call(
        back_out_kernel,
        grid=(parts,),
        out_shape=jax.ShapeDtypeStruct((own, parts * wo), jnp.bfloat16),
        in_specs=[
            pl.BlockSpec(grad.shape, lambda z: (0, 0)),
            pl.BlockSpec((size, 1, rows, wo), lambda z: (0, z, 0, last)),
        ],
        out_specs=pl.BlockSpec((own, wo), lambda z: (0, z)),
        compiler_params=pltpu.CompilerParams(vmem_limit_bytes=VMEM),
        cost_estimate=pl.CostEstimate(
            flops=2 * own * D * parts * wo, bytes_accessed=16 * 1024 * 1024, transcendentals=0
        ),
        name="back_out",
    )(grad, weights)


def back_in_kernel(q_ref, k_ref, v_ref, w_ref, o_ref):
    parts = w_ref.shape[1]
    total = jnp.zeros(o_ref.shape, jnp.float32)
    for z in range(parts):
        start = 0
        for ref in (q_ref, k_ref, v_ref):
            width = ref.shape[1] // parts
            total += contract_last(
                ref[:, z * width : (z + 1) * width], w_ref[0, z, :, start : start + width]
            )
            start += width
    o_ref[...] = total


def back_in(grad_query, grad_key, grad_value, weights):
    size, parts, rows, _ = weights.shape
    own = grad_query.shape[0]
    columns = (grad_query.shape[1] + 2 * grad_key.shape[1]) // parts
    whole = lambda f: (0, 0)
    return pl.pallas_call(
        back_in_kernel,
        grid=(size,),
        out_shape=jax.ShapeDtypeStruct((own, D), jnp.float32),
        in_specs=[
            pl.BlockSpec(grad_query.shape, whole),
            pl.BlockSpec(grad_key.shape, whole),
            pl.BlockSpec(grad_value.shape, whole),
            pl.BlockSpec((1, parts, rows, columns), lambda f: (f, 0, 0, 0)),
        ],
        out_specs=pl.BlockSpec((own, rows), lambda f: (0, f)),
        compiler_params=pltpu.CompilerParams(vmem_limit_bytes=VMEM),
        cost_estimate=pl.CostEstimate(
            flops=2 * own * D * parts * columns, bytes_accessed=24 * 1024 * 1024, transcendentals=0
        ),
        name="back_in",
    )(grad_query, grad_key, grad_value, weights)


def turn(values, cosine, sine):
    return values * cosine + pltpu.roll(values, HD // 2, 1) * sine


def turn_back(grad, cosine, sine):
    return grad * cosine - pltpu.roll(grad, HD // 2, 1) * sine


def split_heads(block, group):
    return jnp.concatenate([block[:, i * HD : (i + 1) * HD] for i in range(group)], axis=0)


def join_heads(stacked, group):
    rows = stacked.shape[0] // group
    return jnp.concatenate([stacked[i * rows : (i + 1) * rows] for i in range(group)], axis=1)


def head_probs(query, keys, bias, group, scale):
    scores = contract_last(query, keys) * scale
    rows, span = scores.shape
    scores = (scores.reshape(group, rows // group, span) + bias[None]).reshape(rows, span)
    weights = jnp.exp(scores - jnp.max(scores, axis=-1, keepdims=True))
    return weights * (1.0 / jnp.sum(weights, axis=-1, keepdims=True))


def attend_kernel(
    group, step, lead, q_ref, k_ref, v_ref, bias_ref, cos_ref, sin_ref, nq_ref, nk_ref, o_ref, keys
):
    tile, span = bias_ref.shape
    scale = HD ** (-0.5)
    index = pl.program_id(1)

    @pl.when(index == 0)
    def _():
        normed = normalize_rows(k_ref[...])[0] * nk_ref[...]
        keys[...] = turn(normed, cos_ref[...], sin_ref[...]).astype(jnp.bfloat16)

    here = pl.ds(pl.multiple_of(lead + index * tile, tile), tile)
    cosine, sine = (cos_ref[here, :], sin_ref[here, :])
    normed = normalize_rows(split_heads(q_ref[...], group))[0] * nq_ref[...]
    cosine, sine = (jnp.concatenate([cosine] * group, 0), jnp.concatenate([sine] * group, 0))
    query = turn(normed, cosine, sine).astype(jnp.bfloat16)
    window = pl.ds(pl.multiple_of(index * step, tile), span)
    probs = head_probs(query, keys[window, :], bias_ref[...], group, scale)
    mixed = dot(probs.astype(jnp.bfloat16), v_ref[window, :])
    o_ref[...] = join_heads(mixed.astype(jnp.bfloat16), group)


def attend_back_kernel(
    group,
    step,
    lead,
    q_ref,
    k_ref,
    v_ref,
    bias_ref,
    cos_ref,
    sin_ref,
    nq_ref,
    nk_ref,
    do_ref,
    dq_ref,
    prev_ref,
    own_ref,
    gq_ref,
    gk_ref,
    keys,
    dk,
    dv,
):
    tile, span = bias_ref.shape
    scale = HD ** (-0.5)
    index = pl.program_id(1)

    @pl.when((pl.program_id(0) == 0) & (index == 0))
    def _():
        gq_ref[...] = jnp.zeros_like(gq_ref)
        gk_ref[...] = jnp.zeros_like(gk_ref)

    @pl.when(index == 0)
    def _():
        normed = normalize_rows(k_ref[...])[0] * nk_ref[...]
        keys[...] = turn(normed, cos_ref[...], sin_ref[...]).astype(jnp.bfloat16)
        dk[...] = jnp.zeros_like(dk)
        dv[...] = jnp.zeros_like(dv)

    here = pl.ds(pl.multiple_of(lead + index * tile, tile), tile)
    cosine, sine = (cos_ref[here, :], sin_ref[here, :])
    cosine, sine = (jnp.concatenate([cosine] * group, 0), jnp.concatenate([sine] * group, 0))
    normed, factor = normalize_rows(split_heads(q_ref[...], group))
    query = turn(normed * nq_ref[...], cosine, sine).astype(jnp.bfloat16)
    window = pl.ds(pl.multiple_of(index * step, tile), span)
    probs = head_probs(query, keys[window, :], bias_ref[...], group, scale)
    grad_out = split_heads(do_ref[...], group)
    dv[window, :] += contract_first(probs.astype(jnp.bfloat16), grad_out)
    grad_probs = contract_last(grad_out, v_ref[window, :])
    centre = jnp.sum(probs * grad_probs, axis=-1, keepdims=True)
    grad_scores = (probs * (grad_probs - centre)).astype(jnp.bfloat16)
    dk[window, :] += contract_first(grad_scores, query) * scale
    grad_query = turn_back(dot(grad_scores, keys[window, :]) * scale, cosine, sine)
    gq_ref[...] += jnp.sum(grad_query * normed, axis=0, keepdims=True)
    grad_raw = norm_back(grad_query, normed, factor, nq_ref[...])
    dq_ref[...] = join_heads(grad_raw.astype(jnp.bfloat16), group)

    @pl.when(index == pl.num_programs(1) - 1)
    def _():
        normed_key, key_factor = normalize_rows(k_ref[...])
        grad_key = turn_back(dk[...], cos_ref[...], sin_ref[...])
        gk_ref[...] += jnp.sum(grad_key * normed_key, axis=0, keepdims=True)
        grad_key = norm_back(grad_key, normed_key, key_factor, nk_ref[...])
        back, _, own, _ = prev_ref.shape
        for hop in range(back):
            rows = slice(lead - (hop + 1) * own, lead - hop * own)
            prev_ref[hop, 0] = grad_key[rows].astype(jnp.bfloat16)
            prev_ref[hop, 1] = dv[rows, :].astype(jnp.bfloat16)
        own_ref[0] = grad_key[lead:]
        own_ref[1] = dv[lead:, :]


def attention_specs(own, rows, group, tile, span):
    whole = lambda g, t: (0, 0)
    return [
        pl.BlockSpec((tile, group * HD), lambda g, t: (t, g)),
        pl.BlockSpec((rows, HD), lambda g, t: (0, g)),
        pl.BlockSpec((rows, HD), lambda g, t: (0, g)),
        pl.BlockSpec((tile, span), lambda g, t: (t, 0)),
        pl.BlockSpec((rows, HD), whole),
        pl.BlockSpec((rows, HD), whole),
        pl.BlockSpec((1, HD), whole),
        pl.BlockSpec((1, HD), whole),
    ]


def attend(queries, keys, values, bias, cosine, sine, norm_query, norm_key, tile, step):
    own, rows = (queries.shape[0], keys.shape[0])
    heads = keys.shape[1] // HD
    group = queries.shape[1] // keys.shape[1]
    span = bias.shape[1]
    return pl.pallas_call(
        functools.partial(attend_kernel, group, step, rows - own),
        grid=(heads, own // tile),
        out_shape=jax.ShapeDtypeStruct(queries.shape, jnp.bfloat16),
        in_specs=attention_specs(own, rows, group, tile, span),
        out_specs=pl.BlockSpec((tile, group * HD), lambda g, t: (t, g)),
        scratch_shapes=[pltpu.VMEM((rows, HD), jnp.bfloat16)],
        compiler_params=pltpu.CompilerParams(vmem_limit_bytes=VMEM),
        cost_estimate=pl.CostEstimate(
            flops=16 * own * span * queries.shape[1],
            bytes_accessed=4 * queries.size + 6 * keys.size,
            transcendentals=own * span * heads * group,
        ),
        name="attend",
    )(queries, keys, values, bias, cosine, sine, norm_query, norm_key)


def attend_back(
    queries, keys, values, bias, cosine, sine, norm_query, norm_key, grad, tile, step
):
    own, rows = (queries.shape[0], keys.shape[0])
    heads = keys.shape[1] // HD
    group = queries.shape[1] // keys.shape[1]
    span = bias.shape[1]
    lead = rows - own
    whole = lambda g, t: (0, 0)
    return pl.pallas_call(
        functools.partial(attend_back_kernel, group, step, lead),
        grid=(heads, own // tile),
        out_shape=(
            jax.ShapeDtypeStruct(queries.shape, jnp.bfloat16),
            jax.ShapeDtypeStruct((lead // own, 2, own, heads * HD), jnp.bfloat16),
            jax.ShapeDtypeStruct((2, own, heads * HD), jnp.float32),
            jax.ShapeDtypeStruct((1, HD), jnp.float32),
            jax.ShapeDtypeStruct((1, HD), jnp.float32),
        ),
        in_specs=attention_specs(own, rows, group, tile, span)
        + [pl.BlockSpec((tile, group * HD), lambda g, t: (t, g))],
        out_specs=(
            pl.BlockSpec((tile, group * HD), lambda g, t: (t, g)),
            pl.BlockSpec((lead // own, 2, own, HD), lambda g, t: (0, 0, 0, g)),
            pl.BlockSpec((2, own, HD), lambda g, t: (0, 0, g)),
            pl.BlockSpec((1, HD), whole),
            pl.BlockSpec((1, HD), whole),
        ),
        scratch_shapes=[
            pltpu.VMEM((rows, HD), jnp.bfloat16),
            pltpu.VMEM((rows, HD), jnp.float32),
            pltpu.VMEM((rows, HD), jnp.float32),
        ],
        compiler_params=pltpu.CompilerParams(vmem_limit_bytes=VMEM),
        cost_estimate=pl.CostEstimate(
            flops=40 * own * span * queries.shape[1],
            bytes_accessed=8 * queries.size + 16 * keys.size,
            transcendentals=own * span * heads * group,
        ),
        name="attend_back",
    )(queries, keys, values, bias, cosine, sine, norm_query, norm_key, grad)


def window_tables(length_row, pad_row, first, own, lead, tile, span):
    places = first - lead + jnp.arange(lead + own, dtype=jnp.int32)
    ends = jnp.cumsum(length_row)
    passed = places[:, None] >= ends[None, :]
    docs = jnp.sum(passed.astype(jnp.int32), axis=1)
    starts = jnp.sum(jnp.where(passed, length_row[None, :], 0), axis=1)
    freqs = THETA ** (-(jnp.arange(HD // 2).astype(jnp.float32) * 2.0 / HD))
    angles = (places - starts).astype(jnp.float32)[:, None] * freqs[None, :]
    cosine, sine = (jnp.cos(angles), jnp.sin(angles))
    padded = jnp.concatenate((jnp.zeros((lead,), pad_row.dtype), pad_row))
    live = lax.dynamic_slice_in_dim(padded, first, lead + own, 0)
    step = tile if lead + own > span else 0
    masks = []
    for index in range(own // tile):
        at = lead + index * tile
        query, key = (places[at : at + tile, None], places[None, index * step : index * step + span])
        same = docs[at : at + tile, None] == docs[None, index * step : index * step + span]
        seen = (live[None, index * step : index * step + span] == 1) | (key == query)
        masks.append((key >= 0) & (key <= query) & (query - key < WINDOW) & same & seen)
    bias = jnp.where(jnp.concatenate(masks, axis=0), 0.0, NEG).astype(jnp.float32)
    cosine = jnp.concatenate((cosine, cosine), axis=1)
    sine = jnp.concatenate((-sine, sine), axis=1)
    return (bias, cosine, sine, step, live[lead:].astype(jnp.float32))


def hidden_rows_grad(grad):
    mine = lax.psum_scatter(grad.astype(jnp.bfloat16), "tp", scatter_dimension=0, tiled=True)
    return lax.all_to_all(mine, "fsdp", 1, 0, tiled=True).astype(jnp.float32)


def over_lanes(grad):
    return lax.psum_scatter(
        grad.astype(jnp.bfloat16), "tp", scatter_dimension=2, tiled=True
    ).astype(jnp.float32)


def shards(
    states,
    lengths,
    padding,
    teacher,
    norm_attn,
    w_query,
    w_key,
    w_value,
    norm_query,
    norm_key,
    w_out,
    norm_mlp,
    w_gate,
    w_up,
    w_down,
):
    own = states.shape[0]
    n_tp, n_fsdp = (lax.axis_size("tp"), lax.axis_size("fsdp"))
    first = lax.axis_index("tp") * own
    back = min(n_tp - 1, -(-WINDOW // own))
    lead = back * own
    tile = min(256, own)
    span = WINDOW + tile if lead >= WINDOW else lead + own
    wq, wk = (w_query.shape[1], w_key.shape[1])
    bias, cosine, sine, step, live = window_tables(
        lengths[0], padding[0], first, own, lead, tile, span
    )
    joined = jnp.concatenate((w_query, w_key, w_value, w_out.T), axis=1)
    wo = w_out.shape[0]
    units = [
        part.reshape(n_fsdp, -1, part.shape[1]) for part in (w_gate.T, w_up.T, w_down)
    ]
    live_here = jnp.full((8, 128), jnp.sum(padding).astype(jnp.float32))
    before, weights_attn, mine, counts = enter(
        n_fsdp, n_tp, back, states, joined, jnp.stack(units, axis=1), live_here
    )
    count = counts[0, 0]
    rows_gate, rows_up, rows_down = [
        lax.all_gather(mine[i], "tp", axis=0, tiled=True) for i in range(3)
    ]
    normed_in, query_raw, key_raw, value = project(
        before, states, norm_attn, weights_attn, wq, wk
    )
    gains = (norm_query.reshape(1, HD), norm_key.reshape(1, HD))
    attended = attend(query_raw, key_raw, value, bias, cosine, sine, *gains, tile, step)
    inputs = states.astype(jnp.float32)
    hidden_one = project_out(attended, weights_attn, states, wo)
    normed_two, factor_two = normalize_rows(hidden_one)
    whole_two, gate, up, product = gate_up(
        n_fsdp, (normed_two * norm_mlp).astype(jnp.bfloat16), rows_gate, rows_up
    )
    outputs = hidden_one + sum_products(n_fsdp, 2, (product,), (rows_down,))
    errors = (outputs - teacher.astype(jnp.float32)) * live[:, None]
    squares = jnp.sum(errors * errors)
    grad_out = errors * (2.0 / (count * D))

    grad_whole, grad_gate, grad_up = grad_hidden_units(
        n_fsdp, grad_out.astype(jnp.bfloat16), rows_down, gate, up
    )
    by_unit = (
        contract_first(product, grad_whole).astype(jnp.bfloat16),
        contract_first(grad_gate, whole_two).astype(jnp.bfloat16),
        contract_first(grad_up, whole_two).astype(jnp.bfloat16),
    )
    by_unit, (grad_gate, grad_up) = lax.optimization_barrier((by_unit, (grad_gate, grad_up)))
    grad_mid = sum_products(n_fsdp, 4, (grad_gate, grad_up), (rows_gate, rows_up))
    grad_w_down, grad_w_gate, grad_w_up = [hidden_rows_grad(part) for part in by_unit]
    grad_norm_mlp = jnp.sum(grad_mid * normed_two, axis=0)
    grad_hidden = grad_out + norm_back(grad_mid, normed_two, factor_two, norm_mlp)

    grad_low_out = grad_hidden.astype(jnp.bfloat16)
    grad_attended = back_out(grad_low_out, weights_attn, wo)
    grad_query, grad_before, grad_own, grad_norm_query, grad_norm_key = attend_back(
        query_raw, key_raw, value, bias, cosine, sine, *gains, grad_attended, tile, step
    )
    sums_early, arrived = flow(
        n_fsdp, n_tp, 6, (normed_in, grad_low_out), (grad_query, attended), grad_before
    )
    grad_own = (grad_own + arrived.astype(jnp.float32)).astype(jnp.bfloat16)
    grad_key, grad_value = (grad_own[0], grad_own[1])
    (sums_late,) = flow(n_fsdp, n_tp, 7, (normed_in, normed_in), (grad_key, grad_value))
    grad_early, grad_late = (over_lanes(sums_early), over_lanes(sums_late))
    grad_low = back_in(grad_query, grad_key, grad_value, weights_attn)
    normed_one, factor_one = normalize_rows(inputs)
    grad_norm_attn = jnp.sum(grad_low * normed_one, axis=0)
    grad_input = grad_hidden + norm_back(grad_low, normed_one, factor_one, norm_attn)
    small = [grad_norm_attn, grad_norm_mlp, grad_norm_query[0], grad_norm_key[0]]
    small.append(jnp.full((HD,), squares))
    joined_small = jnp.concatenate(small).reshape(-1, HD)
    filled = joined_small.shape[0]
    joined_small = jnp.pad(joined_small, ((0, -filled % 8), (0, 0)))
    summed = sum_small(n_fsdp, n_tp, joined_small)[:filled].reshape(-1)
    grad_norm_attn, grad_norm_mlp = (summed[:D], summed[D : 2 * D])
    grad_norm_query, grad_norm_key = (summed[2 * D : 2 * D + HD], summed[2 * D + HD : 2 * D + 2 * HD])
    squares = summed[2 * D + 2 * HD]
    return (
        outputs,
        squares / (count * D),
        grad_input,
        grad_norm_attn,
        grad_early[0],
        grad_late[0],
        grad_late[1],
        grad_norm_query,
        grad_norm_key,
        grad_early[1].T,
        grad_norm_mlp,
        grad_w_gate.T,
        grad_w_up.T,
        grad_w_down,
    )


def solution(mesh):
    tokens = P(("fsdp", "tp"), None)
    rows, columns, sequences = (P("fsdp", "tp"), P("tp", "fsdp"), P("fsdp", None))
    in_specs = (
        tokens,
        sequences,
        sequences,
        tokens,
        P(),
        rows,
        rows,
        rows,
        P(),
        P(),
        columns,
        P(),
        rows,
        rows,
        columns,
    )
    out_specs = (
        tokens,
        P(),
        tokens,
        P(),
        rows,
        rows,
        rows,
        P(),
        P(),
        columns,
        P(),
        rows,
        rows,
        columns,
    )
    return jax.shard_map(shards, mesh=mesh, in_specs=in_specs, out_specs=out_specs, check_vma=False)
```

```python
import functools

import jax
import jax.numpy as jnp
from jax import lax
from jax.experimental import pallas as pl
from jax.experimental.pallas import tpu as pltpu
from jax.sharding import PartitionSpec as P

D = 2048
HD = 128
WINDOW = 1024

EPS = 1e-06
THETA = 1000000.0
NEG = -1e30
VMEM = 56 * 1024 * 1024


def normalize_rows(values):
    factor = lax.rsqrt(jnp.mean(values * values, axis=-1, keepdims=True) + EPS)
    return (values * factor, factor)


def norm_back(grad, normed, factor, gain):
    scaled = grad * gain
    return factor * (scaled - normed * jnp.mean(scaled * normed, axis=-1, keepdims=True))


def contract_last(left, right):
    return lax.dot_general(
        left, right, (((1,), (1,)), ((), ())), preferred_element_type=jnp.float32
    )


def contract_first(left, right):
    return lax.dot_general(
        left, right, (((0,), (0,)), ((), ())), preferred_element_type=jnp.float32
    )


def dot(left, right):
    return jnp.dot(left, right, preferred_element_type=jnp.float32)


MESH = pl.DeviceIdType.MESH
PARTS = 2


def flip(index, mask):
    bit = 1
    while bit <= mask:
        if mask & bit:
            index = index + bit - 2 * bit * lax.rem(lax.div(index, bit), 2)
        bit *= 2
    return index


def chip_bits(size):
    bits = []
    bit = 2
    while bit < size:
        bits.append(bit)
        bit *= 2
    return bits


def orders(size):
    bits = chip_bits(size)
    return (bits, bits[::-1])


def mask_of(pattern, order):
    return sum(bit for i, bit in enumerate(order) if pattern >> i & 1)


def top(pattern):
    return pattern.bit_length() - 1


def greet(me, size):
    barrier = pltpu.get_barrier_semaphore()
    bits = [1] + chip_bits(size)
    for bit in bits:
        pl.semaphore_signal(
            barrier, inc=1, device_id={"fsdp": flip(me, bit)}, device_id_type=MESH
        )
    pl.semaphore_wait(barrier, len(bits))


def pick(part, pair):
    return pair[0] + part * (pair[1] - pair[0])


class Gather:
    def __init__(self, size, me, whole, sems, parts=PARTS, lane=lambda part: part):
        self.size, self.me, self.whole, self.parts, self.lane = (size, me, whole, parts, lane)
        self.chip_send, self.chip_recv, self.core_send, self.core_recv = sems
        self.steps = len(chip_bits(size))
        self.patterns = sorted(range(1 << self.steps), key=lambda m: (top(m), m))

    def order(self, part):
        return orders(self.size)[part % 2]

    def slot(self, part, pattern, sibling):
        return flip(self.me, mask_of(pattern, self.order(part)) + sibling)

    def chip_copy(self, part, step, pattern):
        block = self.whole.at[self.slot(part, pattern, 0), self.lane(part)]
        number = (1 << step) - 1 + pattern
        return pltpu.make_async_remote_copy(
            src_ref=block,
            dst_ref=block,
            send_sem=self.chip_send.at[part, number],
            recv_sem=self.chip_recv.at[part, number],
            device_id={"fsdp": flip(self.me, self.order(part)[step])},
            device_id_type=MESH,
        )

    def core_copy(self, part, pattern):
        block = self.whole.at[self.slot(part, pattern, 0), self.lane(part)]
        return pltpu.make_async_remote_copy(
            src_ref=block,
            dst_ref=block,
            send_sem=self.core_send.at[part, pattern],
            recv_sem=self.core_recv.at[part, pattern],
            device_id={"fsdp": flip(self.me, 1)},
            device_id_type=MESH,
        )

    def arrive(self, part, pattern):
        if pattern:
            step = top(pattern)
            self.chip_copy(part, step, pattern - (1 << step)).wait_recv()

    def forward(self, part, pattern):
        for step in range(top(pattern) + 1, self.steps):
            self.chip_copy(part, step, pattern).start()
        self.core_copy(part, pattern).start()

    def pairs(self, work):
        for pattern in self.patterns:
            for part in range(self.parts):
                self.arrive(part, pattern)
            for part in range(self.parts):
                self.forward(part, pattern)
            work([self.slot(part, pattern, 0) for part in range(self.parts)])
            for part in range(self.parts):
                self.core_copy(part, pattern).wait_recv()
            work([self.slot(part, pattern, 1) for part in range(self.parts)])

    def finish(self):
        for pattern in self.patterns:
            for part in range(self.parts):
                for step in range(top(pattern) + 1, self.steps):
                    self.chip_copy(part, step, pattern).wait_send()
                self.core_copy(part, pattern).wait_send()


def gather_semaphores(size, parts=PARTS):
    moves = max(1, size // 2 - 1)
    return [
        pltpu.SemaphoreType.DMA((parts, moves)),
        pltpu.SemaphoreType.DMA((parts, moves)),
        pltpu.SemaphoreType.DMA((parts, size // 2)),
        pltpu.SemaphoreType.DMA((parts, size // 2)),
    ]


def scatter_steps(size, me, made, held, sent, came, sems, partial, final):
    chip_send, chip_recv, core_send, core_recv = sems
    steps = len(chip_bits(size))
    order = [bits[::-1] for bits in orders(size)]
    first = lambda m: (m & -m).bit_length() - 1 if m else steps
    patterns = sorted(range(1 << steps), key=lambda m: (first(m), -bin(m).count("1"), m))
    place = {m: q for q, m in enumerate(patterns)}
    width = final.shape[-1]
    chunk = min(512, width)

    def slots(pattern, sibling):
        return [flip(me, mask_of(pattern, order[part]) + sibling) for part in range(PARTS)]

    def core_copy(part, q):
        return pltpu.make_async_remote_copy(
            src_ref=made.at[part, q],
            dst_ref=held.at[part, q],
            send_sem=core_send.at[part, q],
            recv_sem=core_recv.at[part, q],
            device_id={"fsdp": flip(me, 1)},
            device_id_type=MESH,
        )

    def chip_copy(part, q):
        return pltpu.make_async_remote_copy(
            src_ref=sent.at[part, q],
            dst_ref=came.at[part, q],
            send_sem=chip_send.at[part, q],
            recv_sem=chip_recv.at[part, q],
            device_id={"fsdp": flip(me, order[part][first(patterns[q])])},
            device_id_type=MESH,
        )

    def for_sibling(q):
        pair = slots(patterns[q], 1)

        @pl.loop(0, PARTS)
        def _(part):
            @pl.loop(0, width // chunk)
            def _(index):
                columns = pl.ds(pl.multiple_of(index * chunk, chunk), chunk)
                made[part, q, :, columns] = partial(part, pick(part, pair), columns).astype(
                    jnp.bfloat16
                )

        for part in range(PARTS):
            core_copy(part, q).start()

    def for_chips(q):
        pattern = patterns[q]
        pair = slots(pattern, 0)
        arrivals = [place[pattern | 1 << step] for step in range(first(pattern))]
        for part in range(PARTS):
            core_copy(part, q).wait_recv()
            for arrival in arrivals:
                chip_copy(part, arrival).wait_recv()

        @pl.loop(0, PARTS)
        def _(part):
            @pl.loop(0, width // chunk)
            def _(index):
                columns = pl.ds(pl.multiple_of(index * chunk, chunk), chunk)
                total = partial(part, pick(part, pair), columns)
                total = total + held[part, q, :, columns].astype(jnp.float32)
                for arrival in arrivals:
                    total = total + came[part, arrival, :, columns].astype(jnp.float32)
                if pattern:
                    sent[part, q, :, columns] = total.astype(jnp.bfloat16)
                else:
                    final[part, :, columns] = total

        if pattern:
            for part in range(PARTS):
                chip_copy(part, q).start()

    def finish():
        for q in range(len(patterns)):
            for part in range(PARTS):
                core_copy(part, q).wait_send()
                if patterns[q]:
                    chip_copy(part, q).wait_send()

    calls = [functools.partial(for_sibling, 0)]
    for q in range(len(patterns)):
        if q + 1 < len(patterns):
            calls.append(functools.partial(for_sibling, q + 1))
        calls.append(functools.partial(for_chips, q))
    return (calls, finish)


def scatter_scratch(size, rows, width):
    held = size // 2
    moved = max(1, held - 1)
    return [
        pltpu.VMEM((PARTS, held, rows, width), jnp.bfloat16),
        pltpu.VMEM((PARTS, held, rows, width), jnp.bfloat16),
        pltpu.VMEM((PARTS, moved, rows, width), jnp.bfloat16),
        pltpu.VMEM((PARTS, moved, rows, width), jnp.bfloat16),
        pltpu.SemaphoreType.DMA((PARTS, moved)),
        pltpu.SemaphoreType.DMA((PARTS, moved)),
        pltpu.SemaphoreType.DMA((PARTS, held)),
        pltpu.SemaphoreType.DMA((PARTS, held)),
    ]


def gate_up_kernel(
    size, x_ref, wg_ref, wu_ref, x_out, gate_out, up_out, prod_out, whole, gate, up, prod, load, keep, store, *sems
):
    me = lax.axis_index("fsdp")
    hidden = wg_ref.shape[0]
    chunk = 256 if hidden % 256 == 0 else 128
    own = pltpu.make_async_copy(x_ref, whole.at[me], load)
    own.start()
    own.wait()
    greet(me, size)
    state = {"count": 0, "last": None}

    def stores(part, at):
        return [
            pltpu.make_async_copy(buffer.at[part], out.at[at, part], store.at[part, i])
            for i, (buffer, out) in enumerate(((gate, gate_out), (up, up_out), (prod, prod_out)))
        ]

    def work(pair):
        count, last = (state["count"], state["last"])
        for part in range(PARTS):
            pltpu.make_async_copy(
                whole.at[pair[part], part], x_out.at[pair[part], part], keep.at[part, count]
            ).start()

        @pl.loop(0, PARTS)
        def _(part):
            at = pick(part, pair)
            if last is not None:
                for copy in stores(part, pick(part, last)):
                    copy.wait()

            @pl.loop(0, hidden // chunk)
            def _(index):
                units = pl.ds(pl.multiple_of(index * chunk, chunk), chunk)
                rows = whole[at, part]
                gates = contract_last(rows, wg_ref[units, :])
                ups = contract_last(rows, wu_ref[units, :])
                gate[part, :, units] = gates
                up[part, :, units] = ups
                prod[part, :, units] = (gates * jax.nn.sigmoid(gates) * ups).astype(jnp.bfloat16)

            for copy in stores(part, at):
                copy.start()

        state["count"], state["last"] = (count + 1, pair)
        state.setdefault("all", []).append(pair)

    gather = Gather(size, me, whole, sems)
    gather.pairs(work)
    gather.finish()
    for part in range(PARTS):
        for copy in stores(part, state["last"][part]):
            copy.wait()
        for count, pair in enumerate(state["all"]):
            pltpu.make_async_copy(
                whole.at[pair[part], part], x_out.at[pair[part], part], keep.at[part, count]
            ).wait()


def gate_up(size, values, rows_gate, rows_up):
    own, width = values.shape
    rows, hidden = (own // PARTS, rows_gate.shape[0])
    any_space = pl.BlockSpec(memory_space=pl.ANY)
    vmem = pl.BlockSpec(memory_space=pltpu.VMEM)
    shape = lambda columns, kind: jax.ShapeDtypeStruct((size, PARTS, rows, columns), kind)
    outs = pl.pallas_call(
        functools.partial(gate_up_kernel, size),
        out_shape=(
            shape(width, jnp.bfloat16),
            shape(hidden, jnp.float32),
            shape(hidden, jnp.float32),
            shape(hidden, jnp.bfloat16),
        ),
        in_specs=[any_space, vmem, vmem],
        out_specs=(any_space,) * 4,
        scratch_shapes=[
            pltpu.VMEM((size, PARTS, rows, width), jnp.bfloat16),
            pltpu.VMEM((PARTS, rows, hidden), jnp.float32),
            pltpu.VMEM((PARTS, rows, hidden), jnp.float32),
            pltpu.VMEM((PARTS, rows, hidden), jnp.bfloat16),
            pltpu.SemaphoreType.DMA,
            pltpu.SemaphoreType.DMA((PARTS, size)),
            pltpu.SemaphoreType.DMA((PARTS, 3)),
            *gather_semaphores(size),
        ],
        compiler_params=pltpu.CompilerParams(
            collective_id=1, has_side_effects=True, vmem_limit_bytes=VMEM
        ),
        cost_estimate=pl.CostEstimate(
            flops=4 * size * own * width * hidden, bytes_accessed=200 * 1024 * 1024, transcendentals=0
        ),
        name="gate_up",
    )(values.reshape(PARTS, rows, width), rows_gate, rows_up)
    return tuple(out.reshape(size * own, -1) for out in outs)


def grad_hidden_kernel(
    size, x_ref, wd_ref, gate_in, up_in, x_out, dgate_out, dup_out, whole, gate, up, dprod, dgate, dup, load, keep, fetch, store, *sems
):
    me = lax.axis_index("fsdp")
    hidden = wd_ref.shape[0]
    chunk = 256 if hidden % 256 == 0 else 128
    own = pltpu.make_async_copy(x_ref, whole.at[me], load)
    own.start()
    own.wait()
    greet(me, size)
    state = {"count": 0, "last": None, "all": []}

    def stores(part, at):
        return [
            pltpu.make_async_copy(buffer.at[part], out.at[at, part], store.at[part, i])
            for i, (buffer, out) in enumerate(((dgate, dgate_out), (dup, dup_out)))
        ]

    def fetches(part, at):
        return [
            pltpu.make_async_copy(source.at[at, part], buffer, fetch.at[i])
            for i, (source, buffer) in enumerate(((gate_in, gate), (up_in, up)))
        ]

    def work(pair):
        count, last = (state["count"], state["last"])
        for part in range(PARTS):
            pltpu.make_async_copy(
                whole.at[pair[part], part], x_out.at[pair[part], part], keep.at[part, count]
            ).start()

        @pl.loop(0, PARTS)
        def _(part):
            at = pick(part, pair)
            for copy in fetches(part, at):
                copy.start()
            if last is not None:
                for copy in stores(part, pick(part, last)):
                    copy.wait()

            @pl.loop(0, hidden // chunk)
            def _(index):
                units = pl.ds(pl.multiple_of(index * chunk, chunk), chunk)
                dprod[:, units] = contract_last(whole[at, part], wd_ref[units, :])

            for copy in fetches(part, at):
                copy.wait()

            @pl.loop(0, hidden // chunk)
            def _(index):
                units = pl.ds(pl.multiple_of(index * chunk, chunk), chunk)
                gates, grads = (gate[:, units], dprod[:, units])
                sigmoid = jax.nn.sigmoid(gates)
                dgate[part, :, units] = (
                    grads * up[:, units] * sigmoid * (1.0 + gates * (1.0 - sigmoid))
                ).astype(jnp.bfloat16)
                dup[part, :, units] = (grads * (gates * sigmoid)).astype(jnp.bfloat16)

            for copy in stores(part, at):
                copy.start()

        state["count"], state["last"] = (count + 1, pair)
        state["all"].append(pair)

    gather = Gather(size, me, whole, sems)
    gather.pairs(work)
    gather.finish()
    for part in range(PARTS):
        for copy in stores(part, state["last"][part]):
            copy.wait()
        for count, pair in enumerate(state["all"]):
            pltpu.make_async_copy(
                whole.at[pair[part], part], x_out.at[pair[part], part], keep.at[part, count]
            ).wait()


def grad_hidden_units(size, values, rows_down, gate, up):
    own, width = values.shape
    rows, hidden = (own // PARTS, rows_down.shape[0])
    any_space = pl.BlockSpec(memory_space=pl.ANY)
    vmem = pl.BlockSpec(memory_space=pltpu.VMEM)
    shape = lambda columns, kind: jax.ShapeDtypeStruct((size, PARTS, rows, columns), kind)
    blocks = lambda array: array.reshape(size, PARTS, rows, hidden)
    outs = pl.pallas_call(
        functools.partial(grad_hidden_kernel, size),
        out_shape=(
            shape(width, jnp.bfloat16),
            shape(hidden, jnp.bfloat16),
            shape(hidden, jnp.bfloat16),
        ),
        in_specs=[any_space, vmem, any_space, any_space],
        out_specs=(any_space,) * 3,
        scratch_shapes=[
            pltpu.VMEM((size, PARTS, rows, width), jnp.bfloat16),
            pltpu.VMEM((rows, hidden), jnp.float32),
            pltpu.VMEM((rows, hidden), jnp.float32),
            pltpu.VMEM((rows, hidden), jnp.float32),
            pltpu.VMEM((PARTS, rows, hidden), jnp.bfloat16),
            pltpu.VMEM((PARTS, rows, hidden), jnp.bfloat16),
            pltpu.SemaphoreType.DMA,
            pltpu.SemaphoreType.DMA((PARTS, size)),
            pltpu.SemaphoreType.DMA((2,)),
            pltpu.SemaphoreType.DMA((PARTS, 2)),
            *gather_semaphores(size),
        ],
        compiler_params=pltpu.CompilerParams(
            collective_id=3, has_side_effects=True, vmem_limit_bytes=VMEM
        ),
        cost_estimate=pl.CostEstimate(
            flops=2 * size * own * width * hidden, bytes_accessed=200 * 1024 * 1024, transcendentals=0
        ),
        name="grad_hidden_units",
    )(values.reshape(PARTS, rows, width), rows_down, blocks(gate), blocks(up))
    return tuple(out.reshape(size * own, -1) for out in outs)


def sum_products_kernel(size, terms, *refs):
    lefts, rights, out = (refs[:terms], refs[terms : 2 * terms], refs[2 * terms])
    made, held, sent, came, *sems = refs[2 * terms + 1 :]
    me = lax.axis_index("fsdp")
    greet(me, size)

    def partial(part, slot, columns):
        return sum(
            dot(left[slot, part], right[:, columns]) for left, right in zip(lefts, rights)
        )

    calls, finish = scatter_steps(size, me, made, held, sent, came, sems, partial, out)
    for call in calls:
        call()
    finish()


def sum_products(size, number, lefts, rights):
    total, hidden = lefts[0].shape
    width = rights[0].shape[1]
    rows = total // size // PARTS
    vmem = pl.BlockSpec(memory_space=pltpu.VMEM)
    terms = len(lefts)
    out = pl.pallas_call(
        functools.partial(sum_products_kernel, size, terms),
        out_shape=jax.ShapeDtypeStruct((PARTS, rows, width), jnp.float32),
        in_specs=[vmem] * (2 * terms),
        out_specs=vmem,
        scratch_shapes=scatter_scratch(size, rows, width),
        compiler_params=pltpu.CompilerParams(
            collective_id=number, has_side_effects=True, vmem_limit_bytes=VMEM
        ),
        cost_estimate=pl.CostEstimate(
            flops=2 * total * hidden * width * terms, bytes_accessed=200 * 1024 * 1024, transcendentals=0
        ),
        name="sum_products",
    )(*[left.reshape(size, PARTS, rows, hidden) for left in lefts], *rights)
    return out.reshape(PARTS * rows, width)


def enter_kernel(
    size, lanes, back, x_ref, w_ref, m_ref, c_ref,
    before, whole, mine, count, counts, loads, z_send, z_recv, x_send, x_recv, m_send, m_recv, c_send, c_recv, *sems
):
    me, z = (lax.axis_index("fsdp"), lax.axis_index("tp"))
    part_of = lambda device: pl.ds(
        pl.multiple_of(device * m_ref.shape[-1], m_ref.shape[-1]), m_ref.shape[-1]
    )
    local = [
        pltpu.make_async_copy(w_ref, whole.at[me, z], loads.at[0]),
        pltpu.make_async_copy(m_ref.at[me], mine.at[:, :, part_of(me)], loads.at[1]),
    ]
    for copy in local:
        copy.start()
    counts[me] = c_ref[...]
    barrier = pltpu.get_barrier_semaphore()
    peers = [{"fsdp": flip(me, other)} for other in range(1, size)]
    peers += [{"tp": lax.rem(z + hop, lanes)} for hop in range(1, lanes)]
    for peer in peers:
        pl.semaphore_signal(barrier, inc=1, device_id=peer, device_id_type=MESH)
    pl.semaphore_wait(barrier, len(peers))
    for copy in local:
        copy.wait()

    def lane(part):
        return lax.rem(z + lanes - part, lanes)

    def lane_copy(hop):
        return pltpu.make_async_remote_copy(
            src_ref=w_ref,
            dst_ref=whole.at[me, z],
            send_sem=z_send.at[hop - 1],
            recv_sem=z_recv.at[hop - 1],
            device_id={"tp": lax.rem(z + hop, lanes)},
            device_id_type=MESH,
        )

    def token_copy(hop):
        return pltpu.make_async_remote_copy(
            src_ref=x_ref if hop == 1 else before.at[hop - 2],
            dst_ref=before.at[hop - 1],
            send_sem=x_send.at[hop - 1],
            recv_sem=x_recv.at[hop - 1],
            device_id={"tp": lax.rem(z + 1, lanes)},
            device_id_type=MESH,
        )

    def unit_copy(other):
        peer = flip(me, other)
        return pltpu.make_async_remote_copy(
            src_ref=m_ref.at[peer],
            dst_ref=mine.at[:, :, part_of(me)],
            send_sem=m_send.at[other - 1],
            recv_sem=m_recv.at[other - 1],
            device_id={"fsdp": peer},
            device_id_type=MESH,
        )

    def count_copy(other):
        return pltpu.make_async_remote_copy(
            src_ref=c_ref,
            dst_ref=counts.at[me],
            send_sem=c_send.at[other - 1],
            recv_sem=c_recv.at[other - 1],
            device_id={"fsdp": flip(me, other)},
            device_id_type=MESH,
        )

    def send_tokens(hop):
        @pl.when((z >= hop - 1) & (z + 1 < lanes))
        def _():
            token_copy(hop).start()

    def take_tokens(hop):
        @pl.when(z >= hop)
        def _():
            token_copy(hop).wait_recv()

    gather = Gather(size, me, whole, sems, lanes, lane)
    gather.forward(0, 0)
    for hop in range(1, lanes):
        lane_copy(hop).start()
    send_tokens(1)
    for other in range(1, size):
        count_copy(other).start()
    events = [(part, pattern) for part in range(lanes) for pattern in gather.patterns]
    events.sort(key=lambda event: (2 * event[0] + top(event[1]) + 1, event))
    for part, pattern in events:
        if (part, pattern) != (0, 0):
            if pattern:
                gather.arrive(part, pattern)
            else:
                lane_copy(part).wait_recv()
            gather.forward(part, pattern)
        if (part, pattern) == (lanes - 1, 0):
            for hop in range(1, back):
                take_tokens(hop)
                send_tokens(hop + 1)
    for other in range(1, size):
        unit_copy(other).start()
    for other in range(1, size):
        count_copy(other).wait_recv()
    count[...] = sum(counts[other] for other in range(size))
    for part, pattern in events:
        gather.core_copy(part, pattern).wait_recv()
    for other in range(1, size):
        unit_copy(other).wait_recv()
    take_tokens(back)
    gather.finish()
    for hop in range(1, lanes):
        lane_copy(hop).wait_send()
    for other in range(1, size):
        unit_copy(other).wait_send()
        count_copy(other).wait_send()
    for hop in range(1, back + 1):

        @pl.when((z >= hop - 1) & (z + 1 < lanes))
        def _():
            token_copy(hop).wait_send()


def enter(size, lanes, back, values, weights, units, count):
    any_space = pl.BlockSpec(memory_space=pl.ANY)
    vmem = pl.BlockSpec(memory_space=pltpu.VMEM)
    _, kinds, rows, columns = units.shape
    others = pltpu.SemaphoreType.DMA((size - 1,))
    lane = pltpu.SemaphoreType.DMA((lanes - 1,))
    hop = pltpu.SemaphoreType.DMA((back,))
    return pl.pallas_call(
        functools.partial(enter_kernel, size, lanes, back),
        out_shape=(
            jax.ShapeDtypeStruct((back, *values.shape), values.dtype),
            jax.ShapeDtypeStruct((size, lanes, *weights.shape), weights.dtype),
            jax.ShapeDtypeStruct((kinds, rows, size * columns), units.dtype),
            jax.ShapeDtypeStruct(count.shape, count.dtype),
        ),
        in_specs=[any_space, any_space, any_space, vmem],
        out_specs=(any_space, any_space, any_space, vmem),
        scratch_shapes=[
            pltpu.VMEM((size, *count.shape), count.dtype),
            pltpu.SemaphoreType.DMA((2,)),
            lane,
            lane,
            hop,
            hop,
            others,
            others,
            others,
            others,
            *gather_semaphores(size, lanes),
        ],
        compiler_params=pltpu.CompilerParams(collective_id=5, has_side_effects=True),
        cost_estimate=pl.CostEstimate(flops=0, bytes_accessed=400 * 1024 * 1024, transcendentals=0),
        name="enter",
    )(values, weights, units, count)


def sum_query_kernel(
    size, left_ref, right_ref, *refs
):
    units, (out, back), (left, right, loads, u_send, u_recv, u_own) = (refs[:3], refs[3:5], refs[5:11])
    made, held, sent, came, *sems = refs[11:]
    me = lax.axis_index("fsdp")
    width, span = (out.shape[-1], back.shape[-1])
    rows = left.shape[1] // size
    copies = [pltpu.make_async_copy(left_ref, left, loads.at[PARTS])]
    copies += [
        pltpu.make_async_copy(
            right_ref.at[:, pl.ds(part * width, width)], right.at[part], loads.at[part]
        )
        for part in range(PARTS)
    ]
    part_of = lambda device: pl.ds(pl.multiple_of(device * span, span), span)
    copies += [
        pltpu.make_async_copy(unit.at[:, part_of(me)], back.at[me, kind], u_own.at[kind])
        for kind, unit in enumerate(units)
    ]
    for copy in copies:
        copy.start()
    barrier = pltpu.get_barrier_semaphore()
    for other in range(1, size):
        pl.semaphore_signal(
            barrier, inc=1, device_id={"fsdp": flip(me, other)}, device_id_type=MESH
        )
    pl.semaphore_wait(barrier, size - 1)
    for copy in copies:
        copy.wait()

    def unit_copy(other, kind):
        peer = flip(me, other)
        return pltpu.make_async_remote_copy(
            src_ref=units[kind].at[:, part_of(peer)],
            dst_ref=back.at[me, kind],
            send_sem=u_send.at[other - 1, kind],
            recv_sem=u_recv.at[other - 1, kind],
            device_id={"fsdp": peer},
            device_id_type=MESH,
        )

    def partial(part, slot, columns):
        block = left[:, pl.ds(pl.multiple_of(slot * rows, rows), rows)]
        return contract_first(block, right[part, :, columns])

    calls, finish = scatter_steps(size, me, made, held, sent, came, sems, partial, out)
    for number, call in enumerate(calls):
        call()
        if number == len(calls) // 2:
            for other in range(1, size):
                for kind in range(3):
                    unit_copy(other, kind).start()
    for other in range(1, size):
        for kind in range(3):
            unit_copy(other, kind).wait()
    finish()


def sum_query(size, left, right, units):
    tokens, depth = left.shape
    width = right.shape[1] // PARTS
    rows = depth // size
    any_space = pl.BlockSpec(memory_space=pl.ANY)
    vmem = pl.BlockSpec(memory_space=pltpu.VMEM)
    return pl.pallas_call(
        functools.partial(sum_query_kernel, size),
        out_shape=(
            jax.ShapeDtypeStruct((PARTS, rows, width), jnp.float32),
            jax.ShapeDtypeStruct((size, 3, units[0].shape[0], rows), jnp.bfloat16),
        ),
        in_specs=[any_space] * 5,
        out_specs=(vmem, any_space),
        scratch_shapes=[
            pltpu.VMEM((tokens, depth), jnp.bfloat16),
            pltpu.VMEM((PARTS, tokens, width), jnp.bfloat16),
            pltpu.SemaphoreType.DMA((PARTS + 1,)),
            pltpu.SemaphoreType.DMA((size - 1, 3)),
            pltpu.SemaphoreType.DMA((size - 1, 3)),
            pltpu.SemaphoreType.DMA((3,)),
            *scatter_scratch(size, rows, width),
        ],
        compiler_params=pltpu.CompilerParams(
            collective_id=6, has_side_effects=True, vmem_limit_bytes=VMEM
        ),
        cost_estimate=pl.CostEstimate(
            flops=4 * tokens * depth * width, bytes_accessed=100 * 1024 * 1024, transcendentals=0
        ),
        name="sum_query",
    )(left, right, *units)


def sum_key_kernel(size, left_ref, q_ref, kv_ref, w_ref, out, low, left, right, loads, tiles, fetch, *refs):
    made, held, sent, came, *sems = refs
    me = lax.axis_index("fsdp")
    rows = left.shape[1] // size
    parts, span = (w_ref.shape[1], tiles.shape[-1])
    copies = [pltpu.make_async_copy(left_ref, left, loads.at[PARTS])]
    copies += [
        pltpu.make_async_copy(kv_ref.at[part], right.at[part], loads.at[part])
        for part in range(PARTS)
    ]
    for copy in copies:
        copy.start()

    def tile_copy(f):
        return pltpu.make_async_copy(
            w_ref.at[f, :, :, pl.ds(0, span)], tiles.at[f % 2], fetch.at[f % 2]
        )

    tile_copy(0).start()
    greet(me, size)
    for copy in copies:
        copy.wait()

    def partial(part, slot, columns):
        block = left[:, pl.ds(pl.multiple_of(slot * rows, rows), rows)]
        return contract_first(block, right[part, :, columns])

    def low_columns(f):
        if f + 1 < size:
            tile_copy(f + 1).start()
        tile_copy(f).wait()
        half = low.shape[0] // 2

        @pl.loop(0, 2)
        def _(index):
            span_rows = pl.ds(pl.multiple_of(index * half, half), half)
            total = jnp.zeros((half, rows), jnp.float32)
            for z in range(parts):
                start = 0
                for source in (q_ref, right.at[0], right.at[1]):
                    width = source.shape[1] // parts
                    total += contract_last(
                        source[span_rows, z * width : (z + 1) * width],
                        tiles[f % 2, z, :, start : start + width],
                    )
                    start += width
            low[span_rows, f * rows : (f + 1) * rows] = total

    calls, finish = scatter_steps(size, me, made, held, sent, came, sems, partial, out)
    done = 0
    for number, call in enumerate(calls):
        call()
        goal = size * max(0, number - 1) // max(1, len(calls) - 3)
        while done < min(size, goal):
            low_columns(done)
            done += 1
    while done < size:
        low_columns(done)
        done += 1
    finish()


def sum_key(size, left, grad_query, grad_pair, weights):
    tokens, depth = left.shape
    width = grad_pair.shape[2]
    rows = depth // size
    parts = weights.shape[1]
    span = (grad_query.shape[1] + PARTS * width) // parts
    any_space = pl.BlockSpec(memory_space=pl.ANY)
    vmem = pl.BlockSpec(memory_space=pltpu.VMEM)
    return pl.pallas_call(
        functools.partial(sum_key_kernel, size),
        out_shape=(
            jax.ShapeDtypeStruct((PARTS, rows, width), jnp.float32),
            jax.ShapeDtypeStruct((tokens, depth), jnp.float32),
        ),
        in_specs=[any_space, vmem, any_space, any_space],
        out_specs=(vmem, vmem),
        scratch_shapes=[
            pltpu.VMEM((tokens, depth), jnp.bfloat16),
            pltpu.VMEM((PARTS, tokens, width), jnp.bfloat16),
            pltpu.SemaphoreType.DMA((PARTS + 1,)),
            pltpu.VMEM((2, parts, rows, span), jnp.bfloat16),
            pltpu.SemaphoreType.DMA((2,)),
            *scatter_scratch(size, rows, width),
        ],
        compiler_params=pltpu.CompilerParams(
            collective_id=7, has_side_effects=True, vmem_limit_bytes=VMEM
        ),
        cost_estimate=pl.CostEstimate(
            flops=8 * tokens * depth * width, bytes_accessed=100 * 1024 * 1024, transcendentals=0
        ),
        name="sum_key",
    )(left, grad_query, grad_pair, weights)


def sum_small_kernel(size, lanes, x_ref, o_ref, came, send, recv):
    me, z = (lax.axis_index("fsdp"), lax.axis_index("tp"))
    peers = []
    for name, index, count in (("fsdp", me, size), ("tp", z, lanes)):
        bit = 1
        while bit < count:
            peers.append({name: flip(index, bit)})
            bit *= 2
    barrier = pltpu.get_barrier_semaphore()
    for peer in peers:
        pl.semaphore_signal(barrier, inc=1, device_id=peer, device_id_type=MESH)
    pl.semaphore_wait(barrier, len(peers))
    sent = came.shape[0] // 2
    came[sent] = x_ref[...]
    for step, peer in enumerate(peers):
        copy = pltpu.make_async_remote_copy(
            src_ref=came.at[sent + step],
            dst_ref=came.at[step],
            send_sem=send.at[step],
            recv_sem=recv.at[step],
            device_id=peer,
            device_id_type=MESH,
        )
        copy.start()
        copy.wait()
        came[sent + step + 1] = came[sent + step] + came[step]
    o_ref[...] = came[sent + len(peers)]


def sum_small(size, lanes, values):
    steps = (size * lanes).bit_length() - 1
    vmem = pl.BlockSpec(memory_space=pltpu.VMEM)
    return pl.pallas_call(
        functools.partial(sum_small_kernel, size, lanes),
        out_shape=jax.ShapeDtypeStruct(values.shape, values.dtype),
        in_specs=[vmem],
        out_specs=vmem,
        scratch_shapes=[
            pltpu.VMEM((2 * (steps + 1), *values.shape), values.dtype),
            pltpu.SemaphoreType.DMA((steps,)),
            pltpu.SemaphoreType.DMA((steps,)),
        ],
        compiler_params=pltpu.CompilerParams(collective_id=8, has_side_effects=True),
        name="sum_small",
    )(values)


def project_kernel(
    wq, wk, before_ref, x_ref, gain_ref, w_ref, n_ref, q_ref, k_ref, v_ref, normed
):
    back, own, _ = before_ref.shape
    lead = back * own
    tile = min(256, own)
    z = lax.axis_index("tp")

    @pl.when(pl.program_id(0) == 0)
    def _():
        for hop in range(back + 1):

            @pl.loop(0, own // tile)
            def _(index):
                span = pl.ds(pl.multiple_of(index * tile, tile), tile)
                values = x_ref[span, :] if hop == 0 else before_ref[hop - 1, span, :]
                values = normalize_rows(values.astype(jnp.float32))[0] * gain_ref[...]
                values = values.astype(jnp.bfloat16)
                if hop:
                    values = jnp.where(z >= hop, values, jnp.zeros_like(values))
                else:
                    n_ref[span, :] = values
                at = lead - hop * own + index * tile
                normed[pl.ds(pl.multiple_of(at, tile), tile), :] = values

    weights = lambda start, size: w_ref[:, 0, :, start : start + size].reshape(D, size)

    @pl.loop(0, (lead + own) // tile)
    def _(index):
        span = pl.ds(pl.multiple_of(index * tile, tile), tile)
        pair = dot(normed[span, :], weights(wq, 2 * wk))
        k_ref[span, :] = pair[:, :wk]
        v_ref[span, :] = pair[:, wk:].astype(jnp.bfloat16)

    @pl.loop(0, own // tile)
    def _(index):
        span = pl.ds(pl.multiple_of(index * tile, tile), tile)
        from_lead = pl.ds(pl.multiple_of(lead + index * tile, tile), tile)
        q_ref[span, :] = dot(normed[from_lead, :], weights(0, wq))


def project(before, values, gain, weights, wq, wk):
    size, parts, rows_in, columns = weights.shape
    back, own, _ = before.shape
    rows = (back + 1) * own
    whole = lambda *_: (0, 0)
    return pl.pallas_call(
        functools.partial(project_kernel, wq, wk),
        grid=(parts,),
        out_shape=(
            jax.ShapeDtypeStruct((own, D), jnp.bfloat16),
            jax.ShapeDtypeStruct((own, parts * wq), jnp.float32),
            jax.ShapeDtypeStruct((rows, parts * wk), jnp.float32),
            jax.ShapeDtypeStruct((rows, parts * wk), jnp.bfloat16),
        ),
        in_specs=[
            pl.BlockSpec((back, own, D), lambda z: (0, 0, 0)),
            pl.BlockSpec((own, D), whole),
            pl.BlockSpec((1, D), whole),
            pl.BlockSpec((size, 1, rows_in, wq + 2 * wk), lambda z: (0, z, 0, 0)),
        ],
        out_specs=(
            pl.BlockSpec((own, D), whole),
            pl.BlockSpec((own, wq), lambda z: (0, z)),
            pl.BlockSpec((rows, wk), lambda z: (0, z)),
            pl.BlockSpec((rows, wk), lambda z: (0, z)),
        ),
        scratch_shapes=[pltpu.VMEM((rows, D), jnp.bfloat16)],
        compiler_params=pltpu.CompilerParams(vmem_limit_bytes=VMEM),
        cost_estimate=pl.CostEstimate(
            flops=2 * D * parts * (own * wq + rows * 2 * wk),
            bytes_accessed=2 * D * parts * (wq + 2 * wk) + 2 * rows * D,
            transcendentals=0,
        ),
        name="project_in",
    )(before, values, gain.reshape(1, D), weights)


def out_kernel(a_ref, w_ref, x_ref, o_ref):
    parts, _, width = w_ref.shape[1:]
    total = x_ref[...].astype(jnp.float32)
    for z in range(parts):
        total += contract_last(a_ref[:, z * width : (z + 1) * width], w_ref[0, z])
    o_ref[...] = total


def project_out(attended, weights, states, wo):
    size, parts, rows, columns = weights.shape
    own = states.shape[0]
    last = columns // wo - 1
    return pl.pallas_call(
        out_kernel,
        grid=(size,),
        out_shape=jax.ShapeDtypeStruct(states.shape, jnp.float32),
        in_specs=[
            pl.BlockSpec(attended.shape, lambda f: (0, 0)),
            pl.BlockSpec((1, parts, rows, wo), lambda f: (f, 0, 0, last)),
            pl.BlockSpec((own, rows), lambda f: (0, f)),
        ],
        out_specs=pl.BlockSpec((own, rows), lambda f: (0, f)),
        compiler_params=pltpu.CompilerParams(vmem_limit_bytes=VMEM),
        cost_estimate=pl.CostEstimate(
            flops=2 * own * D * parts * wo, bytes_accessed=24 * 1024 * 1024, transcendentals=0
        ),
        name="project_out",
    )(attended, weights, states)


def back_out_kernel(g_ref, w_ref, o_ref):
    size, _, rows, width = w_ref.shape
    o_ref[...] = dot(g_ref[...], w_ref[:, 0].reshape(size * rows, width)).astype(jnp.bfloat16)


def back_out(grad, weights, wo):
    size, parts, rows, columns = weights.shape
    own = grad.shape[0]
    last = columns // wo - 1
    return pl.pallas_call(
        back_out_kernel,
        grid=(parts,),
        out_shape=jax.ShapeDtypeStruct((own, parts * wo), jnp.bfloat16),
        in_specs=[
            pl.BlockSpec(grad.shape, lambda z: (0, 0)),
            pl.BlockSpec((size, 1, rows, wo), lambda z: (0, z, 0, last)),
        ],
        out_specs=pl.BlockSpec((own, wo), lambda z: (0, z)),
        compiler_params=pltpu.CompilerParams(vmem_limit_bytes=VMEM),
        cost_estimate=pl.CostEstimate(
            flops=2 * own * D * parts * wo, bytes_accessed=16 * 1024 * 1024, transcendentals=0
        ),
        name="back_out",
    )(grad, weights)


def turn(values, cosine, sine):
    return values * cosine + pltpu.roll(values, HD // 2, 1) * sine


def turn_back(grad, cosine, sine):
    return grad * cosine - pltpu.roll(grad, HD // 2, 1) * sine


def split_heads(block, group):
    return jnp.concatenate([block[:, i * HD : (i + 1) * HD] for i in range(group)], axis=0)


def join_heads(stacked, group):
    rows = stacked.shape[0] // group
    return jnp.concatenate([stacked[i * rows : (i + 1) * rows] for i in range(group)], axis=1)


def head_probs(query, keys, bias, group, scale):
    scores = contract_last(query, keys) * scale
    rows, span = scores.shape
    scores = (scores.reshape(group, rows // group, span) + bias[None]).reshape(rows, span)
    weights = jnp.exp(scores - jnp.max(scores, axis=-1, keepdims=True))
    return weights * (1.0 / jnp.sum(weights, axis=-1, keepdims=True))


def attend_kernel(
    group, step, lead, q_ref, k_ref, v_ref, bias_ref, cos_ref, sin_ref, nq_ref, nk_ref, o_ref, keys
):
    tile, span = bias_ref.shape
    scale = HD ** (-0.5)
    index = pl.program_id(1)

    @pl.when(index == 0)
    def _():
        normed = normalize_rows(k_ref[...])[0] * nk_ref[...]
        keys[...] = turn(normed, cos_ref[...], sin_ref[...]).astype(jnp.bfloat16)

    here = pl.ds(pl.multiple_of(lead + index * tile, tile), tile)
    cosine, sine = (cos_ref[here, :], sin_ref[here, :])
    normed = normalize_rows(split_heads(q_ref[...], group))[0] * nq_ref[...]
    cosine, sine = (jnp.concatenate([cosine] * group, 0), jnp.concatenate([sine] * group, 0))
    query = turn(normed, cosine, sine).astype(jnp.bfloat16)
    window = pl.ds(pl.multiple_of(index * step, tile), span)
    probs = head_probs(query, keys[window, :], bias_ref[...], group, scale)
    mixed = dot(probs.astype(jnp.bfloat16), v_ref[window, :])
    o_ref[...] = join_heads(mixed.astype(jnp.bfloat16), group)


def attend_back_kernel(
    group,
    step,
    lead,
    size,
    lanes,
    q_ref,
    k_ref,
    v_ref,
    bias_ref,
    cos_ref,
    sin_ref,
    nq_ref,
    nk_ref,
    do_ref,
    left_ref,
    right_ref,
    dq_ref,
    pair_ref,
    gq_ref,
    gk_ref,
    out_ref,
    keys,
    dk,
    dv,
    mixed,
    got,
    own_sum,
    left,
    right,
    loads,
    hop_send,
    hop_recv,
    *refs,
):
    made, held, sent, came, *sems = refs
    tile, span = bias_ref.shape
    scale = HD ** (-0.5)
    head, index = (pl.program_id(0), pl.program_id(1))
    heads, tiles = (mixed.shape[0], (k_ref.shape[0] - lead) // tile)
    back, own = (mixed.shape[1], mixed.shape[3])
    me, z = (lax.axis_index("fsdp"), lax.axis_index("tp"))
    width = out_ref.shape[-1]
    rows = left.shape[1] // size

    def hop_copy(at, number):
        return pltpu.make_async_remote_copy(
            src_ref=mixed.at[at, number],
            dst_ref=got.at[at, number],
            send_sem=hop_send.at[at, number],
            recv_sem=hop_recv.at[at, number],
            device_id={"tp": lax.rem(z + lanes - 1, lanes)},
            device_id_type=MESH,
        )

    def relay(at, number):
        @pl.when(z + 1 < lanes)
        def _():
            hop_copy(at, number - 1).wait_recv()
            total = mixed[at, number].astype(jnp.float32)
            total = total + got[at, number - 1].astype(jnp.float32)
            mixed[at, number] = total.astype(jnp.bfloat16)

        @pl.when(z > 0)
        def _():
            hop_copy(at, number).start()

    loads_of = lambda: [pltpu.make_async_copy(left_ref, left, loads.at[PARTS])] + [
        pltpu.make_async_copy(
            right_ref.at[:, pl.ds(part * width, width)], right.at[part], loads.at[part]
        )
        for part in range(PARTS)
    ]

    @pl.when((head == 0) & (index == 0))
    def _():
        for copy in loads_of():
            copy.start()
        barrier = pltpu.get_barrier_semaphore()
        peers = [{"fsdp": flip(me, bit)} for bit in [1] + chip_bits(size)]
        peers += [{"tp": lax.rem(z + 1, lanes)}, {"tp": lax.rem(z + lanes - 1, lanes)}]
        for peer in peers:
            pl.semaphore_signal(barrier, inc=1, device_id=peer, device_id_type=MESH)
        pl.semaphore_wait(barrier, len(peers))
        for copy in loads_of():
            copy.wait()
        gq_ref[...] = jnp.zeros_like(gq_ref)
        gk_ref[...] = jnp.zeros_like(gk_ref)

    def partial(part, slot, columns):
        block = left[:, pl.ds(pl.multiple_of(slot * rows, rows), rows)]
        return contract_first(block, right[part, :, columns])

    calls, finish = scatter_steps(size, me, made, held, sent, came, sems, partial, out_ref)
    at_step = {}
    for number, call in enumerate(calls):
        at_step.setdefault(number * heads * tiles // len(calls), []).append(call)
    for number, some in at_step.items():

        @pl.when(head * tiles + index == number)
        def _():
            for call in some:
                call()

    @pl.when(index == 0)
    def _():
        normed = normalize_rows(k_ref[...])[0] * nk_ref[...]
        keys[...] = turn(normed, cos_ref[...], sin_ref[...]).astype(jnp.bfloat16)
        dk[...] = jnp.zeros_like(dk)
        dv[...] = jnp.zeros_like(dv)

    here = pl.ds(pl.multiple_of(lead + index * tile, tile), tile)
    cosine, sine = (cos_ref[here, :], sin_ref[here, :])
    cosine, sine = (jnp.concatenate([cosine] * group, 0), jnp.concatenate([sine] * group, 0))
    normed, factor = normalize_rows(split_heads(q_ref[...], group))
    query = turn(normed * nq_ref[...], cosine, sine).astype(jnp.bfloat16)
    window = pl.ds(pl.multiple_of(index * step, tile), span)
    probs = head_probs(query, keys[window, :], bias_ref[...], group, scale)
    grad_out = split_heads(do_ref[...], group)
    dv[window, :] += contract_first(probs.astype(jnp.bfloat16), grad_out)
    grad_probs = contract_last(grad_out, v_ref[window, :])
    centre = jnp.sum(probs * grad_probs, axis=-1, keepdims=True)
    grad_scores = (probs * (grad_probs - centre)).astype(jnp.bfloat16)
    dk[window, :] += contract_first(grad_scores, query) * scale
    grad_query = turn_back(dot(grad_scores, keys[window, :]) * scale, cosine, sine)
    gq_ref[...] += jnp.sum(grad_query * normed, axis=0, keepdims=True)
    grad_raw = norm_back(grad_query, normed, factor, nq_ref[...])
    dq_ref[...] = join_heads(grad_raw.astype(jnp.bfloat16), group)

    @pl.when(index == tiles - 1)
    def _():
        normed_key, key_factor = normalize_rows(k_ref[...])
        grad_key = turn_back(dk[...], cos_ref[...], sin_ref[...])
        gk_ref[...] += jnp.sum(grad_key * normed_key, axis=0, keepdims=True)
        grad_key = norm_back(grad_key, normed_key, key_factor, nk_ref[...])
        for number in range(back):
            block = slice(number * own, (number + 1) * own)
            mixed[head, number, 0] = grad_key[block].astype(jnp.bfloat16)
            mixed[head, number, 1] = dv[block, :].astype(jnp.bfloat16)
        own_sum[head, 0] = grad_key[lead:]
        own_sum[head, 1] = dv[lead:, :]

        @pl.when(z > 0)
        def _():
            hop_copy(head, 0).start()

        for number in range(1, back):

            @pl.when(head >= number)
            def _():
                relay(head - number, number)

    @pl.when((head == heads - 1) & (index == tiles - 1))
    def _():
        for number in range(1, back):
            for at in range(heads - number, heads):
                relay(at, number)
        for at in range(heads):
            columns = slice(at * HD, (at + 1) * HD)

            @pl.when(z + 1 < lanes)
            def _():
                hop_copy(at, back - 1).wait_recv()
                total = own_sum[at] + got[at, back - 1].astype(jnp.float32)
                pair_ref[:, :, columns] = total.astype(jnp.bfloat16)

            @pl.when(z + 1 == lanes)
            def _():
                pair_ref[:, :, columns] = own_sum[at].astype(jnp.bfloat16)

            @pl.when(z > 0)
            def _():
                for number in range(back):
                    hop_copy(at, number).wait_send()

        finish()


def attention_specs(own, rows, group, tile, span):
    whole = lambda g, t: (0, 0)
    return [
        pl.BlockSpec((tile, group * HD), lambda g, t: (t, g)),
        pl.BlockSpec((rows, HD), lambda g, t: (0, g)),
        pl.BlockSpec((rows, HD), lambda g, t: (0, g)),
        pl.BlockSpec((tile, span), lambda g, t: (t, 0)),
        pl.BlockSpec((rows, HD), whole),
        pl.BlockSpec((rows, HD), whole),
        pl.BlockSpec((1, HD), whole),
        pl.BlockSpec((1, HD), whole),
    ]


def attend(queries, keys, values, bias, cosine, sine, norm_query, norm_key, tile, step):
    own, rows = (queries.shape[0], keys.shape[0])
    heads = keys.shape[1] // HD
    group = queries.shape[1] // keys.shape[1]
    span = bias.shape[1]
    return pl.pallas_call(
        functools.partial(attend_kernel, group, step, rows - own),
        grid=(heads, own // tile),
        out_shape=jax.ShapeDtypeStruct(queries.shape, jnp.bfloat16),
        in_specs=attention_specs(own, rows, group, tile, span),
        out_specs=pl.BlockSpec((tile, group * HD), lambda g, t: (t, g)),
        scratch_shapes=[pltpu.VMEM((rows, HD), jnp.bfloat16)],
        compiler_params=pltpu.CompilerParams(vmem_limit_bytes=VMEM),
        cost_estimate=pl.CostEstimate(
            flops=16 * own * span * queries.shape[1],
            bytes_accessed=4 * queries.size + 6 * keys.size,
            transcendentals=own * span * heads * group,
        ),
        name="attend",
    )(queries, keys, values, bias, cosine, sine, norm_query, norm_key)


def attend_back(
    queries,
    keys,
    values,
    bias,
    cosine,
    sine,
    norm_query,
    norm_key,
    grad,
    tile,
    step,
    left,
    right,
    size,
    lanes,
):
    own, rows = (queries.shape[0], keys.shape[0])
    heads = keys.shape[1] // HD
    group = queries.shape[1] // keys.shape[1]
    span = bias.shape[1]
    lead = rows - own
    back = lead // own
    tokens, depth = left.shape
    width = right.shape[1] // PARTS
    whole = lambda g, t: (0, 0)
    any_space = pl.BlockSpec(memory_space=pl.ANY)
    return pl.pallas_call(
        functools.partial(attend_back_kernel, group, step, lead, size, lanes),
        grid=(heads, own // tile),
        out_shape=(
            jax.ShapeDtypeStruct(queries.shape, jnp.bfloat16),
            jax.ShapeDtypeStruct((2, own, heads * HD), jnp.bfloat16),
            jax.ShapeDtypeStruct((1, HD), jnp.float32),
            jax.ShapeDtypeStruct((1, HD), jnp.float32),
            jax.ShapeDtypeStruct((PARTS, depth // size, width), jnp.float32),
        ),
        in_specs=attention_specs(own, rows, group, tile, span)
        + [pl.BlockSpec((tile, group * HD), lambda g, t: (t, g)), any_space, any_space],
        out_specs=(
            pl.BlockSpec((tile, group * HD), lambda g, t: (t, g)),
            pl.BlockSpec((2, own, heads * HD), lambda g, t: (0, 0, 0)),
            pl.BlockSpec((1, HD), whole),
            pl.BlockSpec((1, HD), whole),
            pl.BlockSpec((PARTS, depth // size, width), lambda g, t: (0, 0, 0)),
        ),
        scratch_shapes=[
            pltpu.VMEM((rows, HD), jnp.bfloat16),
            pltpu.VMEM((rows, HD), jnp.float32),
            pltpu.VMEM((rows, HD), jnp.float32),
            pltpu.VMEM((heads, back, 2, own, HD), jnp.bfloat16),
            pltpu.VMEM((heads, back, 2, own, HD), jnp.bfloat16),
            pltpu.VMEM((heads, 2, own, HD), jnp.float32),
            pltpu.VMEM((tokens, depth), jnp.bfloat16),
            pltpu.VMEM((PARTS, tokens, width), jnp.bfloat16),
            pltpu.SemaphoreType.DMA((PARTS + 1,)),
            pltpu.SemaphoreType.DMA((heads, back)),
            pltpu.SemaphoreType.DMA((heads, back)),
            *scatter_scratch(size, depth // size, width),
        ],
        compiler_params=pltpu.CompilerParams(
            collective_id=9, has_side_effects=True, vmem_limit_bytes=60 * 1024 * 1024
        ),
        cost_estimate=pl.CostEstimate(
            flops=40 * own * span * queries.shape[1],
            bytes_accessed=8 * queries.size + 16 * keys.size,
            transcendentals=own * span * heads * group,
        ),
        name="attend_back",
    )(queries, keys, values, bias, cosine, sine, norm_query, norm_key, grad, left, right)


def window_tables(length_row, pad_row, first, own, lead, tile, span):
    places = first - lead + jnp.arange(lead + own, dtype=jnp.int32)
    ends = jnp.cumsum(length_row)
    passed = places[:, None] >= ends[None, :]
    docs = jnp.sum(passed.astype(jnp.int32), axis=1)
    starts = jnp.sum(jnp.where(passed, length_row[None, :], 0), axis=1)
    freqs = THETA ** (-(jnp.arange(HD // 2).astype(jnp.float32) * 2.0 / HD))
    angles = (places - starts).astype(jnp.float32)[:, None] * freqs[None, :]
    cosine, sine = (jnp.cos(angles), jnp.sin(angles))
    padded = jnp.concatenate((jnp.zeros((lead,), pad_row.dtype), pad_row))
    live = lax.dynamic_slice_in_dim(padded, first, lead + own, 0)
    step = tile if lead + own > span else 0
    masks = []
    for index in range(own // tile):
        at = lead + index * tile
        query, key = (places[at : at + tile, None], places[None, index * step : index * step + span])
        same = docs[at : at + tile, None] == docs[None, index * step : index * step + span]
        seen = (live[None, index * step : index * step + span] == 1) | (key == query)
        masks.append((key >= 0) & (key <= query) & (query - key < WINDOW) & same & seen)
    bias = jnp.where(jnp.concatenate(masks, axis=0), 0.0, NEG).astype(jnp.float32)
    cosine = jnp.concatenate((cosine, cosine), axis=1)
    sine = jnp.concatenate((-sine, sine), axis=1)
    return (bias, cosine, sine, step, live[lead:].astype(jnp.float32))


def over_lanes(grad):
    return lax.psum_scatter(
        grad.astype(jnp.bfloat16), "tp", scatter_dimension=2, tiled=True
    ).astype(jnp.float32)


def join_parts(halves):
    return jnp.concatenate([halves[part] for part in range(PARTS)], axis=1)


def shards(
    states,
    lengths,
    padding,
    teacher,
    norm_attn,
    w_query,
    w_key,
    w_value,
    norm_query,
    norm_key,
    w_out,
    norm_mlp,
    w_gate,
    w_up,
    w_down,
):
    own = states.shape[0]
    n_tp, n_fsdp = (lax.axis_size("tp"), lax.axis_size("fsdp"))
    first = lax.axis_index("tp") * own
    back = min(n_tp - 1, -(-WINDOW // own))
    lead = back * own
    tile = min(256, own)
    span = WINDOW + tile if lead >= WINDOW else lead + own
    wq, wk = (w_query.shape[1], w_key.shape[1])
    bias, cosine, sine, step, live = window_tables(
        lengths[0], padding[0], first, own, lead, tile, span
    )
    joined = jnp.concatenate((w_query, w_key, w_value, w_out.T), axis=1)
    wo = w_out.shape[0]
    units = [
        part.reshape(n_fsdp, -1, part.shape[1]) for part in (w_gate.T, w_up.T, w_down)
    ]
    live_here = jnp.full((8, 128), jnp.sum(padding).astype(jnp.float32))
    before, weights_attn, mine, counts = enter(
        n_fsdp, n_tp, back, states, joined, jnp.stack(units, axis=1), live_here
    )
    count = counts[0, 0]
    rows_gate, rows_up, rows_down = [
        lax.all_gather(mine[i], "tp", axis=0, tiled=True) for i in range(3)
    ]
    normed_in, query_raw, key_raw, value = project(
        before, states, norm_attn, weights_attn, wq, wk
    )
    gains = (norm_query.reshape(1, HD), norm_key.reshape(1, HD))
    attended = attend(query_raw, key_raw, value, bias, cosine, sine, *gains, tile, step)
    inputs = states.astype(jnp.float32)
    hidden_one = project_out(attended, weights_attn, states, wo)
    normed_two, factor_two = normalize_rows(hidden_one)
    whole_two, gate, up, product = gate_up(
        n_fsdp, (normed_two * norm_mlp).astype(jnp.bfloat16), rows_gate, rows_up
    )
    outputs = hidden_one + sum_products(n_fsdp, 2, (product,), (rows_down,))
    errors = (outputs - teacher.astype(jnp.float32)) * live[:, None]
    squares = jnp.sum(errors * errors)
    grad_out = errors * (2.0 / (count * D))

    grad_whole, grad_gate, grad_up = grad_hidden_units(
        n_fsdp, grad_out.astype(jnp.bfloat16), rows_down, gate, up
    )
    by_unit = (
        contract_first(product, grad_whole).astype(jnp.bfloat16),
        contract_first(grad_gate, whole_two).astype(jnp.bfloat16),
        contract_first(grad_up, whole_two).astype(jnp.bfloat16),
    )
    by_unit, (grad_gate, grad_up) = lax.optimization_barrier((by_unit, (grad_gate, grad_up)))
    grad_mid = sum_products(n_fsdp, 4, (grad_gate, grad_up), (rows_gate, rows_up))
    by_unit = [lax.psum_scatter(part, "tp", scatter_dimension=0, tiled=True) for part in by_unit]
    grad_norm_mlp = jnp.sum(grad_mid * normed_two, axis=0)
    grad_hidden = grad_out + norm_back(grad_mid, normed_two, factor_two, norm_mlp)

    grad_low_out = grad_hidden.astype(jnp.bfloat16)
    grad_attended = back_out(grad_low_out, weights_attn, wo)
    grad_query, grad_pair, grad_norm_query, grad_norm_key, sums_out = attend_back(
        query_raw,
        key_raw,
        value,
        bias,
        cosine,
        sine,
        *gains,
        grad_attended,
        tile,
        step,
        grad_low_out,
        attended,
        n_fsdp,
        n_tp,
    )
    sums_query, units_back = sum_query(n_fsdp, normed_in, grad_query, by_unit)
    sums_pair, grad_low = sum_key(n_fsdp, normed_in, grad_query, grad_pair, weights_attn)
    grad_w_out, grad_w_query = [
        over_lanes(join_parts(sums)[None])[0] for sums in (sums_out, sums_query)
    ]
    grad_w_pair = over_lanes(sums_pair)
    grad_w_down, grad_w_gate, grad_w_up = [
        units_back[:, kind].reshape(-1, units_back.shape[3]).astype(jnp.float32)
        for kind in range(3)
    ]
    normed_one, factor_one = normalize_rows(inputs)
    grad_norm_attn = jnp.sum(grad_low * normed_one, axis=0)
    grad_input = grad_hidden + norm_back(grad_low, normed_one, factor_one, norm_attn)
    small = [grad_norm_attn, grad_norm_mlp, grad_norm_query[0], grad_norm_key[0]]
    small.append(jnp.full((HD,), squares))
    joined_small = jnp.concatenate(small).reshape(-1, HD)
    filled = joined_small.shape[0]
    joined_small = jnp.pad(joined_small, ((0, -filled % 8), (0, 0)))
    summed = sum_small(n_fsdp, n_tp, joined_small)[:filled].reshape(-1)
    grad_norm_attn, grad_norm_mlp = (summed[:D], summed[D : 2 * D])
    grad_norm_query, grad_norm_key = (summed[2 * D : 2 * D + HD], summed[2 * D + HD : 2 * D + 2 * HD])
    squares = summed[2 * D + 2 * HD]
    return (
        outputs,
        squares / (count * D),
        grad_input,
        grad_norm_attn,
        grad_w_query,
        grad_w_pair[0],
        grad_w_pair[1],
        grad_norm_query,
        grad_norm_key,
        grad_w_out.T,
        grad_norm_mlp,
        grad_w_gate.T,
        grad_w_up.T,
        grad_w_down,
    )


def solution(mesh):
    tokens = P(("fsdp", "tp"), None)
    rows, columns, sequences = (P("fsdp", "tp"), P("tp", "fsdp"), P("fsdp", None))
    in_specs = (
        tokens,
        sequences,
        sequences,
        tokens,
        P(),
        rows,
        rows,
        rows,
        P(),
        P(),
        columns,
        P(),
        rows,
        rows,
        columns,
    )
    out_specs = (
        tokens,
        P(),
        tokens,
        P(),
        rows,
        rows,
        rows,
        P(),
        P(),
        columns,
        P(),
        rows,
        rows,
        columns,
    )
    return jax.shard_map(shards, mesh=mesh, in_specs=in_specs, out_specs=out_specs, check_vma=False)
```

```python
import functools

import jax
import jax.numpy as jnp
from jax import lax
from jax.experimental import pallas as pl
from jax.experimental.pallas import tpu as pltpu
from jax.sharding import PartitionSpec as P

D = 2048
HD = 128
WINDOW = 1024

EPS = 1e-06
THETA = 1000000.0
NEG = -1e30
VMEM = 56 * 1024 * 1024


def normalize_rows(values):
    factor = lax.rsqrt(jnp.mean(values * values, axis=-1, keepdims=True) + EPS)
    return (values * factor, factor)


def norm_back(grad, normed, factor, gain):
    scaled = grad * gain
    return factor * (scaled - normed * jnp.mean(scaled * normed, axis=-1, keepdims=True))


def contract_last(left, right):
    return lax.dot_general(
        left, right, (((1,), (1,)), ((), ())), preferred_element_type=jnp.float32
    )


def contract_first(left, right):
    return lax.dot_general(
        left, right, (((0,), (0,)), ((), ())), preferred_element_type=jnp.float32
    )


def dot(left, right):
    return jnp.dot(left, right, preferred_element_type=jnp.float32)


MESH = pl.DeviceIdType.MESH
PARTS = 2


def flip(index, mask):
    bit = 1
    while bit <= mask:
        if mask & bit:
            index = index + bit - 2 * bit * lax.rem(lax.div(index, bit), 2)
        bit *= 2
    return index


def chip_bits(size):
    bits = []
    bit = 2
    while bit < size:
        bits.append(bit)
        bit *= 2
    return bits


def orders(size):
    bits = chip_bits(size)
    return (bits, bits[::-1])


def mask_of(pattern, order):
    return sum(bit for i, bit in enumerate(order) if pattern >> i & 1)


def top(pattern):
    return pattern.bit_length() - 1


def greet(me, size):
    barrier = pltpu.get_barrier_semaphore()
    bits = [1] + chip_bits(size)
    for bit in bits:
        pl.semaphore_signal(
            barrier, inc=1, device_id={"fsdp": flip(me, bit)}, device_id_type=MESH
        )
    pl.semaphore_wait(barrier, len(bits))


def pick(part, pair):
    return pair[0] + part * (pair[1] - pair[0])


class Gather:
    def __init__(self, size, me, whole, sems, parts=PARTS, lane=lambda part: part, parity=lambda part: part, own=None):
        self.size, self.me, self.whole, self.parts = (size, me, whole, parts)
        self.lane, self.parity, self.own = (lane, parity, own)
        self.chip_send, self.chip_recv, self.core_send, self.core_recv = sems
        self.steps = len(chip_bits(size))
        self.patterns = sorted(range(1 << self.steps), key=lambda m: (top(m), m))

    def order(self, part):
        return orders(self.size)[self.parity(part) % 2]

    def slot(self, part, pattern, sibling):
        return flip(self.me, mask_of(pattern, self.order(part)) + sibling)

    def source(self, part, pattern, block):
        return self.own if self.own is not None and part == 0 and pattern == 0 else block

    def chip_copy(self, part, step, pattern):
        block = self.whole.at[self.slot(part, pattern, 0), self.lane(part)]
        number = (1 << step) - 1 + pattern
        return pltpu.make_async_remote_copy(
            src_ref=self.source(part, pattern, block),
            dst_ref=block,
            send_sem=self.chip_send.at[part, number],
            recv_sem=self.chip_recv.at[part, number],
            device_id={"fsdp": flip(self.me, self.order(part)[step])},
            device_id_type=MESH,
        )

    def core_copy(self, part, pattern):
        block = self.whole.at[self.slot(part, pattern, 0), self.lane(part)]
        return pltpu.make_async_remote_copy(
            src_ref=self.source(part, pattern, block),
            dst_ref=block,
            send_sem=self.core_send.at[part, pattern],
            recv_sem=self.core_recv.at[part, pattern],
            device_id={"fsdp": flip(self.me, 1)},
            device_id_type=MESH,
        )

    def arrive(self, part, pattern):
        if pattern:
            step = top(pattern)
            self.chip_copy(part, step, pattern - (1 << step)).wait_recv()

    def forward(self, part, pattern):
        for step in range(top(pattern) + 1, self.steps):
            self.chip_copy(part, step, pattern).start()
        self.core_copy(part, pattern).start()

    def pairs(self, work):
        for pattern in self.patterns:
            for part in range(self.parts):
                self.arrive(part, pattern)
            for part in range(self.parts):
                self.forward(part, pattern)
            work([self.slot(part, pattern, 0) for part in range(self.parts)])
            for part in range(self.parts):
                self.core_copy(part, pattern).wait_recv()
            work([self.slot(part, pattern, 1) for part in range(self.parts)])

    def finish(self):
        for pattern in self.patterns:
            for part in range(self.parts):
                for step in range(top(pattern) + 1, self.steps):
                    self.chip_copy(part, step, pattern).wait_send()
                self.core_copy(part, pattern).wait_send()


def gather_semaphores(size, parts=PARTS):
    moves = max(1, size // 2 - 1)
    return [
        pltpu.SemaphoreType.DMA((parts, moves)),
        pltpu.SemaphoreType.DMA((parts, moves)),
        pltpu.SemaphoreType.DMA((parts, size // 2)),
        pltpu.SemaphoreType.DMA((parts, size // 2)),
    ]


def first_step(pattern, steps):
    return (pattern & -pattern).bit_length() - 1 if pattern else steps


def scatter_order(steps):
    return sorted(range(1 << steps), key=lambda m: (first_step(m, steps), -bin(m).count("1"), m))


def scatter_steps(
    size, me, made, held, sent, came, sems, partial, final, ready=lambda part, slot, q, sibling: None
):
    chip_send, chip_recv, core_send, core_recv = sems
    steps = len(chip_bits(size))
    order = [bits[::-1] for bits in orders(size)]
    first = lambda m: first_step(m, steps)
    patterns = scatter_order(steps)
    place = {m: q for q, m in enumerate(patterns)}
    width = final.shape[-1]
    chunk = min(512, width)

    def slots(pattern, sibling):
        return [flip(me, mask_of(pattern, order[part]) + sibling) for part in range(PARTS)]

    def core_copy(part, q):
        return pltpu.make_async_remote_copy(
            src_ref=made.at[part, q],
            dst_ref=held.at[part, q],
            send_sem=core_send.at[part, q],
            recv_sem=core_recv.at[part, q],
            device_id={"fsdp": flip(me, 1)},
            device_id_type=MESH,
        )

    def chip_copy(part, q):
        return pltpu.make_async_remote_copy(
            src_ref=sent.at[part, q],
            dst_ref=came.at[part, q],
            send_sem=chip_send.at[part, q],
            recv_sem=chip_recv.at[part, q],
            device_id={"fsdp": flip(me, order[part][first(patterns[q])])},
            device_id_type=MESH,
        )

    def for_sibling(q):
        pair = slots(patterns[q], 1)
        for part in range(PARTS):
            ready(part, pair[part], q, 1)

            @pl.loop(0, width // chunk)
            def _(index):
                columns = pl.ds(pl.multiple_of(index * chunk, chunk), chunk)
                made[part, q, :, columns] = partial(part, pair[part], columns).astype(jnp.bfloat16)

            core_copy(part, q).start()

    def for_chips(q):
        pattern = patterns[q]
        pair = slots(pattern, 0)
        arrivals = [place[pattern | 1 << step] for step in range(first(pattern))]
        for part in range(PARTS):
            ready(part, pair[part], q, 0)
            if pattern:
                core_copy(part, q).wait_recv()
                for arrival in arrivals:
                    chip_copy(part, arrival).wait_recv()

            @pl.loop(0, width // chunk)
            def _(index):
                columns = pl.ds(pl.multiple_of(index * chunk, chunk), chunk)
                total = partial(part, pair[part], columns)
                if pattern:
                    total = total + held[part, q, :, columns].astype(jnp.float32)
                    for arrival in arrivals:
                        total = total + came[part, arrival, :, columns].astype(jnp.float32)
                    sent[part, q, :, columns] = total.astype(jnp.bfloat16)
                else:
                    final[part, :, columns] = total

            if pattern:
                chip_copy(part, q).start()
        if not pattern:
            for part in range(PARTS):
                core_copy(part, q).wait_recv()
                for arrival in arrivals:
                    chip_copy(part, arrival).wait_recv()

                @pl.loop(0, width // chunk)
                def _(index):
                    columns = pl.ds(pl.multiple_of(index * chunk, chunk), chunk)
                    total = final[part, :, columns] + held[part, q, :, columns].astype(jnp.float32)
                    for arrival in arrivals:
                        total = total + came[part, arrival, :, columns].astype(jnp.float32)
                    final[part, :, columns] = total

    def finish():
        for q in range(len(patterns)):
            for part in range(PARTS):
                core_copy(part, q).wait_send()
                if patterns[q]:
                    chip_copy(part, q).wait_send()

    calls = []
    for q in range(len(patterns)):
        calls += [functools.partial(for_sibling, q), functools.partial(for_chips, q)]
    return (calls, finish)


def scatter_scratch(size, rows, width):
    held = size // 2
    moved = max(1, held - 1)
    return [
        pltpu.VMEM((PARTS, held, rows, width), jnp.bfloat16),
        pltpu.VMEM((PARTS, held, rows, width), jnp.bfloat16),
        pltpu.VMEM((PARTS, moved, rows, width), jnp.bfloat16),
        pltpu.VMEM((PARTS, moved, rows, width), jnp.bfloat16),
        pltpu.SemaphoreType.DMA((PARTS, moved)),
        pltpu.SemaphoreType.DMA((PARTS, moved)),
        pltpu.SemaphoreType.DMA((PARTS, held)),
        pltpu.SemaphoreType.DMA((PARTS, held)),
    ]


def gate_up_kernel(
    size,
    x_ref,
    wg_in,
    wu_in,
    x_out,
    gate_out,
    up_out,
    prod_out,
    whole,
    wg_ref,
    wu_ref,
    gate,
    up,
    prod,
    load,
    keep,
    store,
    *sems,
):
    me = lax.axis_index("fsdp")
    hidden = wg_ref.shape[0]
    chunk = 256 if hidden % 256 == 0 else 128
    loads = [
        pltpu.make_async_copy(source, target, load.at[i])
        for i, (source, target) in enumerate(
            ((x_ref, whole.at[me]), (wg_in, wg_ref), (wu_in, wu_ref))
        )
    ]
    for copy in loads:
        copy.start()
    greet(me, size)
    loads[0].wait()
    state = {"count": 0, "last": None}

    def stores(part, at):
        return [
            pltpu.make_async_copy(buffer.at[part], out.at[at, part], store.at[part, i])
            for i, (buffer, out) in enumerate(((gate, gate_out), (up, up_out), (prod, prod_out)))
        ]

    def work(pair):
        count, last = (state["count"], state["last"])
        for part in range(PARTS):
            pltpu.make_async_copy(
                whole.at[pair[part], part], x_out.at[pair[part], part], keep.at[part, count]
            ).start()
        if last is None:
            for copy in loads[1:]:
                copy.wait()

        @pl.loop(0, PARTS)
        def _(part):
            at = pick(part, pair)
            if last is not None:
                for copy in stores(part, pick(part, last)):
                    copy.wait()

            @pl.loop(0, hidden // chunk)
            def _(index):
                units = pl.ds(pl.multiple_of(index * chunk, chunk), chunk)
                rows = whole[at, part]
                gates = contract_last(rows, wg_ref[units, :])
                ups = contract_last(rows, wu_ref[units, :])
                gate[part, :, units] = gates
                up[part, :, units] = ups
                prod[part, :, units] = (gates * jax.nn.sigmoid(gates) * ups).astype(jnp.bfloat16)

            for copy in stores(part, at):
                copy.start()

        state["count"], state["last"] = (count + 1, pair)
        state.setdefault("all", []).append(pair)

    gather = Gather(size, me, whole, sems)
    gather.pairs(work)
    gather.finish()
    for part in range(PARTS):
        for copy in stores(part, state["last"][part]):
            copy.wait()
        for count, pair in enumerate(state["all"]):
            pltpu.make_async_copy(
                whole.at[pair[part], part], x_out.at[pair[part], part], keep.at[part, count]
            ).wait()


def gate_up(size, values, rows_gate, rows_up):
    own, width = values.shape
    rows, hidden = (own // PARTS, rows_gate.shape[0])
    any_space = pl.BlockSpec(memory_space=pl.ANY)
    shape = lambda columns, kind: jax.ShapeDtypeStruct((size, PARTS, rows, columns), kind)
    outs = pl.pallas_call(
        functools.partial(gate_up_kernel, size),
        out_shape=(
            shape(width, jnp.bfloat16),
            shape(hidden, jnp.float32),
            shape(hidden, jnp.float32),
            shape(hidden, jnp.bfloat16),
        ),
        in_specs=[any_space] * 3,
        out_specs=(any_space,) * 4,
        scratch_shapes=[
            pltpu.VMEM((size, PARTS, rows, width), jnp.bfloat16),
            pltpu.VMEM((hidden, width), jnp.bfloat16),
            pltpu.VMEM((hidden, width), jnp.bfloat16),
            pltpu.VMEM((PARTS, rows, hidden), jnp.float32),
            pltpu.VMEM((PARTS, rows, hidden), jnp.float32),
            pltpu.VMEM((PARTS, rows, hidden), jnp.bfloat16),
            pltpu.SemaphoreType.DMA((3,)),
            pltpu.SemaphoreType.DMA((PARTS, size)),
            pltpu.SemaphoreType.DMA((PARTS, 3)),
            *gather_semaphores(size),
        ],
        compiler_params=pltpu.CompilerParams(
            collective_id=1, has_side_effects=True, vmem_limit_bytes=VMEM
        ),
        cost_estimate=pl.CostEstimate(
            flops=4 * size * own * width * hidden, bytes_accessed=200 * 1024 * 1024, transcendentals=0
        ),
        name="gate_up",
    )(values.reshape(PARTS, rows, width), rows_gate, rows_up)
    return tuple(out.reshape(size * own, -1) for out in outs)


def grad_hidden_kernel(
    size,
    x_ref,
    wd_in,
    gate_in,
    up_in,
    prod_in,
    two_in,
    dgate_out,
    dup_out,
    dwd_out,
    dwg_out,
    dwu_out,
    whole,
    wd_ref,
    gate,
    up,
    prod,
    two,
    dprod,
    dgate,
    dup,
    sums,
    load,
    fetch,
    store,
    flush,
    *sems,
):
    me = lax.axis_index("fsdp")
    hidden, width = wd_ref.shape
    rows = dprod.shape[0]
    chunk = 256 if hidden % 256 == 0 else 128
    loads = [
        pltpu.make_async_copy(x_ref, whole.at[me], load.at[0]),
        pltpu.make_async_copy(wd_in, wd_ref, load.at[1]),
    ]
    for copy in loads:
        copy.start()

    def stores(part, at):
        return [
            pltpu.make_async_copy(buffer.at[part], out.at[at, part], store.at[part, i])
            for i, (buffer, out) in enumerate(((dgate, dgate_out), (dup, dup_out)))
        ]

    def fetches(part, at):
        pairs = ((gate_in, gate), (up_in, up), (prod_in, prod), (two_in, two))
        return [
            pltpu.make_async_copy(source.at[at, part], buffer.at[part], fetch.at[part, i])
            for i, (source, buffer) in enumerate(pairs)
        ]

    gather = Gather(size, me, whole, sems)
    order = []
    for pattern in gather.patterns:
        for sibling in (0, 1):
            order.append([gather.slot(part, pattern, sibling) for part in range(PARTS)])
    for copy in fetches(0, order[0][0]):
        copy.start()
    sums[...] = jnp.zeros_like(sums)
    greet(me, size)
    loads[0].wait()
    state = {"count": 0}

    def work(pair):
        count = state["count"]
        last = order[count - 1] if count else None
        following = order[count + 1] if count + 1 < len(order) else None
        state["count"] = count + 1
        if count == 0:
            loads[1].wait()

        @pl.loop(0, PARTS)
        def _(part):
            at = pick(part, pair)

            @pl.when(part == 0)
            def _():
                for copy in fetches(1, pair[1]):
                    copy.start()

            if following is not None:

                @pl.when(part == 1)
                def _():
                    for copy in fetches(0, following[0]):
                        copy.start()

            @pl.loop(0, hidden // chunk)
            def _(index):
                units = pl.ds(pl.multiple_of(index * chunk, chunk), chunk)
                dprod[:, units] = contract_last(whole[at, part], wd_ref[units, :])

            for copy in fetches(part, at):
                copy.wait()
            if last is not None:
                for copy in stores(part, pick(part, last)):
                    copy.wait()

            @pl.loop(0, hidden // chunk)
            def _(index):
                units = pl.ds(pl.multiple_of(index * chunk, chunk), chunk)
                gates, grads = (gate[part, :, units], dprod[:, units])
                sigmoid = jax.nn.sigmoid(gates)
                dgate[part, :, units] = (
                    grads * up[part, :, units] * sigmoid * (1.0 + gates * (1.0 - sigmoid))
                ).astype(jnp.bfloat16)
                dup[part, :, units] = (grads * (gates * sigmoid)).astype(jnp.bfloat16)

            for copy in stores(part, at):
                copy.start()

            @pl.loop(0, hidden // chunk)
            def _(index):
                units = pl.ds(pl.multiple_of(index * chunk, chunk), chunk)
                sums[0, units, :] += contract_first(prod[part, :, units], whole[at, part])
                sums[1, units, :] += contract_first(dgate[part, :, units], two[part])
                sums[2, units, :] += contract_first(dup[part, :, units], two[part])

    gather.pairs(work)
    gather.finish()
    for part in range(PARTS):
        for copy in stores(part, order[-1][part]):
            copy.wait()
    outs = (dwd_out, dwg_out, dwu_out)
    pieces = hidden // rows
    copies = []
    for piece in range(3 * pieces):
        kind, first = (piece // pieces, piece % pieces * rows)
        block = whole.at[piece // PARTS, piece % PARTS]
        block[...] = sums[kind, first : first + rows, :].astype(jnp.bfloat16)
        copy = pltpu.make_async_copy(
            block, outs[kind].at[pl.ds(first, rows)], flush.at[piece]
        )
        copy.start()
        copies.append(copy)
    for copy in copies:
        copy.wait()


def grad_hidden_units(size, values, rows_down, gate, up, product, whole_two):
    own, width = values.shape
    rows, hidden = (own // PARTS, rows_down.shape[0])
    any_space = pl.BlockSpec(memory_space=pl.ANY)
    shape = lambda columns, kind: jax.ShapeDtypeStruct((size, PARTS, rows, columns), kind)
    blocks = lambda array: array.reshape(size, PARTS, rows, -1)
    weight = jax.ShapeDtypeStruct((hidden, width), jnp.bfloat16)
    dgate, dup, *grads = pl.pallas_call(
        functools.partial(grad_hidden_kernel, size),
        out_shape=(shape(hidden, jnp.bfloat16), shape(hidden, jnp.bfloat16), weight, weight, weight),
        in_specs=[any_space] * 6,
        out_specs=(any_space,) * 5,
        scratch_shapes=[
            pltpu.VMEM((size, PARTS, rows, width), jnp.bfloat16),
            pltpu.VMEM((hidden, width), jnp.bfloat16),
            pltpu.VMEM((PARTS, rows, hidden), jnp.float32),
            pltpu.VMEM((PARTS, rows, hidden), jnp.float32),
            pltpu.VMEM((PARTS, rows, hidden), jnp.bfloat16),
            pltpu.VMEM((PARTS, rows, width), jnp.bfloat16),
            pltpu.VMEM((rows, hidden), jnp.float32),
            pltpu.VMEM((PARTS, rows, hidden), jnp.bfloat16),
            pltpu.VMEM((PARTS, rows, hidden), jnp.bfloat16),
            pltpu.VMEM((3, hidden, width), jnp.float32),
            pltpu.SemaphoreType.DMA((2,)),
            pltpu.SemaphoreType.DMA((PARTS, 4)),
            pltpu.SemaphoreType.DMA((PARTS, 2)),
            pltpu.SemaphoreType.DMA((3 * (hidden // rows),)),
            *gather_semaphores(size),
        ],
        compiler_params=pltpu.CompilerParams(
            collective_id=3, has_side_effects=True, vmem_limit_bytes=VMEM
        ),
        cost_estimate=pl.CostEstimate(
            flops=8 * size * own * width * hidden, bytes_accessed=200 * 1024 * 1024, transcendentals=0
        ),
        name="grad_hidden_units",
    )(values.reshape(PARTS, rows, width), rows_down, *map(blocks, (gate, up, product, whole_two)))
    return (dgate.reshape(size * own, hidden), dup.reshape(size * own, hidden), grads)


def sum_products_kernel(size, terms, *refs):
    left_in, right_in, out = (refs[:terms], refs[terms : 2 * terms], refs[2 * terms])
    at = 2 * terms + 1
    lefts, rights, (w_load, x_load) = (
        refs[at : at + terms],
        refs[at + terms : at + 2 * terms],
        refs[at + 2 * terms : at + 2 * terms + 2],
    )
    made, held, sent, came, *sems = refs[at + 2 * terms + 2 :]
    me = lax.axis_index("fsdp")

    def partial(part, slot, columns):
        return sum(
            dot(left[slot, part], right[:, columns]) for left, right in zip(lefts, rights)
        )

    def tiles(part, slot, q, sibling):
        return [
            pltpu.make_async_copy(
                source.at[slot, part], left.at[slot, part], x_load.at[2 * q + sibling, part, i]
            )
            for i, (source, left) in enumerate(zip(left_in, lefts))
        ]

    seen = []

    def ready(part, slot, q, sibling):
        if not seen:
            for copy in weights:
                copy.wait()
        seen.append(slot)
        for copy in tiles(part, slot, q, sibling):
            copy.wait()

    weights = [
        pltpu.make_async_copy(source, right, w_load.at[i])
        for i, (source, right) in enumerate(zip(right_in, rights))
    ]
    for copy in weights:
        copy.start()
    order = [bits[::-1] for bits in orders(size)]
    for q, pattern in enumerate(scatter_order(len(order[0]))):
        for sibling in (1, 0):
            for part in range(PARTS):
                slot = flip(me, mask_of(pattern, order[part]) + sibling)
                for copy in tiles(part, slot, q, sibling):
                    copy.start()
    greet(me, size)
    calls, finish = scatter_steps(size, me, made, held, sent, came, sems, partial, out, ready)
    for call in calls:
        call()
    finish()


def sum_products(size, number, lefts, rights):
    total, hidden = lefts[0].shape
    width = rights[0].shape[1]
    rows = total // size // PARTS
    vmem = pl.BlockSpec(memory_space=pltpu.VMEM)
    terms = len(lefts)
    out = pl.pallas_call(
        functools.partial(sum_products_kernel, size, terms),
        out_shape=jax.ShapeDtypeStruct((PARTS, rows, width), jnp.float32),
        in_specs=[pl.BlockSpec(memory_space=pl.ANY)] * (2 * terms),
        out_specs=vmem,
        scratch_shapes=[
            *[pltpu.VMEM((size, PARTS, rows, hidden), jnp.bfloat16)] * terms,
            *[pltpu.VMEM((hidden, width), jnp.bfloat16)] * terms,
            pltpu.SemaphoreType.DMA((terms,)),
            pltpu.SemaphoreType.DMA((size, PARTS, terms)),
            *scatter_scratch(size, rows, width),
        ],
        compiler_params=pltpu.CompilerParams(
            collective_id=number, has_side_effects=True, vmem_limit_bytes=VMEM
        ),
        cost_estimate=pl.CostEstimate(
            flops=2 * total * hidden * width * terms, bytes_accessed=200 * 1024 * 1024, transcendentals=0
        ),
        name="sum_products",
    )(*[left.reshape(size, PARTS, rows, hidden) for left in lefts], *rights)
    return out.reshape(PARTS * rows, width)


def enter_kernel(
    size,
    lanes,
    back,
    x_ref,
    w_ref,
    m_ref,
    c_ref,
    before,
    whole,
    mine_gate,
    mine_up,
    mine_down,
    count,
    counts,
    loads,
    z_send,
    z_recv,
    x_send,
    x_recv,
    m_send,
    m_recv,
    c_send,
    c_recv,
    *sems,
):
    me, z = (lax.axis_index("fsdp"), lax.axis_index("tp"))
    mine = (mine_gate, mine_up, mine_down)
    span = m_ref.shape[-1]
    part_of = lambda device: pl.ds(pl.multiple_of(device * span, span), span)
    local = [pltpu.make_async_copy(w_ref, whole.at[me, z], loads.at[0])]
    local += [
        pltpu.make_async_copy(m_ref.at[me, kind], mine[kind].at[:, part_of(me)], loads.at[kind + 1])
        for kind in range(3)
    ]
    for copy in local:
        copy.start()
    counts[me] = c_ref[...]
    up, down = (lax.rem(z + 1, lanes), lax.rem(z + lanes - 1, lanes))
    barrier = pltpu.get_barrier_semaphore()
    peers = [{"fsdp": flip(me, other)} for other in range(1, size)] + [{"tp": up}, {"tp": down}]
    for peer in peers:
        pl.semaphore_signal(barrier, inc=1, device_id=peer, device_id_type=MESH)
    pl.semaphore_wait(barrier, len(peers))

    def far(part):
        return (part + 1) // 2

    def lane(part):
        if part == 0:
            return z
        return z - far(part) if part % 2 else z + far(part)

    def exists(part):
        return z >= far(part) if part % 2 else z + far(part) < lanes

    def lane_copy(part):
        block = whole.at[me, lane(part - 2) if part > 2 else z]
        return pltpu.make_async_remote_copy(
            src_ref=block if part > 2 else w_ref,
            dst_ref=block,
            send_sem=z_send.at[part - 1],
            recv_sem=z_recv.at[part - 1],
            device_id={"tp": up if part % 2 else down},
            device_id_type=MESH,
        )

    def lane_sends(part):
        if part % 2:
            return (z >= far(part) - 1) & (z + 1 < lanes)
        return (z + far(part) - 1 < lanes) & (z > 0)

    def token_copy(hop):
        return pltpu.make_async_remote_copy(
            src_ref=x_ref if hop == 1 else before.at[hop - 2],
            dst_ref=before.at[hop - 1],
            send_sem=x_send.at[hop - 1],
            recv_sem=x_recv.at[hop - 1],
            device_id={"tp": up},
            device_id_type=MESH,
        )

    def unit_copy(other, kind):
        peer = flip(me, other)
        return pltpu.make_async_remote_copy(
            src_ref=m_ref.at[peer, kind],
            dst_ref=mine[kind].at[:, part_of(me)],
            send_sem=m_send.at[other - 1, kind],
            recv_sem=m_recv.at[other - 1, kind],
            device_id={"fsdp": peer},
            device_id_type=MESH,
        )

    def count_copy(other):
        return pltpu.make_async_remote_copy(
            src_ref=c_ref,
            dst_ref=counts.at[me],
            send_sem=c_send.at[other - 1],
            recv_sem=c_recv.at[other - 1],
            device_id={"fsdp": flip(me, other)},
            device_id_type=MESH,
        )

    def when(condition, run):
        pl.when(condition)(run)

    gather = Gather(size, me, whole, sems, 2 * lanes - 1, lane, far, w_ref)
    for part in (1, 2):
        when(lane_sends(part), lambda: lane_copy(part).start())
    gather.forward(0, 0)
    when(z + 1 < lanes, lambda: token_copy(1).start())
    for other in range(1, size):
        count_copy(other).start()
        for kind in range(3):
            unit_copy(other, kind).start()
    events = [(part, pattern) for part in range(2 * lanes - 1) for pattern in gather.patterns]
    wave = lambda pattern: 3.5 * top(pattern) + 2.5 if pattern else 0
    events.sort(key=lambda event: (2 * far(event[0]) + wave(event[1]), event))

    def run_event(part, pattern):
        if pattern:
            gather.arrive(part, pattern)
        elif part:
            lane_copy(part).wait_recv()
            if part + 2 < 2 * lanes - 1:
                when(lane_sends(part + 2), lambda: lane_copy(part + 2).start())
        gather.forward(part, pattern)

    for part, pattern in events[1:]:
        if part == 0:
            run_event(part, pattern)
        else:
            when(exists(part), lambda: run_event(part, pattern))
        if (part, pattern) == (2 * lanes - 2, 0):
            for hop in range(1, back):
                when(z >= hop, lambda: token_copy(hop).wait_recv())
                when((z >= hop) & (z + 1 < lanes), lambda: token_copy(hop + 1).start())
    for other in range(1, size):
        count_copy(other).wait()
    count[...] = sum(counts[other] for other in range(size))

    def close(part):
        for pattern in gather.patterns:
            gather.core_copy(part, pattern).wait()
            for step in range(top(pattern) + 1, gather.steps):
                gather.chip_copy(part, step, pattern).wait_send()

    close(0)
    for part in range(1, 2 * lanes - 1):
        when(exists(part), lambda: close(part))
        when(lane_sends(part), lambda: lane_copy(part).wait_send())
    for other in range(1, size):
        for kind in range(3):
            unit_copy(other, kind).wait()
    for hop in range(1, back + 1):
        when((z >= hop - 1) & (z + 1 < lanes), lambda: token_copy(hop).wait_send())
    when(z >= back, lambda: token_copy(back).wait_recv())
    for copy in local:
        copy.wait()


def enter(size, lanes, back, values, weights, units, count):
    any_space = pl.BlockSpec(memory_space=pl.ANY)
    vmem = pl.BlockSpec(memory_space=pltpu.VMEM)
    _, kinds, rows, columns = units.shape
    others = pltpu.SemaphoreType.DMA((size - 1,))
    other_kinds = pltpu.SemaphoreType.DMA((size - 1, kinds))
    line = pltpu.SemaphoreType.DMA((2 * lanes - 2,))
    hop = pltpu.SemaphoreType.DMA((back,))
    mine = jax.ShapeDtypeStruct((rows, size * columns), units.dtype)
    return pl.pallas_call(
        functools.partial(enter_kernel, size, lanes, back),
        out_shape=(
            jax.ShapeDtypeStruct((back, *values.shape), values.dtype),
            jax.ShapeDtypeStruct((size, lanes, *weights.shape), weights.dtype),
            mine,
            mine,
            mine,
            jax.ShapeDtypeStruct(count.shape, count.dtype),
        ),
        in_specs=[any_space, any_space, any_space, vmem],
        out_specs=(any_space,) * 5 + (vmem,),
        scratch_shapes=[
            pltpu.VMEM((size, *count.shape), count.dtype),
            pltpu.SemaphoreType.DMA((kinds + 1,)),
            line,
            line,
            hop,
            hop,
            other_kinds,
            other_kinds,
            others,
            others,
            *gather_semaphores(size, 2 * lanes - 1),
        ],
        compiler_params=pltpu.CompilerParams(collective_id=5, has_side_effects=True),
        cost_estimate=pl.CostEstimate(flops=0, bytes_accessed=400 * 1024 * 1024, transcendentals=0),
        name="enter",
    )(values, weights, units, count)


def sum_query_kernel(
    size, left_ref, right_ref, *refs
):
    units, (out, back), (left, right, loads, u_send, u_recv, u_own) = (refs[:3], refs[3:5], refs[5:11])
    made, held, sent, came, *sems = refs[11:]
    me = lax.axis_index("fsdp")
    width, span = (out.shape[-1], back.shape[-1])
    rows = left.shape[1] // size
    copies = [pltpu.make_async_copy(left_ref, left, loads.at[PARTS])]
    copies += [
        pltpu.make_async_copy(
            right_ref.at[:, pl.ds(part * width, width)], right.at[part], loads.at[part]
        )
        for part in range(PARTS)
    ]
    part_of = lambda device: pl.ds(pl.multiple_of(device * span, span), span)
    stay = [
        pltpu.make_async_copy(unit.at[:, part_of(me)], back.at[me, kind], u_own.at[kind])
        for kind, unit in enumerate(units)
    ]
    for copy in copies + stay:
        copy.start()
    barrier = pltpu.get_barrier_semaphore()
    for other in range(1, size):
        pl.semaphore_signal(
            barrier, inc=1, device_id={"fsdp": flip(me, other)}, device_id_type=MESH
        )
    pl.semaphore_wait(barrier, size - 1)
    for copy in copies:
        copy.wait()

    def unit_copy(other, kind):
        peer = flip(me, other)
        return pltpu.make_async_remote_copy(
            src_ref=units[kind].at[:, part_of(peer)],
            dst_ref=back.at[me, kind],
            send_sem=u_send.at[other - 1, kind],
            recv_sem=u_recv.at[other - 1, kind],
            device_id={"fsdp": peer},
            device_id_type=MESH,
        )

    def partial(part, slot, columns):
        block = left[:, pl.ds(pl.multiple_of(slot * rows, rows), rows)]
        return contract_first(block, right[part, :, columns])

    calls, finish = scatter_steps(size, me, made, held, sent, came, sems, partial, out)
    for number, call in enumerate(calls):
        call()
        if number == len(calls) // 2:
            for other in range(1, size):
                for kind in range(3):
                    unit_copy(other, kind).start()
    for other in range(1, size):
        for kind in range(3):
            unit_copy(other, kind).wait()
    finish()
    for copy in stay:
        copy.wait()


def sum_query(size, left, right, units):
    tokens, depth = left.shape
    width = right.shape[1] // PARTS
    rows = depth // size
    any_space = pl.BlockSpec(memory_space=pl.ANY)
    vmem = pl.BlockSpec(memory_space=pltpu.VMEM)
    return pl.pallas_call(
        functools.partial(sum_query_kernel, size),
        out_shape=(
            jax.ShapeDtypeStruct((PARTS, rows, width), jnp.float32),
            jax.ShapeDtypeStruct((size, 3, units[0].shape[0], rows), jnp.bfloat16),
        ),
        in_specs=[any_space] * 5,
        out_specs=(vmem, any_space),
        scratch_shapes=[
            pltpu.VMEM((tokens, depth), jnp.bfloat16),
            pltpu.VMEM((PARTS, tokens, width), jnp.bfloat16),
            pltpu.SemaphoreType.DMA((PARTS + 1,)),
            pltpu.SemaphoreType.DMA((size - 1, 3)),
            pltpu.SemaphoreType.DMA((size - 1, 3)),
            pltpu.SemaphoreType.DMA((3,)),
            *scatter_scratch(size, rows, width),
        ],
        compiler_params=pltpu.CompilerParams(
            collective_id=6, has_side_effects=True, vmem_limit_bytes=VMEM
        ),
        cost_estimate=pl.CostEstimate(
            flops=4 * tokens * depth * width, bytes_accessed=100 * 1024 * 1024, transcendentals=0
        ),
        name="sum_query",
    )(left, right, *units)


def sum_key_kernel(size, left_ref, q_ref, kv_ref, w_ref, out, low, left, right, loads, tiles, fetch, *refs):
    made, held, sent, came, *sems = refs
    me = lax.axis_index("fsdp")
    rows = left.shape[1] // size
    parts, span = (w_ref.shape[1], tiles.shape[-1])
    copies = [pltpu.make_async_copy(left_ref, left, loads.at[PARTS])]
    copies += [
        pltpu.make_async_copy(kv_ref.at[part], right.at[part], loads.at[part])
        for part in range(PARTS)
    ]
    for copy in copies:
        copy.start()

    def tile_copy(f):
        return pltpu.make_async_copy(
            w_ref.at[f, :, :, pl.ds(0, span)], tiles.at[f % 2], fetch.at[f % 2]
        )

    tile_copy(0).start()
    greet(me, size)
    for copy in copies:
        copy.wait()

    def partial(part, slot, columns):
        block = left[:, pl.ds(pl.multiple_of(slot * rows, rows), rows)]
        return contract_first(block, right[part, :, columns])

    def low_columns(f):
        if f + 1 < size:
            tile_copy(f + 1).start()
        tile_copy(f).wait()
        half = low.shape[0] // 2

        @pl.loop(0, 2)
        def _(index):
            span_rows = pl.ds(pl.multiple_of(index * half, half), half)
            total = jnp.zeros((half, rows), jnp.float32)
            for z in range(parts):
                start = 0
                for source in (q_ref, right.at[0], right.at[1]):
                    width = source.shape[1] // parts
                    total += contract_last(
                        source[span_rows, z * width : (z + 1) * width],
                        tiles[f % 2, z, :, start : start + width],
                    )
                    start += width
            low[span_rows, f * rows : (f + 1) * rows] = total

    calls, finish = scatter_steps(size, me, made, held, sent, came, sems, partial, out)
    done = 0
    for number, call in enumerate(calls):
        call()
        goal = size * max(0, number - 1) // max(1, len(calls) - 3)
        while done < min(size, goal):
            low_columns(done)
            done += 1
    while done < size:
        low_columns(done)
        done += 1
    finish()


def sum_key(size, left, grad_query, grad_pair, weights):
    tokens, depth = left.shape
    width = grad_pair.shape[2]
    rows = depth // size
    parts = weights.shape[1]
    span = (grad_query.shape[1] + PARTS * width) // parts
    any_space = pl.BlockSpec(memory_space=pl.ANY)
    vmem = pl.BlockSpec(memory_space=pltpu.VMEM)
    return pl.pallas_call(
        functools.partial(sum_key_kernel, size),
        out_shape=(
            jax.ShapeDtypeStruct((PARTS, rows, width), jnp.float32),
            jax.ShapeDtypeStruct((tokens, depth), jnp.float32),
        ),
        in_specs=[any_space, vmem, any_space, any_space],
        out_specs=(vmem, vmem),
        scratch_shapes=[
            pltpu.VMEM((tokens, depth), jnp.bfloat16),
            pltpu.VMEM((PARTS, tokens, width), jnp.bfloat16),
            pltpu.SemaphoreType.DMA((PARTS + 1,)),
            pltpu.VMEM((2, parts, rows, span), jnp.bfloat16),
            pltpu.SemaphoreType.DMA((2,)),
            *scatter_scratch(size, rows, width),
        ],
        compiler_params=pltpu.CompilerParams(
            collective_id=7, has_side_effects=True, vmem_limit_bytes=VMEM
        ),
        cost_estimate=pl.CostEstimate(
            flops=8 * tokens * depth * width, bytes_accessed=100 * 1024 * 1024, transcendentals=0
        ),
        name="sum_key",
    )(left, grad_query, grad_pair, weights)


def sum_small_kernel(size, lanes, x_ref, o_ref, came, send, recv):
    me, z = (lax.axis_index("fsdp"), lax.axis_index("tp"))
    peers = []
    for name, index, count in (("fsdp", me, size), ("tp", z, lanes)):
        bit = 1
        while bit < count:
            peers.append({name: flip(index, bit)})
            bit *= 2
    barrier = pltpu.get_barrier_semaphore()
    for peer in peers:
        pl.semaphore_signal(barrier, inc=1, device_id=peer, device_id_type=MESH)
    pl.semaphore_wait(barrier, len(peers))
    sent = came.shape[0] // 2
    came[sent] = x_ref[...]
    for step, peer in enumerate(peers):
        copy = pltpu.make_async_remote_copy(
            src_ref=came.at[sent + step],
            dst_ref=came.at[step],
            send_sem=send.at[step],
            recv_sem=recv.at[step],
            device_id=peer,
            device_id_type=MESH,
        )
        copy.start()
        copy.wait()
        came[sent + step + 1] = came[sent + step] + came[step]
    o_ref[...] = came[sent + len(peers)]


def sum_small(size, lanes, values):
    steps = (size * lanes).bit_length() - 1
    vmem = pl.BlockSpec(memory_space=pltpu.VMEM)
    return pl.pallas_call(
        functools.partial(sum_small_kernel, size, lanes),
        out_shape=jax.ShapeDtypeStruct(values.shape, values.dtype),
        in_specs=[vmem],
        out_specs=vmem,
        scratch_shapes=[
            pltpu.VMEM((2 * (steps + 1), *values.shape), values.dtype),
            pltpu.SemaphoreType.DMA((steps,)),
            pltpu.SemaphoreType.DMA((steps,)),
        ],
        compiler_params=pltpu.CompilerParams(collective_id=8, has_side_effects=True),
        name="sum_small",
    )(values)


def project_kernel(
    wq, wk, before_ref, x_ref, gain_ref, w_ref, n_ref, q_ref, k_ref, v_ref, normed
):
    back, own, _ = before_ref.shape
    lead = back * own
    tile = min(256, own)
    z = lax.axis_index("tp")

    @pl.when(pl.program_id(0) == 0)
    def _():
        for hop in range(back + 1):

            @pl.loop(0, own // tile)
            def _(index):
                span = pl.ds(pl.multiple_of(index * tile, tile), tile)
                values = x_ref[span, :] if hop == 0 else before_ref[hop - 1, span, :]
                values = normalize_rows(values.astype(jnp.float32))[0] * gain_ref[...]
                values = values.astype(jnp.bfloat16)
                if hop:
                    values = jnp.where(z >= hop, values, jnp.zeros_like(values))
                else:
                    n_ref[span, :] = values
                at = lead - hop * own + index * tile
                normed[pl.ds(pl.multiple_of(at, tile), tile), :] = values

    weights = lambda start, size: w_ref[:, 0, :, start : start + size].reshape(D, size)

    @pl.loop(0, (lead + own) // tile)
    def _(index):
        span = pl.ds(pl.multiple_of(index * tile, tile), tile)
        pair = dot(normed[span, :], weights(wq, 2 * wk))
        k_ref[span, :] = pair[:, :wk]
        v_ref[span, :] = pair[:, wk:].astype(jnp.bfloat16)

    @pl.loop(0, own // tile)
    def _(index):
        span = pl.ds(pl.multiple_of(index * tile, tile), tile)
        from_lead = pl.ds(pl.multiple_of(lead + index * tile, tile), tile)
        q_ref[span, :] = dot(normed[from_lead, :], weights(0, wq))


def project(before, values, gain, weights, wq, wk):
    size, parts, rows_in, columns = weights.shape
    back, own, _ = before.shape
    rows = (back + 1) * own
    whole = lambda *_: (0, 0)
    return pl.pallas_call(
        functools.partial(project_kernel, wq, wk),
        grid=(parts,),
        out_shape=(
            jax.ShapeDtypeStruct((own, D), jnp.bfloat16),
            jax.ShapeDtypeStruct((own, parts * wq), jnp.float32),
            jax.ShapeDtypeStruct((rows, parts * wk), jnp.float32),
            jax.ShapeDtypeStruct((rows, parts * wk), jnp.bfloat16),
        ),
        in_specs=[
            pl.BlockSpec((back, own, D), lambda z: (0, 0, 0)),
            pl.BlockSpec((own, D), whole),
            pl.BlockSpec((1, D), whole),
            pl.BlockSpec((size, 1, rows_in, wq + 2 * wk), lambda z: (0, z, 0, 0)),
        ],
        out_specs=(
            pl.BlockSpec((own, D), whole),
            pl.BlockSpec((own, wq), lambda z: (0, z)),
            pl.BlockSpec((rows, wk), lambda z: (0, z)),
            pl.BlockSpec((rows, wk), lambda z: (0, z)),
        ),
        scratch_shapes=[pltpu.VMEM((rows, D), jnp.bfloat16)],
        compiler_params=pltpu.CompilerParams(vmem_limit_bytes=VMEM),
        cost_estimate=pl.CostEstimate(
            flops=2 * D * parts * (own * wq + rows * 2 * wk),
            bytes_accessed=2 * D * parts * (wq + 2 * wk) + 2 * rows * D,
            transcendentals=0,
        ),
        name="project_in",
    )(before, values, gain.reshape(1, D), weights)


def out_kernel(a_ref, w_ref, x_ref, o_ref):
    parts, _, width = w_ref.shape[1:]
    total = x_ref[...].astype(jnp.float32)
    for z in range(parts):
        total += contract_last(a_ref[:, z * width : (z + 1) * width], w_ref[0, z])
    o_ref[...] = total


def project_out(attended, weights, states, wo):
    size, parts, rows, columns = weights.shape
    own = states.shape[0]
    last = columns // wo - 1
    return pl.pallas_call(
        out_kernel,
        grid=(size,),
        out_shape=jax.ShapeDtypeStruct(states.shape, jnp.float32),
        in_specs=[
            pl.BlockSpec(attended.shape, lambda f: (0, 0)),
            pl.BlockSpec((1, parts, rows, wo), lambda f: (f, 0, 0, last)),
            pl.BlockSpec((own, rows), lambda f: (0, f)),
        ],
        out_specs=pl.BlockSpec((own, rows), lambda f: (0, f)),
        compiler_params=pltpu.CompilerParams(vmem_limit_bytes=VMEM),
        cost_estimate=pl.CostEstimate(
            flops=2 * own * D * parts * wo, bytes_accessed=24 * 1024 * 1024, transcendentals=0
        ),
        name="project_out",
    )(attended, weights, states)


def back_out_kernel(g_ref, w_ref, o_ref):
    size, _, rows, width = w_ref.shape
    o_ref[...] = dot(g_ref[...], w_ref[:, 0].reshape(size * rows, width)).astype(jnp.bfloat16)


def back_out(grad, weights, wo):
    size, parts, rows, columns = weights.shape
    own = grad.shape[0]
    last = columns // wo - 1
    return pl.pallas_call(
        back_out_kernel,
        grid=(parts,),
        out_shape=jax.ShapeDtypeStruct((own, parts * wo), jnp.bfloat16),
        in_specs=[
            pl.BlockSpec(grad.shape, lambda z: (0, 0)),
            pl.BlockSpec((size, 1, rows, wo), lambda z: (0, z, 0, last)),
        ],
        out_specs=pl.BlockSpec((own, wo), lambda z: (0, z)),
        compiler_params=pltpu.CompilerParams(vmem_limit_bytes=VMEM),
        cost_estimate=pl.CostEstimate(
            flops=2 * own * D * parts * wo, bytes_accessed=16 * 1024 * 1024, transcendentals=0
        ),
        name="back_out",
    )(grad, weights)


def turn(values, cosine, sine):
    return values * cosine + pltpu.roll(values, HD // 2, 1) * sine


def turn_back(grad, cosine, sine):
    return grad * cosine - pltpu.roll(grad, HD // 2, 1) * sine


def split_heads(block, group):
    return jnp.concatenate([block[:, i * HD : (i + 1) * HD] for i in range(group)], axis=0)


def join_heads(stacked, group):
    rows = stacked.shape[0] // group
    return jnp.concatenate([stacked[i * rows : (i + 1) * rows] for i in range(group)], axis=1)


def head_probs(query, keys, bias, group, scale):
    scores = contract_last(query, keys) * scale
    rows, span = scores.shape
    scores = (scores.reshape(group, rows // group, span) + bias[None]).reshape(rows, span)
    weights = jnp.exp(scores - jnp.max(scores, axis=-1, keepdims=True))
    return weights * (1.0 / jnp.sum(weights, axis=-1, keepdims=True))


def attend_kernel(
    group, step, lead, q_ref, k_ref, v_ref, bias_ref, cos_ref, sin_ref, nq_ref, nk_ref, o_ref, keys
):
    tile, span = bias_ref.shape
    scale = HD ** (-0.5)
    index = pl.program_id(1)

    @pl.when(index == 0)
    def _():
        normed = normalize_rows(k_ref[...])[0] * nk_ref[...]
        keys[...] = turn(normed, cos_ref[...], sin_ref[...]).astype(jnp.bfloat16)

    here = pl.ds(pl.multiple_of(lead + index * tile, tile), tile)
    cosine, sine = (cos_ref[here, :], sin_ref[here, :])
    normed = normalize_rows(split_heads(q_ref[...], group))[0] * nq_ref[...]
    cosine, sine = (jnp.concatenate([cosine] * group, 0), jnp.concatenate([sine] * group, 0))
    query = turn(normed, cosine, sine).astype(jnp.bfloat16)
    window = pl.ds(pl.multiple_of(index * step, tile), span)
    probs = head_probs(query, keys[window, :], bias_ref[...], group, scale)
    mixed = dot(probs.astype(jnp.bfloat16), v_ref[window, :])
    o_ref[...] = join_heads(mixed.astype(jnp.bfloat16), group)


def attend_back_kernel(
    group,
    step,
    lead,
    size,
    lanes,
    q_ref,
    k_ref,
    v_ref,
    bias_ref,
    cos_ref,
    sin_ref,
    nq_ref,
    nk_ref,
    do_ref,
    left_ref,
    right_ref,
    dq_ref,
    pair_ref,
    gq_ref,
    gk_ref,
    out_ref,
    keys,
    dk,
    dv,
    mixed,
    got,
    own_sum,
    left,
    right,
    loads,
    hop_send,
    hop_recv,
    *refs,
):
    made, held, sent, came, *sems = refs
    tile, span = bias_ref.shape
    scale = HD ** (-0.5)
    head, index = (pl.program_id(0), pl.program_id(1))
    heads, tiles = (mixed.shape[0], (k_ref.shape[0] - lead) // tile)
    back, own = (mixed.shape[1], mixed.shape[3])
    me, z = (lax.axis_index("fsdp"), lax.axis_index("tp"))
    width = out_ref.shape[-1]
    rows = left.shape[1] // size

    def hop_copy(at, number):
        return pltpu.make_async_remote_copy(
            src_ref=mixed.at[at, number],
            dst_ref=got.at[at, number],
            send_sem=hop_send.at[at, number],
            recv_sem=hop_recv.at[at, number],
            device_id={"tp": lax.rem(z + lanes - 1, lanes)},
            device_id_type=MESH,
        )

    def relay(at, number):
        @pl.when(z + 1 < lanes)
        def _():
            hop_copy(at, number - 1).wait_recv()
            total = mixed[at, number].astype(jnp.float32)
            total = total + got[at, number - 1].astype(jnp.float32)
            mixed[at, number] = total.astype(jnp.bfloat16)

        @pl.when(z > 0)
        def _():
            hop_copy(at, number).start()

    loads_of = lambda: [pltpu.make_async_copy(left_ref, left, loads.at[PARTS])] + [
        pltpu.make_async_copy(
            right_ref.at[:, pl.ds(part * width, width)], right.at[part], loads.at[part]
        )
        for part in range(PARTS)
    ]

    @pl.when((head == 0) & (index == 0))
    def _():
        for copy in loads_of():
            copy.start()
        barrier = pltpu.get_barrier_semaphore()
        peers = [{"fsdp": flip(me, bit)} for bit in [1] + chip_bits(size)]
        peers += [{"tp": lax.rem(z + 1, lanes)}, {"tp": lax.rem(z + lanes - 1, lanes)}]
        for peer in peers:
            pl.semaphore_signal(barrier, inc=1, device_id=peer, device_id_type=MESH)
        pl.semaphore_wait(barrier, len(peers))
        for copy in loads_of():
            copy.wait()
        gq_ref[...] = jnp.zeros_like(gq_ref)
        gk_ref[...] = jnp.zeros_like(gk_ref)

    def partial(part, slot, columns):
        block = left[:, pl.ds(pl.multiple_of(slot * rows, rows), rows)]
        return contract_first(block, right[part, :, columns])

    calls, finish = scatter_steps(size, me, made, held, sent, came, sems, partial, out_ref)
    at_step = {}
    for number, call in enumerate(calls):
        at_step.setdefault(number * heads * tiles // len(calls), []).append(call)
    for number, some in at_step.items():

        @pl.when(head * tiles + index == number)
        def _():
            for call in some:
                call()

    @pl.when(index == 0)
    def _():
        normed = normalize_rows(k_ref[...])[0] * nk_ref[...]
        keys[...] = turn(normed, cos_ref[...], sin_ref[...]).astype(jnp.bfloat16)
        dk[...] = jnp.zeros_like(dk)
        dv[...] = jnp.zeros_like(dv)

    here = pl.ds(pl.multiple_of(lead + index * tile, tile), tile)
    cosine, sine = (cos_ref[here, :], sin_ref[here, :])
    cosine, sine = (jnp.concatenate([cosine] * group, 0), jnp.concatenate([sine] * group, 0))
    normed, factor = normalize_rows(split_heads(q_ref[...], group))
    query = turn(normed * nq_ref[...], cosine, sine).astype(jnp.bfloat16)
    window = pl.ds(pl.multiple_of(index * step, tile), span)
    probs = head_probs(query, keys[window, :], bias_ref[...], group, scale)
    grad_out = split_heads(do_ref[...], group)
    dv[window, :] += contract_first(probs.astype(jnp.bfloat16), grad_out)
    grad_probs = contract_last(grad_out, v_ref[window, :])
    centre = jnp.sum(probs * grad_probs, axis=-1, keepdims=True)
    grad_scores = (probs * (grad_probs - centre)).astype(jnp.bfloat16)
    dk[window, :] += contract_first(grad_scores, query) * scale
    grad_query = turn_back(dot(grad_scores, keys[window, :]) * scale, cosine, sine)
    gq_ref[...] += jnp.sum(grad_query * normed, axis=0, keepdims=True)
    grad_raw = norm_back(grad_query, normed, factor, nq_ref[...])
    dq_ref[...] = join_heads(grad_raw.astype(jnp.bfloat16), group)

    @pl.when(index == tiles - 1)
    def _():
        normed_key, key_factor = normalize_rows(k_ref[...])
        grad_key = turn_back(dk[...], cos_ref[...], sin_ref[...])
        gk_ref[...] += jnp.sum(grad_key * normed_key, axis=0, keepdims=True)
        grad_key = norm_back(grad_key, normed_key, key_factor, nk_ref[...])
        for number in range(back):
            block = slice(number * own, (number + 1) * own)
            mixed[head, number, 0] = grad_key[block].astype(jnp.bfloat16)
            mixed[head, number, 1] = dv[block, :].astype(jnp.bfloat16)
        own_sum[head, 0] = grad_key[lead:]
        own_sum[head, 1] = dv[lead:, :]

        @pl.when(z > 0)
        def _():
            hop_copy(head, 0).start()

        for number in range(1, back):

            @pl.when(head >= number)
            def _():
                relay(head - number, number)

    @pl.when((head == heads - 1) & (index == tiles - 1))
    def _():
        for number in range(1, back):
            for at in range(heads - number, heads):
                relay(at, number)
        for at in range(heads):
            columns = slice(at * HD, (at + 1) * HD)

            @pl.when(z + 1 < lanes)
            def _():
                hop_copy(at, back - 1).wait_recv()
                total = own_sum[at] + got[at, back - 1].astype(jnp.float32)
                pair_ref[:, :, columns] = total.astype(jnp.bfloat16)

            @pl.when(z + 1 == lanes)
            def _():
                pair_ref[:, :, columns] = own_sum[at].astype(jnp.bfloat16)

            @pl.when(z > 0)
            def _():
                for number in range(back):
                    hop_copy(at, number).wait_send()

        finish()


def attention_specs(own, rows, group, tile, span):
    whole = lambda g, t: (0, 0)
    return [
        pl.BlockSpec((tile, group * HD), lambda g, t: (t, g)),
        pl.BlockSpec((rows, HD), lambda g, t: (0, g)),
        pl.BlockSpec((rows, HD), lambda g, t: (0, g)),
        pl.BlockSpec((tile, span), lambda g, t: (t, 0)),
        pl.BlockSpec((rows, HD), whole),
        pl.BlockSpec((rows, HD), whole),
        pl.BlockSpec((1, HD), whole),
        pl.BlockSpec((1, HD), whole),
    ]


def attend(queries, keys, values, bias, cosine, sine, norm_query, norm_key, tile, step):
    own, rows = (queries.shape[0], keys.shape[0])
    heads = keys.shape[1] // HD
    group = queries.shape[1] // keys.shape[1]
    span = bias.shape[1]
    return pl.pallas_call(
        functools.partial(attend_kernel, group, step, rows - own),
        grid=(heads, own // tile),
        out_shape=jax.ShapeDtypeStruct(queries.shape, jnp.bfloat16),
        in_specs=attention_specs(own, rows, group, tile, span),
        out_specs=pl.BlockSpec((tile, group * HD), lambda g, t: (t, g)),
        scratch_shapes=[pltpu.VMEM((rows, HD), jnp.bfloat16)],
        compiler_params=pltpu.CompilerParams(vmem_limit_bytes=VMEM),
        cost_estimate=pl.CostEstimate(
            flops=16 * own * span * queries.shape[1],
            bytes_accessed=4 * queries.size + 6 * keys.size,
            transcendentals=own * span * heads * group,
        ),
        name="attend",
    )(queries, keys, values, bias, cosine, sine, norm_query, norm_key)


def attend_back(
    queries,
    keys,
    values,
    bias,
    cosine,
    sine,
    norm_query,
    norm_key,
    grad,
    tile,
    step,
    left,
    right,
    size,
    lanes,
):
    own, rows = (queries.shape[0], keys.shape[0])
    heads = keys.shape[1] // HD
    group = queries.shape[1] // keys.shape[1]
    span = bias.shape[1]
    lead = rows - own
    back = lead // own
    tokens, depth = left.shape
    width = right.shape[1] // PARTS
    whole = lambda g, t: (0, 0)
    any_space = pl.BlockSpec(memory_space=pl.ANY)
    return pl.pallas_call(
        functools.partial(attend_back_kernel, group, step, lead, size, lanes),
        grid=(heads, own // tile),
        out_shape=(
            jax.ShapeDtypeStruct(queries.shape, jnp.bfloat16),
            jax.ShapeDtypeStruct((2, own, heads * HD), jnp.bfloat16),
            jax.ShapeDtypeStruct((1, HD), jnp.float32),
            jax.ShapeDtypeStruct((1, HD), jnp.float32),
            jax.ShapeDtypeStruct((PARTS, depth // size, width), jnp.float32),
        ),
        in_specs=attention_specs(own, rows, group, tile, span)
        + [pl.BlockSpec((tile, group * HD), lambda g, t: (t, g)), any_space, any_space],
        out_specs=(
            pl.BlockSpec((tile, group * HD), lambda g, t: (t, g)),
            pl.BlockSpec((2, own, heads * HD), lambda g, t: (0, 0, 0)),
            pl.BlockSpec((1, HD), whole),
            pl.BlockSpec((1, HD), whole),
            pl.BlockSpec((PARTS, depth // size, width), lambda g, t: (0, 0, 0)),
        ),
        scratch_shapes=[
            pltpu.VMEM((rows, HD), jnp.bfloat16),
            pltpu.VMEM((rows, HD), jnp.float32),
            pltpu.VMEM((rows, HD), jnp.float32),
            pltpu.VMEM((heads, back, 2, own, HD), jnp.bfloat16),
            pltpu.VMEM((heads, back, 2, own, HD), jnp.bfloat16),
            pltpu.VMEM((heads, 2, own, HD), jnp.float32),
            pltpu.VMEM((tokens, depth), jnp.bfloat16),
            pltpu.VMEM((PARTS, tokens, width), jnp.bfloat16),
            pltpu.SemaphoreType.DMA((PARTS + 1,)),
            pltpu.SemaphoreType.DMA((heads, back)),
            pltpu.SemaphoreType.DMA((heads, back)),
            *scatter_scratch(size, depth // size, width),
        ],
        compiler_params=pltpu.CompilerParams(
            collective_id=9, has_side_effects=True, vmem_limit_bytes=60 * 1024 * 1024
        ),
        cost_estimate=pl.CostEstimate(
            flops=40 * own * span * queries.shape[1],
            bytes_accessed=8 * queries.size + 16 * keys.size,
            transcendentals=own * span * heads * group,
        ),
        name="attend_back",
    )(queries, keys, values, bias, cosine, sine, norm_query, norm_key, grad, left, right)


def window_tables(length_row, pad_row, first, own, lead, tile, span):
    places = first - lead + jnp.arange(lead + own, dtype=jnp.int32)
    ends = jnp.cumsum(length_row)
    passed = places[:, None] >= ends[None, :]
    docs = jnp.sum(passed.astype(jnp.int32), axis=1)
    starts = jnp.sum(jnp.where(passed, length_row[None, :], 0), axis=1)
    freqs = THETA ** (-(jnp.arange(HD // 2).astype(jnp.float32) * 2.0 / HD))
    angles = (places - starts).astype(jnp.float32)[:, None] * freqs[None, :]
    cosine, sine = (jnp.cos(angles), jnp.sin(angles))
    padded = jnp.concatenate((jnp.zeros((lead,), pad_row.dtype), pad_row))
    live = lax.dynamic_slice_in_dim(padded, first, lead + own, 0)
    step = tile if lead + own > span else 0
    masks = []
    for index in range(own // tile):
        at = lead + index * tile
        query, key = (places[at : at + tile, None], places[None, index * step : index * step + span])
        same = docs[at : at + tile, None] == docs[None, index * step : index * step + span]
        seen = (live[None, index * step : index * step + span] == 1) | (key == query)
        masks.append((key >= 0) & (key <= query) & (query - key < WINDOW) & same & seen)
    bias = jnp.where(jnp.concatenate(masks, axis=0), 0.0, NEG).astype(jnp.float32)
    cosine = jnp.concatenate((cosine, cosine), axis=1)
    sine = jnp.concatenate((-sine, sine), axis=1)
    return (bias, cosine, sine, step, live[lead:].astype(jnp.float32))


def over_lanes(grad):
    return lax.psum_scatter(
        grad.astype(jnp.bfloat16), "tp", scatter_dimension=2, tiled=True
    ).astype(jnp.float32)


def join_parts(halves):
    return jnp.concatenate([halves[part] for part in range(PARTS)], axis=1)


def shards(
    states,
    lengths,
    padding,
    teacher,
    norm_attn,
    w_query,
    w_key,
    w_value,
    norm_query,
    norm_key,
    w_out,
    norm_mlp,
    w_gate,
    w_up,
    w_down,
):
    own = states.shape[0]
    n_tp, n_fsdp = (lax.axis_size("tp"), lax.axis_size("fsdp"))
    first = lax.axis_index("tp") * own
    back = min(n_tp - 1, -(-WINDOW // own))
    lead = back * own
    tile = min(256, own)
    span = WINDOW + tile if lead >= WINDOW else lead + own
    wq, wk = (w_query.shape[1], w_key.shape[1])
    bias, cosine, sine, step, live = window_tables(
        lengths[0], padding[0], first, own, lead, tile, span
    )
    joined = jnp.concatenate((w_query, w_key, w_value, w_out.T), axis=1)
    wo = w_out.shape[0]
    units = [
        part.reshape(n_fsdp, -1, part.shape[1]) for part in (w_gate.T, w_up.T, w_down)
    ]
    live_here = jnp.full((8, 128), jnp.sum(padding).astype(jnp.float32))
    before, weights_attn, *mine, counts = enter(
        n_fsdp, n_tp, back, states, joined, jnp.stack(units, axis=1), live_here
    )
    count = counts[0, 0]
    rows_gate, rows_up, rows_down = [
        lax.all_gather(part, "tp", axis=0, tiled=True) for part in mine
    ]
    normed_in, query_raw, key_raw, value = project(
        before, states, norm_attn, weights_attn, wq, wk
    )
    gains = (norm_query.reshape(1, HD), norm_key.reshape(1, HD))
    attended = attend(query_raw, key_raw, value, bias, cosine, sine, *gains, tile, step)
    inputs = states.astype(jnp.float32)
    hidden_one = project_out(attended, weights_attn, states, wo)
    normed_two, factor_two = normalize_rows(hidden_one)
    whole_two, gate, up, product = gate_up(
        n_fsdp, (normed_two * norm_mlp).astype(jnp.bfloat16), rows_gate, rows_up
    )
    outputs = hidden_one + sum_products(n_fsdp, 2, (product,), (rows_down,))
    errors = (outputs - teacher.astype(jnp.float32)) * live[:, None]
    squares = jnp.sum(errors * errors)
    grad_out = errors * (2.0 / (count * D))

    grad_gate, grad_up, by_unit = grad_hidden_units(
        n_fsdp, grad_out.astype(jnp.bfloat16), rows_down, gate, up, product, whole_two
    )
    grad_mid = sum_products(n_fsdp, 4, (grad_gate, grad_up), (rows_gate, rows_up))
    by_unit = [lax.psum_scatter(part, "tp", scatter_dimension=0, tiled=True) for part in by_unit]
    grad_norm_mlp = jnp.sum(grad_mid * normed_two, axis=0)
    grad_hidden = grad_out + norm_back(grad_mid, normed_two, factor_two, norm_mlp)

    grad_low_out = grad_hidden.astype(jnp.bfloat16)
    grad_attended = back_out(grad_low_out, weights_attn, wo)
    grad_query, grad_pair, grad_norm_query, grad_norm_key, sums_out = attend_back(
        query_raw,
        key_raw,
        value,
        bias,
        cosine,
        sine,
        *gains,
        grad_attended,
        tile,
        step,
        grad_low_out,
        attended,
        n_fsdp,
        n_tp,
    )
    by_unit, sums_out = lax.optimization_barrier((by_unit, sums_out))
    sums_query, units_back = sum_query(n_fsdp, normed_in, grad_query, by_unit)
    sums_query, grad_pair = lax.optimization_barrier((sums_query, grad_pair))
    sums_pair, grad_low = sum_key(n_fsdp, normed_in, grad_query, grad_pair, weights_attn)
    grad_w_out, grad_w_query = [
        over_lanes(join_parts(sums)[None])[0] for sums in (sums_out, sums_query)
    ]
    sums_pair, grad_w_query, grad_w_out = lax.optimization_barrier(
        (sums_pair, grad_w_query, grad_w_out)
    )
    grad_w_pair = over_lanes(sums_pair)
    grad_w_down, grad_w_gate, grad_w_up = [
        units_back[:, kind].reshape(-1, units_back.shape[3]).astype(jnp.float32)
        for kind in range(3)
    ]
    normed_one, factor_one = normalize_rows(inputs)
    grad_norm_attn = jnp.sum(grad_low * normed_one, axis=0)
    grad_input = grad_hidden + norm_back(grad_low, normed_one, factor_one, norm_attn)
    small = [grad_norm_attn, grad_norm_mlp, grad_norm_query[0], grad_norm_key[0]]
    small.append(jnp.full((HD,), squares))
    joined_small = jnp.concatenate(small).reshape(-1, HD)
    filled = joined_small.shape[0]
    joined_small = jnp.pad(joined_small, ((0, -filled % 8), (0, 0)))
    summed = sum_small(n_fsdp, n_tp, joined_small)[:filled].reshape(-1)
    grad_norm_attn, grad_norm_mlp = (summed[:D], summed[D : 2 * D])
    grad_norm_query, grad_norm_key = (summed[2 * D : 2 * D + HD], summed[2 * D + HD : 2 * D + 2 * HD])
    squares = summed[2 * D + 2 * HD]
    return (
        outputs,
        squares / (count * D),
        grad_input,
        grad_norm_attn,
        grad_w_query,
        grad_w_pair[0],
        grad_w_pair[1],
        grad_norm_query,
        grad_norm_key,
        grad_w_out.T,
        grad_norm_mlp,
        grad_w_gate.T,
        grad_w_up.T,
        grad_w_down,
    )


def solution(mesh):
    tokens = P(("fsdp", "tp"), None)
    rows, columns, sequences = (P("fsdp", "tp"), P("tp", "fsdp"), P("fsdp", None))
    in_specs = (
        tokens,
        sequences,
        sequences,
        tokens,
        P(),
        rows,
        rows,
        rows,
        P(),
        P(),
        columns,
        P(),
        rows,
        rows,
        columns,
    )
    out_specs = (
        tokens,
        P(),
        tokens,
        P(),
        rows,
        rows,
        rows,
        P(),
        P(),
        columns,
        P(),
        rows,
        rows,
        columns,
    )
    return jax.shard_map(shards, mesh=mesh, in_specs=in_specs, out_specs=out_specs, check_vma=False)
```

```python
import functools

import jax
import jax.numpy as jnp
from jax import lax
from jax.experimental import pallas as pl
from jax.experimental.pallas import tpu as pltpu
from jax.sharding import PartitionSpec as P

D = 2048
HD = 128
WINDOW = 1024

EPS = 1e-06
THETA = 1000000.0
NEG = -1e30
VMEM = 56 * 1024 * 1024


def normalize_rows(values):
    factor = lax.rsqrt(jnp.mean(values * values, axis=-1, keepdims=True) + EPS)
    return (values * factor, factor)


def norm_back(grad, normed, factor, gain):
    scaled = grad * gain
    return factor * (scaled - normed * jnp.mean(scaled * normed, axis=-1, keepdims=True))


def contract_last(left, right):
    return lax.dot_general(
        left, right, (((1,), (1,)), ((), ())), preferred_element_type=jnp.float32
    )


def contract_first(left, right):
    return lax.dot_general(
        left, right, (((0,), (0,)), ((), ())), preferred_element_type=jnp.float32
    )


def dot(left, right):
    return jnp.dot(left, right, preferred_element_type=jnp.float32)


MESH = pl.DeviceIdType.MESH
PARTS = 2


def flip(index, mask):
    bit = 1
    while bit <= mask:
        if mask & bit:
            index = index + bit - 2 * bit * lax.rem(lax.div(index, bit), 2)
        bit *= 2
    return index


def chip_bits(size):
    bits = []
    bit = 2
    while bit < size:
        bits.append(bit)
        bit *= 2
    return bits


def orders(size):
    bits = chip_bits(size)
    return (bits, bits[::-1])


def mask_of(pattern, order):
    return sum(bit for i, bit in enumerate(order) if pattern >> i & 1)


def top(pattern):
    return pattern.bit_length() - 1


def greet(me, size):
    barrier = pltpu.get_barrier_semaphore()
    bits = [1] + chip_bits(size)
    for bit in bits:
        pl.semaphore_signal(
            barrier, inc=1, device_id={"fsdp": flip(me, bit)}, device_id_type=MESH
        )
    pl.semaphore_wait(barrier, len(bits))


def pick(part, pair):
    return pair[0] + part * (pair[1] - pair[0])


def unit_loads(source, kind, target, sems):
    lanes, _, rows, _ = source.shape
    return [
        pltpu.make_async_copy(
            source.at[lane, kind], target.at[pl.ds(lane * rows, rows)], sems.at[lane]
        )
        for lane in range(lanes)
    ]


class Gather:
    def __init__(self, size, me, whole, sems, parts=PARTS, lane=lambda part: part, parity=lambda part: part, own=None):
        self.size, self.me, self.whole, self.parts = (size, me, whole, parts)
        self.lane, self.parity, self.own = (lane, parity, own)
        self.chip_send, self.chip_recv, self.core_send, self.core_recv = sems
        self.steps = len(chip_bits(size))
        self.patterns = sorted(range(1 << self.steps), key=lambda m: (top(m), m))

    def order(self, part):
        return orders(self.size)[self.parity(part) % 2]

    def slot(self, part, pattern, sibling):
        return flip(self.me, mask_of(pattern, self.order(part)) + sibling)

    def source(self, part, pattern, block):
        return self.own if self.own is not None and part == 0 and pattern == 0 else block

    def chip_copy(self, part, step, pattern):
        block = self.whole.at[self.slot(part, pattern, 0), self.lane(part)]
        number = (1 << step) - 1 + pattern
        return pltpu.make_async_remote_copy(
            src_ref=self.source(part, pattern, block),
            dst_ref=block,
            send_sem=self.chip_send.at[part, number],
            recv_sem=self.chip_recv.at[part, number],
            device_id={"fsdp": flip(self.me, self.order(part)[step])},
            device_id_type=MESH,
        )

    def core_copy(self, part, pattern):
        block = self.whole.at[self.slot(part, pattern, 0), self.lane(part)]
        return pltpu.make_async_remote_copy(
            src_ref=self.source(part, pattern, block),
            dst_ref=block,
            send_sem=self.core_send.at[part, pattern],
            recv_sem=self.core_recv.at[part, pattern],
            device_id={"fsdp": flip(self.me, 1)},
            device_id_type=MESH,
        )

    def arrive(self, part, pattern):
        if pattern:
            step = top(pattern)
            self.chip_copy(part, step, pattern - (1 << step)).wait_recv()

    def forward(self, part, pattern):
        for step in range(top(pattern) + 1, self.steps):
            self.chip_copy(part, step, pattern).start()
        self.core_copy(part, pattern).start()

    def pairs(self, work):
        for pattern in self.patterns:
            for part in range(self.parts):
                self.arrive(part, pattern)
            for part in range(self.parts):
                self.forward(part, pattern)
            work([self.slot(part, pattern, 0) for part in range(self.parts)])
            for part in range(self.parts):
                self.core_copy(part, pattern).wait_recv()
            work([self.slot(part, pattern, 1) for part in range(self.parts)])

    def finish(self):
        for pattern in self.patterns:
            for part in range(self.parts):
                for step in range(top(pattern) + 1, self.steps):
                    self.chip_copy(part, step, pattern).wait_send()
                self.core_copy(part, pattern).wait_send()


def gather_semaphores(size, parts=PARTS):
    moves = max(1, size // 2 - 1)
    return [
        pltpu.SemaphoreType.DMA((parts, moves)),
        pltpu.SemaphoreType.DMA((parts, moves)),
        pltpu.SemaphoreType.DMA((parts, size // 2)),
        pltpu.SemaphoreType.DMA((parts, size // 2)),
    ]


def first_step(pattern, steps):
    return (pattern & -pattern).bit_length() - 1 if pattern else steps


def scatter_order(steps):
    return sorted(range(1 << steps), key=lambda m: (first_step(m, steps), -bin(m).count("1"), m))


def scatter_steps(
    size, me, made, held, sent, came, sems, partial, final, ready=lambda part, slot, q, sibling: None
):
    chip_send, chip_recv, core_send, core_recv = sems
    steps = len(chip_bits(size))
    order = [bits[::-1] for bits in orders(size)]
    first = lambda m: first_step(m, steps)
    patterns = scatter_order(steps)
    place = {m: q for q, m in enumerate(patterns)}
    width = final.shape[-1]
    chunk = min(512, width)

    def slots(pattern, sibling):
        return [flip(me, mask_of(pattern, order[part]) + sibling) for part in range(PARTS)]

    def core_copy(part, q):
        return pltpu.make_async_remote_copy(
            src_ref=made.at[part, q],
            dst_ref=held.at[part, q],
            send_sem=core_send.at[part, q],
            recv_sem=core_recv.at[part, q],
            device_id={"fsdp": flip(me, 1)},
            device_id_type=MESH,
        )

    def chip_copy(part, q):
        return pltpu.make_async_remote_copy(
            src_ref=sent.at[part, q],
            dst_ref=came.at[part, q],
            send_sem=chip_send.at[part, q],
            recv_sem=chip_recv.at[part, q],
            device_id={"fsdp": flip(me, order[part][first(patterns[q])])},
            device_id_type=MESH,
        )

    def for_sibling(q):
        pair = slots(patterns[q], 1)
        for part in range(PARTS):
            ready(part, pair[part], q, 1)

            @pl.loop(0, width // chunk)
            def _(index):
                columns = pl.ds(pl.multiple_of(index * chunk, chunk), chunk)
                made[part, q, :, columns] = partial(part, pair[part], columns).astype(jnp.bfloat16)

            core_copy(part, q).start()

    def for_chips(q):
        pattern = patterns[q]
        pair = slots(pattern, 0)
        arrivals = [place[pattern | 1 << step] for step in range(first(pattern))]
        for part in range(PARTS):
            ready(part, pair[part], q, 0)
            if pattern:
                core_copy(part, q).wait_recv()
                for arrival in arrivals:
                    chip_copy(part, arrival).wait_recv()

            @pl.loop(0, width // chunk)
            def _(index):
                columns = pl.ds(pl.multiple_of(index * chunk, chunk), chunk)
                total = partial(part, pair[part], columns)
                if pattern:
                    total = total + held[part, q, :, columns].astype(jnp.float32)
                    for arrival in arrivals:
                        total = total + came[part, arrival, :, columns].astype(jnp.float32)
                    sent[part, q, :, columns] = total.astype(jnp.bfloat16)
                else:
                    final[part, :, columns] = total

            if pattern:
                chip_copy(part, q).start()
        if not pattern:
            for part in range(PARTS):
                core_copy(part, q).wait_recv()
                for arrival in arrivals:
                    chip_copy(part, arrival).wait_recv()

                @pl.loop(0, width // chunk)
                def _(index):
                    columns = pl.ds(pl.multiple_of(index * chunk, chunk), chunk)
                    total = final[part, :, columns] + held[part, q, :, columns].astype(jnp.float32)
                    for arrival in arrivals:
                        total = total + came[part, arrival, :, columns].astype(jnp.float32)
                    final[part, :, columns] = total

    def finish():
        for q in range(len(patterns)):
            for part in range(PARTS):
                core_copy(part, q).wait_send()
                if patterns[q]:
                    chip_copy(part, q).wait_send()

    calls = []
    for q in range(len(patterns)):
        calls += [functools.partial(for_sibling, q), functools.partial(for_chips, q)]
    return (calls, finish)


def scatter_scratch(size, rows, width):
    held = size // 2
    moved = max(1, held - 1)
    return [
        pltpu.VMEM((PARTS, held, rows, width), jnp.bfloat16),
        pltpu.VMEM((PARTS, held, rows, width), jnp.bfloat16),
        pltpu.VMEM((PARTS, moved, rows, width), jnp.bfloat16),
        pltpu.VMEM((PARTS, moved, rows, width), jnp.bfloat16),
        pltpu.SemaphoreType.DMA((PARTS, moved)),
        pltpu.SemaphoreType.DMA((PARTS, moved)),
        pltpu.SemaphoreType.DMA((PARTS, held)),
        pltpu.SemaphoreType.DMA((PARTS, held)),
    ]


def gate_up_kernel(
    size,
    x_ref,
    w_in,
    x_out,
    gate_out,
    up_out,
    prod_out,
    whole,
    wg_ref,
    wu_ref,
    gate,
    up,
    prod,
    load,
    keep,
    store,
    *sems,
):
    me = lax.axis_index("fsdp")
    hidden = wg_ref.shape[0]
    chunk = 256 if hidden % 256 == 0 else 128
    lanes = w_in.shape[0]
    loads = [pltpu.make_async_copy(x_ref, whole.at[me], load.at[0])]
    loads += unit_loads(w_in, 0, wg_ref, load.at[pl.ds(1, lanes)])
    loads += unit_loads(w_in, 1, wu_ref, load.at[pl.ds(1 + lanes, lanes)])
    for copy in loads:
        copy.start()
    greet(me, size)
    loads[0].wait()
    state = {"count": 0, "last": None}

    def stores(part, at):
        return [
            pltpu.make_async_copy(buffer.at[part], out.at[at, part], store.at[part, i])
            for i, (buffer, out) in enumerate(((gate, gate_out), (up, up_out), (prod, prod_out)))
        ]

    def work(pair):
        count, last = (state["count"], state["last"])
        for part in range(PARTS):
            pltpu.make_async_copy(
                whole.at[pair[part], part], x_out.at[pair[part], part], keep.at[part, count]
            ).start()
        if last is None:
            for copy in loads[1:]:
                copy.wait()

        @pl.loop(0, PARTS)
        def _(part):
            at = pick(part, pair)
            if last is not None:
                for copy in stores(part, pick(part, last)):
                    copy.wait()

            @pl.loop(0, hidden // chunk)
            def _(index):
                units = pl.ds(pl.multiple_of(index * chunk, chunk), chunk)
                rows = whole[at, part]
                gates = contract_last(rows, wg_ref[units, :])
                ups = contract_last(rows, wu_ref[units, :])
                gate[part, :, units] = gates
                up[part, :, units] = ups
                prod[part, :, units] = (gates * jax.nn.sigmoid(gates) * ups).astype(jnp.bfloat16)

            for copy in stores(part, at):
                copy.start()

        state["count"], state["last"] = (count + 1, pair)
        state.setdefault("all", []).append(pair)

    gather = Gather(size, me, whole, sems)
    gather.pairs(work)
    gather.finish()
    for part in range(PARTS):
        for copy in stores(part, state["last"][part]):
            copy.wait()
        for count, pair in enumerate(state["all"]):
            pltpu.make_async_copy(
                whole.at[pair[part], part], x_out.at[pair[part], part], keep.at[part, count]
            ).wait()


def gate_up(size, values, units):
    own, width = values.shape
    lanes, _, each, _ = units.shape
    rows, hidden = (own // PARTS, lanes * each)
    any_space = pl.BlockSpec(memory_space=pl.ANY)
    shape = lambda columns, kind: jax.ShapeDtypeStruct((size, PARTS, rows, columns), kind)
    outs = pl.pallas_call(
        functools.partial(gate_up_kernel, size),
        out_shape=(
            shape(width, jnp.bfloat16),
            shape(hidden, jnp.float32),
            shape(hidden, jnp.float32),
            shape(hidden, jnp.bfloat16),
        ),
        in_specs=[any_space] * 2,
        out_specs=(any_space,) * 4,
        scratch_shapes=[
            pltpu.VMEM((size, PARTS, rows, width), jnp.bfloat16),
            pltpu.VMEM((hidden, width), jnp.bfloat16),
            pltpu.VMEM((hidden, width), jnp.bfloat16),
            pltpu.VMEM((PARTS, rows, hidden), jnp.float32),
            pltpu.VMEM((PARTS, rows, hidden), jnp.float32),
            pltpu.VMEM((PARTS, rows, hidden), jnp.bfloat16),
            pltpu.SemaphoreType.DMA((1 + 2 * lanes,)),
            pltpu.SemaphoreType.DMA((PARTS, size)),
            pltpu.SemaphoreType.DMA((PARTS, 3)),
            *gather_semaphores(size),
        ],
        compiler_params=pltpu.CompilerParams(
            collective_id=1, has_side_effects=True, vmem_limit_bytes=VMEM
        ),
        cost_estimate=pl.CostEstimate(
            flops=4 * size * own * width * hidden, bytes_accessed=200 * 1024 * 1024, transcendentals=0
        ),
        name="gate_up",
    )(values.reshape(PARTS, rows, width), units)
    return tuple(out.reshape(size * own, -1) for out in outs)


def grad_hidden_kernel(
    size,
    x_ref,
    wd_in,
    gate_in,
    up_in,
    prod_in,
    two_in,
    dgate_out,
    dup_out,
    early_out,
    late_out,
    whole,
    wd_ref,
    gate,
    up,
    prod,
    two,
    dgate,
    dup,
    sums,
    load,
    fetch,
    store,
    flush,
    *sems,
):
    me = lax.axis_index("fsdp")
    hidden, width = wd_ref.shape
    lanes, _, each, _ = wd_in.shape
    chunk = 256 if hidden % 256 == 0 else 128
    loads = [pltpu.make_async_copy(x_ref, whole.at[me], load.at[0])]
    loads += unit_loads(wd_in, 0, wd_ref, load.at[pl.ds(1, lanes)])
    for copy in loads:
        copy.start()

    def stores(part, at):
        return [
            pltpu.make_async_copy(buffer.at[part], out.at[at, part], store.at[part, i])
            for i, (buffer, out) in enumerate(((dgate, dgate_out), (dup, dup_out)))
        ]

    def fetches(count, kinds):
        copies = []
        for part in range(PARTS):
            at = order[count][part]
            pairs = (
                (gate_in, gate.at[part]),
                (up_in, up.at[part]),
                (prod_in, prod.at[count % 2, part]),
                (two_in, two.at[count % 2, part]),
            )
            copies += [
                pltpu.make_async_copy(pairs[i][0].at[at, part], pairs[i][1], fetch.at[count % 2, part, i])
                for i in kinds
            ]
        return copies

    gather = Gather(size, me, whole, sems)
    order = []
    for pattern in gather.patterns:
        for sibling in (0, 1):
            order.append([gather.slot(part, pattern, sibling) for part in range(PARTS)])
    for copy in fetches(0, (0, 1, 2, 3)):
        copy.start()
    greet(me, size)
    loads[0].wait()
    state = {"count": 0}

    def work(pair):
        count = state["count"]
        state["count"] = count + 1
        more = count + 1 < len(order)
        if count == 0:
            for copy in loads[1:]:
                copy.wait()
        if more:
            for copy in fetches(count + 1, (2, 3)):
                copy.start()
        for copy in fetches(count, (0, 1)):
            copy.wait()
        if count:
            for part in range(PARTS):
                for copy in stores(part, order[count - 1][part]):
                    copy.wait()

        @pl.loop(0, PARTS)
        def _(part):
            at = pick(part, pair)

            @pl.loop(0, hidden // chunk)
            def _(index):
                units = pl.ds(pl.multiple_of(index * chunk, chunk), chunk)
                grads = contract_last(whole[at, part], wd_ref[units, :])
                gates = gate[part, :, units]
                sigmoid = jax.nn.sigmoid(gates)
                dgate[part, :, units] = (
                    grads * up[part, :, units] * sigmoid * (1.0 + gates * (1.0 - sigmoid))
                ).astype(jnp.bfloat16)
                dup[part, :, units] = (grads * (gates * sigmoid)).astype(jnp.bfloat16)

        for part in range(PARTS):
            for copy in stores(part, pair[part]):
                copy.start()
        if more:
            for copy in fetches(count + 1, (0, 1)):
                copy.start()
        for copy in fetches(count, (2, 3)):
            copy.wait()

        @pl.loop(0, hidden // chunk)
        def _(index):
            units = pl.ds(pl.multiple_of(index * chunk, chunk), chunk)
            here = count % 2
            for kind, (lefts, rights) in enumerate(
                (
                    ((prod.at[here, 0], prod.at[here, 1]), (whole.at[pair[0], 0], whole.at[pair[1], 1])),
                    ((dgate.at[0], dgate.at[1]), (two.at[here, 0], two.at[here, 1])),
                    ((dup.at[0], dup.at[1]), (two.at[here, 0], two.at[here, 1])),
                )
            ):
                total = contract_first(lefts[0][:, units], rights[0][...])
                total += contract_first(lefts[1][:, units], rights[1][...])
                if count:
                    total += sums[kind, units, :]
                sums[kind, units, :] = total

    gather.pairs(work)
    gather.finish()
    for part in range(PARTS):
        for copy in stores(part, order[-1][part]):
            copy.wait()
    copies = []
    for piece in range(3 * lanes):
        kind, lane = (piece // lanes, piece % lanes)
        block = whole.at[piece // PARTS, piece % PARTS, pl.ds(0, each)]
        block[...] = sums[kind, lane * each : (lane + 1) * each, :].astype(jnp.bfloat16)
        out = early_out.at[lane, kind] if kind < 2 else late_out.at[lane, 0]
        copy = pltpu.make_async_copy(block, out, flush.at[piece])
        copy.start()
        copies.append(copy)
    for copy in copies:
        copy.wait()


def grad_hidden_units(size, values, units, gate, up, product, whole_two):
    own, width = values.shape
    lanes, _, each, _ = units.shape
    rows, hidden = (own // PARTS, lanes * each)
    any_space = pl.BlockSpec(memory_space=pl.ANY)
    shape = lambda columns, kind: jax.ShapeDtypeStruct((size, PARTS, rows, columns), kind)
    blocks = lambda array: array.reshape(size, PARTS, rows, -1)
    weight = lambda kinds: jax.ShapeDtypeStruct((lanes, kinds, each, width), jnp.bfloat16)
    dgate, dup, early, late = pl.pallas_call(
        functools.partial(grad_hidden_kernel, size),
        out_shape=(shape(hidden, jnp.bfloat16), shape(hidden, jnp.bfloat16), weight(2), weight(1)),
        in_specs=[any_space] * 6,
        out_specs=(any_space,) * 4,
        scratch_shapes=[
            pltpu.VMEM((size, PARTS, rows, width), jnp.bfloat16),
            pltpu.VMEM((hidden, width), jnp.bfloat16),
            pltpu.VMEM((PARTS, rows, hidden), jnp.float32),
            pltpu.VMEM((PARTS, rows, hidden), jnp.float32),
            pltpu.VMEM((2, PARTS, rows, hidden), jnp.bfloat16),
            pltpu.VMEM((2, PARTS, rows, width), jnp.bfloat16),
            pltpu.VMEM((PARTS, rows, hidden), jnp.bfloat16),
            pltpu.VMEM((PARTS, rows, hidden), jnp.bfloat16),
            pltpu.VMEM((3, hidden, width), jnp.float32),
            pltpu.SemaphoreType.DMA((1 + lanes,)),
            pltpu.SemaphoreType.DMA((2, PARTS, 4)),
            pltpu.SemaphoreType.DMA((PARTS, 2)),
            pltpu.SemaphoreType.DMA((3 * lanes,)),
            *gather_semaphores(size),
        ],
        compiler_params=pltpu.CompilerParams(
            collective_id=3, has_side_effects=True, vmem_limit_bytes=60 * 1024 * 1024
        ),
        cost_estimate=pl.CostEstimate(
            flops=8 * size * own * width * hidden, bytes_accessed=200 * 1024 * 1024, transcendentals=0
        ),
        name="grad_hidden_units",
    )(values.reshape(PARTS, rows, width), units, *map(blocks, (gate, up, product, whole_two)))
    return (dgate.reshape(size * own, hidden), dup.reshape(size * own, hidden), early, late)


def sum_products_kernel(size, terms, *refs):
    left_in, right_in, out = (refs[:terms], refs[terms], refs[terms + 1])
    at = terms + 2
    lefts, rights, (w_load, x_load) = (
        refs[at : at + terms],
        refs[at + terms : at + 2 * terms],
        refs[at + 2 * terms : at + 2 * terms + 2],
    )
    made, held, sent, came, *sems = refs[at + 2 * terms + 2 :]
    me = lax.axis_index("fsdp")

    def partial(part, slot, columns):
        return sum(
            dot(left[slot, part], right[:, columns]) for left, right in zip(lefts, rights)
        )

    def tiles(part, slot, q, sibling):
        return [
            pltpu.make_async_copy(
                source.at[slot, part], left.at[slot, part], x_load.at[2 * q + sibling, part, i]
            )
            for i, (source, left) in enumerate(zip(left_in, lefts))
        ]

    seen = []

    def ready(part, slot, q, sibling):
        if not seen:
            for copy in weights:
                copy.wait()
        seen.append(slot)
        for copy in tiles(part, slot, q, sibling):
            copy.wait()

    weights = []
    for kind, right in enumerate(rights):
        weights += unit_loads(right_in, kind, right, w_load.at[kind])
    for copy in weights:
        copy.start()
    order = [bits[::-1] for bits in orders(size)]
    for q, pattern in enumerate(scatter_order(len(order[0]))):
        for sibling in (1, 0):
            for part in range(PARTS):
                slot = flip(me, mask_of(pattern, order[part]) + sibling)
                for copy in tiles(part, slot, q, sibling):
                    copy.start()
    greet(me, size)
    calls, finish = scatter_steps(size, me, made, held, sent, came, sems, partial, out, ready)
    for call in calls:
        call()
    finish()


def sum_products(size, number, lefts, units):
    total, hidden = lefts[0].shape
    lanes, _, _, width = units.shape
    rows = total // size // PARTS
    vmem = pl.BlockSpec(memory_space=pltpu.VMEM)
    terms = len(lefts)
    out = pl.pallas_call(
        functools.partial(sum_products_kernel, size, terms),
        out_shape=jax.ShapeDtypeStruct((PARTS, rows, width), jnp.float32),
        in_specs=[pl.BlockSpec(memory_space=pl.ANY)] * (terms + 1),
        out_specs=vmem,
        scratch_shapes=[
            *[pltpu.VMEM((size, PARTS, rows, hidden), jnp.bfloat16)] * terms,
            *[pltpu.VMEM((hidden, width), jnp.bfloat16)] * terms,
            pltpu.SemaphoreType.DMA((terms, lanes)),
            pltpu.SemaphoreType.DMA((size, PARTS, terms)),
            *scatter_scratch(size, rows, width),
        ],
        compiler_params=pltpu.CompilerParams(
            collective_id=number, has_side_effects=True, vmem_limit_bytes=VMEM
        ),
        cost_estimate=pl.CostEstimate(
            flops=2 * total * hidden * width * terms, bytes_accessed=200 * 1024 * 1024, transcendentals=0
        ),
        name="sum_products",
    )(*[left.reshape(size, PARTS, rows, hidden) for left in lefts], units)
    return out.reshape(PARTS * rows, width)


def enter_kernel(
    size,
    lanes,
    back,
    x_ref,
    w_ref,
    m_ref,
    c_ref,
    before,
    whole,
    mine_pair,
    mine_down,
    count,
    counts,
    loads,
    z_send,
    z_recv,
    x_send,
    x_recv,
    m_send,
    m_recv,
    c_send,
    c_recv,
    *sems,
):
    me, z = (lax.axis_index("fsdp"), lax.axis_index("tp"))
    mine = (mine_pair.at[0], mine_pair.at[1], mine_down.at[0])
    span = m_ref.shape[-1]
    part_of = lambda device: pl.ds(pl.multiple_of(device * span, span), span)
    local = [pltpu.make_async_copy(w_ref, whole.at[me, z], loads.at[0])]
    local += [
        pltpu.make_async_copy(m_ref.at[me, kind], mine[kind].at[:, part_of(me)], loads.at[kind + 1])
        for kind in range(3)
    ]
    for copy in local:
        copy.start()
    counts[me] = c_ref[...]
    up, down = (lax.rem(z + 1, lanes), lax.rem(z + lanes - 1, lanes))
    barrier = pltpu.get_barrier_semaphore()
    peers = [{"fsdp": flip(me, other)} for other in range(1, size)] + [{"tp": up}, {"tp": down}]
    for peer in peers:
        pl.semaphore_signal(barrier, inc=1, device_id=peer, device_id_type=MESH)
    pl.semaphore_wait(barrier, len(peers))

    def far(part):
        return (part + 1) // 2

    def lane(part):
        if part == 0:
            return z
        return z - far(part) if part % 2 else z + far(part)

    def exists(part):
        return z >= far(part) if part % 2 else z + far(part) < lanes

    def lane_copy(part):
        block = whole.at[me, lane(part - 2) if part > 2 else z]
        return pltpu.make_async_remote_copy(
            src_ref=block if part > 2 else w_ref,
            dst_ref=block,
            send_sem=z_send.at[part - 1],
            recv_sem=z_recv.at[part - 1],
            device_id={"tp": up if part % 2 else down},
            device_id_type=MESH,
        )

    def lane_sends(part):
        if part % 2:
            return (z >= far(part) - 1) & (z + 1 < lanes)
        return (z + far(part) - 1 < lanes) & (z > 0)

    def token_copy(hop):
        return pltpu.make_async_remote_copy(
            src_ref=x_ref if hop == 1 else before.at[hop - 2],
            dst_ref=before.at[hop - 1],
            send_sem=x_send.at[hop - 1],
            recv_sem=x_recv.at[hop - 1],
            device_id={"tp": up},
            device_id_type=MESH,
        )

    def unit_copy(other, kind):
        peer = flip(me, other)
        return pltpu.make_async_remote_copy(
            src_ref=m_ref.at[peer, kind],
            dst_ref=mine[kind].at[:, part_of(me)],
            send_sem=m_send.at[other - 1, kind],
            recv_sem=m_recv.at[other - 1, kind],
            device_id={"fsdp": peer},
            device_id_type=MESH,
        )

    def count_copy(other):
        return pltpu.make_async_remote_copy(
            src_ref=c_ref,
            dst_ref=counts.at[me],
            send_sem=c_send.at[other - 1],
            recv_sem=c_recv.at[other - 1],
            device_id={"fsdp": flip(me, other)},
            device_id_type=MESH,
        )

    def when(condition, run):
        pl.when(condition)(run)

    gather = Gather(size, me, whole, sems, 2 * lanes - 1, lane, far, w_ref)
    for part in (1, 2):
        when(lane_sends(part), lambda: lane_copy(part).start())
    gather.forward(0, 0)
    when(z + 1 < lanes, lambda: token_copy(1).start())
    for other in range(1, size):
        count_copy(other).start()
        for kind in range(3):
            unit_copy(other, kind).start()
    events = [(part, pattern) for part in range(2 * lanes - 1) for pattern in gather.patterns]
    wave = lambda pattern: 3.5 * top(pattern) + 2.5 if pattern else 0
    events.sort(key=lambda event: (2 * far(event[0]) + wave(event[1]), event))

    def run_event(part, pattern):
        if pattern:
            gather.arrive(part, pattern)
        elif part:
            lane_copy(part).wait_recv()
            if part + 2 < 2 * lanes - 1:
                when(lane_sends(part + 2), lambda: lane_copy(part + 2).start())
        gather.forward(part, pattern)

    for part, pattern in events[1:]:
        if part == 0:
            run_event(part, pattern)
        else:
            when(exists(part), lambda: run_event(part, pattern))
        if (part, pattern) == (2 * lanes - 2, 0):
            for hop in range(1, back):
                when(z >= hop, lambda: token_copy(hop).wait_recv())
                when((z >= hop) & (z + 1 < lanes), lambda: token_copy(hop + 1).start())
    for other in range(1, size):
        count_copy(other).wait()
    count[...] = sum(counts[other] for other in range(size))

    def close(part):
        for pattern in gather.patterns:
            gather.core_copy(part, pattern).wait()
            for step in range(top(pattern) + 1, gather.steps):
                gather.chip_copy(part, step, pattern).wait_send()

    close(0)
    for part in range(1, 2 * lanes - 1):
        when(exists(part), lambda: close(part))
        when(lane_sends(part), lambda: lane_copy(part).wait_send())
    for other in range(1, size):
        for kind in range(3):
            unit_copy(other, kind).wait()
    for hop in range(1, back + 1):
        when((z >= hop - 1) & (z + 1 < lanes), lambda: token_copy(hop).wait_send())
    when(z >= back, lambda: token_copy(back).wait_recv())
    for copy in local:
        copy.wait()


def enter(size, lanes, back, values, weights, units, count):
    any_space = pl.BlockSpec(memory_space=pl.ANY)
    vmem = pl.BlockSpec(memory_space=pltpu.VMEM)
    _, kinds, rows, columns = units.shape
    others = pltpu.SemaphoreType.DMA((size - 1,))
    other_kinds = pltpu.SemaphoreType.DMA((size - 1, kinds))
    line = pltpu.SemaphoreType.DMA((2 * lanes - 2,))
    hop = pltpu.SemaphoreType.DMA((back,))
    mine = lambda number: jax.ShapeDtypeStruct((number, rows, size * columns), units.dtype)
    return pl.pallas_call(
        functools.partial(enter_kernel, size, lanes, back),
        out_shape=(
            jax.ShapeDtypeStruct((back, *values.shape), values.dtype),
            jax.ShapeDtypeStruct((size, lanes, *weights.shape), weights.dtype),
            mine(2),
            mine(1),
            jax.ShapeDtypeStruct(count.shape, count.dtype),
        ),
        in_specs=[any_space, any_space, any_space, vmem],
        out_specs=(any_space,) * 4 + (vmem,),
        scratch_shapes=[
            pltpu.VMEM((size, *count.shape), count.dtype),
            pltpu.SemaphoreType.DMA((kinds + 1,)),
            line,
            line,
            hop,
            hop,
            other_kinds,
            other_kinds,
            others,
            others,
            *gather_semaphores(size, 2 * lanes - 1),
        ],
        compiler_params=pltpu.CompilerParams(collective_id=5, has_side_effects=True),
        cost_estimate=pl.CostEstimate(flops=0, bytes_accessed=400 * 1024 * 1024, transcendentals=0),
        name="enter",
    )(values, weights, units, count)


class Units:
    def __init__(self, size, me, units, back, sems):
        self.size, self.me, self.units, self.back = (size, me, units, back)
        self.send, self.recv, self.own = sems
        self.kinds, self.span = (units.shape[0], back.shape[-1])

    def part_of(self, device):
        return pl.ds(pl.multiple_of(device * self.span, self.span), self.span)

    def stay(self):
        return [
            pltpu.make_async_copy(
                self.units.at[kind, :, self.part_of(self.me)],
                self.back.at[self.me, kind],
                self.own.at[kind],
            )
            for kind in range(self.kinds)
        ]

    def moves(self):
        copies = []
        for other in range(1, self.size):
            peer = flip(self.me, other)
            copies += [
                pltpu.make_async_remote_copy(
                    src_ref=self.units.at[kind, :, self.part_of(peer)],
                    dst_ref=self.back.at[self.me, kind],
                    send_sem=self.send.at[other - 1, kind],
                    recv_sem=self.recv.at[other - 1, kind],
                    device_id={"fsdp": peer},
                    device_id_type=MESH,
                )
                for kind in range(self.kinds)
            ]
        return copies

    def start(self):
        for copy in self.stay() + self.moves():
            copy.start()

    def finish(self):
        for copy in self.moves() + self.stay():
            copy.wait()


def units_scratch(size, kinds):
    return [
        pltpu.SemaphoreType.DMA((size - 1, kinds)),
        pltpu.SemaphoreType.DMA((size - 1, kinds)),
        pltpu.SemaphoreType.DMA((kinds,)),
    ]


class Lanes:
    def __init__(self, lanes, z, values, out, low, came, send, recv):
        self.lanes, self.z, self.values, self.out = (lanes, z, values, out)
        self.low, self.came, self.send, self.recv = (low, came, send, recv)

    def block(self, lane):
        each = self.lanes // PARTS
        width = self.out.shape[1]
        start = pl.multiple_of(lax.rem(lane, each) * width, width)
        return self.values[lax.div(lane, each), :, pl.ds(start, width)]

    def copy(self, hop):
        return pltpu.make_async_remote_copy(
            src_ref=self.low.at[hop - 1],
            dst_ref=self.came.at[hop - 1],
            send_sem=self.send.at[hop - 1],
            recv_sem=self.recv.at[hop - 1],
            device_id={"tp": lax.rem(self.z + hop, self.lanes)},
            device_id_type=MESH,
        )

    def start(self):
        for hop in range(1, self.lanes):
            self.low[hop - 1] = self.block(lax.rem(self.z + hop, self.lanes)).astype(jnp.bfloat16)
            self.copy(hop).start()

    def finish(self):
        for hop in range(1, self.lanes):
            self.copy(hop).wait()
        total = self.block(self.z)
        for hop in range(1, self.lanes):
            total = total + self.came[hop - 1].astype(jnp.float32)
        self.out[...] = total


def lanes_scratch(lanes, rows, width):
    return [
        pltpu.VMEM((lanes - 1, rows, width), jnp.bfloat16),
        pltpu.VMEM((lanes - 1, rows, width), jnp.bfloat16),
        pltpu.SemaphoreType.DMA((lanes - 1,)),
        pltpu.SemaphoreType.DMA((lanes - 1,)),
    ]


def greet_all(me, z, size, lanes):
    barrier = pltpu.get_barrier_semaphore()
    peers = [{"fsdp": flip(me, other)} for other in range(1, size)]
    peers += [{"tp": lax.rem(z + hop, lanes)} for hop in range(1, lanes)]
    for peer in peers:
        pl.semaphore_signal(barrier, inc=1, device_id=peer, device_id_type=MESH)
    pl.semaphore_wait(barrier, len(peers))


def sum_query_kernel(
    size, lanes, left_ref, right_ref, units_ref, sums_ref, out, back, lane_out, left, right, loads, *refs
):
    units_sems, lane_refs = (refs[:3], refs[3:7])
    made, held, sent, came, *sems = refs[7:]
    me, z = (lax.axis_index("fsdp"), lax.axis_index("tp"))
    width = out.shape[-1]
    rows = left.shape[1] // size
    copies = [pltpu.make_async_copy(left_ref, left, loads.at[PARTS])]
    copies += [
        pltpu.make_async_copy(
            right_ref.at[:, pl.ds(part * width, width)], right.at[part], loads.at[part]
        )
        for part in range(PARTS)
    ]
    for copy in copies:
        copy.start()
    greet_all(me, z, size, lanes)
    for copy in copies:
        copy.wait()

    def partial(part, slot, columns):
        block = left[:, pl.ds(pl.multiple_of(slot * rows, rows), rows)]
        return contract_first(block, right[part, :, columns])

    units = Units(size, me, units_ref, back, units_sems)
    across = Lanes(lanes, z, sums_ref, lane_out, *lane_refs)
    calls, finish = scatter_steps(size, me, made, held, sent, came, sems, partial, out)
    for number, call in enumerate(calls):
        call()
        if number == 1:
            across.start()
        if number == len(calls) // 2:
            units.start()
    across.finish()
    units.finish()
    finish()


def sum_query(size, lanes, left, right, units, sums):
    tokens, depth = left.shape
    width = right.shape[1] // PARTS
    rows = depth // size
    lane_width = sums.shape[2] * PARTS // lanes
    any_space = pl.BlockSpec(memory_space=pl.ANY)
    vmem = pl.BlockSpec(memory_space=pltpu.VMEM)
    return pl.pallas_call(
        functools.partial(sum_query_kernel, size, lanes),
        out_shape=(
            jax.ShapeDtypeStruct((PARTS, rows, width), jnp.float32),
            jax.ShapeDtypeStruct((size, *units.shape[:2], rows), jnp.bfloat16),
            jax.ShapeDtypeStruct((rows, lane_width), jnp.float32),
        ),
        in_specs=[any_space] * 3 + [vmem],
        out_specs=(vmem, any_space, vmem),
        scratch_shapes=[
            pltpu.VMEM((tokens, depth), jnp.bfloat16),
            pltpu.VMEM((PARTS, tokens, width), jnp.bfloat16),
            pltpu.SemaphoreType.DMA((PARTS + 1,)),
            *units_scratch(size, units.shape[0]),
            *lanes_scratch(lanes, rows, lane_width),
            *scatter_scratch(size, rows, width),
        ],
        compiler_params=pltpu.CompilerParams(
            collective_id=6, has_side_effects=True, vmem_limit_bytes=VMEM
        ),
        cost_estimate=pl.CostEstimate(
            flops=4 * tokens * depth * width, bytes_accessed=100 * 1024 * 1024, transcendentals=0
        ),
        name="sum_query",
    )(left, right, units, sums)


def sum_key_kernel(
    size,
    lanes,
    left_ref,
    q_ref,
    kv_ref,
    w_ref,
    units_ref,
    sums_ref,
    out,
    low,
    back,
    lane_out,
    left,
    right,
    loads,
    tiles,
    fetch,
    *refs,
):
    units_sems, lane_refs = (refs[:3], refs[3:7])
    made, held, sent, came, *sems = refs[7:]
    me, z = (lax.axis_index("fsdp"), lax.axis_index("tp"))
    rows = left.shape[1] // size
    parts, span = (w_ref.shape[1], tiles.shape[-1])
    copies = [pltpu.make_async_copy(left_ref, left, loads.at[PARTS])]
    copies += [
        pltpu.make_async_copy(kv_ref.at[part], right.at[part], loads.at[part])
        for part in range(PARTS)
    ]
    for copy in copies:
        copy.start()

    def tile_copy(f):
        return pltpu.make_async_copy(
            w_ref.at[f, :, :, pl.ds(0, span)], tiles.at[f % 2], fetch.at[f % 2]
        )

    tile_copy(0).start()
    greet_all(me, z, size, lanes)
    for copy in copies:
        copy.wait()

    def partial(part, slot, columns):
        block = left[:, pl.ds(pl.multiple_of(slot * rows, rows), rows)]
        return contract_first(block, right[part, :, columns])

    def low_columns(f):
        if f + 1 < size:
            tile_copy(f + 1).start()
        tile_copy(f).wait()
        half = low.shape[0] // 2

        @pl.loop(0, 2)
        def _(index):
            span_rows = pl.ds(pl.multiple_of(index * half, half), half)
            total = jnp.zeros((half, rows), jnp.float32)
            for z in range(parts):
                start = 0
                for source in (q_ref, right.at[0], right.at[1]):
                    width = source.shape[1] // parts
                    total += contract_last(
                        source[span_rows, z * width : (z + 1) * width],
                        tiles[f % 2, z, :, start : start + width],
                    )
                    start += width
            low[span_rows, f * rows : (f + 1) * rows] = total

    units = Units(size, me, units_ref, back, units_sems)
    across = Lanes(lanes, z, sums_ref, lane_out, *lane_refs)
    calls, finish = scatter_steps(size, me, made, held, sent, came, sems, partial, out)
    done = 0
    for number, call in enumerate(calls):
        call()
        if number == 1:
            across.start()
        if number == len(calls) // 2:
            units.start()
        goal = size * max(0, number - 1) // max(1, len(calls) - 3)
        while done < min(size, goal):
            low_columns(done)
            done += 1
    while done < size:
        low_columns(done)
        done += 1
    across.finish()
    units.finish()
    finish()


def sum_key(size, lanes, left, grad_query, grad_pair, weights, units, sums):
    tokens, depth = left.shape
    width = grad_pair.shape[2]
    rows = depth // size
    parts = weights.shape[1]
    span = (grad_query.shape[1] + PARTS * width) // parts
    lane_width = sums.shape[2] * PARTS // lanes
    any_space = pl.BlockSpec(memory_space=pl.ANY)
    vmem = pl.BlockSpec(memory_space=pltpu.VMEM)
    return pl.pallas_call(
        functools.partial(sum_key_kernel, size, lanes),
        out_shape=(
            jax.ShapeDtypeStruct((PARTS, rows, width), jnp.float32),
            jax.ShapeDtypeStruct((tokens, depth), jnp.float32),
            jax.ShapeDtypeStruct((size, *units.shape[:2], rows), jnp.bfloat16),
            jax.ShapeDtypeStruct((rows, lane_width), jnp.float32),
        ),
        in_specs=[any_space, vmem, any_space, any_space, any_space, vmem],
        out_specs=(vmem, vmem, any_space, vmem),
        scratch_shapes=[
            pltpu.VMEM((tokens, depth), jnp.bfloat16),
            pltpu.VMEM((PARTS, tokens, width), jnp.bfloat16),
            pltpu.SemaphoreType.DMA((PARTS + 1,)),
            pltpu.VMEM((2, parts, rows, span), jnp.bfloat16),
            pltpu.SemaphoreType.DMA((2,)),
            *units_scratch(size, units.shape[0]),
            *lanes_scratch(lanes, rows, lane_width),
            *scatter_scratch(size, rows, width),
        ],
        compiler_params=pltpu.CompilerParams(
            collective_id=7, has_side_effects=True, vmem_limit_bytes=VMEM
        ),
        cost_estimate=pl.CostEstimate(
            flops=8 * tokens * depth * width, bytes_accessed=100 * 1024 * 1024, transcendentals=0
        ),
        name="sum_key",
    )(left, grad_query, grad_pair, weights, units, sums)


def sum_small_kernel(size, lanes, x_ref, o_ref, came, send, recv):
    me, z = (lax.axis_index("fsdp"), lax.axis_index("tp"))
    peers = []
    for name, index, count in (("fsdp", me, size), ("tp", z, lanes)):
        bit = 1
        while bit < count:
            peers.append({name: flip(index, bit)})
            bit *= 2
    barrier = pltpu.get_barrier_semaphore()
    for peer in peers:
        pl.semaphore_signal(barrier, inc=1, device_id=peer, device_id_type=MESH)
    pl.semaphore_wait(barrier, len(peers))
    sent = came.shape[0] // 2
    came[sent] = x_ref[...]
    for step, peer in enumerate(peers):
        copy = pltpu.make_async_remote_copy(
            src_ref=came.at[sent + step],
            dst_ref=came.at[step],
            send_sem=send.at[step],
            recv_sem=recv.at[step],
            device_id=peer,
            device_id_type=MESH,
        )
        copy.start()
        copy.wait()
        came[sent + step + 1] = came[sent + step] + came[step]
    o_ref[...] = came[sent + len(peers)]


def sum_small(size, lanes, values):
    steps = (size * lanes).bit_length() - 1
    vmem = pl.BlockSpec(memory_space=pltpu.VMEM)
    return pl.pallas_call(
        functools.partial(sum_small_kernel, size, lanes),
        out_shape=jax.ShapeDtypeStruct(values.shape, values.dtype),
        in_specs=[vmem],
        out_specs=vmem,
        scratch_shapes=[
            pltpu.VMEM((2 * (steps + 1), *values.shape), values.dtype),
            pltpu.SemaphoreType.DMA((steps,)),
            pltpu.SemaphoreType.DMA((steps,)),
        ],
        compiler_params=pltpu.CompilerParams(collective_id=8, has_side_effects=True),
        name="sum_small",
    )(values)


def project_kernel(
    wq, wk, before_ref, x_ref, gain_ref, w_ref, n_ref, q_ref, k_ref, v_ref, normed
):
    back, own, _ = before_ref.shape
    lead = back * own
    tile = min(256, own)
    z = lax.axis_index("tp")

    @pl.when(pl.program_id(0) == 0)
    def _():
        for hop in range(back + 1):

            @pl.loop(0, own // tile)
            def _(index):
                span = pl.ds(pl.multiple_of(index * tile, tile), tile)
                values = x_ref[span, :] if hop == 0 else before_ref[hop - 1, span, :]
                values = normalize_rows(values.astype(jnp.float32))[0] * gain_ref[...]
                values = values.astype(jnp.bfloat16)
                if hop:
                    values = jnp.where(z >= hop, values, jnp.zeros_like(values))
                else:
                    n_ref[span, :] = values
                at = lead - hop * own + index * tile
                normed[pl.ds(pl.multiple_of(at, tile), tile), :] = values

    weights = lambda start, size: w_ref[:, 0, :, start : start + size].reshape(D, size)

    @pl.loop(0, (lead + own) // tile)
    def _(index):
        span = pl.ds(pl.multiple_of(index * tile, tile), tile)
        pair = dot(normed[span, :], weights(wq, 2 * wk))
        k_ref[span, :] = pair[:, :wk]
        v_ref[span, :] = pair[:, wk:].astype(jnp.bfloat16)

    @pl.loop(0, own // tile)
    def _(index):
        span = pl.ds(pl.multiple_of(index * tile, tile), tile)
        from_lead = pl.ds(pl.multiple_of(lead + index * tile, tile), tile)
        q_ref[span, :] = dot(normed[from_lead, :], weights(0, wq))


def project(before, values, gain, weights, wq, wk):
    size, parts, rows_in, columns = weights.shape
    back, own, _ = before.shape
    rows = (back + 1) * own
    whole = lambda *_: (0, 0)
    return pl.pallas_call(
        functools.partial(project_kernel, wq, wk),
        grid=(parts,),
        out_shape=(
            jax.ShapeDtypeStruct((own, D), jnp.bfloat16),
            jax.ShapeDtypeStruct((own, parts * wq), jnp.float32),
            jax.ShapeDtypeStruct((rows, parts * wk), jnp.float32),
            jax.ShapeDtypeStruct((rows, parts * wk), jnp.bfloat16),
        ),
        in_specs=[
            pl.BlockSpec((back, own, D), lambda z: (0, 0, 0)),
            pl.BlockSpec((own, D), whole),
            pl.BlockSpec((1, D), whole),
            pl.BlockSpec((size, 1, rows_in, wq + 2 * wk), lambda z: (0, z, 0, 0)),
        ],
        out_specs=(
            pl.BlockSpec((own, D), whole),
            pl.BlockSpec((own, wq), lambda z: (0, z)),
            pl.BlockSpec((rows, wk), lambda z: (0, z)),
            pl.BlockSpec((rows, wk), lambda z: (0, z)),
        ),
        scratch_shapes=[pltpu.VMEM((rows, D), jnp.bfloat16)],
        compiler_params=pltpu.CompilerParams(vmem_limit_bytes=VMEM),
        cost_estimate=pl.CostEstimate(
            flops=2 * D * parts * (own * wq + rows * 2 * wk),
            bytes_accessed=2 * D * parts * (wq + 2 * wk) + 2 * rows * D,
            transcendentals=0,
        ),
        name="project_in",
    )(before, values, gain.reshape(1, D), weights)


def out_kernel(a_ref, w_ref, x_ref, o_ref):
    parts, _, width = w_ref.shape[1:]
    total = x_ref[...].astype(jnp.float32)
    for z in range(parts):
        total += contract_last(a_ref[:, z * width : (z + 1) * width], w_ref[0, z])
    o_ref[...] = total


def project_out(attended, weights, states, wo):
    size, parts, rows, columns = weights.shape
    own = states.shape[0]
    last = columns // wo - 1
    return pl.pallas_call(
        out_kernel,
        grid=(size,),
        out_shape=jax.ShapeDtypeStruct(states.shape, jnp.float32),
        in_specs=[
            pl.BlockSpec(attended.shape, lambda f: (0, 0)),
            pl.BlockSpec((1, parts, rows, wo), lambda f: (f, 0, 0, last)),
            pl.BlockSpec((own, rows), lambda f: (0, f)),
        ],
        out_specs=pl.BlockSpec((own, rows), lambda f: (0, f)),
        compiler_params=pltpu.CompilerParams(vmem_limit_bytes=VMEM),
        cost_estimate=pl.CostEstimate(
            flops=2 * own * D * parts * wo, bytes_accessed=24 * 1024 * 1024, transcendentals=0
        ),
        name="project_out",
    )(attended, weights, states)


def back_out_kernel(g_ref, w_ref, o_ref):
    size, _, rows, width = w_ref.shape
    o_ref[...] = dot(g_ref[...], w_ref[:, 0].reshape(size * rows, width)).astype(jnp.bfloat16)


def back_out(grad, weights, wo):
    size, parts, rows, columns = weights.shape
    own = grad.shape[0]
    last = columns // wo - 1
    return pl.pallas_call(
        back_out_kernel,
        grid=(parts,),
        out_shape=jax.ShapeDtypeStruct((own, parts * wo), jnp.bfloat16),
        in_specs=[
            pl.BlockSpec(grad.shape, lambda z: (0, 0)),
            pl.BlockSpec((size, 1, rows, wo), lambda z: (0, z, 0, last)),
        ],
        out_specs=pl.BlockSpec((own, wo), lambda z: (0, z)),
        compiler_params=pltpu.CompilerParams(vmem_limit_bytes=VMEM),
        cost_estimate=pl.CostEstimate(
            flops=2 * own * D * parts * wo, bytes_accessed=16 * 1024 * 1024, transcendentals=0
        ),
        name="back_out",
    )(grad, weights)


def turn(values, cosine, sine):
    return values * cosine + pltpu.roll(values, HD // 2, 1) * sine


def turn_back(grad, cosine, sine):
    return grad * cosine - pltpu.roll(grad, HD // 2, 1) * sine


def split_heads(block, group):
    return jnp.concatenate([block[:, i * HD : (i + 1) * HD] for i in range(group)], axis=0)


def join_heads(stacked, group):
    rows = stacked.shape[0] // group
    return jnp.concatenate([stacked[i * rows : (i + 1) * rows] for i in range(group)], axis=1)


def head_probs(query, keys, bias, group, scale):
    scores = contract_last(query, keys) * scale
    rows, span = scores.shape
    scores = (scores.reshape(group, rows // group, span) + bias[None]).reshape(rows, span)
    weights = jnp.exp(scores - jnp.max(scores, axis=-1, keepdims=True))
    return weights * (1.0 / jnp.sum(weights, axis=-1, keepdims=True))


def attend_kernel(
    group, step, lead, q_ref, k_ref, v_ref, bias_ref, cos_ref, sin_ref, nq_ref, nk_ref, o_ref, keys
):
    tile, span = bias_ref.shape
    scale = HD ** (-0.5)
    index = pl.program_id(1)

    @pl.when(index == 0)
    def _():
        normed = normalize_rows(k_ref[...])[0] * nk_ref[...]
        keys[...] = turn(normed, cos_ref[...], sin_ref[...]).astype(jnp.bfloat16)

    here = pl.ds(pl.multiple_of(lead + index * tile, tile), tile)
    cosine, sine = (cos_ref[here, :], sin_ref[here, :])
    normed = normalize_rows(split_heads(q_ref[...], group))[0] * nq_ref[...]
    cosine, sine = (jnp.concatenate([cosine] * group, 0), jnp.concatenate([sine] * group, 0))
    query = turn(normed, cosine, sine).astype(jnp.bfloat16)
    window = pl.ds(pl.multiple_of(index * step, tile), span)
    probs = head_probs(query, keys[window, :], bias_ref[...], group, scale)
    mixed = dot(probs.astype(jnp.bfloat16), v_ref[window, :])
    o_ref[...] = join_heads(mixed.astype(jnp.bfloat16), group)


def attend_back_kernel(
    group,
    step,
    lead,
    size,
    lanes,
    q_ref,
    k_ref,
    v_ref,
    bias_ref,
    cos_ref,
    sin_ref,
    nq_ref,
    nk_ref,
    do_ref,
    left_ref,
    right_ref,
    dq_ref,
    pair_ref,
    gq_ref,
    gk_ref,
    out_ref,
    keys,
    dk,
    dv,
    mixed,
    got,
    own_sum,
    left,
    right,
    loads,
    hop_send,
    hop_recv,
    *refs,
):
    made, held, sent, came, *sems = refs
    tile, span = bias_ref.shape
    scale = HD ** (-0.5)
    head, index = (pl.program_id(0), pl.program_id(1))
    heads, tiles = (mixed.shape[0], (k_ref.shape[0] - lead) // tile)
    back, own = (mixed.shape[1], mixed.shape[3])
    me, z = (lax.axis_index("fsdp"), lax.axis_index("tp"))
    width = out_ref.shape[-1]
    rows = left.shape[1] // size

    def hop_copy(at, number):
        return pltpu.make_async_remote_copy(
            src_ref=mixed.at[at, number],
            dst_ref=got.at[at, number],
            send_sem=hop_send.at[at, number],
            recv_sem=hop_recv.at[at, number],
            device_id={"tp": lax.rem(z + lanes - 1, lanes)},
            device_id_type=MESH,
        )

    def relay(at, number):
        @pl.when(z + 1 < lanes)
        def _():
            hop_copy(at, number - 1).wait_recv()
            total = mixed[at, number].astype(jnp.float32)
            total = total + got[at, number - 1].astype(jnp.float32)
            mixed[at, number] = total.astype(jnp.bfloat16)

        @pl.when(z > 0)
        def _():
            hop_copy(at, number).start()

    loads_of = lambda: [pltpu.make_async_copy(left_ref, left, loads.at[PARTS])] + [
        pltpu.make_async_copy(
            right_ref.at[:, pl.ds(part * width, width)], right.at[part], loads.at[part]
        )
        for part in range(PARTS)
    ]

    @pl.when((head == 0) & (index == 0))
    def _():
        for copy in loads_of():
            copy.start()
        barrier = pltpu.get_barrier_semaphore()
        peers = [{"fsdp": flip(me, bit)} for bit in [1] + chip_bits(size)]
        peers += [{"tp": lax.rem(z + 1, lanes)}, {"tp": lax.rem(z + lanes - 1, lanes)}]
        for peer in peers:
            pl.semaphore_signal(barrier, inc=1, device_id=peer, device_id_type=MESH)
        pl.semaphore_wait(barrier, len(peers))
        for copy in loads_of():
            copy.wait()
        gq_ref[...] = jnp.zeros_like(gq_ref)
        gk_ref[...] = jnp.zeros_like(gk_ref)

    def partial(part, slot, columns):
        block = left[:, pl.ds(pl.multiple_of(slot * rows, rows), rows)]
        return contract_first(block, right[part, :, columns])

    calls, finish = scatter_steps(size, me, made, held, sent, came, sems, partial, out_ref)
    at_step = {}
    for number, call in enumerate(calls):
        at_step.setdefault(number * heads * tiles // len(calls), []).append(call)
    for number, some in at_step.items():

        @pl.when(head * tiles + index == number)
        def _():
            for call in some:
                call()

    @pl.when(index == 0)
    def _():
        normed = normalize_rows(k_ref[...])[0] * nk_ref[...]
        keys[...] = turn(normed, cos_ref[...], sin_ref[...]).astype(jnp.bfloat16)
        dk[...] = jnp.zeros_like(dk)
        dv[...] = jnp.zeros_like(dv)

    here = pl.ds(pl.multiple_of(lead + index * tile, tile), tile)
    cosine, sine = (cos_ref[here, :], sin_ref[here, :])
    cosine, sine = (jnp.concatenate([cosine] * group, 0), jnp.concatenate([sine] * group, 0))
    normed, factor = normalize_rows(split_heads(q_ref[...], group))
    query = turn(normed * nq_ref[...], cosine, sine).astype(jnp.bfloat16)
    window = pl.ds(pl.multiple_of(index * step, tile), span)
    probs = head_probs(query, keys[window, :], bias_ref[...], group, scale)
    grad_out = split_heads(do_ref[...], group)
    dv[window, :] += contract_first(probs.astype(jnp.bfloat16), grad_out)
    grad_probs = contract_last(grad_out, v_ref[window, :])
    centre = jnp.sum(probs * grad_probs, axis=-1, keepdims=True)
    grad_scores = (probs * (grad_probs - centre)).astype(jnp.bfloat16)
    dk[window, :] += contract_first(grad_scores, query) * scale
    grad_query = turn_back(dot(grad_scores, keys[window, :]) * scale, cosine, sine)
    gq_ref[...] += jnp.sum(grad_query * normed, axis=0, keepdims=True)
    grad_raw = norm_back(grad_query, normed, factor, nq_ref[...])
    dq_ref[...] = join_heads(grad_raw.astype(jnp.bfloat16), group)

    @pl.when(index == tiles - 1)
    def _():
        normed_key, key_factor = normalize_rows(k_ref[...])
        grad_key = turn_back(dk[...], cos_ref[...], sin_ref[...])
        gk_ref[...] += jnp.sum(grad_key * normed_key, axis=0, keepdims=True)
        grad_key = norm_back(grad_key, normed_key, key_factor, nk_ref[...])
        for number in range(back):
            block = slice(number * own, (number + 1) * own)
            mixed[head, number, 0] = grad_key[block].astype(jnp.bfloat16)
            mixed[head, number, 1] = dv[block, :].astype(jnp.bfloat16)
        own_sum[head, 0] = grad_key[lead:]
        own_sum[head, 1] = dv[lead:, :]

        @pl.when(z > 0)
        def _():
            hop_copy(head, 0).start()

        for number in range(1, back):

            @pl.when(head >= number)
            def _():
                relay(head - number, number)

    @pl.when((head == heads - 1) & (index == tiles - 1))
    def _():
        for number in range(1, back):
            for at in range(heads - number, heads):
                relay(at, number)
        for at in range(heads):
            columns = slice(at * HD, (at + 1) * HD)

            @pl.when(z + 1 < lanes)
            def _():
                hop_copy(at, back - 1).wait_recv()
                total = own_sum[at] + got[at, back - 1].astype(jnp.float32)
                pair_ref[:, :, columns] = total.astype(jnp.bfloat16)

            @pl.when(z + 1 == lanes)
            def _():
                pair_ref[:, :, columns] = own_sum[at].astype(jnp.bfloat16)

            @pl.when(z > 0)
            def _():
                for number in range(back):
                    hop_copy(at, number).wait_send()

        finish()


def attention_specs(own, rows, group, tile, span):
    whole = lambda g, t: (0, 0)
    return [
        pl.BlockSpec((tile, group * HD), lambda g, t: (t, g)),
        pl.BlockSpec((rows, HD), lambda g, t: (0, g)),
        pl.BlockSpec((rows, HD), lambda g, t: (0, g)),
        pl.BlockSpec((tile, span), lambda g, t: (t, 0)),
        pl.BlockSpec((rows, HD), whole),
        pl.BlockSpec((rows, HD), whole),
        pl.BlockSpec((1, HD), whole),
        pl.BlockSpec((1, HD), whole),
    ]


def attend(queries, keys, values, bias, cosine, sine, norm_query, norm_key, tile, step):
    own, rows = (queries.shape[0], keys.shape[0])
    heads = keys.shape[1] // HD
    group = queries.shape[1] // keys.shape[1]
    span = bias.shape[1]
    return pl.pallas_call(
        functools.partial(attend_kernel, group, step, rows - own),
        grid=(heads, own // tile),
        out_shape=jax.ShapeDtypeStruct(queries.shape, jnp.bfloat16),
        in_specs=attention_specs(own, rows, group, tile, span),
        out_specs=pl.BlockSpec((tile, group * HD), lambda g, t: (t, g)),
        scratch_shapes=[pltpu.VMEM((rows, HD), jnp.bfloat16)],
        compiler_params=pltpu.CompilerParams(vmem_limit_bytes=VMEM),
        cost_estimate=pl.CostEstimate(
            flops=16 * own * span * queries.shape[1],
            bytes_accessed=4 * queries.size + 6 * keys.size,
            transcendentals=own * span * heads * group,
        ),
        name="attend",
    )(queries, keys, values, bias, cosine, sine, norm_query, norm_key)


def attend_back(
    queries,
    keys,
    values,
    bias,
    cosine,
    sine,
    norm_query,
    norm_key,
    grad,
    tile,
    step,
    left,
    right,
    size,
    lanes,
):
    own, rows = (queries.shape[0], keys.shape[0])
    heads = keys.shape[1] // HD
    group = queries.shape[1] // keys.shape[1]
    span = bias.shape[1]
    lead = rows - own
    back = lead // own
    tokens, depth = left.shape
    width = right.shape[1] // PARTS
    whole = lambda g, t: (0, 0)
    any_space = pl.BlockSpec(memory_space=pl.ANY)
    return pl.pallas_call(
        functools.partial(attend_back_kernel, group, step, lead, size, lanes),
        grid=(heads, own // tile),
        out_shape=(
            jax.ShapeDtypeStruct(queries.shape, jnp.bfloat16),
            jax.ShapeDtypeStruct((2, own, heads * HD), jnp.bfloat16),
            jax.ShapeDtypeStruct((1, HD), jnp.float32),
            jax.ShapeDtypeStruct((1, HD), jnp.float32),
            jax.ShapeDtypeStruct((PARTS, depth // size, width), jnp.float32),
        ),
        in_specs=attention_specs(own, rows, group, tile, span)
        + [pl.BlockSpec((tile, group * HD), lambda g, t: (t, g)), any_space, any_space],
        out_specs=(
            pl.BlockSpec((tile, group * HD), lambda g, t: (t, g)),
            pl.BlockSpec((2, own, heads * HD), lambda g, t: (0, 0, 0)),
            pl.BlockSpec((1, HD), whole),
            pl.BlockSpec((1, HD), whole),
            pl.BlockSpec((PARTS, depth // size, width), lambda g, t: (0, 0, 0)),
        ),
        scratch_shapes=[
            pltpu.VMEM((rows, HD), jnp.bfloat16),
            pltpu.VMEM((rows, HD), jnp.float32),
            pltpu.VMEM((rows, HD), jnp.float32),
            pltpu.VMEM((heads, back, 2, own, HD), jnp.bfloat16),
            pltpu.VMEM((heads, back, 2, own, HD), jnp.bfloat16),
            pltpu.VMEM((heads, 2, own, HD), jnp.float32),
            pltpu.VMEM((tokens, depth), jnp.bfloat16),
            pltpu.VMEM((PARTS, tokens, width), jnp.bfloat16),
            pltpu.SemaphoreType.DMA((PARTS + 1,)),
            pltpu.SemaphoreType.DMA((heads, back)),
            pltpu.SemaphoreType.DMA((heads, back)),
            *scatter_scratch(size, depth // size, width),
        ],
        compiler_params=pltpu.CompilerParams(
            collective_id=9, has_side_effects=True, vmem_limit_bytes=60 * 1024 * 1024
        ),
        cost_estimate=pl.CostEstimate(
            flops=40 * own * span * queries.shape[1],
            bytes_accessed=8 * queries.size + 16 * keys.size,
            transcendentals=own * span * heads * group,
        ),
        name="attend_back",
    )(queries, keys, values, bias, cosine, sine, norm_query, norm_key, grad, left, right)


def window_tables(length_row, pad_row, first, own, lead, tile, span):
    places = first - lead + jnp.arange(lead + own, dtype=jnp.int32)
    ends = jnp.cumsum(length_row)
    passed = places[:, None] >= ends[None, :]
    docs = jnp.sum(passed.astype(jnp.int32), axis=1)
    starts = jnp.sum(jnp.where(passed, length_row[None, :], 0), axis=1)
    freqs = THETA ** (-(jnp.arange(HD // 2).astype(jnp.float32) * 2.0 / HD))
    angles = (places - starts).astype(jnp.float32)[:, None] * freqs[None, :]
    cosine, sine = (jnp.cos(angles), jnp.sin(angles))
    padded = jnp.concatenate((jnp.zeros((lead,), pad_row.dtype), pad_row))
    live = lax.dynamic_slice_in_dim(padded, first, lead + own, 0)
    step = tile if lead + own > span else 0
    masks = []
    for index in range(own // tile):
        at = lead + index * tile
        query, key = (places[at : at + tile, None], places[None, index * step : index * step + span])
        same = docs[at : at + tile, None] == docs[None, index * step : index * step + span]
        seen = (live[None, index * step : index * step + span] == 1) | (key == query)
        masks.append((key >= 0) & (key <= query) & (query - key < WINDOW) & same & seen)
    bias = jnp.where(jnp.concatenate(masks, axis=0), 0.0, NEG).astype(jnp.float32)
    cosine = jnp.concatenate((cosine, cosine), axis=1)
    sine = jnp.concatenate((-sine, sine), axis=1)
    return (bias, cosine, sine, step, live[lead:].astype(jnp.float32))


def over_lanes(grad):
    return lax.psum_scatter(
        grad.astype(jnp.bfloat16), "tp", scatter_dimension=2, tiled=True
    ).astype(jnp.float32)


def shards(
    states,
    lengths,
    padding,
    teacher,
    norm_attn,
    w_query,
    w_key,
    w_value,
    norm_query,
    norm_key,
    w_out,
    norm_mlp,
    w_gate,
    w_up,
    w_down,
):
    own = states.shape[0]
    n_tp, n_fsdp = (lax.axis_size("tp"), lax.axis_size("fsdp"))
    first = lax.axis_index("tp") * own
    back = min(n_tp - 1, -(-WINDOW // own))
    lead = back * own
    tile = min(256, own)
    span = WINDOW + tile if lead >= WINDOW else lead + own
    wq, wk = (w_query.shape[1], w_key.shape[1])
    bias, cosine, sine, step, live = window_tables(
        lengths[0], padding[0], first, own, lead, tile, span
    )
    joined = jnp.concatenate((w_query, w_key, w_value, w_out.T), axis=1)
    wo = w_out.shape[0]
    units = [
        part.reshape(n_fsdp, -1, part.shape[1]) for part in (w_gate.T, w_up.T, w_down)
    ]
    live_here = jnp.full((8, 128), jnp.sum(padding).astype(jnp.float32))
    before, weights_attn, mine_pair, mine_down, counts = enter(
        n_fsdp, n_tp, back, states, joined, jnp.stack(units, axis=1), live_here
    )
    count = counts[0, 0]
    units_pair = lax.all_gather(mine_pair, "tp", axis=0)
    units_down = lax.all_gather(mine_down, "tp", axis=0)
    normed_in, query_raw, key_raw, value = project(
        before, states, norm_attn, weights_attn, wq, wk
    )
    gains = (norm_query.reshape(1, HD), norm_key.reshape(1, HD))
    attended = attend(query_raw, key_raw, value, bias, cosine, sine, *gains, tile, step)
    inputs = states.astype(jnp.float32)
    hidden_one = project_out(attended, weights_attn, states, wo)
    normed_two, factor_two = normalize_rows(hidden_one)
    whole_two, gate, up, product = gate_up(
        n_fsdp, (normed_two * norm_mlp).astype(jnp.bfloat16), units_pair
    )
    outputs = hidden_one + sum_products(n_fsdp, 2, (product,), units_down)
    errors = (outputs - teacher.astype(jnp.float32)) * live[:, None]
    squares = jnp.sum(errors * errors)
    grad_out = errors * (2.0 / (count * D))

    grad_gate, grad_up, units_early, units_late = grad_hidden_units(
        n_fsdp, grad_out.astype(jnp.bfloat16), units_down, gate, up, product, whole_two
    )
    units_early = lax.psum_scatter(units_early, "tp", scatter_dimension=0)
    grad_mid = sum_products(n_fsdp, 4, (grad_gate, grad_up), units_pair)
    grad_norm_mlp = jnp.sum(grad_mid * normed_two, axis=0)
    grad_hidden = grad_out + norm_back(grad_mid, normed_two, factor_two, norm_mlp)

    grad_low_out = grad_hidden.astype(jnp.bfloat16)
    grad_attended = back_out(grad_low_out, weights_attn, wo)
    grad_query, grad_pair, grad_norm_query, grad_norm_key, sums_out = attend_back(
        query_raw,
        key_raw,
        value,
        bias,
        cosine,
        sine,
        *gains,
        grad_attended,
        tile,
        step,
        grad_low_out,
        attended,
        n_fsdp,
        n_tp,
    )
    units_late, grad_query = lax.optimization_barrier((units_late, grad_query))
    units_late = lax.psum_scatter(units_late, "tp", scatter_dimension=0)
    sums_query, back_early, grad_w_out = sum_query(
        n_fsdp, n_tp, normed_in, grad_query, units_early, sums_out
    )
    sums_pair, grad_low, back_late, grad_w_query = sum_key(
        n_fsdp, n_tp, normed_in, grad_query, grad_pair, weights_attn, units_late, sums_query
    )
    grad_w_pair = over_lanes(sums_pair)
    grad_w_down, grad_w_gate, grad_w_up = [
        part.reshape(-1, part.shape[2]).astype(jnp.float32)
        for part in (back_early[:, 0], back_early[:, 1], back_late[:, 0])
    ]
    normed_one, factor_one = normalize_rows(inputs)
    grad_norm_attn = jnp.sum(grad_low * normed_one, axis=0)
    grad_input = grad_hidden + norm_back(grad_low, normed_one, factor_one, norm_attn)
    small = [grad_norm_attn, grad_norm_mlp, grad_norm_query[0], grad_norm_key[0]]
    small.append(jnp.full((HD,), squares))
    joined_small = jnp.concatenate(small).reshape(-1, HD)
    filled = joined_small.shape[0]
    joined_small = jnp.pad(joined_small, ((0, -filled % 8), (0, 0)))
    summed = sum_small(n_fsdp, n_tp, joined_small)[:filled].reshape(-1)
    grad_norm_attn, grad_norm_mlp = (summed[:D], summed[D : 2 * D])
    grad_norm_query, grad_norm_key = (summed[2 * D : 2 * D + HD], summed[2 * D + HD : 2 * D + 2 * HD])
    squares = summed[2 * D + 2 * HD]
    return (
        outputs,
        squares / (count * D),
        grad_input,
        grad_norm_attn,
        grad_w_query,
        grad_w_pair[0],
        grad_w_pair[1],
        grad_norm_query,
        grad_norm_key,
        grad_w_out.T,
        grad_norm_mlp,
        grad_w_gate.T,
        grad_w_up.T,
        grad_w_down,
    )


def solution(mesh):
    tokens = P(("fsdp", "tp"), None)
    rows, columns, sequences = (P("fsdp", "tp"), P("tp", "fsdp"), P("fsdp", None))
    in_specs = (
        tokens,
        sequences,
        sequences,
        tokens,
        P(),
        rows,
        rows,
        rows,
        P(),
        P(),
        columns,
        P(),
        rows,
        rows,
        columns,
    )
    out_specs = (
        tokens,
        P(),
        tokens,
        P(),
        rows,
        rows,
        rows,
        P(),
        P(),
        columns,
        P(),
        rows,
        rows,
        columns,
    )
    return jax.shard_map(shards, mesh=mesh, in_specs=in_specs, out_specs=out_specs, check_vma=False)
```

```python
import functools

import jax
import jax.numpy as jnp
from jax import lax
from jax.experimental import pallas as pl
from jax.experimental.pallas import tpu as pltpu
from jax.sharding import PartitionSpec as P

D = 2048
HD = 128
WINDOW = 1024

EPS = 1e-06
THETA = 1000000.0
NEG = -1e30
LOG2E = 1.4426950408889634
VMEM = 56 * 1024 * 1024


def normalize_rows(values):
    factor = lax.rsqrt(jnp.mean(values * values, axis=-1, keepdims=True) + EPS)
    return (values * factor, factor)


def norm_back(grad, normed, factor, gain):
    scaled = grad * gain
    return factor * (scaled - normed * jnp.mean(scaled * normed, axis=-1, keepdims=True))


def contract_last(left, right):
    return lax.dot_general(
        left, right, (((1,), (1,)), ((), ())), preferred_element_type=jnp.float32
    )


def contract_first(left, right):
    return lax.dot_general(
        left, right, (((0,), (0,)), ((), ())), preferred_element_type=jnp.float32
    )


def dot(left, right):
    return jnp.dot(left, right, preferred_element_type=jnp.float32)


MESH = pl.DeviceIdType.MESH
PARTS = 2


def flip(index, mask):
    bit = 1
    while bit <= mask:
        if mask & bit:
            index = index + bit - 2 * bit * lax.rem(lax.div(index, bit), 2)
        bit *= 2
    return index


def chip_bits(size):
    bits = []
    bit = 2
    while bit < size:
        bits.append(bit)
        bit *= 2
    return bits


def orders(size):
    bits = chip_bits(size)
    return (bits, bits[::-1])


def mask_of(pattern, order):
    return sum(bit for i, bit in enumerate(order) if pattern >> i & 1)


def top(pattern):
    return pattern.bit_length() - 1


def greet(me, size):
    barrier = pltpu.get_barrier_semaphore()
    bits = [1] + chip_bits(size)
    for bit in bits:
        pl.semaphore_signal(
            barrier, inc=1, device_id={"fsdp": flip(me, bit)}, device_id_type=MESH
        )
    pl.semaphore_wait(barrier, len(bits))


def pick(part, pair):
    return pair[0] + part * (pair[1] - pair[0])


def unit_loads(source, kind, target, sems):
    lanes, _, rows, _ = source.shape
    return [
        pltpu.make_async_copy(
            source.at[lane, kind], target.at[pl.ds(lane * rows, rows)], sems.at[lane]
        )
        for lane in range(lanes)
    ]


class Gather:
    def __init__(self, size, me, whole, sems, parts=PARTS, lane=lambda part: part, parity=lambda part: part, own=None):
        self.size, self.me, self.whole, self.parts = (size, me, whole, parts)
        self.lane, self.parity, self.own = (lane, parity, own)
        self.chip_send, self.chip_recv, self.core_send, self.core_recv = sems
        self.steps = len(chip_bits(size))
        self.patterns = sorted(range(1 << self.steps), key=lambda m: (top(m), m))

    def order(self, part):
        return orders(self.size)[self.parity(part) % 2]

    def slot(self, part, pattern, sibling):
        return flip(self.me, mask_of(pattern, self.order(part)) + sibling)

    def source(self, part, pattern, block):
        return self.own if self.own is not None and part == 0 and pattern == 0 else block

    def chip_copy(self, part, step, pattern):
        block = self.whole.at[self.slot(part, pattern, 0), self.lane(part)]
        number = (1 << step) - 1 + pattern
        return pltpu.make_async_remote_copy(
            src_ref=self.source(part, pattern, block),
            dst_ref=block,
            send_sem=self.chip_send.at[part, number],
            recv_sem=self.chip_recv.at[part, number],
            device_id={"fsdp": flip(self.me, self.order(part)[step])},
            device_id_type=MESH,
        )

    def core_copy(self, part, pattern):
        block = self.whole.at[self.slot(part, pattern, 0), self.lane(part)]
        return pltpu.make_async_remote_copy(
            src_ref=self.source(part, pattern, block),
            dst_ref=block,
            send_sem=self.core_send.at[part, pattern],
            recv_sem=self.core_recv.at[part, pattern],
            device_id={"fsdp": flip(self.me, 1)},
            device_id_type=MESH,
        )

    def arrive(self, part, pattern):
        if pattern:
            step = top(pattern)
            self.chip_copy(part, step, pattern - (1 << step)).wait_recv()

    def forward(self, part, pattern):
        for step in range(top(pattern) + 1, self.steps):
            self.chip_copy(part, step, pattern).start()
        self.core_copy(part, pattern).start()

    def pairs(self, work):
        for pattern in self.patterns:
            for part in range(self.parts):
                self.arrive(part, pattern)
            for part in range(self.parts):
                self.forward(part, pattern)
            work([self.slot(part, pattern, 0) for part in range(self.parts)])
            for part in range(self.parts):
                self.core_copy(part, pattern).wait_recv()
            work([self.slot(part, pattern, 1) for part in range(self.parts)])

    def finish(self):
        for pattern in self.patterns:
            for part in range(self.parts):
                for step in range(top(pattern) + 1, self.steps):
                    self.chip_copy(part, step, pattern).wait_send()
                self.core_copy(part, pattern).wait_send()


def gather_semaphores(size, parts=PARTS):
    moves = max(1, size // 2 - 1)
    return [
        pltpu.SemaphoreType.DMA((parts, moves)),
        pltpu.SemaphoreType.DMA((parts, moves)),
        pltpu.SemaphoreType.DMA((parts, size // 2)),
        pltpu.SemaphoreType.DMA((parts, size // 2)),
    ]


def first_step(pattern, steps):
    return (pattern & -pattern).bit_length() - 1 if pattern else steps


def scatter_order(steps):
    return sorted(range(1 << steps), key=lambda m: (first_step(m, steps), -bin(m).count("1"), m))


def scatter_steps(
    size, me, made, held, sent, came, sems, partial, final, ready=lambda part, slot, q, sibling: None
):
    chip_send, chip_recv, core_send, core_recv = sems
    steps = len(chip_bits(size))
    order = [bits[::-1] for bits in orders(size)]
    first = lambda m: first_step(m, steps)
    patterns = scatter_order(steps)
    place = {m: q for q, m in enumerate(patterns)}
    width = final.shape[-1]
    chunk = min(1024, width)

    def slots(pattern, sibling):
        return [flip(me, mask_of(pattern, order[part]) + sibling) for part in range(PARTS)]

    def core_copy(part, q):
        return pltpu.make_async_remote_copy(
            src_ref=made.at[part, q],
            dst_ref=held.at[part, q],
            send_sem=core_send.at[part, q],
            recv_sem=core_recv.at[part, q],
            device_id={"fsdp": flip(me, 1)},
            device_id_type=MESH,
        )

    def chip_copy(part, q):
        return pltpu.make_async_remote_copy(
            src_ref=sent.at[part, q],
            dst_ref=came.at[part, q],
            send_sem=chip_send.at[part, q],
            recv_sem=chip_recv.at[part, q],
            device_id={"fsdp": flip(me, order[part][first(patterns[q])])},
            device_id_type=MESH,
        )

    def for_sibling(q):
        pair = slots(patterns[q], 1)
        for part in range(PARTS):
            ready(part, pair[part], q, 1)

            @pl.loop(0, width // chunk)
            def _(index):
                columns = pl.ds(pl.multiple_of(index * chunk, chunk), chunk)
                made[part, q, :, columns] = partial(part, pair[part], columns).astype(jnp.bfloat16)

            core_copy(part, q).start()

    def for_chips(q):
        pattern = patterns[q]
        pair = slots(pattern, 0)
        arrivals = [place[pattern | 1 << step] for step in range(first(pattern))]
        for part in range(PARTS):
            ready(part, pair[part], q, 0)
            if pattern:
                core_copy(part, q).wait_recv()
                for arrival in arrivals:
                    chip_copy(part, arrival).wait_recv()

            @pl.loop(0, width // chunk)
            def _(index):
                columns = pl.ds(pl.multiple_of(index * chunk, chunk), chunk)
                total = partial(part, pair[part], columns)
                if pattern:
                    total = total + held[part, q, :, columns].astype(jnp.float32)
                    for arrival in arrivals:
                        total = total + came[part, arrival, :, columns].astype(jnp.float32)
                    sent[part, q, :, columns] = total.astype(jnp.bfloat16)
                else:
                    final[part, :, columns] = total

            if pattern:
                chip_copy(part, q).start()
        if not pattern:
            for part in range(PARTS):
                core_copy(part, q).wait_recv()
                for arrival in arrivals:
                    chip_copy(part, arrival).wait_recv()

                @pl.loop(0, width // chunk)
                def _(index):
                    columns = pl.ds(pl.multiple_of(index * chunk, chunk), chunk)
                    total = final[part, :, columns] + held[part, q, :, columns].astype(jnp.float32)
                    for arrival in arrivals:
                        total = total + came[part, arrival, :, columns].astype(jnp.float32)
                    final[part, :, columns] = total

    def finish():
        for q in range(len(patterns)):
            for part in range(PARTS):
                core_copy(part, q).wait_send()
                if patterns[q]:
                    chip_copy(part, q).wait_send()

    calls = []
    for q in range(len(patterns)):
        calls += [functools.partial(for_sibling, q), functools.partial(for_chips, q)]
    return (calls, finish)


def scatter_scratch(size, rows, width):
    held = size // 2
    moved = max(1, held - 1)
    return [
        pltpu.VMEM((PARTS, held, rows, width), jnp.bfloat16),
        pltpu.VMEM((PARTS, held, rows, width), jnp.bfloat16),
        pltpu.VMEM((PARTS, moved, rows, width), jnp.bfloat16),
        pltpu.VMEM((PARTS, moved, rows, width), jnp.bfloat16),
        pltpu.SemaphoreType.DMA((PARTS, moved)),
        pltpu.SemaphoreType.DMA((PARTS, moved)),
        pltpu.SemaphoreType.DMA((PARTS, held)),
        pltpu.SemaphoreType.DMA((PARTS, held)),
    ]


def gate_up_kernel(
    size,
    x_ref,
    wg_in,
    mine_in,
    x_out,
    gate_out,
    up_out,
    prod_out,
    wu_out,
    whole,
    wg_ref,
    wu_ref,
    gate,
    up,
    prod,
    load,
    keep,
    keep_gate,
    keep_units,
    store,
    z_send,
    z_recv,
    *sems,
):
    me, z = (lax.axis_index("fsdp"), lax.axis_index("tp"))
    lanes, _, each, _ = wg_in.shape
    hidden = wg_ref.shape[0]
    chunk = hidden
    above, below = (lax.rem(z + 1, lanes), lax.rem(z + lanes - 1, lanes))
    rows_of = lambda lane: wu_ref.at[pl.ds(pl.multiple_of(lane * each, each), each)]
    loads = [
        pltpu.make_async_copy(x_ref, whole.at[me], load.at[0]),
        pltpu.make_async_copy(mine_in.at[0], rows_of(z), load.at[1]),
    ]
    loads += unit_loads(wg_in, 0, wg_ref, load.at[pl.ds(2, lanes)])
    for copy in loads:
        copy.start()
    barrier = pltpu.get_barrier_semaphore()
    peers = [{"fsdp": flip(me, bit)} for bit in [1] + chip_bits(size)] + [{"tp": above}, {"tp": below}]
    for peer in peers:
        pl.semaphore_signal(barrier, inc=1, device_id=peer, device_id_type=MESH)
    pl.semaphore_wait(barrier, len(peers))
    for copy in loads[:2]:
        copy.wait()

    def lane_copy(side, distance):
        lane = z - (distance - 1) if side == 0 else z + (distance - 1)
        return pltpu.make_async_remote_copy(
            src_ref=rows_of(lane),
            dst_ref=rows_of(lane),
            send_sem=z_send.at[side, distance - 1],
            recv_sem=z_recv.at[side, distance - 1],
            device_id={"tp": above if side == 0 else below},
            device_id_type=MESH,
        )

    def sends(side, distance):
        if side == 0:
            return (z >= distance - 1) & (z + 1 < lanes)
        return (z + distance - 1 < lanes) & (z > 0)

    def comes(side, distance):
        return z >= distance if side == 0 else z + distance < lanes

    def lane_send(distance):
        for side in (0, 1):

            @pl.when(sends(side, distance))
            def _():
                lane_copy(side, distance).start()

    def lane_take(distance):
        for side in (0, 1):

            @pl.when(comes(side, distance))
            def _():
                lane_copy(side, distance).wait_recv()

    def relay(distance):
        lane_take(distance)
        if distance + 1 < lanes:
            lane_send(distance + 1)

    gather = Gather(size, me, whole, sems)
    groups = [(pattern, sibling) for pattern in gather.patterns for sibling in (0, 1)]

    def pair_of(number):
        pattern, sibling = groups[number]
        return [gather.slot(part, pattern, sibling) for part in range(PARTS)]

    def keeps(number):
        pair = pair_of(number)
        copies = []
        for part in range(PARTS):
            copies += [
                pltpu.make_async_copy(
                    whole.at[pair[part], part], x_out.at[pair[part], part], keep.at[part, number]
                ),
                pltpu.make_async_copy(
                    gate.at[number, part], gate_out.at[pair[part], part], keep_gate.at[part, number]
                ),
            ]
        return copies

    def stores(part, at):
        return [
            pltpu.make_async_copy(buffer.at[part], out.at[at, part], store.at[part, i])
            for i, (buffer, out) in enumerate(((up, up_out), (prod, prod_out)))
        ]

    def gates(number):
        pair = pair_of(number)

        @pl.loop(0, PARTS)
        def _(part):
            at = pick(part, pair)

            @pl.loop(0, hidden // chunk)
            def _(index):
                units = pl.ds(pl.multiple_of(index * chunk, chunk), chunk)
                gate[number, part, :, units] = contract_last(whole[at, part], wg_ref[units, :])

        for copy in keeps(number):
            copy.start()

    def ups(number):
        pair = pair_of(number)

        @pl.loop(0, PARTS)
        def _(part):
            at = pick(part, pair)
            if number:
                for copy in stores(part, pick(part, pair_of(number - 1))):
                    copy.wait()

            @pl.loop(0, hidden // chunk)
            def _(index):
                units = pl.ds(pl.multiple_of(index * chunk, chunk), chunk)
                value = contract_last(whole[at, part], wu_ref[units, :])
                gates = gate[number, part, :, units]
                up[part, :, units] = value
                prod[part, :, units] = (gates * jax.nn.sigmoid(gates) * value).astype(jnp.bfloat16)

            for copy in stores(part, at):
                copy.start()

    def unit_stores():
        return [
            pltpu.make_async_copy(
                wu_ref.at[pl.ds(lane * each, each)], wu_out.at[lane, 0], keep_units.at[lane]
            )
            for lane in range(lanes)
        ]

    last = len(gather.patterns) - 1
    done = 0
    lane_send(1)
    for index, pattern in enumerate(gather.patterns):
        if index:
            passed = range(index, index + 1) if index < last else range(last, lanes)
            for distance in passed:
                if distance < lanes:
                    relay(distance)
        if index == last:
            for copy in unit_stores():
                copy.start()
            while done < 2 * last:
                ups(done)
                done += 1
        for part in range(PARTS):
            gather.arrive(part, pattern)
        for part in range(PARTS):
            gather.forward(part, pattern)
        if index == 0:
            for copy in loads[2:]:
                copy.wait()
        gates(2 * index)
        for part in range(PARTS):
            gather.core_copy(part, pattern).wait_recv()
        gates(2 * index + 1)
    while done < len(groups):
        ups(done)
        done += 1
    gather.finish()
    for distance in range(1, lanes):
        for side in (0, 1):

            @pl.when(sends(side, distance))
            def _():
                lane_copy(side, distance).wait_send()

    for part in range(PARTS):
        for copy in stores(part, pair_of(len(groups) - 1)[part]):
            copy.wait()
    for number in range(len(groups)):
        for copy in keeps(number):
            copy.wait()
    for copy in unit_stores():
        copy.wait()


def gate_up(size, values, units_gate, mine_up):
    own, width = values.shape
    lanes, _, each, _ = units_gate.shape
    rows, hidden = (own // PARTS, lanes * each)
    any_space = pl.BlockSpec(memory_space=pl.ANY)
    shape = lambda columns, kind: jax.ShapeDtypeStruct((size, PARTS, rows, columns), kind)
    *outs, units_up = pl.pallas_call(
        functools.partial(gate_up_kernel, size),
        out_shape=(
            shape(width, jnp.bfloat16),
            shape(hidden, jnp.float32),
            shape(hidden, jnp.float32),
            shape(hidden, jnp.bfloat16),
            jax.ShapeDtypeStruct(units_gate.shape, jnp.bfloat16),
        ),
        in_specs=[any_space] * 3,
        out_specs=(any_space,) * 5,
        scratch_shapes=[
            pltpu.VMEM((size, PARTS, rows, width), jnp.bfloat16),
            pltpu.VMEM((hidden, width), jnp.bfloat16),
            pltpu.VMEM((hidden, width), jnp.bfloat16),
            pltpu.VMEM((size, PARTS, rows, hidden), jnp.float32),
            pltpu.VMEM((PARTS, rows, hidden), jnp.float32),
            pltpu.VMEM((PARTS, rows, hidden), jnp.bfloat16),
            pltpu.SemaphoreType.DMA((2 + lanes,)),
            pltpu.SemaphoreType.DMA((PARTS, size)),
            pltpu.SemaphoreType.DMA((PARTS, size)),
            pltpu.SemaphoreType.DMA((lanes,)),
            pltpu.SemaphoreType.DMA((PARTS, 2)),
            pltpu.SemaphoreType.DMA((2, lanes - 1)),
            pltpu.SemaphoreType.DMA((2, lanes - 1)),
            *gather_semaphores(size),
        ],
        compiler_params=pltpu.CompilerParams(
            collective_id=1, has_side_effects=True, vmem_limit_bytes=VMEM
        ),
        cost_estimate=pl.CostEstimate(
            flops=4 * size * own * width * hidden, bytes_accessed=200 * 1024 * 1024, transcendentals=0
        ),
        name="gate_up",
    )(values.reshape(PARTS, rows, width), units_gate, mine_up)
    return (*[out.reshape(size * own, -1) for out in outs], units_up)


def grad_hidden_kernel(
    size,
    x_ref,
    wd_in,
    gate_in,
    up_in,
    prod_in,
    two_in,
    dgate_out,
    dup_out,
    early_out,
    late_out,
    whole,
    wd_ref,
    gate,
    up,
    prod,
    two,
    dgate,
    dup,
    sums,
    load,
    fetch,
    store,
    flush,
    *sems,
):
    me = lax.axis_index("fsdp")
    hidden, width = wd_ref.shape
    lanes, _, each, _ = wd_in.shape
    chunk = 256 if hidden % 256 == 0 else 128
    loads = [pltpu.make_async_copy(x_ref, whole.at[me], load.at[0])]
    loads += unit_loads(wd_in, 0, wd_ref, load.at[pl.ds(1, lanes)])
    for copy in loads:
        copy.start()

    def stores(part, at):
        return [
            pltpu.make_async_copy(buffer.at[part], out.at[at, part], store.at[part, i])
            for i, (buffer, out) in enumerate(((dgate, dgate_out), (dup, dup_out)))
        ]

    def fetches(count, kinds):
        copies = []
        for part in range(PARTS):
            at = order[count][part]
            pairs = (
                (gate_in, gate.at[part]),
                (up_in, up.at[part]),
                (prod_in, prod.at[count % 2, part]),
                (two_in, two.at[count % 2, part]),
            )
            copies += [
                pltpu.make_async_copy(pairs[i][0].at[at, part], pairs[i][1], fetch.at[count % 2, part, i])
                for i in kinds
            ]
        return copies

    gather = Gather(size, me, whole, sems)
    order = []
    for pattern in gather.patterns:
        for sibling in (0, 1):
            order.append([gather.slot(part, pattern, sibling) for part in range(PARTS)])
    for copy in fetches(0, (0, 1, 2, 3)):
        copy.start()
    greet(me, size)
    loads[0].wait()
    state = {"count": 0}

    def work(pair):
        count = state["count"]
        state["count"] = count + 1
        more = count + 1 < len(order)
        if count == 0:
            for copy in loads[1:]:
                copy.wait()
        if more:
            for copy in fetches(count + 1, (2, 3)):
                copy.start()
        for copy in fetches(count, (0, 1)):
            copy.wait()
        if count:
            for part in range(PARTS):
                for copy in stores(part, order[count - 1][part]):
                    copy.wait()

        @pl.loop(0, PARTS)
        def _(part):
            at = pick(part, pair)

            grads = contract_last(whole[at, part], wd_ref[...])
            gates = gate[part]
            sigmoid = jax.nn.sigmoid(gates)
            dgate[part] = (
                grads * up[part] * sigmoid * (1.0 + gates * (1.0 - sigmoid))
            ).astype(jnp.bfloat16)
            dup[part] = (grads * (gates * sigmoid)).astype(jnp.bfloat16)

        for part in range(PARTS):
            for copy in stores(part, pair[part]):
                copy.start()
        if more:
            for copy in fetches(count + 1, (0, 1)):
                copy.start()
        for copy in fetches(count, (2, 3)):
            copy.wait()

        @pl.loop(0, hidden // chunk)
        def _(index):
            units = pl.ds(pl.multiple_of(index * chunk, chunk), chunk)
            here = count % 2
            for kind, (lefts, rights) in enumerate(
                (
                    ((prod.at[here, 0], prod.at[here, 1]), (whole.at[pair[0], 0], whole.at[pair[1], 1])),
                    ((dgate.at[0], dgate.at[1]), (two.at[here, 0], two.at[here, 1])),
                    ((dup.at[0], dup.at[1]), (two.at[here, 0], two.at[here, 1])),
                )
            ):
                total = contract_first(lefts[0][:, units], rights[0][...])
                total += contract_first(lefts[1][:, units], rights[1][...])
                if count:
                    total += sums[kind, units, :]
                sums[kind, units, :] = total

    gather.pairs(work)
    gather.finish()
    for part in range(PARTS):
        for copy in stores(part, order[-1][part]):
            copy.wait()
    copies = []
    for piece in range(3 * lanes):
        kind, lane = (piece // lanes, piece % lanes)
        block = whole.at[piece // PARTS, piece % PARTS, pl.ds(0, each)]
        block[...] = sums[kind, lane * each : (lane + 1) * each, :].astype(jnp.bfloat16)
        out = early_out.at[lane, kind] if kind < 2 else late_out.at[lane, 0]
        copy = pltpu.make_async_copy(block, out, flush.at[piece])
        copy.start()
        copies.append(copy)
    for copy in copies:
        copy.wait()


def grad_hidden_units(size, values, units, gate, up, product, whole_two):
    own, width = values.shape
    lanes, _, each, _ = units.shape
    rows, hidden = (own // PARTS, lanes * each)
    any_space = pl.BlockSpec(memory_space=pl.ANY)
    shape = lambda columns, kind: jax.ShapeDtypeStruct((size, PARTS, rows, columns), kind)
    blocks = lambda array: array.reshape(size, PARTS, rows, -1)
    weight = lambda kinds: jax.ShapeDtypeStruct((lanes, kinds, each, width), jnp.bfloat16)
    dgate, dup, early, late = pl.pallas_call(
        functools.partial(grad_hidden_kernel, size),
        out_shape=(shape(hidden, jnp.bfloat16), shape(hidden, jnp.bfloat16), weight(2), weight(1)),
        in_specs=[any_space] * 6,
        out_specs=(any_space,) * 4,
        scratch_shapes=[
            pltpu.VMEM((size, PARTS, rows, width), jnp.bfloat16),
            pltpu.VMEM((hidden, width), jnp.bfloat16),
            pltpu.VMEM((PARTS, rows, hidden), jnp.float32),
            pltpu.VMEM((PARTS, rows, hidden), jnp.float32),
            pltpu.VMEM((2, PARTS, rows, hidden), jnp.bfloat16),
            pltpu.VMEM((2, PARTS, rows, width), jnp.bfloat16),
            pltpu.VMEM((PARTS, rows, hidden), jnp.bfloat16),
            pltpu.VMEM((PARTS, rows, hidden), jnp.bfloat16),
            pltpu.VMEM((3, hidden, width), jnp.float32),
            pltpu.SemaphoreType.DMA((1 + lanes,)),
            pltpu.SemaphoreType.DMA((2, PARTS, 4)),
            pltpu.SemaphoreType.DMA((PARTS, 2)),
            pltpu.SemaphoreType.DMA((3 * lanes,)),
            *gather_semaphores(size),
        ],
        compiler_params=pltpu.CompilerParams(
            collective_id=3, has_side_effects=True, vmem_limit_bytes=60 * 1024 * 1024
        ),
        cost_estimate=pl.CostEstimate(
            flops=8 * size * own * width * hidden, bytes_accessed=200 * 1024 * 1024, transcendentals=0
        ),
        name="grad_hidden_units",
    )(values.reshape(PARTS, rows, width), units, *map(blocks, (gate, up, product, whole_two)))
    return (dgate.reshape(size * own, hidden), dup.reshape(size * own, hidden), early, late)


def sum_products_kernel(size, terms, *refs):
    left_in, right_in, out = (refs[:terms], refs[terms : 2 * terms], refs[2 * terms])
    at = 2 * terms + 1
    lefts, rights, (w_load, x_load) = (
        refs[at : at + terms],
        refs[at + terms : at + 2 * terms],
        refs[at + 2 * terms : at + 2 * terms + 2],
    )
    made, held, sent, came, *sems = refs[at + 2 * terms + 2 :]
    me = lax.axis_index("fsdp")

    def partial(part, slot, columns):
        return sum(
            dot(left[slot, part], right[:, columns]) for left, right in zip(lefts, rights)
        )

    def tiles(part, slot, q, sibling):
        return [
            pltpu.make_async_copy(
                source.at[slot, part], left.at[slot, part], x_load.at[2 * q + sibling, part, i]
            )
            for i, (source, left) in enumerate(zip(left_in, lefts))
        ]

    seen = []

    def ready(part, slot, q, sibling):
        if not seen:
            for copy in weights:
                copy.wait()
        seen.append(slot)
        for copy in tiles(part, slot, q, sibling):
            copy.wait()

    weights = []
    for i, (source, right) in enumerate(zip(right_in, rights)):
        weights += unit_loads(source, 0, right, w_load.at[i])
    for copy in weights:
        copy.start()
    order = [bits[::-1] for bits in orders(size)]
    for q, pattern in enumerate(scatter_order(len(order[0]))):
        for sibling in (1, 0):
            for part in range(PARTS):
                slot = flip(me, mask_of(pattern, order[part]) + sibling)
                for copy in tiles(part, slot, q, sibling):
                    copy.start()
    greet(me, size)
    calls, finish = scatter_steps(size, me, made, held, sent, came, sems, partial, out, ready)
    for call in calls:
        call()
    finish()


def sum_products(size, number, lefts, units):
    total, hidden = lefts[0].shape
    lanes, _, _, width = units[0].shape
    rows = total // size // PARTS
    vmem = pl.BlockSpec(memory_space=pltpu.VMEM)
    terms = len(lefts)
    out = pl.pallas_call(
        functools.partial(sum_products_kernel, size, terms),
        out_shape=jax.ShapeDtypeStruct((PARTS, rows, width), jnp.float32),
        in_specs=[pl.BlockSpec(memory_space=pl.ANY)] * (2 * terms),
        out_specs=vmem,
        scratch_shapes=[
            *[pltpu.VMEM((size, PARTS, rows, hidden), jnp.bfloat16)] * terms,
            *[pltpu.VMEM((hidden, width), jnp.bfloat16)] * terms,
            pltpu.SemaphoreType.DMA((terms, lanes)),
            pltpu.SemaphoreType.DMA((size, PARTS, terms)),
            *scatter_scratch(size, rows, width),
        ],
        compiler_params=pltpu.CompilerParams(
            collective_id=number, has_side_effects=True, vmem_limit_bytes=VMEM
        ),
        cost_estimate=pl.CostEstimate(
            flops=2 * total * hidden * width * terms, bytes_accessed=200 * 1024 * 1024, transcendentals=0
        ),
        name="sum_products",
    )(*[left.reshape(size, PARTS, rows, hidden) for left in lefts], *units)
    return out.reshape(PARTS * rows, width)


def enter_kernel(
    size,
    lanes,
    back,
    x_ref,
    w_ref,
    m_ref,
    c_ref,
    before,
    whole,
    mine_gate,
    mine_up,
    mine_down,
    count,
    counts,
    loads,
    z_send,
    z_recv,
    x_send,
    x_recv,
    m_send,
    m_recv,
    c_send,
    c_recv,
    *sems,
):
    me, z = (lax.axis_index("fsdp"), lax.axis_index("tp"))
    mine = (mine_gate.at[0], mine_up.at[0], mine_down.at[0])
    span = m_ref.shape[-1]
    part_of = lambda device: pl.ds(pl.multiple_of(device * span, span), span)
    local = [pltpu.make_async_copy(w_ref, whole.at[me, z], loads.at[0])]
    local += [
        pltpu.make_async_copy(m_ref.at[me, kind], mine[kind].at[:, part_of(me)], loads.at[kind + 1])
        for kind in range(3)
    ]
    for copy in local:
        copy.start()
    counts[me] = c_ref[...]
    up, down = (lax.rem(z + 1, lanes), lax.rem(z + lanes - 1, lanes))
    barrier = pltpu.get_barrier_semaphore()
    peers = [{"fsdp": flip(me, other)} for other in range(1, size)] + [{"tp": up}, {"tp": down}]
    for peer in peers:
        pl.semaphore_signal(barrier, inc=1, device_id=peer, device_id_type=MESH)
    pl.semaphore_wait(barrier, len(peers))

    def far(part):
        return (part + 1) // 2

    def lane(part):
        if part == 0:
            return z
        return z - far(part) if part % 2 else z + far(part)

    def exists(part):
        return z >= far(part) if part % 2 else z + far(part) < lanes

    def lane_copy(part):
        block = whole.at[me, lane(part - 2) if part > 2 else z]
        return pltpu.make_async_remote_copy(
            src_ref=block if part > 2 else w_ref,
            dst_ref=block,
            send_sem=z_send.at[part - 1],
            recv_sem=z_recv.at[part - 1],
            device_id={"tp": up if part % 2 else down},
            device_id_type=MESH,
        )

    def lane_sends(part):
        if part % 2:
            return (z >= far(part) - 1) & (z + 1 < lanes)
        return (z + far(part) - 1 < lanes) & (z > 0)

    def token_copy(hop):
        return pltpu.make_async_remote_copy(
            src_ref=x_ref if hop == 1 else before.at[hop - 2],
            dst_ref=before.at[hop - 1],
            send_sem=x_send.at[hop - 1],
            recv_sem=x_recv.at[hop - 1],
            device_id={"tp": up},
            device_id_type=MESH,
        )

    def unit_copy(other, kind):
        peer = flip(me, other)
        return pltpu.make_async_remote_copy(
            src_ref=m_ref.at[peer, kind],
            dst_ref=mine[kind].at[:, part_of(me)],
            send_sem=m_send.at[other - 1, kind],
            recv_sem=m_recv.at[other - 1, kind],
            device_id={"fsdp": peer},
            device_id_type=MESH,
        )

    def count_copy(other):
        return pltpu.make_async_remote_copy(
            src_ref=c_ref,
            dst_ref=counts.at[me],
            send_sem=c_send.at[other - 1],
            recv_sem=c_recv.at[other - 1],
            device_id={"fsdp": flip(me, other)},
            device_id_type=MESH,
        )

    def when(condition, run):
        pl.when(condition)(run)

    gather = Gather(size, me, whole, sems, 2 * lanes - 1, lane, far, w_ref)
    for part in (1, 2):
        when(lane_sends(part), lambda: lane_copy(part).start())
    gather.forward(0, 0)
    when(z + 1 < lanes, lambda: token_copy(1).start())
    for other in range(1, size):
        count_copy(other).start()
        for kind in range(3):
            unit_copy(other, kind).start()
    events = [(part, pattern) for part in range(2 * lanes - 1) for pattern in gather.patterns]
    wave = lambda pattern: 3.5 * top(pattern) + 2.5 if pattern else 0
    events.sort(key=lambda event: (2 * far(event[0]) + wave(event[1]), event))

    def run_event(part, pattern):
        if pattern:
            gather.arrive(part, pattern)
        elif part:
            lane_copy(part).wait_recv()
            if part + 2 < 2 * lanes - 1:
                when(lane_sends(part + 2), lambda: lane_copy(part + 2).start())
        gather.forward(part, pattern)

    for part, pattern in events[1:]:
        if part == 0:
            run_event(part, pattern)
        else:
            when(exists(part), lambda: run_event(part, pattern))
        if (part, pattern) == (2 * lanes - 2, 0):
            for hop in range(1, back):
                when(z >= hop, lambda: token_copy(hop).wait_recv())
                when((z >= hop) & (z + 1 < lanes), lambda: token_copy(hop + 1).start())
    for other in range(1, size):
        count_copy(other).wait()
    count[...] = sum(counts[other] for other in range(size))

    def close(part):
        for pattern in gather.patterns:
            gather.core_copy(part, pattern).wait()
            for step in range(top(pattern) + 1, gather.steps):
                gather.chip_copy(part, step, pattern).wait_send()

    close(0)
    for part in range(1, 2 * lanes - 1):
        when(exists(part), lambda: close(part))
        when(lane_sends(part), lambda: lane_copy(part).wait_send())
    for other in range(1, size):
        for kind in range(3):
            unit_copy(other, kind).wait()
    for hop in range(1, back + 1):
        when((z >= hop - 1) & (z + 1 < lanes), lambda: token_copy(hop).wait_send())
    when(z >= back, lambda: token_copy(back).wait_recv())
    for copy in local:
        copy.wait()


def enter(size, lanes, back, values, weights, units, count):
    any_space = pl.BlockSpec(memory_space=pl.ANY)
    vmem = pl.BlockSpec(memory_space=pltpu.VMEM)
    _, kinds, rows, columns = units.shape
    others = pltpu.SemaphoreType.DMA((size - 1,))
    other_kinds = pltpu.SemaphoreType.DMA((size - 1, kinds))
    line = pltpu.SemaphoreType.DMA((2 * lanes - 2,))
    hop = pltpu.SemaphoreType.DMA((back,))
    mine = jax.ShapeDtypeStruct((1, rows, size * columns), units.dtype)
    return pl.pallas_call(
        functools.partial(enter_kernel, size, lanes, back),
        out_shape=(
            jax.ShapeDtypeStruct((back, *values.shape), values.dtype),
            jax.ShapeDtypeStruct((size, lanes, *weights.shape), weights.dtype),
            *[mine] * kinds,
            jax.ShapeDtypeStruct(count.shape, count.dtype),
        ),
        in_specs=[any_space, any_space, any_space, vmem],
        out_specs=(any_space,) * 5 + (vmem,),
        scratch_shapes=[
            pltpu.VMEM((size, *count.shape), count.dtype),
            pltpu.SemaphoreType.DMA((kinds + 1,)),
            line,
            line,
            hop,
            hop,
            other_kinds,
            other_kinds,
            others,
            others,
            *gather_semaphores(size, 2 * lanes - 1),
        ],
        compiler_params=pltpu.CompilerParams(collective_id=5, has_side_effects=True),
        cost_estimate=pl.CostEstimate(flops=0, bytes_accessed=400 * 1024 * 1024, transcendentals=0),
        name="enter",
    )(values, weights, units, count)


class Units:
    def __init__(self, size, me, units, back, sems):
        self.size, self.me, self.units, self.back = (size, me, units, back)
        self.send, self.recv, self.own = sems
        self.kinds, self.span = (units.shape[0], back.shape[-1])

    def part_of(self, device):
        return pl.ds(pl.multiple_of(device * self.span, self.span), self.span)

    def stay(self):
        return [
            pltpu.make_async_copy(
                self.units.at[kind, :, self.part_of(self.me)],
                self.back.at[self.me, kind],
                self.own.at[kind],
            )
            for kind in range(self.kinds)
        ]

    def moves(self):
        copies = []
        for other in range(1, self.size):
            peer = flip(self.me, other)
            copies += [
                pltpu.make_async_remote_copy(
                    src_ref=self.units.at[kind, :, self.part_of(peer)],
                    dst_ref=self.back.at[self.me, kind],
                    send_sem=self.send.at[other - 1, kind],
                    recv_sem=self.recv.at[other - 1, kind],
                    device_id={"fsdp": peer},
                    device_id_type=MESH,
                )
                for kind in range(self.kinds)
            ]
        return copies

    def start(self):
        for copy in self.stay() + self.moves():
            copy.start()

    def finish(self):
        for copy in self.moves() + self.stay():
            copy.wait()


def units_scratch(size, kinds):
    return [
        pltpu.SemaphoreType.DMA((size - 1, kinds)),
        pltpu.SemaphoreType.DMA((size - 1, kinds)),
        pltpu.SemaphoreType.DMA((kinds,)),
    ]


class Lanes:
    def __init__(self, lanes, z, values, out, low, came, send, recv):
        self.lanes, self.z, self.values, self.out = (lanes, z, values, out)
        self.low, self.came, self.send, self.recv = (low, came, send, recv)

    def block(self, lane):
        each = self.lanes // PARTS
        width = self.out.shape[1]
        start = pl.multiple_of(lax.rem(lane, each) * width, width)
        return self.values[lax.div(lane, each), :, pl.ds(start, width)]

    def copy(self, hop):
        return pltpu.make_async_remote_copy(
            src_ref=self.low.at[hop - 1],
            dst_ref=self.came.at[hop - 1],
            send_sem=self.send.at[hop - 1],
            recv_sem=self.recv.at[hop - 1],
            device_id={"tp": lax.rem(self.z + hop, self.lanes)},
            device_id_type=MESH,
        )

    def start(self):
        for hop in range(1, self.lanes):
            self.low[hop - 1] = self.block(lax.rem(self.z + hop, self.lanes)).astype(jnp.bfloat16)
            self.copy(hop).start()

    def finish(self):
        for hop in range(1, self.lanes):
            self.copy(hop).wait()
        total = self.block(self.z)
        for hop in range(1, self.lanes):
            total = total + self.came[hop - 1].astype(jnp.float32)
        self.out[...] = total


class PartLanes(Lanes):
    def block(self, lane):
        width = self.out.shape[2]
        return self.values[:, :, pl.ds(pl.multiple_of(lane * width, width), width)]


def lanes_scratch(lanes, shape):
    return [
        pltpu.VMEM((lanes - 1, *shape), jnp.bfloat16),
        pltpu.VMEM((lanes - 1, *shape), jnp.bfloat16),
        pltpu.SemaphoreType.DMA((lanes - 1,)),
        pltpu.SemaphoreType.DMA((lanes - 1,)),
    ]


def greet_all(me, z, size, lanes):
    barrier = pltpu.get_barrier_semaphore()
    peers = [{"fsdp": flip(me, other)} for other in range(1, size)]
    peers += [{"tp": lax.rem(z + hop, lanes)} for hop in range(1, lanes)]
    for peer in peers:
        pl.semaphore_signal(barrier, inc=1, device_id=peer, device_id_type=MESH)
    pl.semaphore_wait(barrier, len(peers))


def sum_query_kernel(
    size, left_ref, right_ref, units_ref, out, back, left, right, loads, *refs
):
    units_sems = refs[:3]
    made, held, sent, came, *sems = refs[3:]
    me = lax.axis_index("fsdp")
    width = out.shape[-1]
    rows = left.shape[1] // size
    copies = [pltpu.make_async_copy(left_ref, left, loads.at[PARTS])]
    copies += [
        pltpu.make_async_copy(
            right_ref.at[:, pl.ds(part * width, width)], right.at[part], loads.at[part]
        )
        for part in range(PARTS)
    ]
    for copy in copies:
        copy.start()
    barrier = pltpu.get_barrier_semaphore()
    for other in range(1, size):
        pl.semaphore_signal(
            barrier, inc=1, device_id={"fsdp": flip(me, other)}, device_id_type=MESH
        )
    pl.semaphore_wait(barrier, size - 1)
    for copy in copies:
        copy.wait()

    def partial(part, slot, columns):
        block = left[:, pl.ds(pl.multiple_of(slot * rows, rows), rows)]
        return contract_first(block, right[part, :, columns])

    units = Units(size, me, units_ref, back, units_sems)
    calls, finish = scatter_steps(size, me, made, held, sent, came, sems, partial, out)
    for number, call in enumerate(calls):
        call()
        if number == len(calls) // 2:
            units.start()
    units.finish()
    finish()


def sum_query(size, left, right, units):
    tokens, depth = left.shape
    width = right.shape[1] // PARTS
    rows = depth // size
    any_space = pl.BlockSpec(memory_space=pl.ANY)
    vmem = pl.BlockSpec(memory_space=pltpu.VMEM)
    return pl.pallas_call(
        functools.partial(sum_query_kernel, size),
        out_shape=(
            jax.ShapeDtypeStruct((PARTS, rows, width), jnp.float32),
            jax.ShapeDtypeStruct((size, *units.shape[:2], rows), jnp.bfloat16),
        ),
        in_specs=[any_space] * 3,
        out_specs=(vmem, any_space),
        scratch_shapes=[
            pltpu.VMEM((tokens, depth), jnp.bfloat16),
            pltpu.VMEM((PARTS, tokens, width), jnp.bfloat16),
            pltpu.SemaphoreType.DMA((PARTS + 1,)),
            *units_scratch(size, units.shape[0]),
            *scatter_scratch(size, rows, width),
        ],
        compiler_params=pltpu.CompilerParams(
            collective_id=6, has_side_effects=True, vmem_limit_bytes=VMEM
        ),
        cost_estimate=pl.CostEstimate(
            flops=4 * tokens * depth * width, bytes_accessed=100 * 1024 * 1024, transcendentals=0
        ),
        name="sum_query",
    )(left, right, units)


def sum_key_kernel(
    size,
    lanes,
    left_ref,
    q_ref,
    kv_ref,
    w_ref,
    units_ref,
    out_sums,
    query_sums,
    out,
    low,
    back,
    lane_out,
    lane_query,
    left,
    right,
    loads,
    tiles,
    fetch,
    *refs,
):
    units_sems, lane_refs = (refs[:3], refs[3:11])
    made, held, sent, came, *sems = refs[11:]
    me, z = (lax.axis_index("fsdp"), lax.axis_index("tp"))
    rows = left.shape[1] // size
    parts, span = (w_ref.shape[1], tiles.shape[-1])
    copies = [pltpu.make_async_copy(left_ref, left, loads.at[PARTS])]
    copies += [
        pltpu.make_async_copy(kv_ref.at[part], right.at[part], loads.at[part])
        for part in range(PARTS)
    ]
    for copy in copies:
        copy.start()

    def tile_copy(f):
        return pltpu.make_async_copy(
            w_ref.at[f, :, :, pl.ds(0, span)], tiles.at[f % 2], fetch.at[f % 2]
        )

    tile_copy(0).start()
    greet_all(me, z, size, lanes)
    for copy in copies:
        copy.wait()

    def partial(part, slot, columns):
        block = left[:, pl.ds(pl.multiple_of(slot * rows, rows), rows)]
        return contract_first(block, right[part, :, columns])

    def low_columns(f):
        if f + 1 < size:
            tile_copy(f + 1).start()
        tile_copy(f).wait()
        half = low.shape[0] // 2

        @pl.loop(0, 2)
        def _(index):
            span_rows = pl.ds(pl.multiple_of(index * half, half), half)
            total = jnp.zeros((half, rows), jnp.float32)
            for z in range(parts):
                start = 0
                for source in (q_ref, right.at[0], right.at[1]):
                    width = source.shape[1] // parts
                    total += contract_last(
                        source[span_rows, z * width : (z + 1) * width],
                        tiles[f % 2, z, :, start : start + width],
                    )
                    start += width
            low[span_rows, f * rows : (f + 1) * rows] = total

    units = Units(size, me, units_ref, back, units_sems)
    across = (
        Lanes(lanes, z, out_sums, lane_out, *lane_refs[:4]),
        Lanes(lanes, z, query_sums, lane_query, *lane_refs[4:]),
    )
    calls, finish = scatter_steps(size, me, made, held, sent, came, sems, partial, out)
    done = 0
    for number, call in enumerate(calls):
        call()
        if number < 2:
            across[number].start()
        if number == len(calls) // 2:
            units.start()
        goal = size * max(0, number - 1) // max(1, len(calls) - 3)
        while done < min(size, goal):
            low_columns(done)
            done += 1
    while done < size:
        low_columns(done)
        done += 1
    for one in across:
        one.finish()
    units.finish()
    finish()


def sum_key(size, lanes, left, grad_query, grad_pair, weights, units, *sums):
    tokens, depth = left.shape
    width = grad_pair.shape[2]
    rows = depth // size
    parts = weights.shape[1]
    span = (grad_query.shape[1] + PARTS * width) // parts
    lane_width = sums[0].shape[2] * PARTS // lanes
    any_space = pl.BlockSpec(memory_space=pl.ANY)
    vmem = pl.BlockSpec(memory_space=pltpu.VMEM)
    return pl.pallas_call(
        functools.partial(sum_key_kernel, size, lanes),
        out_shape=(
            jax.ShapeDtypeStruct((PARTS, rows, width), jnp.float32),
            jax.ShapeDtypeStruct((tokens, depth), jnp.float32),
            jax.ShapeDtypeStruct((size, *units.shape[:2], rows), jnp.bfloat16),
            *[jax.ShapeDtypeStruct((rows, lane_width), jnp.float32)] * 2,
        ),
        in_specs=[any_space, vmem, any_space, any_space, any_space, vmem, vmem],
        out_specs=(vmem, vmem, any_space, vmem, vmem),
        scratch_shapes=[
            pltpu.VMEM((tokens, depth), jnp.bfloat16),
            pltpu.VMEM((PARTS, tokens, width), jnp.bfloat16),
            pltpu.SemaphoreType.DMA((PARTS + 1,)),
            pltpu.VMEM((2, parts, rows, span), jnp.bfloat16),
            pltpu.SemaphoreType.DMA((2,)),
            *units_scratch(size, units.shape[0]),
            *lanes_scratch(lanes, (rows, lane_width)),
            *lanes_scratch(lanes, (rows, lane_width)),
            *scatter_scratch(size, rows, width),
        ],
        compiler_params=pltpu.CompilerParams(
            collective_id=7, has_side_effects=True, vmem_limit_bytes=VMEM
        ),
        cost_estimate=pl.CostEstimate(
            flops=8 * tokens * depth * width, bytes_accessed=100 * 1024 * 1024, transcendentals=0
        ),
        name="sum_key",
    )(left, grad_query, grad_pair, weights, units, *sums)


def last_kernel(size, lanes, x_ref, sums_ref, o_ref, lane_out, came, send, recv, *lane_refs):
    me, z = (lax.axis_index("fsdp"), lax.axis_index("tp"))
    peers = []
    for name, index, count in (("fsdp", me, size), ("tp", z, lanes)):
        bit = 1
        while bit < count:
            peers.append({name: flip(index, bit)})
            bit *= 2
    barrier = pltpu.get_barrier_semaphore()
    greeted = [{"fsdp": flip(me, bit)} for bit in [1] + chip_bits(size)]
    greeted += [{"tp": lax.rem(z + hop, lanes)} for hop in range(1, lanes)]
    for peer in greeted:
        pl.semaphore_signal(barrier, inc=1, device_id=peer, device_id_type=MESH)
    pl.semaphore_wait(barrier, len(greeted))
    across = PartLanes(lanes, z, sums_ref, lane_out, *lane_refs)
    across.start()
    sent = came.shape[0] // 2
    came[sent] = x_ref[...]
    for step, peer in enumerate(peers):
        copy = pltpu.make_async_remote_copy(
            src_ref=came.at[sent + step],
            dst_ref=came.at[step],
            send_sem=send.at[step],
            recv_sem=recv.at[step],
            device_id=peer,
            device_id_type=MESH,
        )
        copy.start()
        copy.wait()
        came[sent + step + 1] = came[sent + step] + came[step]
    o_ref[...] = came[sent + len(peers)]
    across.finish()


def last_sums(size, lanes, values, sums):
    steps = (size * lanes).bit_length() - 1
    vmem = pl.BlockSpec(memory_space=pltpu.VMEM)
    parts, rows, columns = sums.shape
    shape = (parts, rows, columns // lanes)
    return pl.pallas_call(
        functools.partial(last_kernel, size, lanes),
        out_shape=(
            jax.ShapeDtypeStruct(values.shape, values.dtype),
            jax.ShapeDtypeStruct(shape, jnp.float32),
        ),
        in_specs=[vmem, vmem],
        out_specs=(vmem, vmem),
        scratch_shapes=[
            pltpu.VMEM((2 * (steps + 1), *values.shape), values.dtype),
            pltpu.SemaphoreType.DMA((steps,)),
            pltpu.SemaphoreType.DMA((steps,)),
            *lanes_scratch(lanes, shape),
        ],
        compiler_params=pltpu.CompilerParams(
            collective_id=8, has_side_effects=True, vmem_limit_bytes=VMEM
        ),
        name="last_sums",
    )(values, sums)


def project_kernel(
    wq, wk, before_ref, x_ref, gain_ref, w_ref, n_ref, q_ref, k_ref, v_ref, normed
):
    back, own, _ = before_ref.shape
    lead = back * own
    tile = min(512, own)
    z = lax.axis_index("tp")

    @pl.when(pl.program_id(0) == 0)
    def _():
        for hop in range(back + 1):

            @pl.loop(0, own // tile)
            def _(index):
                span = pl.ds(pl.multiple_of(index * tile, tile), tile)
                values = x_ref[span, :] if hop == 0 else before_ref[hop - 1, span, :]
                values = normalize_rows(values.astype(jnp.float32))[0] * gain_ref[...]
                values = values.astype(jnp.bfloat16)
                if hop:
                    values = jnp.where(z >= hop, values, jnp.zeros_like(values))
                else:
                    n_ref[span, :] = values
                at = lead - hop * own + index * tile
                normed[pl.ds(pl.multiple_of(at, tile), tile), :] = values

    weights = lambda start, size: w_ref[:, 0, :, start : start + size].reshape(D, size)

    @pl.loop(0, (lead + own) // tile)
    def _(index):
        span = pl.ds(pl.multiple_of(index * tile, tile), tile)
        pair = dot(normed[span, :], weights(wq, 2 * wk))
        k_ref[span, :] = pair[:, :wk]
        v_ref[span, :] = pair[:, wk:].astype(jnp.bfloat16)

    @pl.loop(0, own // tile)
    def _(index):
        span = pl.ds(pl.multiple_of(index * tile, tile), tile)
        from_lead = pl.ds(pl.multiple_of(lead + index * tile, tile), tile)
        q_ref[span, :] = dot(normed[from_lead, :], weights(0, wq))


def project(before, values, gain, weights, wq, wk):
    size, parts, rows_in, columns = weights.shape
    back, own, _ = before.shape
    rows = (back + 1) * own
    whole = lambda *_: (0, 0)
    return pl.pallas_call(
        functools.partial(project_kernel, wq, wk),
        grid=(parts,),
        out_shape=(
            jax.ShapeDtypeStruct((own, D), jnp.bfloat16),
            jax.ShapeDtypeStruct((own, parts * wq), jnp.float32),
            jax.ShapeDtypeStruct((rows, parts * wk), jnp.float32),
            jax.ShapeDtypeStruct((rows, parts * wk), jnp.bfloat16),
        ),
        in_specs=[
            pl.BlockSpec((back, own, D), lambda z: (0, 0, 0)),
            pl.BlockSpec((own, D), whole),
            pl.BlockSpec((1, D), whole),
            pl.BlockSpec((size, 1, rows_in, wq + 2 * wk), lambda z: (0, z, 0, 0)),
        ],
        out_specs=(
            pl.BlockSpec((own, D), whole),
            pl.BlockSpec((own, wq), lambda z: (0, z)),
            pl.BlockSpec((rows, wk), lambda z: (0, z)),
            pl.BlockSpec((rows, wk), lambda z: (0, z)),
        ),
        scratch_shapes=[pltpu.VMEM((rows, D), jnp.bfloat16)],
        compiler_params=pltpu.CompilerParams(vmem_limit_bytes=VMEM),
        cost_estimate=pl.CostEstimate(
            flops=2 * D * parts * (own * wq + rows * 2 * wk),
            bytes_accessed=2 * D * parts * (wq + 2 * wk) + 2 * rows * D,
            transcendentals=0,
        ),
        name="project_in",
    )(before, values, gain.reshape(1, D), weights)


def out_kernel(a_ref, w_ref, x_ref, o_ref):
    parts, _, width = w_ref.shape[1:]
    total = x_ref[...].astype(jnp.float32)
    for z in range(parts):
        total += contract_last(a_ref[:, z * width : (z + 1) * width], w_ref[0, z])
    o_ref[...] = total


def project_out(attended, weights, states, wo):
    size, parts, rows, columns = weights.shape
    own = states.shape[0]
    last = columns // wo - 1
    return pl.pallas_call(
        out_kernel,
        grid=(size,),
        out_shape=jax.ShapeDtypeStruct(states.shape, jnp.float32),
        in_specs=[
            pl.BlockSpec(attended.shape, lambda f: (0, 0)),
            pl.BlockSpec((1, parts, rows, wo), lambda f: (f, 0, 0, last)),
            pl.BlockSpec((own, rows), lambda f: (0, f)),
        ],
        out_specs=pl.BlockSpec((own, rows), lambda f: (0, f)),
        compiler_params=pltpu.CompilerParams(vmem_limit_bytes=VMEM),
        cost_estimate=pl.CostEstimate(
            flops=2 * own * D * parts * wo, bytes_accessed=24 * 1024 * 1024, transcendentals=0
        ),
        name="project_out",
    )(attended, weights, states)


def back_out_kernel(g_ref, w_ref, o_ref):
    size, _, rows, width = w_ref.shape
    o_ref[...] = dot(g_ref[...], w_ref[:, 0].reshape(size * rows, width)).astype(jnp.bfloat16)


def back_out(grad, weights, wo):
    size, parts, rows, columns = weights.shape
    own = grad.shape[0]
    last = columns // wo - 1
    return pl.pallas_call(
        back_out_kernel,
        grid=(parts,),
        out_shape=jax.ShapeDtypeStruct((own, parts * wo), jnp.bfloat16),
        in_specs=[
            pl.BlockSpec(grad.shape, lambda z: (0, 0)),
            pl.BlockSpec((size, 1, rows, wo), lambda z: (0, z, 0, last)),
        ],
        out_specs=pl.BlockSpec((own, wo), lambda z: (0, z)),
        compiler_params=pltpu.CompilerParams(vmem_limit_bytes=VMEM),
        cost_estimate=pl.CostEstimate(
            flops=2 * own * D * parts * wo, bytes_accessed=16 * 1024 * 1024, transcendentals=0
        ),
        name="back_out",
    )(grad, weights)


def turn(values, cosine, sine):
    return values * cosine + pltpu.roll(values, HD // 2, 1) * sine


def turn_back(grad, cosine, sine):
    return grad * cosine - pltpu.roll(grad, HD // 2, 1) * sine


def split_heads(block, group):
    return jnp.concatenate([block[:, i * HD : (i + 1) * HD] for i in range(group)], axis=0)


def join_heads(stacked, group):
    rows = stacked.shape[0] // group
    return jnp.concatenate([stacked[i * rows : (i + 1) * rows] for i in range(group)], axis=1)


def head_probs(query, keys, bias, group, scale):
    scores = contract_last(query, keys) * (scale * LOG2E)
    rows, span = scores.shape
    scores = (scores.reshape(group, rows // group, span) + bias[None]).reshape(rows, span)
    weights = jnp.exp2(scores)
    return weights * (1.0 / jnp.sum(weights, axis=-1, keepdims=True))


def attend_kernel(
    group, step, lead, q_ref, k_ref, v_ref, bias_ref, cos_ref, sin_ref, nq_ref, nk_ref, o_ref, keys
):
    tile, span = bias_ref.shape
    scale = HD ** (-0.5)
    index = pl.program_id(1)

    @pl.when(index == 0)
    def _():
        normed = normalize_rows(k_ref[...])[0] * nk_ref[...]
        keys[...] = turn(normed, cos_ref[...], sin_ref[...]).astype(jnp.bfloat16)

    here = pl.ds(pl.multiple_of(lead + index * tile, tile), tile)
    cosine, sine = (cos_ref[here, :], sin_ref[here, :])
    normed = normalize_rows(split_heads(q_ref[...], group))[0] * nq_ref[...]
    cosine, sine = (jnp.concatenate([cosine] * group, 0), jnp.concatenate([sine] * group, 0))
    query = turn(normed, cosine, sine).astype(jnp.bfloat16)
    window = pl.ds(pl.multiple_of(index * step, tile), span)
    probs = head_probs(query, keys[window, :], bias_ref[...], group, scale)
    mixed = dot(probs.astype(jnp.bfloat16), v_ref[window, :])
    o_ref[...] = join_heads(mixed.astype(jnp.bfloat16), group)


def attend_back_kernel(
    group,
    step,
    lead,
    size,
    lanes,
    q_ref,
    k_ref,
    v_ref,
    bias_ref,
    cos_ref,
    sin_ref,
    nq_ref,
    nk_ref,
    do_ref,
    left_ref,
    right_ref,
    dq_ref,
    pair_ref,
    gq_ref,
    gk_ref,
    out_ref,
    keys,
    dk,
    dv,
    mixed,
    got,
    own_sum,
    left,
    right,
    loads,
    hop_send,
    hop_recv,
    *refs,
):
    made, held, sent, came, *sems = refs
    tile, span = bias_ref.shape
    scale = HD ** (-0.5)
    head, index = (pl.program_id(0), pl.program_id(1))
    heads, tiles = (mixed.shape[0], (k_ref.shape[0] - lead) // tile)
    back, own = (mixed.shape[1], mixed.shape[3])
    me, z = (lax.axis_index("fsdp"), lax.axis_index("tp"))
    width = out_ref.shape[-1]
    rows = left.shape[1] // size

    def hop_copy(at, number):
        return pltpu.make_async_remote_copy(
            src_ref=mixed.at[at, number],
            dst_ref=got.at[at, number],
            send_sem=hop_send.at[at, number],
            recv_sem=hop_recv.at[at, number],
            device_id={"tp": lax.rem(z + lanes - 1, lanes)},
            device_id_type=MESH,
        )

    def relay(at, number):
        @pl.when(z + 1 < lanes)
        def _():
            hop_copy(at, number - 1).wait_recv()
            total = mixed[at, number].astype(jnp.float32)
            total = total + got[at, number - 1].astype(jnp.float32)
            mixed[at, number] = total.astype(jnp.bfloat16)

        @pl.when(z > 0)
        def _():
            hop_copy(at, number).start()

    loads_of = lambda: [pltpu.make_async_copy(left_ref, left, loads.at[PARTS])] + [
        pltpu.make_async_copy(
            right_ref.at[:, pl.ds(part * width, width)], right.at[part], loads.at[part]
        )
        for part in range(PARTS)
    ]

    @pl.when((head == 0) & (index == 0))
    def _():
        for copy in loads_of():
            copy.start()
        barrier = pltpu.get_barrier_semaphore()
        peers = [{"fsdp": flip(me, bit)} for bit in [1] + chip_bits(size)]
        peers += [{"tp": lax.rem(z + 1, lanes)}, {"tp": lax.rem(z + lanes - 1, lanes)}]
        for peer in peers:
            pl.semaphore_signal(barrier, inc=1, device_id=peer, device_id_type=MESH)
        pl.semaphore_wait(barrier, len(peers))
        for copy in loads_of():
            copy.wait()
        gq_ref[...] = jnp.zeros_like(gq_ref)
        gk_ref[...] = jnp.zeros_like(gk_ref)

    def partial(part, slot, columns):
        block = left[:, pl.ds(pl.multiple_of(slot * rows, rows), rows)]
        return contract_first(block, right[part, :, columns])

    calls, finish = scatter_steps(size, me, made, held, sent, came, sems, partial, out_ref)
    at_step = {}
    for number, call in enumerate(calls):
        at_step.setdefault(number * heads * tiles // len(calls), []).append(call)
    for number, some in at_step.items():

        @pl.when(head * tiles + index == number)
        def _():
            for call in some:
                call()

    @pl.when(index == 0)
    def _():
        normed = normalize_rows(k_ref[...])[0] * nk_ref[...]
        keys[...] = turn(normed, cos_ref[...], sin_ref[...]).astype(jnp.bfloat16)
        dk[...] = jnp.zeros_like(dk)
        dv[...] = jnp.zeros_like(dv)

    here = pl.ds(pl.multiple_of(lead + index * tile, tile), tile)
    cosine, sine = (cos_ref[here, :], sin_ref[here, :])
    cosine, sine = (jnp.concatenate([cosine] * group, 0), jnp.concatenate([sine] * group, 0))
    normed, factor = normalize_rows(split_heads(q_ref[...], group))
    query = turn(normed * nq_ref[...], cosine, sine).astype(jnp.bfloat16)
    window = pl.ds(pl.multiple_of(index * step, tile), span)
    probs = head_probs(query, keys[window, :], bias_ref[...], group, scale)
    grad_out = split_heads(do_ref[...], group)
    dv[window, :] += contract_first(probs.astype(jnp.bfloat16), grad_out)
    grad_probs = contract_last(grad_out, v_ref[window, :])
    centre = jnp.sum(probs * grad_probs, axis=-1, keepdims=True)
    grad_scores = (probs * (grad_probs - centre)).astype(jnp.bfloat16)
    dk[window, :] += contract_first(grad_scores, query) * scale
    grad_query = turn_back(dot(grad_scores, keys[window, :]) * scale, cosine, sine)
    gq_ref[...] += jnp.sum(grad_query * normed, axis=0, keepdims=True)
    grad_raw = norm_back(grad_query, normed, factor, nq_ref[...])
    dq_ref[...] = join_heads(grad_raw.astype(jnp.bfloat16), group)

    @pl.when(index == tiles - 1)
    def _():
        normed_key, key_factor = normalize_rows(k_ref[...])
        grad_key = turn_back(dk[...], cos_ref[...], sin_ref[...])
        gk_ref[...] += jnp.sum(grad_key * normed_key, axis=0, keepdims=True)
        grad_key = norm_back(grad_key, normed_key, key_factor, nk_ref[...])
        for number in range(back):
            block = slice(number * own, (number + 1) * own)
            mixed[head, number, 0] = grad_key[block].astype(jnp.bfloat16)
            mixed[head, number, 1] = dv[block, :].astype(jnp.bfloat16)
        own_sum[head, 0] = grad_key[lead:]
        own_sum[head, 1] = dv[lead:, :]

        @pl.when(z > 0)
        def _():
            hop_copy(head, 0).start()

        for number in range(1, back):

            @pl.when(head >= number)
            def _():
                relay(head - number, number)

    @pl.when((head == heads - 1) & (index == tiles - 1))
    def _():
        for number in range(1, back):
            for at in range(heads - number, heads):
                relay(at, number)
        for at in range(heads):
            columns = slice(at * HD, (at + 1) * HD)

            @pl.when(z + 1 < lanes)
            def _():
                hop_copy(at, back - 1).wait_recv()
                total = own_sum[at] + got[at, back - 1].astype(jnp.float32)
                pair_ref[:, :, columns] = total.astype(jnp.bfloat16)

            @pl.when(z + 1 == lanes)
            def _():
                pair_ref[:, :, columns] = own_sum[at].astype(jnp.bfloat16)

            @pl.when(z > 0)
            def _():
                for number in range(back):
                    hop_copy(at, number).wait_send()

        finish()


def attention_specs(own, rows, group, tile, span):
    whole = lambda g, t: (0, 0)
    return [
        pl.BlockSpec((tile, group * HD), lambda g, t: (t, g)),
        pl.BlockSpec((rows, HD), lambda g, t: (0, g)),
        pl.BlockSpec((rows, HD), lambda g, t: (0, g)),
        pl.BlockSpec((tile, span), lambda g, t: (t, 0)),
        pl.BlockSpec((rows, HD), whole),
        pl.BlockSpec((rows, HD), whole),
        pl.BlockSpec((1, HD), whole),
        pl.BlockSpec((1, HD), whole),
    ]


def attend(queries, keys, values, bias, cosine, sine, norm_query, norm_key, tile, step):
    own, rows = (queries.shape[0], keys.shape[0])
    heads = keys.shape[1] // HD
    group = queries.shape[1] // keys.shape[1]
    span = bias.shape[1]
    return pl.pallas_call(
        functools.partial(attend_kernel, group, step, rows - own),
        grid=(heads, own // tile),
        out_shape=jax.ShapeDtypeStruct(queries.shape, jnp.bfloat16),
        in_specs=attention_specs(own, rows, group, tile, span),
        out_specs=pl.BlockSpec((tile, group * HD), lambda g, t: (t, g)),
        scratch_shapes=[pltpu.VMEM((rows, HD), jnp.bfloat16)],
        compiler_params=pltpu.CompilerParams(vmem_limit_bytes=VMEM),
        cost_estimate=pl.CostEstimate(
            flops=16 * own * span * queries.shape[1],
            bytes_accessed=4 * queries.size + 6 * keys.size,
            transcendentals=own * span * heads * group,
        ),
        name="attend",
    )(queries, keys, values, bias, cosine, sine, norm_query, norm_key)


def attend_back(
    queries,
    keys,
    values,
    bias,
    cosine,
    sine,
    norm_query,
    norm_key,
    grad,
    tile,
    step,
    left,
    right,
    size,
    lanes,
):
    own, rows = (queries.shape[0], keys.shape[0])
    heads = keys.shape[1] // HD
    group = queries.shape[1] // keys.shape[1]
    span = bias.shape[1]
    lead = rows - own
    back = lead // own
    tokens, depth = left.shape
    width = right.shape[1] // PARTS
    whole = lambda g, t: (0, 0)
    any_space = pl.BlockSpec(memory_space=pl.ANY)
    return pl.pallas_call(
        functools.partial(attend_back_kernel, group, step, lead, size, lanes),
        grid=(heads, own // tile),
        out_shape=(
            jax.ShapeDtypeStruct(queries.shape, jnp.bfloat16),
            jax.ShapeDtypeStruct((2, own, heads * HD), jnp.bfloat16),
            jax.ShapeDtypeStruct((1, HD), jnp.float32),
            jax.ShapeDtypeStruct((1, HD), jnp.float32),
            jax.ShapeDtypeStruct((PARTS, depth // size, width), jnp.float32),
        ),
        in_specs=attention_specs(own, rows, group, tile, span)
        + [pl.BlockSpec((tile, group * HD), lambda g, t: (t, g)), any_space, any_space],
        out_specs=(
            pl.BlockSpec((tile, group * HD), lambda g, t: (t, g)),
            pl.BlockSpec((2, own, heads * HD), lambda g, t: (0, 0, 0)),
            pl.BlockSpec((1, HD), whole),
            pl.BlockSpec((1, HD), whole),
            pl.BlockSpec((PARTS, depth // size, width), lambda g, t: (0, 0, 0)),
        ),
        scratch_shapes=[
            pltpu.VMEM((rows, HD), jnp.bfloat16),
            pltpu.VMEM((rows, HD), jnp.float32),
            pltpu.VMEM((rows, HD), jnp.float32),
            pltpu.VMEM((heads, back, 2, own, HD), jnp.bfloat16),
            pltpu.VMEM((heads, back, 2, own, HD), jnp.bfloat16),
            pltpu.VMEM((heads, 2, own, HD), jnp.float32),
            pltpu.VMEM((tokens, depth), jnp.bfloat16),
            pltpu.VMEM((PARTS, tokens, width), jnp.bfloat16),
            pltpu.SemaphoreType.DMA((PARTS + 1,)),
            pltpu.SemaphoreType.DMA((heads, back)),
            pltpu.SemaphoreType.DMA((heads, back)),
            *scatter_scratch(size, depth // size, width),
        ],
        compiler_params=pltpu.CompilerParams(
            collective_id=9, has_side_effects=True, vmem_limit_bytes=60 * 1024 * 1024
        ),
        cost_estimate=pl.CostEstimate(
            flops=40 * own * span * queries.shape[1],
            bytes_accessed=8 * queries.size + 16 * keys.size,
            transcendentals=own * span * heads * group,
        ),
        name="attend_back",
    )(queries, keys, values, bias, cosine, sine, norm_query, norm_key, grad, left, right)


def window_tables(length_row, pad_row, first, own, lead, tile, span):
    places = first - lead + jnp.arange(lead + own, dtype=jnp.int32)
    ends = jnp.cumsum(length_row)
    passed = places[:, None] >= ends[None, :]
    docs = jnp.sum(passed.astype(jnp.int32), axis=1)
    starts = jnp.sum(jnp.where(passed, length_row[None, :], 0), axis=1)
    freqs = THETA ** (-(jnp.arange(HD // 2).astype(jnp.float32) * 2.0 / HD))
    angles = (places - starts).astype(jnp.float32)[:, None] * freqs[None, :]
    cosine, sine = (jnp.cos(angles), jnp.sin(angles))
    padded = jnp.concatenate((jnp.zeros((lead,), pad_row.dtype), pad_row))
    live = lax.dynamic_slice_in_dim(padded, first, lead + own, 0)
    step = tile if lead + own > span else 0
    masks = []
    for index in range(own // tile):
        at = lead + index * tile
        query, key = (places[at : at + tile, None], places[None, index * step : index * step + span])
        same = docs[at : at + tile, None] == docs[None, index * step : index * step + span]
        seen = (live[None, index * step : index * step + span] == 1) | (key == query)
        masks.append((key >= 0) & (key <= query) & (query - key < WINDOW) & same & seen)
    bias = jnp.where(jnp.concatenate(masks, axis=0), 0.0, NEG).astype(jnp.float32)
    cosine = jnp.concatenate((cosine, cosine), axis=1)
    sine = jnp.concatenate((-sine, sine), axis=1)
    return (bias, cosine, sine, step, live[lead:].astype(jnp.float32))


def shards(
    states,
    lengths,
    padding,
    teacher,
    norm_attn,
    w_query,
    w_key,
    w_value,
    norm_query,
    norm_key,
    w_out,
    norm_mlp,
    w_gate,
    w_up,
    w_down,
):
    own = states.shape[0]
    n_tp, n_fsdp = (lax.axis_size("tp"), lax.axis_size("fsdp"))
    first = lax.axis_index("tp") * own
    back = min(n_tp - 1, -(-WINDOW // own))
    lead = back * own
    tile = min(256, own)
    span = WINDOW + tile if lead >= WINDOW else lead + own
    wq, wk = (w_query.shape[1], w_key.shape[1])
    bias, cosine, sine, step, live = window_tables(
        lengths[0], padding[0], first, own, lead, tile, span
    )
    joined = jnp.concatenate((w_query, w_key, w_value, w_out.T), axis=1)
    wo = w_out.shape[0]
    units = [
        part.reshape(n_fsdp, -1, part.shape[1]) for part in (w_gate.T, w_up.T, w_down)
    ]
    live_here = jnp.full((8, 128), jnp.sum(padding).astype(jnp.float32))
    before, weights_attn, mine_gate, mine_up, mine_down, counts = enter(
        n_fsdp, n_tp, back, states, joined, jnp.stack(units, axis=1), live_here
    )
    count = counts[0, 0]
    units_gate = lax.all_gather(mine_gate, "tp", axis=0)
    units_down = lax.all_gather(mine_down, "tp", axis=0)
    normed_in, query_raw, key_raw, value = project(
        before, states, norm_attn, weights_attn, wq, wk
    )
    gains = (norm_query.reshape(1, HD), norm_key.reshape(1, HD))
    attended = attend(query_raw, key_raw, value, bias, cosine, sine, *gains, tile, step)
    inputs = states.astype(jnp.float32)
    hidden_one = project_out(attended, weights_attn, states, wo)
    normed_two, factor_two = normalize_rows(hidden_one)
    whole_two, gate, up, product, units_up = gate_up(
        n_fsdp, (normed_two * norm_mlp).astype(jnp.bfloat16), units_gate, mine_up
    )
    outputs = hidden_one + sum_products(n_fsdp, 2, (product,), (units_down,))
    errors = (outputs - teacher.astype(jnp.float32)) * live[:, None]
    squares = jnp.sum(errors * errors)
    grad_out = errors * (2.0 / (count * D))

    grad_gate, grad_up, units_early, units_late = grad_hidden_units(
        n_fsdp, grad_out.astype(jnp.bfloat16), units_down, gate, up, product, whole_two
    )
    units_early = lax.psum_scatter(units_early, "tp", scatter_dimension=0)
    grad_mid = sum_products(n_fsdp, 4, (grad_gate, grad_up), (units_gate, units_up))
    grad_norm_mlp = jnp.sum(grad_mid * normed_two, axis=0)
    grad_hidden = grad_out + norm_back(grad_mid, normed_two, factor_two, norm_mlp)

    grad_low_out = grad_hidden.astype(jnp.bfloat16)
    grad_attended = back_out(grad_low_out, weights_attn, wo)
    grad_query, grad_pair, grad_norm_query, grad_norm_key, sums_out = attend_back(
        query_raw,
        key_raw,
        value,
        bias,
        cosine,
        sine,
        *gains,
        grad_attended,
        tile,
        step,
        grad_low_out,
        attended,
        n_fsdp,
        n_tp,
    )
    units_late, grad_query = lax.optimization_barrier((units_late, grad_query))
    units_late = lax.psum_scatter(units_late, "tp", scatter_dimension=0)
    sums_query, back_early = sum_query(n_fsdp, normed_in, grad_query, units_early)
    sums_pair, grad_low, back_late, grad_w_out, grad_w_query = sum_key(
        n_fsdp,
        n_tp,
        normed_in,
        grad_query,
        grad_pair,
        weights_attn,
        units_late,
        sums_out,
        sums_query,
    )
    grad_w_down, grad_w_gate, grad_w_up = [
        part.reshape(-1, part.shape[2]).astype(jnp.float32)
        for part in (back_early[:, 0], back_early[:, 1], back_late[:, 0])
    ]
    normed_one, factor_one = normalize_rows(inputs)
    grad_norm_attn = jnp.sum(grad_low * normed_one, axis=0)
    grad_input = grad_hidden + norm_back(grad_low, normed_one, factor_one, norm_attn)
    small = [grad_norm_attn, grad_norm_mlp, grad_norm_query[0], grad_norm_key[0]]
    small.append(jnp.full((HD,), squares))
    joined_small = jnp.concatenate(small).reshape(-1, HD)
    filled = joined_small.shape[0]
    joined_small = jnp.pad(joined_small, ((0, -filled % 8), (0, 0)))
    summed, grad_w_pair = last_sums(n_fsdp, n_tp, joined_small, sums_pair)
    summed = summed[:filled].reshape(-1)
    grad_norm_attn, grad_norm_mlp = (summed[:D], summed[D : 2 * D])
    grad_norm_query, grad_norm_key = (summed[2 * D : 2 * D + HD], summed[2 * D + HD : 2 * D + 2 * HD])
    squares = summed[2 * D + 2 * HD]
    return (
        outputs,
        squares / (count * D),
        grad_input,
        grad_norm_attn,
        grad_w_query,
        grad_w_pair[0],
        grad_w_pair[1],
        grad_norm_query,
        grad_norm_key,
        grad_w_out.T,
        grad_norm_mlp,
        grad_w_gate.T,
        grad_w_up.T,
        grad_w_down,
    )


def solution(mesh):
    tokens = P(("fsdp", "tp"), None)
    rows, columns, sequences = (P("fsdp", "tp"), P("tp", "fsdp"), P("fsdp", None))
    in_specs = (
        tokens,
        sequences,
        sequences,
        tokens,
        P(),
        rows,
        rows,
        rows,
        P(),
        P(),
        columns,
        P(),
        rows,
        rows,
        columns,
    )
    out_specs = (
        tokens,
        P(),
        tokens,
        P(),
        rows,
        rows,
        rows,
        P(),
        P(),
        columns,
        P(),
        rows,
        rows,
        columns,
    )
    return jax.shard_map(shards, mesh=mesh, in_specs=in_specs, out_specs=out_specs, check_vma=False)
```

```python
import functools

import jax
import jax.numpy as jnp
from jax import lax
from jax.experimental import pallas as pl
from jax.experimental.pallas import tpu as pltpu
from jax.sharding import PartitionSpec as P

D = 2048
HD = 128
WINDOW = 1024

EPS = 1e-06
THETA = 1000000.0
NEG = -1e30
LOG2E = 1.4426950408889634
VMEM = 56 * 1024 * 1024


def normalize_rows(values):
    factor = lax.rsqrt(jnp.mean(values * values, axis=-1, keepdims=True) + EPS)
    return (values * factor, factor)


def norm_back(grad, normed, factor, gain):
    scaled = grad * gain
    return factor * (scaled - normed * jnp.mean(scaled * normed, axis=-1, keepdims=True))


def contract_last(left, right):
    return lax.dot_general(
        left, right, (((1,), (1,)), ((), ())), preferred_element_type=jnp.float32
    )


def contract_first(left, right):
    return lax.dot_general(
        left, right, (((0,), (0,)), ((), ())), preferred_element_type=jnp.float32
    )


def dot(left, right):
    return jnp.dot(left, right, preferred_element_type=jnp.float32)


MESH = pl.DeviceIdType.MESH
PARTS = 2


def flip(index, mask):
    bit = 1
    while bit <= mask:
        if mask & bit:
            index = index + bit - 2 * bit * lax.rem(lax.div(index, bit), 2)
        bit *= 2
    return index


def chip_bits(size):
    bits = []
    bit = 2
    while bit < size:
        bits.append(bit)
        bit *= 2
    return bits


def orders(size):
    bits = chip_bits(size)
    return (bits, bits[::-1])


def mask_of(pattern, order):
    return sum(bit for i, bit in enumerate(order) if pattern >> i & 1)


def top(pattern):
    return pattern.bit_length() - 1


def greet(me, size):
    barrier = pltpu.get_barrier_semaphore()
    bits = [1] + chip_bits(size)
    for bit in bits:
        pl.semaphore_signal(
            barrier, inc=1, device_id={"fsdp": flip(me, bit)}, device_id_type=MESH
        )
    pl.semaphore_wait(barrier, len(bits))


def pick(part, pair):
    return pair[0] + part * (pair[1] - pair[0])


def unit_loads(source, kind, target, sems):
    lanes, _, rows, _ = source.shape
    return [
        pltpu.make_async_copy(
            source.at[lane, kind], target.at[pl.ds(lane * rows, rows)], sems.at[lane]
        )
        for lane in range(lanes)
    ]


class Gather:
    def __init__(self, size, me, whole, sems, parts=PARTS, lane=lambda part: part, parity=lambda part: part, own=None):
        self.size, self.me, self.whole, self.parts = (size, me, whole, parts)
        self.lane, self.parity, self.own = (lane, parity, own)
        self.chip_send, self.chip_recv, self.core_send, self.core_recv = sems
        self.steps = len(chip_bits(size))
        self.patterns = sorted(range(1 << self.steps), key=lambda m: (top(m), m))

    def order(self, part):
        return orders(self.size)[self.parity(part) % 2]

    def slot(self, part, pattern, sibling):
        return flip(self.me, mask_of(pattern, self.order(part)) + sibling)

    def source(self, part, pattern, block):
        return self.own if self.own is not None and part == 0 and pattern == 0 else block

    def chip_copy(self, part, step, pattern):
        block = self.whole.at[self.slot(part, pattern, 0), self.lane(part)]
        number = (1 << step) - 1 + pattern
        return pltpu.make_async_remote_copy(
            src_ref=self.source(part, pattern, block),
            dst_ref=block,
            send_sem=self.chip_send.at[part, number],
            recv_sem=self.chip_recv.at[part, number],
            device_id={"fsdp": flip(self.me, self.order(part)[step])},
            device_id_type=MESH,
        )

    def core_copy(self, part, pattern):
        block = self.whole.at[self.slot(part, pattern, 0), self.lane(part)]
        return pltpu.make_async_remote_copy(
            src_ref=self.source(part, pattern, block),
            dst_ref=block,
            send_sem=self.core_send.at[part, pattern],
            recv_sem=self.core_recv.at[part, pattern],
            device_id={"fsdp": flip(self.me, 1)},
            device_id_type=MESH,
        )

    def arrive(self, part, pattern):
        if pattern:
            step = top(pattern)
            self.chip_copy(part, step, pattern - (1 << step)).wait_recv()

    def forward(self, part, pattern):
        for step in range(top(pattern) + 1, self.steps):
            self.chip_copy(part, step, pattern).start()
        self.core_copy(part, pattern).start()

    def pairs(self, work):
        for pattern in self.patterns:
            for part in range(self.parts):
                self.arrive(part, pattern)
            for part in range(self.parts):
                self.forward(part, pattern)
            work([self.slot(part, pattern, 0) for part in range(self.parts)])
            for part in range(self.parts):
                self.core_copy(part, pattern).wait_recv()
            work([self.slot(part, pattern, 1) for part in range(self.parts)])

    def finish(self):
        for pattern in self.patterns:
            for part in range(self.parts):
                for step in range(top(pattern) + 1, self.steps):
                    self.chip_copy(part, step, pattern).wait_send()
                self.core_copy(part, pattern).wait_send()


def gather_semaphores(size, parts=PARTS):
    moves = max(1, size // 2 - 1)
    return [
        pltpu.SemaphoreType.DMA((parts, moves)),
        pltpu.SemaphoreType.DMA((parts, moves)),
        pltpu.SemaphoreType.DMA((parts, size // 2)),
        pltpu.SemaphoreType.DMA((parts, size // 2)),
    ]


def first_step(pattern, steps):
    return (pattern & -pattern).bit_length() - 1 if pattern else steps


def scatter_order(steps):
    return sorted(range(1 << steps), key=lambda m: (first_step(m, steps), -bin(m).count("1"), m))


def scatter_steps(
    size, me, made, held, sent, came, sems, partial, final, ready=lambda part, slot, q, sibling: None
):
    chip_send, chip_recv, core_send, core_recv = sems
    steps = len(chip_bits(size))
    order = [bits[::-1] for bits in orders(size)]
    first = lambda m: first_step(m, steps)
    patterns = scatter_order(steps)
    place = {m: q for q, m in enumerate(patterns)}
    width = final.shape[-1]
    chunk = min(1024, width)

    def slots(pattern, sibling):
        return [flip(me, mask_of(pattern, order[part]) + sibling) for part in range(PARTS)]

    def core_copy(part, q):
        return pltpu.make_async_remote_copy(
            src_ref=made.at[part, q],
            dst_ref=held.at[part, q],
            send_sem=core_send.at[part, q],
            recv_sem=core_recv.at[part, q],
            device_id={"fsdp": flip(me, 1)},
            device_id_type=MESH,
        )

    def chip_copy(part, q):
        return pltpu.make_async_remote_copy(
            src_ref=sent.at[part, q],
            dst_ref=came.at[part, q],
            send_sem=chip_send.at[part, q],
            recv_sem=chip_recv.at[part, q],
            device_id={"fsdp": flip(me, order[part][first(patterns[q])])},
            device_id_type=MESH,
        )

    def for_sibling(q):
        pair = slots(patterns[q], 1)
        for part in range(PARTS):
            ready(part, pair[part], q, 1)

            @pl.loop(0, width // chunk)
            def _(index):
                columns = pl.ds(pl.multiple_of(index * chunk, chunk), chunk)
                made[part, q, :, columns] = partial(part, pair[part], columns).astype(jnp.bfloat16)

            core_copy(part, q).start()

    def for_chips(q):
        pattern = patterns[q]
        pair = slots(pattern, 0)
        arrivals = [place[pattern | 1 << step] for step in range(first(pattern))]
        for part in range(PARTS):
            ready(part, pair[part], q, 0)
            if pattern:
                core_copy(part, q).wait_recv()
                for arrival in arrivals:
                    chip_copy(part, arrival).wait_recv()

            @pl.loop(0, width // chunk)
            def _(index):
                columns = pl.ds(pl.multiple_of(index * chunk, chunk), chunk)
                total = partial(part, pair[part], columns)
                if pattern:
                    total = total + held[part, q, :, columns].astype(jnp.float32)
                    for arrival in arrivals:
                        total = total + came[part, arrival, :, columns].astype(jnp.float32)
                    sent[part, q, :, columns] = total.astype(jnp.bfloat16)
                else:
                    final[part, :, columns] = total

            if pattern:
                chip_copy(part, q).start()
        if not pattern:
            for part in range(PARTS):
                core_copy(part, q).wait_recv()
                for arrival in arrivals:
                    chip_copy(part, arrival).wait_recv()

                @pl.loop(0, width // chunk)
                def _(index):
                    columns = pl.ds(pl.multiple_of(index * chunk, chunk), chunk)
                    total = final[part, :, columns] + held[part, q, :, columns].astype(jnp.float32)
                    for arrival in arrivals:
                        total = total + came[part, arrival, :, columns].astype(jnp.float32)
                    final[part, :, columns] = total

    def finish():
        for q in range(len(patterns)):
            for part in range(PARTS):
                core_copy(part, q).wait_send()
                if patterns[q]:
                    chip_copy(part, q).wait_send()

    calls = []
    for q in range(len(patterns)):
        calls += [functools.partial(for_sibling, q), functools.partial(for_chips, q)]
    return (calls, finish)


def scatter_scratch(size, rows, width):
    held = size // 2
    moved = max(1, held - 1)
    return [
        pltpu.VMEM((PARTS, held, rows, width), jnp.bfloat16),
        pltpu.VMEM((PARTS, held, rows, width), jnp.bfloat16),
        pltpu.VMEM((PARTS, moved, rows, width), jnp.bfloat16),
        pltpu.VMEM((PARTS, moved, rows, width), jnp.bfloat16),
        pltpu.SemaphoreType.DMA((PARTS, moved)),
        pltpu.SemaphoreType.DMA((PARTS, moved)),
        pltpu.SemaphoreType.DMA((PARTS, held)),
        pltpu.SemaphoreType.DMA((PARTS, held)),
    ]


def gate_up_kernel(
    size,
    x_ref,
    w_in,
    x_out,
    gate_out,
    up_out,
    prod_out,
    whole,
    wg_ref,
    wu_ref,
    gate,
    up,
    prod,
    load,
    keep,
    store,
    *sems,
):
    me = lax.axis_index("fsdp")
    hidden = wg_ref.shape[0]
    lanes = w_in.shape[0]
    loads = [pltpu.make_async_copy(x_ref, whole.at[me], load.at[0])]
    loads += unit_loads(w_in, 0, wg_ref, load.at[pl.ds(1, lanes)])
    loads += unit_loads(w_in, 1, wu_ref, load.at[pl.ds(1 + lanes, lanes)])
    for copy in loads:
        copy.start()
    greet(me, size)
    loads[0].wait()
    state = {"count": 0, "last": None}

    def stores(part, at):
        return [
            pltpu.make_async_copy(buffer.at[part], out.at[at, part], store.at[part, i])
            for i, (buffer, out) in enumerate(((gate, gate_out), (up, up_out), (prod, prod_out)))
        ]

    def work(pair):
        count, last = (state["count"], state["last"])
        for part in range(PARTS):
            pltpu.make_async_copy(
                whole.at[pair[part], part], x_out.at[pair[part], part], keep.at[part, count]
            ).start()
        if last is None:
            for copy in loads[1:]:
                copy.wait()

        @pl.loop(0, PARTS)
        def _(part):
            at = pick(part, pair)
            if last is not None:
                for copy in stores(part, pick(part, last)):
                    copy.wait()

            rows = whole[at, part]
            gates = contract_last(rows, wg_ref[...])
            ups = contract_last(rows, wu_ref[...])
            gate[part] = gates
            up[part] = ups
            prod[part] = (gates * jax.nn.sigmoid(gates) * ups).astype(jnp.bfloat16)

            for copy in stores(part, at):
                copy.start()

        state["count"], state["last"] = (count + 1, pair)
        state.setdefault("all", []).append(pair)

    gather = Gather(size, me, whole, sems)
    gather.pairs(work)
    gather.finish()
    for part in range(PARTS):
        for copy in stores(part, state["last"][part]):
            copy.wait()
        for count, pair in enumerate(state["all"]):
            pltpu.make_async_copy(
                whole.at[pair[part], part], x_out.at[pair[part], part], keep.at[part, count]
            ).wait()


def gate_up(size, values, units):
    own, width = values.shape
    lanes, _, each, _ = units.shape
    rows, hidden = (own // PARTS, lanes * each)
    any_space = pl.BlockSpec(memory_space=pl.ANY)
    shape = lambda columns, kind: jax.ShapeDtypeStruct((size, PARTS, rows, columns), kind)
    outs = pl.pallas_call(
        functools.partial(gate_up_kernel, size),
        out_shape=(
            shape(width, jnp.bfloat16),
            shape(hidden, jnp.float32),
            shape(hidden, jnp.float32),
            shape(hidden, jnp.bfloat16),
        ),
        in_specs=[any_space] * 2,
        out_specs=(any_space,) * 4,
        scratch_shapes=[
            pltpu.VMEM((size, PARTS, rows, width), jnp.bfloat16),
            pltpu.VMEM((hidden, width), jnp.bfloat16),
            pltpu.VMEM((hidden, width), jnp.bfloat16),
            pltpu.VMEM((PARTS, rows, hidden), jnp.float32),
            pltpu.VMEM((PARTS, rows, hidden), jnp.float32),
            pltpu.VMEM((PARTS, rows, hidden), jnp.bfloat16),
            pltpu.SemaphoreType.DMA((1 + 2 * lanes,)),
            pltpu.SemaphoreType.DMA((PARTS, size)),
            pltpu.SemaphoreType.DMA((PARTS, 3)),
            *gather_semaphores(size),
        ],
        compiler_params=pltpu.CompilerParams(
            collective_id=1, has_side_effects=True, vmem_limit_bytes=VMEM
        ),
        cost_estimate=pl.CostEstimate(
            flops=4 * size * own * width * hidden, bytes_accessed=200 * 1024 * 1024, transcendentals=0
        ),
        name="gate_up",
    )(values.reshape(PARTS, rows, width), units)
    return tuple(out.reshape(size * own, -1) for out in outs)


def grad_hidden_kernel(
    size,
    x_ref,
    wd_in,
    gate_in,
    up_in,
    prod_in,
    two_in,
    dgate_out,
    dup_out,
    early_out,
    late_out,
    whole,
    wd_ref,
    gate,
    up,
    prod,
    two,
    dgate,
    dup,
    sums,
    load,
    fetch,
    store,
    flush,
    *sems,
):
    me = lax.axis_index("fsdp")
    hidden, width = wd_ref.shape
    lanes, _, each, _ = wd_in.shape
    chunk = 256 if hidden % 256 == 0 else 128
    loads = [pltpu.make_async_copy(x_ref, whole.at[me], load.at[0])]
    loads += unit_loads(wd_in, 0, wd_ref, load.at[pl.ds(1, lanes)])
    for copy in loads:
        copy.start()

    def stores(part, at):
        return [
            pltpu.make_async_copy(buffer.at[part], out.at[at, part], store.at[part, i])
            for i, (buffer, out) in enumerate(((dgate, dgate_out), (dup, dup_out)))
        ]

    def fetches(count, kinds):
        copies = []
        for part in range(PARTS):
            at = order[count][part]
            pairs = (
                (gate_in, gate.at[part]),
                (up_in, up.at[part]),
                (prod_in, prod.at[count % 2, part]),
                (two_in, two.at[count % 2, part]),
            )
            copies += [
                pltpu.make_async_copy(pairs[i][0].at[at, part], pairs[i][1], fetch.at[count % 2, part, i])
                for i in kinds
            ]
        return copies

    gather = Gather(size, me, whole, sems)
    order = []
    for pattern in gather.patterns:
        for sibling in (0, 1):
            order.append([gather.slot(part, pattern, sibling) for part in range(PARTS)])
    for copy in fetches(0, (0, 1, 2, 3)):
        copy.start()
    greet(me, size)
    loads[0].wait()
    state = {"count": 0}

    def work(pair):
        count = state["count"]
        state["count"] = count + 1
        more = count + 1 < len(order)
        if count == 0:
            for copy in loads[1:]:
                copy.wait()
        if more:
            for copy in fetches(count + 1, (2, 3)):
                copy.start()
        for copy in fetches(count, (0, 1)):
            copy.wait()
        if count:
            for part in range(PARTS):
                for copy in stores(part, order[count - 1][part]):
                    copy.wait()

        @pl.loop(0, PARTS)
        def _(part):
            at = pick(part, pair)

            grads = contract_last(whole[at, part], wd_ref[...])
            gates = gate[part]
            sigmoid = jax.nn.sigmoid(gates)
            dgate[part] = (
                grads * up[part] * sigmoid * (1.0 + gates * (1.0 - sigmoid))
            ).astype(jnp.bfloat16)
            dup[part] = (grads * (gates * sigmoid)).astype(jnp.bfloat16)

        for part in range(PARTS):
            for copy in stores(part, pair[part]):
                copy.start()
        if more:
            for copy in fetches(count + 1, (0, 1)):
                copy.start()
        for copy in fetches(count, (2, 3)):
            copy.wait()

        @pl.loop(0, hidden // chunk)
        def _(index):
            units = pl.ds(pl.multiple_of(index * chunk, chunk), chunk)
            here = count % 2
            for kind, (lefts, rights) in enumerate(
                (
                    ((prod.at[here, 0], prod.at[here, 1]), (whole.at[pair[0], 0], whole.at[pair[1], 1])),
                    ((dgate.at[0], dgate.at[1]), (two.at[here, 0], two.at[here, 1])),
                    ((dup.at[0], dup.at[1]), (two.at[here, 0], two.at[here, 1])),
                )
            ):
                total = contract_first(lefts[0][:, units], rights[0][...])
                total += contract_first(lefts[1][:, units], rights[1][...])
                if count:
                    total += sums[kind, units, :]
                sums[kind, units, :] = total

    gather.pairs(work)
    gather.finish()
    for part in range(PARTS):
        for copy in stores(part, order[-1][part]):
            copy.wait()
    copies = []
    for piece in range(3 * lanes):
        kind, lane = (piece // lanes, piece % lanes)
        block = whole.at[piece // PARTS, piece % PARTS, pl.ds(0, each)]
        block[...] = sums[kind, lane * each : (lane + 1) * each, :].astype(jnp.bfloat16)
        out = early_out.at[lane, kind] if kind < 2 else late_out.at[lane, 0]
        copy = pltpu.make_async_copy(block, out, flush.at[piece])
        copy.start()
        copies.append(copy)
    for copy in copies:
        copy.wait()


def grad_hidden_units(size, values, units, gate, up, product, whole_two):
    own, width = values.shape
    lanes, _, each, _ = units.shape
    rows, hidden = (own // PARTS, lanes * each)
    any_space = pl.BlockSpec(memory_space=pl.ANY)
    shape = lambda columns, kind: jax.ShapeDtypeStruct((size, PARTS, rows, columns), kind)
    blocks = lambda array: array.reshape(size, PARTS, rows, -1)
    weight = lambda kinds: jax.ShapeDtypeStruct((lanes, kinds, each, width), jnp.bfloat16)
    dgate, dup, early, late = pl.pallas_call(
        functools.partial(grad_hidden_kernel, size),
        out_shape=(shape(hidden, jnp.bfloat16), shape(hidden, jnp.bfloat16), weight(2), weight(1)),
        in_specs=[any_space] * 6,
        out_specs=(any_space,) * 4,
        scratch_shapes=[
            pltpu.VMEM((size, PARTS, rows, width), jnp.bfloat16),
            pltpu.VMEM((hidden, width), jnp.bfloat16),
            pltpu.VMEM((PARTS, rows, hidden), jnp.float32),
            pltpu.VMEM((PARTS, rows, hidden), jnp.float32),
            pltpu.VMEM((2, PARTS, rows, hidden), jnp.bfloat16),
            pltpu.VMEM((2, PARTS, rows, width), jnp.bfloat16),
            pltpu.VMEM((PARTS, rows, hidden), jnp.bfloat16),
            pltpu.VMEM((PARTS, rows, hidden), jnp.bfloat16),
            pltpu.VMEM((3, hidden, width), jnp.float32),
            pltpu.SemaphoreType.DMA((1 + lanes,)),
            pltpu.SemaphoreType.DMA((2, PARTS, 4)),
            pltpu.SemaphoreType.DMA((PARTS, 2)),
            pltpu.SemaphoreType.DMA((3 * lanes,)),
            *gather_semaphores(size),
        ],
        compiler_params=pltpu.CompilerParams(
            collective_id=3, has_side_effects=True, vmem_limit_bytes=60 * 1024 * 1024
        ),
        cost_estimate=pl.CostEstimate(
            flops=8 * size * own * width * hidden, bytes_accessed=200 * 1024 * 1024, transcendentals=0
        ),
        name="grad_hidden_units",
    )(values.reshape(PARTS, rows, width), units, *map(blocks, (gate, up, product, whole_two)))
    return (dgate.reshape(size * own, hidden), dup.reshape(size * own, hidden), early, late)


def sum_products_kernel(size, kinds, *refs):
    terms = len(kinds)
    left_in, right_in, out = (refs[:terms], refs[terms : 2 * terms], refs[2 * terms])
    at = 2 * terms + 1
    lefts, rights, (w_load, x_load) = (
        refs[at : at + terms],
        refs[at + terms : at + 2 * terms],
        refs[at + 2 * terms : at + 2 * terms + 2],
    )
    made, held, sent, came, *sems = refs[at + 2 * terms + 2 :]
    me = lax.axis_index("fsdp")

    def partial(part, slot, columns):
        return sum(
            dot(left[slot, part], right[:, columns]) for left, right in zip(lefts, rights)
        )

    def tiles(part, slot, q, sibling):
        return [
            pltpu.make_async_copy(
                source.at[slot, part], left.at[slot, part], x_load.at[2 * q + sibling, part, i]
            )
            for i, (source, left) in enumerate(zip(left_in, lefts))
        ]

    seen = []

    def ready(part, slot, q, sibling):
        if not seen:
            for copy in weights:
                copy.wait()
        seen.append(slot)
        for copy in tiles(part, slot, q, sibling):
            copy.wait()

    weights = []
    for i, (source, right) in enumerate(zip(right_in, rights)):
        weights += unit_loads(source, kinds[i], right, w_load.at[i])
    for copy in weights:
        copy.start()
    order = [bits[::-1] for bits in orders(size)]
    for q, pattern in enumerate(scatter_order(len(order[0]))):
        for sibling in (1, 0):
            for part in range(PARTS):
                slot = flip(me, mask_of(pattern, order[part]) + sibling)
                for copy in tiles(part, slot, q, sibling):
                    copy.start()
    greet(me, size)
    calls, finish = scatter_steps(size, me, made, held, sent, came, sems, partial, out, ready)
    for call in calls:
        call()
    finish()


def sum_products(size, number, lefts, units):
    total, hidden = lefts[0].shape
    lanes, _, _, width = units[0][0].shape
    rows = total // size // PARTS
    vmem = pl.BlockSpec(memory_space=pltpu.VMEM)
    terms = len(lefts)
    out = pl.pallas_call(
        functools.partial(sum_products_kernel, size, tuple(kind for _, kind in units)),
        out_shape=jax.ShapeDtypeStruct((PARTS, rows, width), jnp.float32),
        in_specs=[pl.BlockSpec(memory_space=pl.ANY)] * (2 * terms),
        out_specs=vmem,
        scratch_shapes=[
            *[pltpu.VMEM((size, PARTS, rows, hidden), jnp.bfloat16)] * terms,
            *[pltpu.VMEM((hidden, width), jnp.bfloat16)] * terms,
            pltpu.SemaphoreType.DMA((terms, lanes)),
            pltpu.SemaphoreType.DMA((size, PARTS, terms)),
            *scatter_scratch(size, rows, width),
        ],
        compiler_params=pltpu.CompilerParams(
            collective_id=number, has_side_effects=True, vmem_limit_bytes=VMEM
        ),
        cost_estimate=pl.CostEstimate(
            flops=2 * total * hidden * width * terms, bytes_accessed=200 * 1024 * 1024, transcendentals=0
        ),
        name="sum_products",
    )(*[left.reshape(size, PARTS, rows, hidden) for left in lefts], *[array for array, _ in units])
    return out.reshape(PARTS * rows, width)


def enter_kernel(
    size,
    lanes,
    back,
    x_ref,
    w_ref,
    m_ref,
    c_ref,
    before,
    whole,
    mine_pair,
    mine_down,
    count,
    counts,
    loads,
    z_send,
    z_recv,
    x_send,
    x_recv,
    m_send,
    m_recv,
    c_send,
    c_recv,
    *sems,
):
    me, z = (lax.axis_index("fsdp"), lax.axis_index("tp"))
    mine = (mine_pair.at[0], mine_pair.at[1], mine_down.at[0])
    span = m_ref.shape[-1]
    part_of = lambda device: pl.ds(pl.multiple_of(device * span, span), span)
    local = [pltpu.make_async_copy(w_ref, whole.at[me, z], loads.at[0])]
    local += [
        pltpu.make_async_copy(m_ref.at[me, kind], mine[kind].at[:, part_of(me)], loads.at[kind + 1])
        for kind in range(3)
    ]
    for copy in local:
        copy.start()
    counts[me] = c_ref[...]
    up, down = (lax.rem(z + 1, lanes), lax.rem(z + lanes - 1, lanes))
    barrier = pltpu.get_barrier_semaphore()
    peers = [{"fsdp": flip(me, other)} for other in range(1, size)] + [{"tp": up}, {"tp": down}]
    for peer in peers:
        pl.semaphore_signal(barrier, inc=1, device_id=peer, device_id_type=MESH)
    pl.semaphore_wait(barrier, len(peers))

    def far(part):
        return (part + 1) // 2

    def lane(part):
        if part == 0:
            return z
        return z - far(part) if part % 2 else z + far(part)

    def exists(part):
        return z >= far(part) if part % 2 else z + far(part) < lanes

    def lane_copy(part):
        block = whole.at[me, lane(part - 2) if part > 2 else z]
        return pltpu.make_async_remote_copy(
            src_ref=block if part > 2 else w_ref,
            dst_ref=block,
            send_sem=z_send.at[part - 1],
            recv_sem=z_recv.at[part - 1],
            device_id={"tp": up if part % 2 else down},
            device_id_type=MESH,
        )

    def lane_sends(part):
        if part % 2:
            return (z >= far(part) - 1) & (z + 1 < lanes)
        return (z + far(part) - 1 < lanes) & (z > 0)

    def token_copy(hop):
        return pltpu.make_async_remote_copy(
            src_ref=x_ref if hop == 1 else before.at[hop - 2],
            dst_ref=before.at[hop - 1],
            send_sem=x_send.at[hop - 1],
            recv_sem=x_recv.at[hop - 1],
            device_id={"tp": up},
            device_id_type=MESH,
        )

    def unit_copy(other, kind):
        peer = flip(me, other)
        return pltpu.make_async_remote_copy(
            src_ref=m_ref.at[peer, kind],
            dst_ref=mine[kind].at[:, part_of(me)],
            send_sem=m_send.at[other - 1, kind],
            recv_sem=m_recv.at[other - 1, kind],
            device_id={"fsdp": peer},
            device_id_type=MESH,
        )

    def count_copy(other):
        return pltpu.make_async_remote_copy(
            src_ref=c_ref,
            dst_ref=counts.at[me],
            send_sem=c_send.at[other - 1],
            recv_sem=c_recv.at[other - 1],
            device_id={"fsdp": flip(me, other)},
            device_id_type=MESH,
        )

    def when(condition, run):
        pl.when(condition)(run)

    gather = Gather(size, me, whole, sems, 2 * lanes - 1, lane, far, w_ref)
    for part in (1, 2):
        when(lane_sends(part), lambda: lane_copy(part).start())
    gather.forward(0, 0)
    when(z + 1 < lanes, lambda: token_copy(1).start())
    for other in range(1, size):
        count_copy(other).start()
        for kind in range(3):
            unit_copy(other, kind).start()
    events = [(part, pattern) for part in range(2 * lanes - 1) for pattern in gather.patterns]
    wave = lambda pattern: 3.5 * top(pattern) + 2.5 if pattern else 0
    events.sort(key=lambda event: (2 * far(event[0]) + wave(event[1]), event))

    def run_event(part, pattern):
        if pattern:
            gather.arrive(part, pattern)
        elif part:
            lane_copy(part).wait_recv()
            if part + 2 < 2 * lanes - 1:
                when(lane_sends(part + 2), lambda: lane_copy(part + 2).start())
        gather.forward(part, pattern)

    for part, pattern in events[1:]:
        if part == 0:
            run_event(part, pattern)
        else:
            when(exists(part), lambda: run_event(part, pattern))
        if (part, pattern) == (2 * lanes - 2, 0):
            for hop in range(1, back):
                when(z >= hop, lambda: token_copy(hop).wait_recv())
                when((z >= hop) & (z + 1 < lanes), lambda: token_copy(hop + 1).start())
    for other in range(1, size):
        count_copy(other).wait()
    count[...] = sum(counts[other] for other in range(size))

    def close(part):
        for pattern in gather.patterns:
            gather.core_copy(part, pattern).wait()
            for step in range(top(pattern) + 1, gather.steps):
                gather.chip_copy(part, step, pattern).wait_send()

    close(0)
    for part in range(1, 2 * lanes - 1):
        when(exists(part), lambda: close(part))
        when(lane_sends(part), lambda: lane_copy(part).wait_send())
    for other in range(1, size):
        for kind in range(3):
            unit_copy(other, kind).wait()
    for hop in range(1, back + 1):
        when((z >= hop - 1) & (z + 1 < lanes), lambda: token_copy(hop).wait_send())
    when(z >= back, lambda: token_copy(back).wait_recv())
    for copy in local:
        copy.wait()


def enter(size, lanes, back, values, weights, units, count):
    any_space = pl.BlockSpec(memory_space=pl.ANY)
    vmem = pl.BlockSpec(memory_space=pltpu.VMEM)
    _, kinds, rows, columns = units.shape
    others = pltpu.SemaphoreType.DMA((size - 1,))
    other_kinds = pltpu.SemaphoreType.DMA((size - 1, kinds))
    line = pltpu.SemaphoreType.DMA((2 * lanes - 2,))
    hop = pltpu.SemaphoreType.DMA((back,))
    mine = lambda number: jax.ShapeDtypeStruct((number, rows, size * columns), units.dtype)
    return pl.pallas_call(
        functools.partial(enter_kernel, size, lanes, back),
        out_shape=(
            jax.ShapeDtypeStruct((back, *values.shape), values.dtype),
            jax.ShapeDtypeStruct((size, lanes, *weights.shape), weights.dtype),
            mine(kinds - 1),
            mine(1),
            jax.ShapeDtypeStruct(count.shape, count.dtype),
        ),
        in_specs=[any_space, any_space, any_space, vmem],
        out_specs=(any_space,) * 4 + (vmem,),
        scratch_shapes=[
            pltpu.VMEM((size, *count.shape), count.dtype),
            pltpu.SemaphoreType.DMA((kinds + 1,)),
            line,
            line,
            hop,
            hop,
            other_kinds,
            other_kinds,
            others,
            others,
            *gather_semaphores(size, 2 * lanes - 1),
        ],
        compiler_params=pltpu.CompilerParams(collective_id=5, has_side_effects=True),
        cost_estimate=pl.CostEstimate(flops=0, bytes_accessed=400 * 1024 * 1024, transcendentals=0),
        name="enter",
    )(values, weights, units, count)


class Units:
    def __init__(self, size, me, units, back, sems):
        self.size, self.me, self.units, self.back = (size, me, units, back)
        self.send, self.recv, self.own = sems
        self.kinds, self.span = (units.shape[0], back.shape[-1])

    def part_of(self, device):
        return pl.ds(pl.multiple_of(device * self.span, self.span), self.span)

    def stay(self):
        return [
            pltpu.make_async_copy(
                self.units.at[kind, :, self.part_of(self.me)],
                self.back.at[self.me, kind],
                self.own.at[kind],
            )
            for kind in range(self.kinds)
        ]

    def moves(self):
        copies = []
        for other in range(1, self.size):
            peer = flip(self.me, other)
            copies += [
                pltpu.make_async_remote_copy(
                    src_ref=self.units.at[kind, :, self.part_of(peer)],
                    dst_ref=self.back.at[self.me, kind],
                    send_sem=self.send.at[other - 1, kind],
                    recv_sem=self.recv.at[other - 1, kind],
                    device_id={"fsdp": peer},
                    device_id_type=MESH,
                )
                for kind in range(self.kinds)
            ]
        return copies

    def start(self):
        for copy in self.stay() + self.moves():
            copy.start()

    def finish(self):
        for copy in self.moves() + self.stay():
            copy.wait()


def units_scratch(size, kinds):
    return [
        pltpu.SemaphoreType.DMA((size - 1, kinds)),
        pltpu.SemaphoreType.DMA((size - 1, kinds)),
        pltpu.SemaphoreType.DMA((kinds,)),
    ]


class Lanes:
    def __init__(self, lanes, z, values, out, low, came, send, recv):
        self.lanes, self.z, self.values, self.out = (lanes, z, values, out)
        self.low, self.came, self.send, self.recv = (low, came, send, recv)

    def block(self, lane):
        each = self.lanes // PARTS
        width = self.out.shape[1]
        start = pl.multiple_of(lax.rem(lane, each) * width, width)
        return self.values[lax.div(lane, each), :, pl.ds(start, width)]

    def copy(self, hop):
        return pltpu.make_async_remote_copy(
            src_ref=self.low.at[hop - 1],
            dst_ref=self.came.at[hop - 1],
            send_sem=self.send.at[hop - 1],
            recv_sem=self.recv.at[hop - 1],
            device_id={"tp": lax.rem(self.z + hop, self.lanes)},
            device_id_type=MESH,
        )

    def start(self):
        for hop in range(1, self.lanes):
            self.low[hop - 1] = self.block(lax.rem(self.z + hop, self.lanes)).astype(jnp.bfloat16)
            self.copy(hop).start()

    def finish(self):
        for hop in range(1, self.lanes):
            self.copy(hop).wait()
        total = self.block(self.z)
        for hop in range(1, self.lanes):
            total = total + self.came[hop - 1].astype(jnp.float32)
        self.out[...] = total


def lanes_scratch(lanes, shape):
    return [
        pltpu.VMEM((lanes - 1, *shape), jnp.bfloat16),
        pltpu.VMEM((lanes - 1, *shape), jnp.bfloat16),
        pltpu.SemaphoreType.DMA((lanes - 1,)),
        pltpu.SemaphoreType.DMA((lanes - 1,)),
    ]


def greet_all(me, z, size, lanes):
    barrier = pltpu.get_barrier_semaphore()
    peers = [{"fsdp": flip(me, other)} for other in range(1, size)]
    peers += [{"tp": lax.rem(z + hop, lanes)} for hop in range(1, lanes)]
    for peer in peers:
        pl.semaphore_signal(barrier, inc=1, device_id=peer, device_id_type=MESH)
    pl.semaphore_wait(barrier, len(peers))


def sum_query_kernel(
    size, left_ref, right_ref, units_ref, out, back, left, right, loads, *refs
):
    units_sems = refs[:3]
    made, held, sent, came, *sems = refs[3:]
    me = lax.axis_index("fsdp")
    width = out.shape[-1]
    rows = left.shape[1] // size
    copies = [pltpu.make_async_copy(left_ref, left, loads.at[PARTS])]
    copies += [
        pltpu.make_async_copy(
            right_ref.at[:, pl.ds(part * width, width)], right.at[part], loads.at[part]
        )
        for part in range(PARTS)
    ]
    for copy in copies:
        copy.start()
    barrier = pltpu.get_barrier_semaphore()
    for other in range(1, size):
        pl.semaphore_signal(
            barrier, inc=1, device_id={"fsdp": flip(me, other)}, device_id_type=MESH
        )
    pl.semaphore_wait(barrier, size - 1)
    for copy in copies:
        copy.wait()

    def partial(part, slot, columns):
        block = left[:, pl.ds(pl.multiple_of(slot * rows, rows), rows)]
        return contract_first(block, right[part, :, columns])

    units = Units(size, me, units_ref, back, units_sems)
    calls, finish = scatter_steps(size, me, made, held, sent, came, sems, partial, out)
    for number, call in enumerate(calls):
        call()
        if number == len(calls) // 2:
            units.start()
    units.finish()
    finish()


def sum_query(size, left, right, units):
    tokens, depth = left.shape
    width = right.shape[1] // PARTS
    rows = depth // size
    any_space = pl.BlockSpec(memory_space=pl.ANY)
    vmem = pl.BlockSpec(memory_space=pltpu.VMEM)
    return pl.pallas_call(
        functools.partial(sum_query_kernel, size),
        out_shape=(
            jax.ShapeDtypeStruct((PARTS, rows, width), jnp.float32),
            jax.ShapeDtypeStruct((size, *units.shape[:2], rows), jnp.bfloat16),
        ),
        in_specs=[any_space] * 3,
        out_specs=(vmem, any_space),
        scratch_shapes=[
            pltpu.VMEM((tokens, depth), jnp.bfloat16),
            pltpu.VMEM((PARTS, tokens, width), jnp.bfloat16),
            pltpu.SemaphoreType.DMA((PARTS + 1,)),
            *units_scratch(size, units.shape[0]),
            *scatter_scratch(size, rows, width),
        ],
        compiler_params=pltpu.CompilerParams(
            collective_id=6, has_side_effects=True, vmem_limit_bytes=VMEM
        ),
        cost_estimate=pl.CostEstimate(
            flops=4 * tokens * depth * width, bytes_accessed=100 * 1024 * 1024, transcendentals=0
        ),
        name="sum_query",
    )(left, right, units)


def sum_key_kernel(
    size,
    lanes,
    left_ref,
    q_ref,
    kv_ref,
    w_ref,
    units_ref,
    out_sums,
    query_sums,
    pair_out,
    low,
    back,
    lane_out,
    lane_query,
    left,
    right,
    loads,
    tiles,
    fetch,
    out,
    *refs,
):
    units_sems, lane_refs = (refs[:3], refs[3:11])
    made, held, sent, came, *sems = refs[11:]
    me, z = (lax.axis_index("fsdp"), lax.axis_index("tp"))
    rows = left.shape[1] // size
    parts, span = (w_ref.shape[1], tiles.shape[-1])
    copies = [pltpu.make_async_copy(left_ref, left, loads.at[PARTS])]
    copies += [
        pltpu.make_async_copy(kv_ref.at[part], right.at[part], loads.at[part])
        for part in range(PARTS)
    ]
    for copy in copies:
        copy.start()

    def tile_copy(f):
        return pltpu.make_async_copy(
            w_ref.at[f, :, :, pl.ds(0, span)], tiles.at[f % 2], fetch.at[f % 2]
        )

    tile_copy(0).start()
    greet_all(me, z, size, lanes)
    for copy in copies:
        copy.wait()

    def partial(part, slot, columns):
        block = left[:, pl.ds(pl.multiple_of(slot * rows, rows), rows)]
        return contract_first(block, right[part, :, columns])

    def low_columns(f):
        if f + 1 < size:
            tile_copy(f + 1).start()
        tile_copy(f).wait()
        half = low.shape[0] // 2

        @pl.loop(0, 2)
        def _(index):
            span_rows = pl.ds(pl.multiple_of(index * half, half), half)
            total = jnp.zeros((half, rows), jnp.float32)
            for z in range(parts):
                start = 0
                for source in (q_ref, right.at[0], right.at[1]):
                    width = source.shape[1] // parts
                    total += contract_last(
                        source[span_rows, z * width : (z + 1) * width],
                        tiles[f % 2, z, :, start : start + width],
                    )
                    start += width
            low[span_rows, f * rows : (f + 1) * rows] = total

    units = Units(size, me, units_ref, back, units_sems)
    across = (
        Lanes(lanes, z, out_sums, lane_out, *lane_refs[:4]),
        Lanes(lanes, z, query_sums, lane_query, *lane_refs[4:]),
    )
    calls, finish = scatter_steps(size, me, made, held, sent, came, sems, partial, out)
    done = 0
    for number, call in enumerate(calls):
        call()
        if number < 2:
            across[number].start()
        if number == len(calls) // 2:
            units.start()
        goal = size * max(0, number - 1) // max(1, len(calls) - 3)
        while done < min(size, goal):
            low_columns(done)
            done += 1
    while done < size:
        low_columns(done)
        done += 1
    for one in across:
        one.finish()
    units.finish()
    finish()
    pair_out[...] = out[...].astype(jnp.bfloat16)


def sum_key(size, lanes, left, grad_query, grad_pair, weights, units, *sums):
    tokens, depth = left.shape
    width = grad_pair.shape[2]
    rows = depth // size
    parts = weights.shape[1]
    span = (grad_query.shape[1] + PARTS * width) // parts
    lane_width = sums[0].shape[2] * PARTS // lanes
    any_space = pl.BlockSpec(memory_space=pl.ANY)
    vmem = pl.BlockSpec(memory_space=pltpu.VMEM)
    return pl.pallas_call(
        functools.partial(sum_key_kernel, size, lanes),
        out_shape=(
            jax.ShapeDtypeStruct((PARTS, rows, width), jnp.bfloat16),
            jax.ShapeDtypeStruct((tokens, depth), jnp.float32),
            jax.ShapeDtypeStruct((size, *units.shape[:2], rows), jnp.bfloat16),
            *[jax.ShapeDtypeStruct((rows, lane_width), jnp.float32)] * 2,
        ),
        in_specs=[any_space, vmem, any_space, any_space, any_space, vmem, vmem],
        out_specs=(vmem, vmem, any_space, vmem, vmem),
        scratch_shapes=[
            pltpu.VMEM((tokens, depth), jnp.bfloat16),
            pltpu.VMEM((PARTS, tokens, width), jnp.bfloat16),
            pltpu.SemaphoreType.DMA((PARTS + 1,)),
            pltpu.VMEM((2, parts, rows, span), jnp.bfloat16),
            pltpu.SemaphoreType.DMA((2,)),
            pltpu.VMEM((PARTS, rows, width), jnp.float32),
            *units_scratch(size, units.shape[0]),
            *lanes_scratch(lanes, (rows, lane_width)),
            *lanes_scratch(lanes, (rows, lane_width)),
            *scatter_scratch(size, rows, width),
        ],
        compiler_params=pltpu.CompilerParams(
            collective_id=7, has_side_effects=True, vmem_limit_bytes=VMEM
        ),
        cost_estimate=pl.CostEstimate(
            flops=8 * tokens * depth * width, bytes_accessed=100 * 1024 * 1024, transcendentals=0
        ),
        name="sum_key",
    )(left, grad_query, grad_pair, weights, units, *sums)


def sum_small_kernel(size, lanes, sizes, x_ref, *refs):
    outs, (came, send, recv) = (refs[: len(sizes)], refs[len(sizes) :])
    me, z = (lax.axis_index("fsdp"), lax.axis_index("tp"))
    peers = []
    for name, index, count in (("fsdp", me, size), ("tp", z, lanes)):
        bit = 1
        while bit < count:
            peers.append({name: flip(index, bit)})
            bit *= 2
    barrier = pltpu.get_barrier_semaphore()
    for peer in peers:
        pl.semaphore_signal(barrier, inc=1, device_id=peer, device_id_type=MESH)
    pl.semaphore_wait(barrier, len(peers))
    sent = came.shape[0] // 2
    came[sent] = x_ref[...]
    for step, peer in enumerate(peers):
        copy = pltpu.make_async_remote_copy(
            src_ref=came.at[sent + step],
            dst_ref=came.at[step],
            send_sem=send.at[step],
            recv_sem=recv.at[step],
            device_id=peer,
            device_id_type=MESH,
        )
        copy.start()
        copy.wait()
        came[sent + step + 1] = came[sent + step] + came[step]
    start = 0
    for out, rows in zip(outs, sizes):
        out[...] = came[sent + len(peers), start : start + rows]
        start += rows


def sum_small(size, lanes, values, sizes):
    steps = (size * lanes).bit_length() - 1
    vmem = pl.BlockSpec(memory_space=pltpu.VMEM)
    return pl.pallas_call(
        functools.partial(sum_small_kernel, size, lanes, sizes),
        out_shape=tuple(jax.ShapeDtypeStruct((rows, values.shape[1]), values.dtype) for rows in sizes),
        in_specs=[vmem],
        out_specs=(vmem,) * len(sizes),
        scratch_shapes=[
            pltpu.VMEM((2 * (steps + 1), *values.shape), values.dtype),
            pltpu.SemaphoreType.DMA((steps,)),
            pltpu.SemaphoreType.DMA((steps,)),
        ],
        compiler_params=pltpu.CompilerParams(collective_id=8, has_side_effects=True),
        name="sum_small",
    )(values)


def project_kernel(
    wq, wk, before_ref, x_ref, gain_ref, w_ref, n_ref, q_ref, k_ref, v_ref, normed
):
    back, own, _ = before_ref.shape
    lead = back * own
    tile = min(512, own)
    z = lax.axis_index("tp")

    @pl.when(pl.program_id(0) == 0)
    def _():
        for hop in range(back + 1):

            @pl.loop(0, own // tile)
            def _(index):
                span = pl.ds(pl.multiple_of(index * tile, tile), tile)
                values = x_ref[span, :] if hop == 0 else before_ref[hop - 1, span, :]
                values = normalize_rows(values.astype(jnp.float32))[0] * gain_ref[...]
                values = values.astype(jnp.bfloat16)
                if hop:
                    values = jnp.where(z >= hop, values, jnp.zeros_like(values))
                else:
                    n_ref[span, :] = values
                at = lead - hop * own + index * tile
                normed[pl.ds(pl.multiple_of(at, tile), tile), :] = values

    weights = lambda start, size: w_ref[:, 0, :, start : start + size].reshape(D, size)

    @pl.loop(0, (lead + own) // tile)
    def _(index):
        span = pl.ds(pl.multiple_of(index * tile, tile), tile)
        pair = dot(normed[span, :], weights(wq, 2 * wk))
        k_ref[span, :] = pair[:, :wk]
        v_ref[span, :] = pair[:, wk:].astype(jnp.bfloat16)

    @pl.loop(0, own // tile)
    def _(index):
        span = pl.ds(pl.multiple_of(index * tile, tile), tile)
        from_lead = pl.ds(pl.multiple_of(lead + index * tile, tile), tile)
        q_ref[span, :] = dot(normed[from_lead, :], weights(0, wq))


def project(before, values, gain, weights, wq, wk):
    size, parts, rows_in, columns = weights.shape
    back, own, _ = before.shape
    rows = (back + 1) * own
    whole = lambda *_: (0, 0)
    return pl.pallas_call(
        functools.partial(project_kernel, wq, wk),
        grid=(parts,),
        out_shape=(
            jax.ShapeDtypeStruct((own, D), jnp.bfloat16),
            jax.ShapeDtypeStruct((own, parts * wq), jnp.float32),
            jax.ShapeDtypeStruct((rows, parts * wk), jnp.float32),
            jax.ShapeDtypeStruct((rows, parts * wk), jnp.bfloat16),
        ),
        in_specs=[
            pl.BlockSpec((back, own, D), lambda z: (0, 0, 0)),
            pl.BlockSpec((own, D), whole),
            pl.BlockSpec((1, D), whole),
            pl.BlockSpec((size, 1, rows_in, wq + 2 * wk), lambda z: (0, z, 0, 0)),
        ],
        out_specs=(
            pl.BlockSpec((own, D), whole),
            pl.BlockSpec((own, wq), lambda z: (0, z)),
            pl.BlockSpec((rows, wk), lambda z: (0, z)),
            pl.BlockSpec((rows, wk), lambda z: (0, z)),
        ),
        scratch_shapes=[pltpu.VMEM((rows, D), jnp.bfloat16)],
        compiler_params=pltpu.CompilerParams(vmem_limit_bytes=VMEM),
        cost_estimate=pl.CostEstimate(
            flops=2 * D * parts * (own * wq + rows * 2 * wk),
            bytes_accessed=2 * D * parts * (wq + 2 * wk) + 2 * rows * D,
            transcendentals=0,
        ),
        name="project_in",
    )(before, values, gain.reshape(1, D), weights)


def out_kernel(a_ref, w_ref, x_ref, o_ref):
    parts, _, width = w_ref.shape[1:]
    total = x_ref[...].astype(jnp.float32)
    for z in range(parts):
        total += contract_last(a_ref[:, z * width : (z + 1) * width], w_ref[0, z])
    o_ref[...] = total


def project_out(attended, weights, states, wo):
    size, parts, rows, columns = weights.shape
    own = states.shape[0]
    last = columns // wo - 1
    return pl.pallas_call(
        out_kernel,
        grid=(size,),
        out_shape=jax.ShapeDtypeStruct(states.shape, jnp.float32),
        in_specs=[
            pl.BlockSpec(attended.shape, lambda f: (0, 0)),
            pl.BlockSpec((1, parts, rows, wo), lambda f: (f, 0, 0, last)),
            pl.BlockSpec((own, rows), lambda f: (0, f)),
        ],
        out_specs=pl.BlockSpec((own, rows), lambda f: (0, f)),
        compiler_params=pltpu.CompilerParams(vmem_limit_bytes=VMEM),
        cost_estimate=pl.CostEstimate(
            flops=2 * own * D * parts * wo, bytes_accessed=24 * 1024 * 1024, transcendentals=0
        ),
        name="project_out",
    )(attended, weights, states)


def back_out_kernel(g_ref, w_ref, o_ref):
    size, _, rows, width = w_ref.shape
    o_ref[...] = dot(g_ref[...], w_ref[:, 0].reshape(size * rows, width)).astype(jnp.bfloat16)


def back_out(grad, weights, wo):
    size, parts, rows, columns = weights.shape
    own = grad.shape[0]
    last = columns // wo - 1
    return pl.pallas_call(
        back_out_kernel,
        grid=(parts,),
        out_shape=jax.ShapeDtypeStruct((own, parts * wo), jnp.bfloat16),
        in_specs=[
            pl.BlockSpec(grad.shape, lambda z: (0, 0)),
            pl.BlockSpec((size, 1, rows, wo), lambda z: (0, z, 0, last)),
        ],
        out_specs=pl.BlockSpec((own, wo), lambda z: (0, z)),
        compiler_params=pltpu.CompilerParams(vmem_limit_bytes=VMEM),
        cost_estimate=pl.CostEstimate(
            flops=2 * own * D * parts * wo, bytes_accessed=16 * 1024 * 1024, transcendentals=0
        ),
        name="back_out",
    )(grad, weights)


def turn(values, cosine, sine):
    return values * cosine + pltpu.roll(values, HD // 2, 1) * sine


def turn_back(grad, cosine, sine):
    return grad * cosine - pltpu.roll(grad, HD // 2, 1) * sine


def split_heads(block, group):
    return jnp.concatenate([block[:, i * HD : (i + 1) * HD] for i in range(group)], axis=0)


def join_heads(stacked, group):
    rows = stacked.shape[0] // group
    return jnp.concatenate([stacked[i * rows : (i + 1) * rows] for i in range(group)], axis=1)


def head_probs(query, keys, bias, group, scale):
    scores = contract_last(query, keys) * (scale * LOG2E)
    rows, span = scores.shape
    scores = (scores.reshape(group, rows // group, span) + bias[None]).reshape(rows, span)
    weights = jnp.exp2(scores)
    return weights * (1.0 / jnp.sum(weights, axis=-1, keepdims=True))


def attend_kernel(
    group, step, lead, q_ref, k_ref, v_ref, bias_ref, cos_ref, sin_ref, nq_ref, nk_ref, o_ref, keys
):
    tile, span = bias_ref.shape
    scale = HD ** (-0.5)
    index = pl.program_id(1)

    @pl.when(index == 0)
    def _():
        normed = normalize_rows(k_ref[...])[0] * nk_ref[...]
        keys[...] = turn(normed, cos_ref[...], sin_ref[...]).astype(jnp.bfloat16)

    here = pl.ds(pl.multiple_of(lead + index * tile, tile), tile)
    cosine, sine = (cos_ref[here, :], sin_ref[here, :])
    normed = normalize_rows(split_heads(q_ref[...], group))[0] * nq_ref[...]
    cosine, sine = (jnp.concatenate([cosine] * group, 0), jnp.concatenate([sine] * group, 0))
    query = turn(normed, cosine, sine).astype(jnp.bfloat16)
    window = pl.ds(pl.multiple_of(index * step, tile), span)
    probs = head_probs(query, keys[window, :], bias_ref[...], group, scale)
    mixed = dot(probs.astype(jnp.bfloat16), v_ref[window, :])
    o_ref[...] = join_heads(mixed.astype(jnp.bfloat16), group)


def attend_back_kernel(
    group,
    step,
    lead,
    size,
    lanes,
    q_ref,
    k_ref,
    v_ref,
    bias_ref,
    cos_ref,
    sin_ref,
    nq_ref,
    nk_ref,
    do_ref,
    left_ref,
    right_ref,
    dq_ref,
    pair_ref,
    gq_ref,
    gk_ref,
    out_ref,
    keys,
    dk,
    dv,
    mixed,
    got,
    own_sum,
    left,
    right,
    loads,
    hop_send,
    hop_recv,
    *refs,
):
    made, held, sent, came, *sems = refs
    tile, span = bias_ref.shape
    scale = HD ** (-0.5)
    head, index = (pl.program_id(0), pl.program_id(1))
    heads, tiles = (mixed.shape[0], (k_ref.shape[0] - lead) // tile)
    back, own = (mixed.shape[1], mixed.shape[3])
    me, z = (lax.axis_index("fsdp"), lax.axis_index("tp"))
    width = out_ref.shape[-1]
    rows = left.shape[1] // size

    def hop_copy(at, number):
        return pltpu.make_async_remote_copy(
            src_ref=mixed.at[at, number],
            dst_ref=got.at[at, number],
            send_sem=hop_send.at[at, number],
            recv_sem=hop_recv.at[at, number],
            device_id={"tp": lax.rem(z + lanes - 1, lanes)},
            device_id_type=MESH,
        )

    def relay(at, number):
        @pl.when(z + 1 < lanes)
        def _():
            hop_copy(at, number - 1).wait_recv()
            total = mixed[at, number].astype(jnp.float32)
            total = total + got[at, number - 1].astype(jnp.float32)
            mixed[at, number] = total.astype(jnp.bfloat16)

        @pl.when(z > 0)
        def _():
            hop_copy(at, number).start()

    loads_of = lambda: [pltpu.make_async_copy(left_ref, left, loads.at[PARTS])] + [
        pltpu.make_async_copy(
            right_ref.at[:, pl.ds(part * width, width)], right.at[part], loads.at[part]
        )
        for part in range(PARTS)
    ]

    @pl.when((head == 0) & (index == 0))
    def _():
        for copy in loads_of():
            copy.start()
        barrier = pltpu.get_barrier_semaphore()
        peers = [{"fsdp": flip(me, bit)} for bit in [1] + chip_bits(size)]
        peers += [{"tp": lax.rem(z + 1, lanes)}, {"tp": lax.rem(z + lanes - 1, lanes)}]
        for peer in peers:
            pl.semaphore_signal(barrier, inc=1, device_id=peer, device_id_type=MESH)
        pl.semaphore_wait(barrier, len(peers))
        for copy in loads_of():
            copy.wait()
        gq_ref[...] = jnp.zeros_like(gq_ref)
        gk_ref[...] = jnp.zeros_like(gk_ref)

    def partial(part, slot, columns):
        block = left[:, pl.ds(pl.multiple_of(slot * rows, rows), rows)]
        return contract_first(block, right[part, :, columns])

    calls, finish = scatter_steps(size, me, made, held, sent, came, sems, partial, out_ref)
    at_step = {}
    for number, call in enumerate(calls):
        at_step.setdefault(number * heads * tiles // len(calls), []).append(call)
    for number, some in at_step.items():

        @pl.when(head * tiles + index == number)
        def _():
            for call in some:
                call()

    @pl.when(index == 0)
    def _():
        normed = normalize_rows(k_ref[...])[0] * nk_ref[...]
        keys[...] = turn(normed, cos_ref[...], sin_ref[...]).astype(jnp.bfloat16)
        dk[...] = jnp.zeros_like(dk)
        dv[...] = jnp.zeros_like(dv)

    here = pl.ds(pl.multiple_of(lead + index * tile, tile), tile)
    cosine, sine = (cos_ref[here, :], sin_ref[here, :])
    cosine, sine = (jnp.concatenate([cosine] * group, 0), jnp.concatenate([sine] * group, 0))
    normed, factor = normalize_rows(split_heads(q_ref[...], group))
    query = turn(normed * nq_ref[...], cosine, sine).astype(jnp.bfloat16)
    window = pl.ds(pl.multiple_of(index * step, tile), span)
    probs = head_probs(query, keys[window, :], bias_ref[...], group, scale)
    grad_out = split_heads(do_ref[...], group)
    dv[window, :] += contract_first(probs.astype(jnp.bfloat16), grad_out)
    grad_probs = contract_last(grad_out, v_ref[window, :])
    centre = jnp.sum(probs * grad_probs, axis=-1, keepdims=True)
    grad_scores = (probs * (grad_probs - centre)).astype(jnp.bfloat16)
    dk[window, :] += contract_first(grad_scores, query) * scale
    grad_query = turn_back(dot(grad_scores, keys[window, :]) * scale, cosine, sine)
    gq_ref[...] += jnp.sum(grad_query * normed, axis=0, keepdims=True)
    grad_raw = norm_back(grad_query, normed, factor, nq_ref[...])
    dq_ref[...] = join_heads(grad_raw.astype(jnp.bfloat16), group)

    @pl.when(index == tiles - 1)
    def _():
        normed_key, key_factor = normalize_rows(k_ref[...])
        grad_key = turn_back(dk[...], cos_ref[...], sin_ref[...])
        gk_ref[...] += jnp.sum(grad_key * normed_key, axis=0, keepdims=True)
        grad_key = norm_back(grad_key, normed_key, key_factor, nk_ref[...])
        for number in range(back):
            block = slice(number * own, (number + 1) * own)
            mixed[head, number, 0] = grad_key[block].astype(jnp.bfloat16)
            mixed[head, number, 1] = dv[block, :].astype(jnp.bfloat16)
        own_sum[head, 0] = grad_key[lead:]
        own_sum[head, 1] = dv[lead:, :]

        @pl.when(z > 0)
        def _():
            hop_copy(head, 0).start()

        for number in range(1, back):

            @pl.when(head >= number)
            def _():
                relay(head - number, number)

    @pl.when((head == heads - 1) & (index == tiles - 1))
    def _():
        for number in range(1, back):
            for at in range(heads - number, heads):
                relay(at, number)
        for at in range(heads):
            columns = slice(at * HD, (at + 1) * HD)

            @pl.when(z + 1 < lanes)
            def _():
                hop_copy(at, back - 1).wait_recv()
                total = own_sum[at] + got[at, back - 1].astype(jnp.float32)
                pair_ref[:, :, columns] = total.astype(jnp.bfloat16)

            @pl.when(z + 1 == lanes)
            def _():
                pair_ref[:, :, columns] = own_sum[at].astype(jnp.bfloat16)

            @pl.when(z > 0)
            def _():
                for number in range(back):
                    hop_copy(at, number).wait_send()

        finish()


def attention_specs(own, rows, group, tile, span):
    whole = lambda g, t: (0, 0)
    return [
        pl.BlockSpec((tile, group * HD), lambda g, t: (t, g)),
        pl.BlockSpec((rows, HD), lambda g, t: (0, g)),
        pl.BlockSpec((rows, HD), lambda g, t: (0, g)),
        pl.BlockSpec((tile, span), lambda g, t: (t, 0)),
        pl.BlockSpec((rows, HD), whole),
        pl.BlockSpec((rows, HD), whole),
        pl.BlockSpec((1, HD), whole),
        pl.BlockSpec((1, HD), whole),
    ]


def attend(queries, keys, values, bias, cosine, sine, norm_query, norm_key, tile, step):
    own, rows = (queries.shape[0], keys.shape[0])
    heads = keys.shape[1] // HD
    group = queries.shape[1] // keys.shape[1]
    span = bias.shape[1]
    return pl.pallas_call(
        functools.partial(attend_kernel, group, step, rows - own),
        grid=(heads, own // tile),
        out_shape=jax.ShapeDtypeStruct(queries.shape, jnp.bfloat16),
        in_specs=attention_specs(own, rows, group, tile, span),
        out_specs=pl.BlockSpec((tile, group * HD), lambda g, t: (t, g)),
        scratch_shapes=[pltpu.VMEM((rows, HD), jnp.bfloat16)],
        compiler_params=pltpu.CompilerParams(vmem_limit_bytes=VMEM),
        cost_estimate=pl.CostEstimate(
            flops=16 * own * span * queries.shape[1],
            bytes_accessed=4 * queries.size + 6 * keys.size,
            transcendentals=own * span * heads * group,
        ),
        name="attend",
    )(queries, keys, values, bias, cosine, sine, norm_query, norm_key)


def attend_back(
    queries,
    keys,
    values,
    bias,
    cosine,
    sine,
    norm_query,
    norm_key,
    grad,
    tile,
    step,
    left,
    right,
    size,
    lanes,
):
    own, rows = (queries.shape[0], keys.shape[0])
    heads = keys.shape[1] // HD
    group = queries.shape[1] // keys.shape[1]
    span = bias.shape[1]
    lead = rows - own
    back = lead // own
    tokens, depth = left.shape
    width = right.shape[1] // PARTS
    whole = lambda g, t: (0, 0)
    any_space = pl.BlockSpec(memory_space=pl.ANY)
    return pl.pallas_call(
        functools.partial(attend_back_kernel, group, step, lead, size, lanes),
        grid=(heads, own // tile),
        out_shape=(
            jax.ShapeDtypeStruct(queries.shape, jnp.bfloat16),
            jax.ShapeDtypeStruct((2, own, heads * HD), jnp.bfloat16),
            jax.ShapeDtypeStruct((1, HD), jnp.float32),
            jax.ShapeDtypeStruct((1, HD), jnp.float32),
            jax.ShapeDtypeStruct((PARTS, depth // size, width), jnp.float32),
        ),
        in_specs=attention_specs(own, rows, group, tile, span)
        + [pl.BlockSpec((tile, group * HD), lambda g, t: (t, g)), any_space, any_space],
        out_specs=(
            pl.BlockSpec((tile, group * HD), lambda g, t: (t, g)),
            pl.BlockSpec((2, own, heads * HD), lambda g, t: (0, 0, 0)),
            pl.BlockSpec((1, HD), whole),
            pl.BlockSpec((1, HD), whole),
            pl.BlockSpec((PARTS, depth // size, width), lambda g, t: (0, 0, 0)),
        ),
        scratch_shapes=[
            pltpu.VMEM((rows, HD), jnp.bfloat16),
            pltpu.VMEM((rows, HD), jnp.float32),
            pltpu.VMEM((rows, HD), jnp.float32),
            pltpu.VMEM((heads, back, 2, own, HD), jnp.bfloat16),
            pltpu.VMEM((heads, back, 2, own, HD), jnp.bfloat16),
            pltpu.VMEM((heads, 2, own, HD), jnp.float32),
            pltpu.VMEM((tokens, depth), jnp.bfloat16),
            pltpu.VMEM((PARTS, tokens, width), jnp.bfloat16),
            pltpu.SemaphoreType.DMA((PARTS + 1,)),
            pltpu.SemaphoreType.DMA((heads, back)),
            pltpu.SemaphoreType.DMA((heads, back)),
            *scatter_scratch(size, depth // size, width),
        ],
        compiler_params=pltpu.CompilerParams(
            collective_id=9, has_side_effects=True, vmem_limit_bytes=60 * 1024 * 1024
        ),
        cost_estimate=pl.CostEstimate(
            flops=40 * own * span * queries.shape[1],
            bytes_accessed=8 * queries.size + 16 * keys.size,
            transcendentals=own * span * heads * group,
        ),
        name="attend_back",
    )(queries, keys, values, bias, cosine, sine, norm_query, norm_key, grad, left, right)


def window_tables(length_row, pad_row, first, own, lead, tile, span):
    places = first - lead + jnp.arange(lead + own, dtype=jnp.int32)
    ends = jnp.cumsum(length_row)
    passed = places[:, None] >= ends[None, :]
    docs = jnp.sum(passed.astype(jnp.int32), axis=1)
    starts = jnp.sum(jnp.where(passed, length_row[None, :], 0), axis=1)
    freqs = THETA ** (-(jnp.arange(HD // 2).astype(jnp.float32) * 2.0 / HD))
    angles = (places - starts).astype(jnp.float32)[:, None] * freqs[None, :]
    cosine, sine = (jnp.cos(angles), jnp.sin(angles))
    padded = jnp.concatenate((jnp.zeros((lead,), pad_row.dtype), pad_row))
    live = lax.dynamic_slice_in_dim(padded, first, lead + own, 0)
    step = tile if lead + own > span else 0
    masks = []
    for index in range(own // tile):
        at = lead + index * tile
        query, key = (places[at : at + tile, None], places[None, index * step : index * step + span])
        same = docs[at : at + tile, None] == docs[None, index * step : index * step + span]
        seen = (live[None, index * step : index * step + span] == 1) | (key == query)
        masks.append((key >= 0) & (key <= query) & (query - key < WINDOW) & same & seen)
    bias = jnp.where(jnp.concatenate(masks, axis=0), 0.0, NEG).astype(jnp.float32)
    cosine = jnp.concatenate((cosine, cosine), axis=1)
    sine = jnp.concatenate((-sine, sine), axis=1)
    return (bias, cosine, sine, step, live[lead:].astype(jnp.float32))


def shards(
    states,
    lengths,
    padding,
    teacher,
    norm_attn,
    w_query,
    w_key,
    w_value,
    norm_query,
    norm_key,
    w_out,
    norm_mlp,
    w_gate,
    w_up,
    w_down,
):
    own = states.shape[0]
    n_tp, n_fsdp = (lax.axis_size("tp"), lax.axis_size("fsdp"))
    first = lax.axis_index("tp") * own
    back = min(n_tp - 1, -(-WINDOW // own))
    lead = back * own
    tile = min(256, own)
    span = WINDOW + tile if lead >= WINDOW else lead + own
    wq, wk = (w_query.shape[1], w_key.shape[1])
    bias, cosine, sine, step, live = window_tables(
        lengths[0], padding[0], first, own, lead, tile, span
    )
    joined = jnp.concatenate((w_query, w_key, w_value, w_out.T), axis=1)
    wo = w_out.shape[0]
    units = [
        part.reshape(n_fsdp, -1, part.shape[1]) for part in (w_gate.T, w_up.T, w_down)
    ]
    live_here = jnp.full((8, 128), jnp.sum(padding).astype(jnp.float32))
    before, weights_attn, mine_pair, mine_down, counts = enter(
        n_fsdp, n_tp, back, states, joined, jnp.stack(units, axis=1), live_here
    )
    count = counts[0, 0]
    units_pair = lax.all_gather(mine_pair, "tp", axis=0)
    units_down = lax.all_gather(mine_down, "tp", axis=0)
    normed_in, query_raw, key_raw, value = project(
        before, states, norm_attn, weights_attn, wq, wk
    )
    gains = (norm_query.reshape(1, HD), norm_key.reshape(1, HD))
    attended = attend(query_raw, key_raw, value, bias, cosine, sine, *gains, tile, step)
    inputs = states.astype(jnp.float32)
    hidden_one = project_out(attended, weights_attn, states, wo)
    normed_two, factor_two = normalize_rows(hidden_one)
    whole_two, gate, up, product = gate_up(
        n_fsdp, (normed_two * norm_mlp).astype(jnp.bfloat16), units_pair
    )
    outputs = hidden_one + sum_products(n_fsdp, 2, (product,), ((units_down, 0),))
    errors = (outputs - teacher.astype(jnp.float32)) * live[:, None]
    squares = jnp.sum(errors * errors)
    grad_out = errors * (2.0 / (count * D))

    grad_gate, grad_up, units_early, units_late = grad_hidden_units(
        n_fsdp, grad_out.astype(jnp.bfloat16), units_down, gate, up, product, whole_two
    )
    units_early = lax.psum_scatter(units_early, "tp", scatter_dimension=0)
    grad_mid = sum_products(n_fsdp, 4, (grad_gate, grad_up), ((units_pair, 0), (units_pair, 1)))
    grad_norm_mlp = jnp.sum(grad_mid * normed_two, axis=0)
    grad_hidden = grad_out + norm_back(grad_mid, normed_two, factor_two, norm_mlp)

    grad_low_out = grad_hidden.astype(jnp.bfloat16)
    grad_attended = back_out(grad_low_out, weights_attn, wo)
    grad_query, grad_pair, grad_norm_query, grad_norm_key, sums_out = attend_back(
        query_raw,
        key_raw,
        value,
        bias,
        cosine,
        sine,
        *gains,
        grad_attended,
        tile,
        step,
        grad_low_out,
        attended,
        n_fsdp,
        n_tp,
    )
    units_late, grad_query = lax.optimization_barrier((units_late, grad_query))
    units_late = lax.psum_scatter(units_late, "tp", scatter_dimension=0)
    sums_query, back_early = sum_query(n_fsdp, normed_in, grad_query, units_early)
    sums_pair, grad_low, back_late, grad_w_out, grad_w_query = sum_key(
        n_fsdp,
        n_tp,
        normed_in,
        grad_query,
        grad_pair,
        weights_attn,
        units_late,
        sums_out,
        sums_query,
    )
    grad_w_down, grad_w_gate, grad_w_up = [
        part.reshape(-1, part.shape[2]).astype(jnp.float32)
        for part in (back_early[:, 0], back_early[:, 1], back_late[:, 0])
    ]
    normed_one, factor_one = normalize_rows(inputs)
    grad_norm_attn = jnp.sum(grad_low * normed_one, axis=0)
    grad_input = grad_hidden + norm_back(grad_low, normed_one, factor_one, norm_attn)
    lines = D // HD
    small = [
        grad_norm_attn.reshape(lines, HD),
        grad_norm_mlp.reshape(lines, HD),
        grad_norm_query,
        grad_norm_key,
        jnp.full((6, HD), squares),
    ]
    small, grad_input, grad_w_down, grad_w_gate, grad_w_up = lax.optimization_barrier(
        (jnp.concatenate(small, axis=0), grad_input, grad_w_down, grad_w_gate.T, grad_w_up.T)
    )
    grad_norm_attn, grad_norm_mlp, rest = sum_small(n_fsdp, n_tp, small, (lines, lines, 8))
    grad_norm_attn, grad_norm_mlp = (grad_norm_attn.reshape(D), grad_norm_mlp.reshape(D))
    grad_norm_query, grad_norm_key, squares = (rest[0], rest[1], rest[2, 0])
    grad_w_pair = lax.psum_scatter(sums_pair, "tp", scatter_dimension=2, tiled=True)
    grad_w_pair = grad_w_pair.astype(jnp.float32)
    return (
        outputs,
        squares / (count * D),
        grad_input,
        grad_norm_attn,
        grad_w_query,
        grad_w_pair[0],
        grad_w_pair[1],
        grad_norm_query,
        grad_norm_key,
        grad_w_out.T,
        grad_norm_mlp,
        grad_w_gate,
        grad_w_up,
        grad_w_down,
    )


def solution(mesh):
    tokens = P(("fsdp", "tp"), None)
    rows, columns, sequences = (P("fsdp", "tp"), P("tp", "fsdp"), P("fsdp", None))
    in_specs = (
        tokens,
        sequences,
        sequences,
        tokens,
        P(),
        rows,
        rows,
        rows,
        P(),
        P(),
        columns,
        P(),
        rows,
        rows,
        columns,
    )
    out_specs = (
        tokens,
        P(),
        tokens,
        P(),
        rows,
        rows,
        rows,
        P(),
        P(),
        columns,
        P(),
        rows,
        rows,
        columns,
    )
    return jax.shard_map(shards, mesh=mesh, in_specs=in_specs, out_specs=out_specs, check_vma=False)
```

```python
import functools

import jax
import jax.numpy as jnp
from jax import lax
from jax.experimental import pallas as pl
from jax.experimental.pallas import tpu as pltpu
from jax.sharding import PartitionSpec as P

D = 2048
HD = 128
WINDOW = 1024

EPS = 1e-06
THETA = 1000000.0
NEG = -1e30
LOG2E = 1.4426950408889634
VMEM = 56 * 1024 * 1024


def normalize_rows(values):
    factor = lax.rsqrt(jnp.mean(values * values, axis=-1, keepdims=True) + EPS)
    return (values * factor, factor)


def norm_back(grad, normed, factor, gain):
    scaled = grad * gain
    return factor * (scaled - normed * jnp.mean(scaled * normed, axis=-1, keepdims=True))


def contract_last(left, right):
    return lax.dot_general(
        left, right, (((1,), (1,)), ((), ())), preferred_element_type=jnp.float32
    )


def contract_first(left, right):
    return lax.dot_general(
        left, right, (((0,), (0,)), ((), ())), preferred_element_type=jnp.float32
    )


def dot(left, right):
    return jnp.dot(left, right, preferred_element_type=jnp.float32)


MESH = pl.DeviceIdType.MESH
PARTS = 2


def flip(index, mask):
    bit = 1
    while bit <= mask:
        if mask & bit:
            index = index + bit - 2 * bit * lax.rem(lax.div(index, bit), 2)
        bit *= 2
    return index


def chip_bits(size):
    bits = []
    bit = 2
    while bit < size:
        bits.append(bit)
        bit *= 2
    return bits


def orders(size):
    bits = chip_bits(size)
    return (bits, bits[::-1])


def mask_of(pattern, order):
    return sum(bit for i, bit in enumerate(order) if pattern >> i & 1)


def top(pattern):
    return pattern.bit_length() - 1


def greet(me, size):
    barrier = pltpu.get_barrier_semaphore()
    bits = [1] + chip_bits(size)
    for bit in bits:
        pl.semaphore_signal(
            barrier, inc=1, device_id={"fsdp": flip(me, bit)}, device_id_type=MESH
        )
    pl.semaphore_wait(barrier, len(bits))


def pick(part, pair):
    return pair[0] + part * (pair[1] - pair[0])


def unit_loads(source, kind, target, sems):
    lanes, _, rows, _ = source.shape
    return [
        pltpu.make_async_copy(
            source.at[lane, kind], target.at[pl.ds(lane * rows, rows)], sems.at[lane]
        )
        for lane in range(lanes)
    ]


class Gather:
    def __init__(self, size, me, whole, sems, parts=PARTS, lane=lambda part: part, parity=lambda part: part, own=None):
        self.size, self.me, self.whole, self.parts = (size, me, whole, parts)
        self.lane, self.parity, self.own = (lane, parity, own)
        self.chip_send, self.chip_recv, self.core_send, self.core_recv = sems
        self.steps = len(chip_bits(size))
        self.patterns = sorted(range(1 << self.steps), key=lambda m: (top(m), m))

    def order(self, part):
        return orders(self.size)[self.parity(part) % 2]

    def slot(self, part, pattern, sibling):
        return flip(self.me, mask_of(pattern, self.order(part)) + sibling)

    def source(self, part, pattern, block):
        return self.own if self.own is not None and part == 0 and pattern == 0 else block

    def chip_copy(self, part, step, pattern):
        block = self.whole.at[self.slot(part, pattern, 0), self.lane(part)]
        number = (1 << step) - 1 + pattern
        return pltpu.make_async_remote_copy(
            src_ref=self.source(part, pattern, block),
            dst_ref=block,
            send_sem=self.chip_send.at[part, number],
            recv_sem=self.chip_recv.at[part, number],
            device_id={"fsdp": flip(self.me, self.order(part)[step])},
            device_id_type=MESH,
        )

    def core_copy(self, part, pattern):
        block = self.whole.at[self.slot(part, pattern, 0), self.lane(part)]
        return pltpu.make_async_remote_copy(
            src_ref=self.source(part, pattern, block),
            dst_ref=block,
            send_sem=self.core_send.at[part, pattern],
            recv_sem=self.core_recv.at[part, pattern],
            device_id={"fsdp": flip(self.me, 1)},
            device_id_type=MESH,
        )

    def arrive(self, part, pattern):
        if pattern:
            step = top(pattern)
            self.chip_copy(part, step, pattern - (1 << step)).wait_recv()

    def forward(self, part, pattern):
        for step in range(top(pattern) + 1, self.steps):
            self.chip_copy(part, step, pattern).start()
        self.core_copy(part, pattern).start()

    def pairs(self, work):
        for pattern in self.patterns:
            for part in range(self.parts):
                self.arrive(part, pattern)
            for part in range(self.parts):
                self.forward(part, pattern)
            work([self.slot(part, pattern, 0) for part in range(self.parts)])
            for part in range(self.parts):
                self.core_copy(part, pattern).wait_recv()
            work([self.slot(part, pattern, 1) for part in range(self.parts)])

    def finish(self):
        for pattern in self.patterns:
            for part in range(self.parts):
                for step in range(top(pattern) + 1, self.steps):
                    self.chip_copy(part, step, pattern).wait_send()
                self.core_copy(part, pattern).wait_send()


def gather_semaphores(size, parts=PARTS):
    moves = max(1, size // 2 - 1)
    return [
        pltpu.SemaphoreType.DMA((parts, moves)),
        pltpu.SemaphoreType.DMA((parts, moves)),
        pltpu.SemaphoreType.DMA((parts, size // 2)),
        pltpu.SemaphoreType.DMA((parts, size // 2)),
    ]


def first_step(pattern, steps):
    return (pattern & -pattern).bit_length() - 1 if pattern else steps


def scatter_order(steps):
    return sorted(range(1 << steps), key=lambda m: (first_step(m, steps), -bin(m).count("1"), m))


def scatter_steps(
    size, me, made, held, sent, came, sems, partial, final, ready=lambda part, slot, q, sibling: None
):
    chip_send, chip_recv, core_send, core_recv = sems
    steps = len(chip_bits(size))
    order = [bits[::-1] for bits in orders(size)]
    first = lambda m: first_step(m, steps)
    patterns = scatter_order(steps)
    place = {m: q for q, m in enumerate(patterns)}
    width = final.shape[-1]
    chunk = min(1024, width)

    def slots(pattern, sibling):
        return [flip(me, mask_of(pattern, order[part]) + sibling) for part in range(PARTS)]

    def core_copy(part, q):
        return pltpu.make_async_remote_copy(
            src_ref=made.at[part, q],
            dst_ref=held.at[part, q],
            send_sem=core_send.at[part, q],
            recv_sem=core_recv.at[part, q],
            device_id={"fsdp": flip(me, 1)},
            device_id_type=MESH,
        )

    def chip_copy(part, q):
        return pltpu.make_async_remote_copy(
            src_ref=sent.at[part, q],
            dst_ref=came.at[part, q],
            send_sem=chip_send.at[part, q],
            recv_sem=chip_recv.at[part, q],
            device_id={"fsdp": flip(me, order[part][first(patterns[q])])},
            device_id_type=MESH,
        )

    def for_sibling(q):
        pair = slots(patterns[q], 1)
        for part in range(PARTS):
            ready(part, pair[part], q, 1)

            @pl.loop(0, width // chunk)
            def _(index):
                columns = pl.ds(pl.multiple_of(index * chunk, chunk), chunk)
                made[part, q, :, columns] = partial(part, pair[part], columns).astype(jnp.bfloat16)

            core_copy(part, q).start()

    def for_chips(q):
        pattern = patterns[q]
        pair = slots(pattern, 0)
        arrivals = [place[pattern | 1 << step] for step in range(first(pattern))]
        for part in range(PARTS):
            ready(part, pair[part], q, 0)
            if pattern:
                core_copy(part, q).wait_recv()
                for arrival in arrivals:
                    chip_copy(part, arrival).wait_recv()

            @pl.loop(0, width // chunk)
            def _(index):
                columns = pl.ds(pl.multiple_of(index * chunk, chunk), chunk)
                total = partial(part, pair[part], columns)
                if pattern:
                    total = total + held[part, q, :, columns].astype(jnp.float32)
                    for arrival in arrivals:
                        total = total + came[part, arrival, :, columns].astype(jnp.float32)
                    sent[part, q, :, columns] = total.astype(jnp.bfloat16)
                else:
                    final[part, :, columns] = total

            if pattern:
                chip_copy(part, q).start()
        if not pattern:
            for part in range(PARTS):
                core_copy(part, q).wait_recv()
                for arrival in arrivals:
                    chip_copy(part, arrival).wait_recv()

                @pl.loop(0, width // chunk)
                def _(index):
                    columns = pl.ds(pl.multiple_of(index * chunk, chunk), chunk)
                    total = final[part, :, columns] + held[part, q, :, columns].astype(jnp.float32)
                    for arrival in arrivals:
                        total = total + came[part, arrival, :, columns].astype(jnp.float32)
                    final[part, :, columns] = total

    def finish():
        for q in range(len(patterns)):
            for part in range(PARTS):
                core_copy(part, q).wait_send()
                if patterns[q]:
                    chip_copy(part, q).wait_send()

    calls = []
    for q in range(len(patterns)):
        calls += [functools.partial(for_sibling, q), functools.partial(for_chips, q)]
    return (calls, finish)


def scatter_scratch(size, rows, width):
    held = size // 2
    moved = max(1, held - 1)
    return [
        pltpu.VMEM((PARTS, held, rows, width), jnp.bfloat16),
        pltpu.VMEM((PARTS, held, rows, width), jnp.bfloat16),
        pltpu.VMEM((PARTS, moved, rows, width), jnp.bfloat16),
        pltpu.VMEM((PARTS, moved, rows, width), jnp.bfloat16),
        pltpu.SemaphoreType.DMA((PARTS, moved)),
        pltpu.SemaphoreType.DMA((PARTS, moved)),
        pltpu.SemaphoreType.DMA((PARTS, held)),
        pltpu.SemaphoreType.DMA((PARTS, held)),
    ]


def gate_up_kernel(
    size,
    x_ref,
    w_in,
    x_out,
    gate_out,
    up_out,
    prod_out,
    whole,
    wg_ref,
    wu_ref,
    gate,
    up,
    prod,
    load,
    keep,
    store,
    *sems,
):
    me = lax.axis_index("fsdp")
    hidden = wg_ref.shape[0]
    lanes = w_in.shape[0]
    loads = [pltpu.make_async_copy(x_ref, whole.at[me], load.at[0])]
    loads += unit_loads(w_in, 0, wg_ref, load.at[pl.ds(1, lanes)])
    loads += unit_loads(w_in, 1, wu_ref, load.at[pl.ds(1 + lanes, lanes)])
    for copy in loads:
        copy.start()
    greet(me, size)
    loads[0].wait()
    state = {"count": 0, "last": None}

    def stores(part, at):
        return [
            pltpu.make_async_copy(buffer.at[part], out.at[at, part], store.at[part, i])
            for i, (buffer, out) in enumerate(((gate, gate_out), (up, up_out), (prod, prod_out)))
        ]

    def work(pair):
        count, last = (state["count"], state["last"])
        for part in range(PARTS):
            pltpu.make_async_copy(
                whole.at[pair[part], part], x_out.at[pair[part], part], keep.at[part, count]
            ).start()
        if last is None:
            for copy in loads[1:]:
                copy.wait()

        @pl.loop(0, PARTS)
        def _(part):
            at = pick(part, pair)
            if last is not None:
                for copy in stores(part, pick(part, last)):
                    copy.wait()

            rows = whole[at, part]
            gates = contract_last(rows, wg_ref[...])
            ups = contract_last(rows, wu_ref[...])
            gate[part] = gates
            up[part] = ups
            prod[part] = (gates * jax.nn.sigmoid(gates) * ups).astype(jnp.bfloat16)

            for copy in stores(part, at):
                copy.start()

        state["count"], state["last"] = (count + 1, pair)
        state.setdefault("all", []).append(pair)

    gather = Gather(size, me, whole, sems)
    gather.pairs(work)
    gather.finish()
    for part in range(PARTS):
        for copy in stores(part, state["last"][part]):
            copy.wait()
        for count, pair in enumerate(state["all"]):
            pltpu.make_async_copy(
                whole.at[pair[part], part], x_out.at[pair[part], part], keep.at[part, count]
            ).wait()


def gate_up(size, values, units):
    own, width = values.shape
    lanes, _, each, _ = units.shape
    rows, hidden = (own // PARTS, lanes * each)
    any_space = pl.BlockSpec(memory_space=pl.ANY)
    shape = lambda columns, kind: jax.ShapeDtypeStruct((size, PARTS, rows, columns), kind)
    outs = pl.pallas_call(
        functools.partial(gate_up_kernel, size),
        out_shape=(
            shape(width, jnp.bfloat16),
            shape(hidden, jnp.float32),
            shape(hidden, jnp.float32),
            shape(hidden, jnp.bfloat16),
        ),
        in_specs=[any_space] * 2,
        out_specs=(any_space,) * 4,
        scratch_shapes=[
            pltpu.VMEM((size, PARTS, rows, width), jnp.bfloat16),
            pltpu.VMEM((hidden, width), jnp.bfloat16),
            pltpu.VMEM((hidden, width), jnp.bfloat16),
            pltpu.VMEM((PARTS, rows, hidden), jnp.float32),
            pltpu.VMEM((PARTS, rows, hidden), jnp.float32),
            pltpu.VMEM((PARTS, rows, hidden), jnp.bfloat16),
            pltpu.SemaphoreType.DMA((1 + 2 * lanes,)),
            pltpu.SemaphoreType.DMA((PARTS, size)),
            pltpu.SemaphoreType.DMA((PARTS, 3)),
            *gather_semaphores(size),
        ],
        compiler_params=pltpu.CompilerParams(
            collective_id=1, has_side_effects=True, vmem_limit_bytes=VMEM
        ),
        cost_estimate=pl.CostEstimate(
            flops=4 * size * own * width * hidden, bytes_accessed=200 * 1024 * 1024, transcendentals=0
        ),
        name="gate_up",
    )(values.reshape(PARTS, rows, width), units)
    return tuple(out.reshape(size * own, -1) for out in outs)


def grad_hidden_kernel(
    size,
    x_ref,
    wd_in,
    gate_in,
    up_in,
    prod_in,
    two_in,
    dgate_out,
    dup_out,
    early_out,
    whole,
    wd_ref,
    gate,
    up,
    prod,
    two,
    dgate,
    dup,
    sums,
    load,
    fetch,
    store,
    flush,
    *sems,
):
    me = lax.axis_index("fsdp")
    hidden, width = wd_ref.shape
    lanes, _, each, _ = wd_in.shape
    chunk = 256 if hidden % 256 == 0 else 128
    loads = [pltpu.make_async_copy(x_ref, whole.at[me], load.at[0])]
    loads += unit_loads(wd_in, 0, wd_ref, load.at[pl.ds(1, lanes)])
    for copy in loads:
        copy.start()

    def stores(part, at):
        return [
            pltpu.make_async_copy(buffer.at[part], out.at[at, part], store.at[part, i])
            for i, (buffer, out) in enumerate(((dgate, dgate_out), (dup, dup_out)))
        ]

    def fetches(count, kinds):
        copies = []
        for part in range(PARTS):
            at = order[count][part]
            pairs = (
                (gate_in, gate.at[part]),
                (up_in, up.at[part]),
                (prod_in, prod.at[count % 2, part]),
                (two_in, two.at[count % 2, part]),
            )
            copies += [
                pltpu.make_async_copy(pairs[i][0].at[at, part], pairs[i][1], fetch.at[count % 2, part, i])
                for i in kinds
            ]
        return copies

    gather = Gather(size, me, whole, sems)
    order = []
    for pattern in gather.patterns:
        for sibling in (0, 1):
            order.append([gather.slot(part, pattern, sibling) for part in range(PARTS)])
    for copy in fetches(0, (0, 1, 2, 3)):
        copy.start()
    greet(me, size)
    loads[0].wait()
    state = {"count": 0}

    def work(pair):
        count = state["count"]
        state["count"] = count + 1
        more = count + 1 < len(order)
        if count == 0:
            for copy in loads[1:]:
                copy.wait()
        if more:
            for copy in fetches(count + 1, (2, 3)):
                copy.start()
        for copy in fetches(count, (0, 1)):
            copy.wait()
        if count:
            for part in range(PARTS):
                for copy in stores(part, order[count - 1][part]):
                    copy.wait()

        @pl.loop(0, PARTS)
        def _(part):
            at = pick(part, pair)

            grads = contract_last(whole[at, part], wd_ref[...])
            gates = gate[part]
            sigmoid = jax.nn.sigmoid(gates)
            dgate[part] = (
                grads * up[part] * sigmoid * (1.0 + gates * (1.0 - sigmoid))
            ).astype(jnp.bfloat16)
            dup[part] = (grads * (gates * sigmoid)).astype(jnp.bfloat16)

        for part in range(PARTS):
            for copy in stores(part, pair[part]):
                copy.start()
        if more:
            for copy in fetches(count + 1, (0, 1)):
                copy.start()
        for copy in fetches(count, (2, 3)):
            copy.wait()

        @pl.loop(0, hidden // chunk)
        def _(index):
            units = pl.ds(pl.multiple_of(index * chunk, chunk), chunk)
            here = count % 2
            for kind, (lefts, rights) in enumerate(
                (
                    ((prod.at[here, 0], prod.at[here, 1]), (whole.at[pair[0], 0], whole.at[pair[1], 1])),
                    ((dgate.at[0], dgate.at[1]), (two.at[here, 0], two.at[here, 1])),
                )
            ):
                total = contract_first(lefts[0][:, units], rights[0][...])
                total += contract_first(lefts[1][:, units], rights[1][...])
                if count:
                    total += sums[kind, units, :]
                sums[kind, units, :] = total

    gather.pairs(work)
    gather.finish()
    for part in range(PARTS):
        for copy in stores(part, order[-1][part]):
            copy.wait()
    copies = []
    for piece in range(2 * lanes):
        kind, lane = (piece // lanes, piece % lanes)
        block = whole.at[piece // PARTS, piece % PARTS, pl.ds(0, each)]
        block[...] = sums[kind, lane * each : (lane + 1) * each, :].astype(jnp.bfloat16)
        copy = pltpu.make_async_copy(block, early_out.at[lane, kind], flush.at[piece])
        copy.start()
        copies.append(copy)
    for copy in copies:
        copy.wait()


def grad_hidden_units(size, values, units, gate, up, product, whole_two):
    own, width = values.shape
    lanes, _, each, _ = units.shape
    rows, hidden = (own // PARTS, lanes * each)
    any_space = pl.BlockSpec(memory_space=pl.ANY)
    shape = lambda columns, kind: jax.ShapeDtypeStruct((size, PARTS, rows, columns), kind)
    blocks = lambda array: array.reshape(size, PARTS, rows, -1)
    weights = jax.ShapeDtypeStruct((lanes, 2, each, width), jnp.bfloat16)
    dgate, dup, early = pl.pallas_call(
        functools.partial(grad_hidden_kernel, size),
        out_shape=(shape(hidden, jnp.bfloat16), shape(hidden, jnp.bfloat16), weights),
        in_specs=[any_space] * 6,
        out_specs=(any_space,) * 3,
        scratch_shapes=[
            pltpu.VMEM((size, PARTS, rows, width), jnp.bfloat16),
            pltpu.VMEM((hidden, width), jnp.bfloat16),
            pltpu.VMEM((PARTS, rows, hidden), jnp.float32),
            pltpu.VMEM((PARTS, rows, hidden), jnp.float32),
            pltpu.VMEM((2, PARTS, rows, hidden), jnp.bfloat16),
            pltpu.VMEM((2, PARTS, rows, width), jnp.bfloat16),
            pltpu.VMEM((PARTS, rows, hidden), jnp.bfloat16),
            pltpu.VMEM((PARTS, rows, hidden), jnp.bfloat16),
            pltpu.VMEM((2, hidden, width), jnp.float32),
            pltpu.SemaphoreType.DMA((1 + lanes,)),
            pltpu.SemaphoreType.DMA((2, PARTS, 4)),
            pltpu.SemaphoreType.DMA((PARTS, 2)),
            pltpu.SemaphoreType.DMA((2 * lanes,)),
            *gather_semaphores(size),
        ],
        compiler_params=pltpu.CompilerParams(
            collective_id=3, has_side_effects=True, vmem_limit_bytes=60 * 1024 * 1024
        ),
        cost_estimate=pl.CostEstimate(
            flops=6 * size * own * width * hidden, bytes_accessed=200 * 1024 * 1024, transcendentals=0
        ),
        name="grad_hidden_units",
    )(values.reshape(PARTS, rows, width), units, *map(blocks, (gate, up, product, whole_two)))
    return (dgate.reshape(size * own, hidden), dup.reshape(size * own, hidden), early)


def sum_products_kernel(size, kinds, *refs):
    terms = len(kinds)
    left_in, right_in, out = (refs[:terms], refs[terms : 2 * terms], refs[2 * terms])
    at = 2 * terms + 1
    lefts, rights, (w_load, x_load) = (
        refs[at : at + terms],
        refs[at + terms : at + 2 * terms],
        refs[at + 2 * terms : at + 2 * terms + 2],
    )
    made, held, sent, came, *sems = refs[at + 2 * terms + 2 :]
    me = lax.axis_index("fsdp")

    def partial(part, slot, columns):
        return sum(
            dot(left[slot, part], right[:, columns]) for left, right in zip(lefts, rights)
        )

    def tiles(part, slot, q, sibling):
        return [
            pltpu.make_async_copy(
                source.at[slot, part], left.at[slot, part], x_load.at[2 * q + sibling, part, i]
            )
            for i, (source, left) in enumerate(zip(left_in, lefts))
        ]

    seen = []

    def ready(part, slot, q, sibling):
        if not seen:
            for copy in weights:
                copy.wait()
        seen.append(slot)
        for copy in tiles(part, slot, q, sibling):
            copy.wait()

    weights = []
    for i, (source, right) in enumerate(zip(right_in, rights)):
        weights += unit_loads(source, kinds[i], right, w_load.at[i])
    for copy in weights:
        copy.start()
    order = [bits[::-1] for bits in orders(size)]
    for q, pattern in enumerate(scatter_order(len(order[0]))):
        for sibling in (1, 0):
            for part in range(PARTS):
                slot = flip(me, mask_of(pattern, order[part]) + sibling)
                for copy in tiles(part, slot, q, sibling):
                    copy.start()
    greet(me, size)
    calls, finish = scatter_steps(size, me, made, held, sent, came, sems, partial, out, ready)
    for call in calls:
        call()
    finish()


def sum_products(size, number, lefts, units):
    total, hidden = lefts[0].shape
    lanes, _, _, width = units[0][0].shape
    rows = total // size // PARTS
    vmem = pl.BlockSpec(memory_space=pltpu.VMEM)
    terms = len(lefts)
    out = pl.pallas_call(
        functools.partial(sum_products_kernel, size, tuple(kind for _, kind in units)),
        out_shape=jax.ShapeDtypeStruct((PARTS, rows, width), jnp.float32),
        in_specs=[pl.BlockSpec(memory_space=pl.ANY)] * (2 * terms),
        out_specs=vmem,
        scratch_shapes=[
            *[pltpu.VMEM((size, PARTS, rows, hidden), jnp.bfloat16)] * terms,
            *[pltpu.VMEM((hidden, width), jnp.bfloat16)] * terms,
            pltpu.SemaphoreType.DMA((terms, lanes)),
            pltpu.SemaphoreType.DMA((size, PARTS, terms)),
            *scatter_scratch(size, rows, width),
        ],
        compiler_params=pltpu.CompilerParams(
            collective_id=number, has_side_effects=True, vmem_limit_bytes=VMEM
        ),
        cost_estimate=pl.CostEstimate(
            flops=2 * total * hidden * width * terms, bytes_accessed=200 * 1024 * 1024, transcendentals=0
        ),
        name="sum_products",
    )(*[left.reshape(size, PARTS, rows, hidden) for left in lefts], *[array for array, _ in units])
    return out.reshape(PARTS * rows, width)


def sum_gradients_kernel(
    size,
    dgate_in,
    dup_in,
    two_in,
    wg_in,
    wu_in,
    out,
    units_out,
    lefts,
    two,
    wg_ref,
    wu_ref,
    sums,
    w_load,
    fetch,
    flush,
    made,
    held,
    sent,
    came,
    *sems,
):
    me = lax.axis_index("fsdp")
    lanes, _, each, _ = units_out.shape
    hidden = wg_ref.shape[0]
    chunk = 256 if hidden % 256 == 0 else 128
    weights = unit_loads(wg_in, 0, wg_ref, w_load.at[0]) + unit_loads(wu_in, 1, wu_ref, w_load.at[1])
    order = [bits[::-1] for bits in orders(size)]
    patterns = scatter_order(len(order[0]))
    state = {"block": 0, "first": True}
    taken = []

    def fetches(q, sibling, part, kinds=(0, 1, 2)):
        slot = flip(me, mask_of(patterns[q], order[part]) + sibling)
        block = 1 - sibling
        pairs = (
            (dgate_in, lefts.at[0, block, part]),
            (dup_in, lefts.at[1, block, part]),
            (two_in, two.at[block, part]),
        )
        return [
            pltpu.make_async_copy(
                pairs[i][0].at[slot, part], pairs[i][1], fetch.at[block, part, i]
            )
            for i in kinds
        ]

    def fetch_all(q):
        for sibling in (1, 0):
            for part in range(PARTS):
                for copy in fetches(q, sibling, part):
                    copy.start()

    def ready(part, slot, q, sibling):
        if state["first"]:
            for copy in weights:
                copy.wait()
        state["first"], state["block"] = (False, 1 - sibling)
        take(q, sibling, part)

    def take(q, sibling, part):
        if (q, sibling, part) not in taken:
            taken.append((q, sibling, part))
            for copy in fetches(q, sibling, part, (0, 1)):
                copy.wait()

    def partial(part, slot, columns):
        block = state["block"]
        return dot(lefts[0, block, part], wg_ref[:, columns]) + dot(
            lefts[1, block, part], wu_ref[:, columns]
        )

    def add_units(q):
        for sibling in (1, 0):
            for part in range(PARTS):
                take(q, sibling, part)
                fetches(q, sibling, part, (2,))[0].wait()

        @pl.loop(0, hidden // chunk)
        def _(index):
            units = pl.ds(pl.multiple_of(index * chunk, chunk), chunk)
            total = sums[units, :] if q else 0.0
            for block in (0, 1):
                for part in range(PARTS):
                    total += contract_first(lefts[1, block, part, :, units], two[block, part])
            sums[units, :] = total

    for copy in weights:
        copy.start()
    fetch_all(0)
    greet(me, size)
    calls, finish = scatter_steps(size, me, made, held, sent, came, sems, partial, out, ready)
    copies = []
    for number, call in enumerate(calls):
        if number + 1 < len(calls):
            call()
            if number % 2:
                add_units(number // 2)
                fetch_all(number // 2 + 1)
            continue
        add_units(number // 2)
        for lane in range(lanes):
            block = two.at[lane % 2, lane // 2 % PARTS, pl.ds(lane // 4 * each, each)]
            block[...] = sums[lane * each : (lane + 1) * each, :].astype(jnp.bfloat16)
            copies.append(pltpu.make_async_copy(block, units_out.at[lane, 0], flush.at[lane]))
            copies[-1].start()
        call()
    finish()
    for copy in copies:
        copy.wait()


def sum_gradients(size, grad_gate, grad_up, whole_two, units):
    lanes, _, each, width = units.shape
    hidden = lanes * each
    rows = grad_gate.shape[0] // size // PARTS
    any_space = pl.BlockSpec(memory_space=pl.ANY)
    blocks = lambda array: array.reshape(size, PARTS, rows, -1)
    out, late = pl.pallas_call(
        functools.partial(sum_gradients_kernel, size),
        out_shape=(
            jax.ShapeDtypeStruct((PARTS, rows, width), jnp.float32),
            jax.ShapeDtypeStruct((lanes, 1, each, width), jnp.bfloat16),
        ),
        in_specs=[any_space] * 5,
        out_specs=(pl.BlockSpec(memory_space=pltpu.VMEM), any_space),
        scratch_shapes=[
            pltpu.VMEM((2, 2, PARTS, rows, hidden), jnp.bfloat16),
            pltpu.VMEM((2, PARTS, rows, width), jnp.bfloat16),
            pltpu.VMEM((hidden, width), jnp.bfloat16),
            pltpu.VMEM((hidden, width), jnp.bfloat16),
            pltpu.VMEM((hidden, width), jnp.float32),
            pltpu.SemaphoreType.DMA((2, lanes)),
            pltpu.SemaphoreType.DMA((2, PARTS, 3)),
            pltpu.SemaphoreType.DMA((lanes,)),
            *scatter_scratch(size, rows, width),
        ],
        compiler_params=pltpu.CompilerParams(
            collective_id=4, has_side_effects=True, vmem_limit_bytes=60 * 1024 * 1024
        ),
        cost_estimate=pl.CostEstimate(
            flops=6 * grad_gate.size * width, bytes_accessed=200 * 1024 * 1024, transcendentals=0
        ),
        name="sum_gradients",
    )(*map(blocks, (grad_gate, grad_up, whole_two)), units, units)
    return (out.reshape(PARTS * rows, width), late)


def enter_kernel(
    size,
    lanes,
    back,
    x_ref,
    w_ref,
    m_ref,
    c_ref,
    before,
    whole,
    mine_pair,
    mine_down,
    count,
    counts,
    loads,
    z_send,
    z_recv,
    x_send,
    x_recv,
    m_send,
    m_recv,
    c_send,
    c_recv,
    *sems,
):
    me, z = (lax.axis_index("fsdp"), lax.axis_index("tp"))
    mine = (mine_pair.at[0], mine_pair.at[1], mine_down.at[0])
    span = m_ref.shape[-1]
    part_of = lambda device: pl.ds(pl.multiple_of(device * span, span), span)
    local = [pltpu.make_async_copy(w_ref, whole.at[me, z], loads.at[0])]
    local += [
        pltpu.make_async_copy(m_ref.at[me, kind], mine[kind].at[:, part_of(me)], loads.at[kind + 1])
        for kind in range(3)
    ]
    for copy in local:
        copy.start()
    counts[me] = c_ref[...]
    up, down = (lax.rem(z + 1, lanes), lax.rem(z + lanes - 1, lanes))
    barrier = pltpu.get_barrier_semaphore()
    peers = [{"fsdp": flip(me, other)} for other in range(1, size)] + [{"tp": up}, {"tp": down}]
    for peer in peers:
        pl.semaphore_signal(barrier, inc=1, device_id=peer, device_id_type=MESH)
    pl.semaphore_wait(barrier, len(peers))

    def far(part):
        return (part + 1) // 2

    def lane(part):
        if part == 0:
            return z
        return z - far(part) if part % 2 else z + far(part)

    def exists(part):
        return z >= far(part) if part % 2 else z + far(part) < lanes

    def lane_copy(part):
        block = whole.at[me, lane(part - 2) if part > 2 else z]
        return pltpu.make_async_remote_copy(
            src_ref=block if part > 2 else w_ref,
            dst_ref=block,
            send_sem=z_send.at[part - 1],
            recv_sem=z_recv.at[part - 1],
            device_id={"tp": up if part % 2 else down},
            device_id_type=MESH,
        )

    def lane_sends(part):
        if part % 2:
            return (z >= far(part) - 1) & (z + 1 < lanes)
        return (z + far(part) - 1 < lanes) & (z > 0)

    def token_copy(hop):
        return pltpu.make_async_remote_copy(
            src_ref=x_ref if hop == 1 else before.at[hop - 2],
            dst_ref=before.at[hop - 1],
            send_sem=x_send.at[hop - 1],
            recv_sem=x_recv.at[hop - 1],
            device_id={"tp": up},
            device_id_type=MESH,
        )

    def unit_copy(other, kind):
        peer = flip(me, other)
        return pltpu.make_async_remote_copy(
            src_ref=m_ref.at[peer, kind],
            dst_ref=mine[kind].at[:, part_of(me)],
            send_sem=m_send.at[other - 1, kind],
            recv_sem=m_recv.at[other - 1, kind],
            device_id={"fsdp": peer},
            device_id_type=MESH,
        )

    def count_copy(other):
        return pltpu.make_async_remote_copy(
            src_ref=c_ref,
            dst_ref=counts.at[me],
            send_sem=c_send.at[other - 1],
            recv_sem=c_recv.at[other - 1],
            device_id={"fsdp": flip(me, other)},
            device_id_type=MESH,
        )

    def when(condition, run):
        pl.when(condition)(run)

    gather = Gather(size, me, whole, sems, 2 * lanes - 1, lane, far, w_ref)
    for part in (1, 2):
        when(lane_sends(part), lambda: lane_copy(part).start())
    gather.forward(0, 0)
    when(z + 1 < lanes, lambda: token_copy(1).start())
    for other in range(1, size):
        count_copy(other).start()
        for kind in range(3):
            unit_copy(other, kind).start()
    events = [(part, pattern) for part in range(2 * lanes - 1) for pattern in gather.patterns]
    wave = lambda pattern: 3.5 * top(pattern) + 2.5 if pattern else 0
    events.sort(key=lambda event: (2 * far(event[0]) + wave(event[1]), event))

    def run_event(part, pattern):
        if pattern:
            gather.arrive(part, pattern)
        elif part:
            lane_copy(part).wait_recv()
            if part + 2 < 2 * lanes - 1:
                when(lane_sends(part + 2), lambda: lane_copy(part + 2).start())
        gather.forward(part, pattern)

    for part, pattern in events[1:]:
        if part == 0:
            run_event(part, pattern)
        else:
            when(exists(part), lambda: run_event(part, pattern))
        if (part, pattern) == (2 * lanes - 2, 0):
            for hop in range(1, back):
                when(z >= hop, lambda: token_copy(hop).wait_recv())
                when((z >= hop) & (z + 1 < lanes), lambda: token_copy(hop + 1).start())
    for other in range(1, size):
        count_copy(other).wait()
    count[...] = sum(counts[other] for other in range(size))

    def close(part):
        for pattern in gather.patterns:
            gather.core_copy(part, pattern).wait()
            for step in range(top(pattern) + 1, gather.steps):
                gather.chip_copy(part, step, pattern).wait_send()

    close(0)
    for part in range(1, 2 * lanes - 1):
        when(exists(part), lambda: close(part))
        when(lane_sends(part), lambda: lane_copy(part).wait_send())
    for other in range(1, size):
        for kind in range(3):
            unit_copy(other, kind).wait()
    for hop in range(1, back + 1):
        when((z >= hop - 1) & (z + 1 < lanes), lambda: token_copy(hop).wait_send())
    when(z >= back, lambda: token_copy(back).wait_recv())
    for copy in local:
        copy.wait()


def enter(size, lanes, back, values, weights, units, count):
    any_space = pl.BlockSpec(memory_space=pl.ANY)
    vmem = pl.BlockSpec(memory_space=pltpu.VMEM)
    _, kinds, rows, columns = units.shape
    others = pltpu.SemaphoreType.DMA((size - 1,))
    other_kinds = pltpu.SemaphoreType.DMA((size - 1, kinds))
    line = pltpu.SemaphoreType.DMA((2 * lanes - 2,))
    hop = pltpu.SemaphoreType.DMA((back,))
    mine = lambda number: jax.ShapeDtypeStruct((number, rows, size * columns), units.dtype)
    return pl.pallas_call(
        functools.partial(enter_kernel, size, lanes, back),
        out_shape=(
            jax.ShapeDtypeStruct((back, *values.shape), values.dtype),
            jax.ShapeDtypeStruct((size, lanes, *weights.shape), weights.dtype),
            mine(kinds - 1),
            mine(1),
            jax.ShapeDtypeStruct(count.shape, count.dtype),
        ),
        in_specs=[any_space, any_space, any_space, vmem],
        out_specs=(any_space,) * 4 + (vmem,),
        scratch_shapes=[
            pltpu.VMEM((size, *count.shape), count.dtype),
            pltpu.SemaphoreType.DMA((kinds + 1,)),
            line,
            line,
            hop,
            hop,
            other_kinds,
            other_kinds,
            others,
            others,
            *gather_semaphores(size, 2 * lanes - 1),
        ],
        compiler_params=pltpu.CompilerParams(collective_id=5, has_side_effects=True),
        cost_estimate=pl.CostEstimate(flops=0, bytes_accessed=400 * 1024 * 1024, transcendentals=0),
        name="enter",
    )(values, weights, units, count)


class Units:
    def __init__(self, size, me, units, back, sems):
        self.size, self.me, self.units, self.back = (size, me, units, back)
        self.send, self.recv, self.own = sems
        self.kinds, self.span = (units.shape[0], back.shape[-1])

    def part_of(self, device):
        return pl.ds(pl.multiple_of(device * self.span, self.span), self.span)

    def stay(self):
        return [
            pltpu.make_async_copy(
                self.units.at[kind, :, self.part_of(self.me)],
                self.back.at[self.me, kind],
                self.own.at[kind],
            )
            for kind in range(self.kinds)
        ]

    def moves(self):
        copies = []
        for other in range(1, self.size):
            peer = flip(self.me, other)
            copies += [
                pltpu.make_async_remote_copy(
                    src_ref=self.units.at[kind, :, self.part_of(peer)],
                    dst_ref=self.back.at[self.me, kind],
                    send_sem=self.send.at[other - 1, kind],
                    recv_sem=self.recv.at[other - 1, kind],
                    device_id={"fsdp": peer},
                    device_id_type=MESH,
                )
                for kind in range(self.kinds)
            ]
        return copies

    def start(self):
        for copy in self.stay() + self.moves():
            copy.start()

    def finish(self):
        for copy in self.moves() + self.stay():
            copy.wait()


def units_scratch(size, kinds):
    return [
        pltpu.SemaphoreType.DMA((size - 1, kinds)),
        pltpu.SemaphoreType.DMA((size - 1, kinds)),
        pltpu.SemaphoreType.DMA((kinds,)),
    ]


class Lanes:
    def __init__(self, lanes, z, values, out, low, came, send, recv):
        self.lanes, self.z, self.values, self.out = (lanes, z, values, out)
        self.low, self.came, self.send, self.recv = (low, came, send, recv)

    def block(self, lane):
        each = self.lanes // PARTS
        width = self.out.shape[1]
        start = pl.multiple_of(lax.rem(lane, each) * width, width)
        return self.values[lax.div(lane, each), :, pl.ds(start, width)]

    def copy(self, hop):
        return pltpu.make_async_remote_copy(
            src_ref=self.low.at[hop - 1],
            dst_ref=self.came.at[hop - 1],
            send_sem=self.send.at[hop - 1],
            recv_sem=self.recv.at[hop - 1],
            device_id={"tp": lax.rem(self.z + hop, self.lanes)},
            device_id_type=MESH,
        )

    def start(self):
        for hop in range(1, self.lanes):
            self.low[hop - 1] = self.block(lax.rem(self.z + hop, self.lanes)).astype(jnp.bfloat16)
            self.copy(hop).start()

    def finish(self):
        for hop in range(1, self.lanes):
            self.copy(hop).wait()
        total = self.block(self.z)
        for hop in range(1, self.lanes):
            total = total + self.came[hop - 1].astype(jnp.float32)
        self.out[...] = total


def lanes_scratch(lanes, shape):
    return [
        pltpu.VMEM((lanes - 1, *shape), jnp.bfloat16),
        pltpu.VMEM((lanes - 1, *shape), jnp.bfloat16),
        pltpu.SemaphoreType.DMA((lanes - 1,)),
        pltpu.SemaphoreType.DMA((lanes - 1,)),
    ]


def greet_all(me, z, size, lanes):
    barrier = pltpu.get_barrier_semaphore()
    peers = [{"fsdp": flip(me, other)} for other in range(1, size)]
    peers += [{"tp": lax.rem(z + hop, lanes)} for hop in range(1, lanes)]
    for peer in peers:
        pl.semaphore_signal(barrier, inc=1, device_id=peer, device_id_type=MESH)
    pl.semaphore_wait(barrier, len(peers))


def sum_query_kernel(
    size, left_ref, right_ref, units_ref, out, back, left, right, loads, *refs
):
    units_sems = refs[:3]
    made, held, sent, came, *sems = refs[3:]
    me = lax.axis_index("fsdp")
    width = out.shape[-1]
    rows = left.shape[1] // size
    copies = [pltpu.make_async_copy(left_ref, left, loads.at[PARTS])]
    copies += [
        pltpu.make_async_copy(
            right_ref.at[:, pl.ds(part * width, width)], right.at[part], loads.at[part]
        )
        for part in range(PARTS)
    ]
    for copy in copies:
        copy.start()
    barrier = pltpu.get_barrier_semaphore()
    for other in range(1, size):
        pl.semaphore_signal(
            barrier, inc=1, device_id={"fsdp": flip(me, other)}, device_id_type=MESH
        )
    pl.semaphore_wait(barrier, size - 1)
    for copy in copies:
        copy.wait()

    def partial(part, slot, columns):
        block = left[:, pl.ds(pl.multiple_of(slot * rows, rows), rows)]
        return contract_first(block, right[part, :, columns])

    units = Units(size, me, units_ref, back, units_sems)
    calls, finish = scatter_steps(size, me, made, held, sent, came, sems, partial, out)
    for number, call in enumerate(calls):
        call()
        if number == len(calls) // 2:
            units.start()
    units.finish()
    finish()


def sum_query(size, left, right, units):
    tokens, depth = left.shape
    width = right.shape[1] // PARTS
    rows = depth // size
    any_space = pl.BlockSpec(memory_space=pl.ANY)
    vmem = pl.BlockSpec(memory_space=pltpu.VMEM)
    return pl.pallas_call(
        functools.partial(sum_query_kernel, size),
        out_shape=(
            jax.ShapeDtypeStruct((PARTS, rows, width), jnp.float32),
            jax.ShapeDtypeStruct((size, *units.shape[:2], rows), jnp.bfloat16),
        ),
        in_specs=[any_space] * 3,
        out_specs=(vmem, any_space),
        scratch_shapes=[
            pltpu.VMEM((tokens, depth), jnp.bfloat16),
            pltpu.VMEM((PARTS, tokens, width), jnp.bfloat16),
            pltpu.SemaphoreType.DMA((PARTS + 1,)),
            *units_scratch(size, units.shape[0]),
            *scatter_scratch(size, rows, width),
        ],
        compiler_params=pltpu.CompilerParams(
            collective_id=6, has_side_effects=True, vmem_limit_bytes=VMEM
        ),
        cost_estimate=pl.CostEstimate(
            flops=4 * tokens * depth * width, bytes_accessed=100 * 1024 * 1024, transcendentals=0
        ),
        name="sum_query",
    )(left, right, units)


def sum_key_kernel(
    size,
    lanes,
    left_ref,
    q_ref,
    kv_ref,
    w_ref,
    units_ref,
    out_sums,
    query_sums,
    pair_out,
    low,
    back,
    lane_out,
    lane_query,
    left,
    right,
    loads,
    tiles,
    fetch,
    out,
    *refs,
):
    units_sems, lane_refs = (refs[:3], refs[3:11])
    made, held, sent, came, *sems = refs[11:]
    me, z = (lax.axis_index("fsdp"), lax.axis_index("tp"))
    rows = left.shape[1] // size
    parts, span = (w_ref.shape[1], tiles.shape[-1])
    copies = [pltpu.make_async_copy(left_ref, left, loads.at[PARTS])]
    copies += [
        pltpu.make_async_copy(kv_ref.at[part], right.at[part], loads.at[part])
        for part in range(PARTS)
    ]
    for copy in copies:
        copy.start()

    def tile_copy(f):
        return pltpu.make_async_copy(
            w_ref.at[f, :, :, pl.ds(0, span)], tiles.at[f % 2], fetch.at[f % 2]
        )

    tile_copy(0).start()
    greet_all(me, z, size, lanes)
    for copy in copies:
        copy.wait()

    def partial(part, slot, columns):
        block = left[:, pl.ds(pl.multiple_of(slot * rows, rows), rows)]
        return contract_first(block, right[part, :, columns])

    def low_columns(f):
        if f + 1 < size:
            tile_copy(f + 1).start()
        tile_copy(f).wait()
        half = low.shape[0] // 2

        @pl.loop(0, 2)
        def _(index):
            span_rows = pl.ds(pl.multiple_of(index * half, half), half)
            total = jnp.zeros((half, rows), jnp.float32)
            for z in range(parts):
                start = 0
                for source in (q_ref, right.at[0], right.at[1]):
                    width = source.shape[1] // parts
                    total += contract_last(
                        source[span_rows, z * width : (z + 1) * width],
                        tiles[f % 2, z, :, start : start + width],
                    )
                    start += width
            low[span_rows, f * rows : (f + 1) * rows] = total

    units = Units(size, me, units_ref, back, units_sems)
    across = (
        Lanes(lanes, z, out_sums, lane_out, *lane_refs[:4]),
        Lanes(lanes, z, query_sums, lane_query, *lane_refs[4:]),
    )
    calls, finish = scatter_steps(size, me, made, held, sent, came, sems, partial, out)
    done = 0
    for number, call in enumerate(calls):
        call()
        if number < 2:
            across[number].start()
        if number == len(calls) // 2:
            units.start()
        goal = size * max(0, number - 1) // max(1, len(calls) - 3)
        while done < min(size, goal):
            low_columns(done)
            done += 1
    while done < size:
        low_columns(done)
        done += 1
    for one in across:
        one.finish()
    units.finish()
    finish()
    pair_out[...] = out[...].astype(jnp.bfloat16)


def sum_key(size, lanes, left, grad_query, grad_pair, weights, units, *sums):
    tokens, depth = left.shape
    width = grad_pair.shape[2]
    rows = depth // size
    parts = weights.shape[1]
    span = (grad_query.shape[1] + PARTS * width) // parts
    lane_width = sums[0].shape[2] * PARTS // lanes
    any_space = pl.BlockSpec(memory_space=pl.ANY)
    vmem = pl.BlockSpec(memory_space=pltpu.VMEM)
    return pl.pallas_call(
        functools.partial(sum_key_kernel, size, lanes),
        out_shape=(
            jax.ShapeDtypeStruct((PARTS, rows, width), jnp.bfloat16),
            jax.ShapeDtypeStruct((tokens, depth), jnp.float32),
            jax.ShapeDtypeStruct((size, *units.shape[:2], rows), jnp.bfloat16),
            *[jax.ShapeDtypeStruct((rows, lane_width), jnp.float32)] * 2,
        ),
        in_specs=[any_space, vmem, any_space, any_space, any_space, vmem, vmem],
        out_specs=(vmem, vmem, any_space, vmem, vmem),
        scratch_shapes=[
            pltpu.VMEM((tokens, depth), jnp.bfloat16),
            pltpu.VMEM((PARTS, tokens, width), jnp.bfloat16),
            pltpu.SemaphoreType.DMA((PARTS + 1,)),
            pltpu.VMEM((2, parts, rows, span), jnp.bfloat16),
            pltpu.SemaphoreType.DMA((2,)),
            pltpu.VMEM((PARTS, rows, width), jnp.float32),
            *units_scratch(size, units.shape[0]),
            *lanes_scratch(lanes, (rows, lane_width)),
            *lanes_scratch(lanes, (rows, lane_width)),
            *scatter_scratch(size, rows, width),
        ],
        compiler_params=pltpu.CompilerParams(
            collective_id=7, has_side_effects=True, vmem_limit_bytes=VMEM
        ),
        cost_estimate=pl.CostEstimate(
            flops=8 * tokens * depth * width, bytes_accessed=100 * 1024 * 1024, transcendentals=0
        ),
        name="sum_key",
    )(left, grad_query, grad_pair, weights, units, *sums)


def sum_small_kernel(size, lanes, sizes, x_ref, *refs):
    outs, (came, send, recv) = (refs[: len(sizes)], refs[len(sizes) :])
    me, z = (lax.axis_index("fsdp"), lax.axis_index("tp"))
    peers = []
    for name, index, count in (("fsdp", me, size), ("tp", z, lanes)):
        bit = 1
        while bit < count:
            peers.append({name: flip(index, bit)})
            bit *= 2
    barrier = pltpu.get_barrier_semaphore()
    for peer in peers:
        pl.semaphore_signal(barrier, inc=1, device_id=peer, device_id_type=MESH)
    pl.semaphore_wait(barrier, len(peers))
    sent = came.shape[0] // 2
    came[sent] = x_ref[...]
    for step, peer in enumerate(peers):
        copy = pltpu.make_async_remote_copy(
            src_ref=came.at[sent + step],
            dst_ref=came.at[step],
            send_sem=send.at[step],
            recv_sem=recv.at[step],
            device_id=peer,
            device_id_type=MESH,
        )
        copy.start()
        copy.wait()
        came[sent + step + 1] = came[sent + step] + came[step]
    start = 0
    for out, rows in zip(outs, sizes):
        out[...] = came[sent + len(peers), start : start + rows]
        start += rows


def sum_small(size, lanes, values, sizes):
    steps = (size * lanes).bit_length() - 1
    vmem = pl.BlockSpec(memory_space=pltpu.VMEM)
    return pl.pallas_call(
        functools.partial(sum_small_kernel, size, lanes, sizes),
        out_shape=tuple(jax.ShapeDtypeStruct((rows, values.shape[1]), values.dtype) for rows in sizes),
        in_specs=[vmem],
        out_specs=(vmem,) * len(sizes),
        scratch_shapes=[
            pltpu.VMEM((2 * (steps + 1), *values.shape), values.dtype),
            pltpu.SemaphoreType.DMA((steps,)),
            pltpu.SemaphoreType.DMA((steps,)),
        ],
        compiler_params=pltpu.CompilerParams(collective_id=8, has_side_effects=True),
        name="sum_small",
    )(values)


def project_kernel(
    wq, wk, before_ref, x_ref, gain_ref, w_ref, n_ref, q_ref, k_ref, v_ref, normed
):
    back, own, _ = before_ref.shape
    lead = back * own
    tile = min(512, own)
    z = lax.axis_index("tp")

    @pl.when(pl.program_id(0) == 0)
    def _():
        for hop in range(back + 1):

            @pl.loop(0, own // tile)
            def _(index):
                span = pl.ds(pl.multiple_of(index * tile, tile), tile)
                values = x_ref[span, :] if hop == 0 else before_ref[hop - 1, span, :]
                values = normalize_rows(values.astype(jnp.float32))[0] * gain_ref[...]
                values = values.astype(jnp.bfloat16)
                if hop:
                    values = jnp.where(z >= hop, values, jnp.zeros_like(values))
                else:
                    n_ref[span, :] = values
                at = lead - hop * own + index * tile
                normed[pl.ds(pl.multiple_of(at, tile), tile), :] = values

    weights = lambda start, size: w_ref[:, 0, :, start : start + size].reshape(D, size)

    @pl.loop(0, (lead + own) // tile)
    def _(index):
        span = pl.ds(pl.multiple_of(index * tile, tile), tile)
        pair = dot(normed[span, :], weights(wq, 2 * wk))
        k_ref[span, :] = pair[:, :wk]
        v_ref[span, :] = pair[:, wk:].astype(jnp.bfloat16)

    @pl.loop(0, own // tile)
    def _(index):
        span = pl.ds(pl.multiple_of(index * tile, tile), tile)
        from_lead = pl.ds(pl.multiple_of(lead + index * tile, tile), tile)
        q_ref[span, :] = dot(normed[from_lead, :], weights(0, wq))


def project(before, values, gain, weights, wq, wk):
    size, parts, rows_in, columns = weights.shape
    back, own, _ = before.shape
    rows = (back + 1) * own
    whole = lambda *_: (0, 0)
    return pl.pallas_call(
        functools.partial(project_kernel, wq, wk),
        grid=(parts,),
        out_shape=(
            jax.ShapeDtypeStruct((own, D), jnp.bfloat16),
            jax.ShapeDtypeStruct((own, parts * wq), jnp.float32),
            jax.ShapeDtypeStruct((rows, parts * wk), jnp.float32),
            jax.ShapeDtypeStruct((rows, parts * wk), jnp.bfloat16),
        ),
        in_specs=[
            pl.BlockSpec((back, own, D), lambda z: (0, 0, 0)),
            pl.BlockSpec((own, D), whole),
            pl.BlockSpec((1, D), whole),
            pl.BlockSpec((size, 1, rows_in, wq + 2 * wk), lambda z: (0, z, 0, 0)),
        ],
        out_specs=(
            pl.BlockSpec((own, D), whole),
            pl.BlockSpec((own, wq), lambda z: (0, z)),
            pl.BlockSpec((rows, wk), lambda z: (0, z)),
            pl.BlockSpec((rows, wk), lambda z: (0, z)),
        ),
        scratch_shapes=[pltpu.VMEM((rows, D), jnp.bfloat16)],
        compiler_params=pltpu.CompilerParams(vmem_limit_bytes=VMEM),
        cost_estimate=pl.CostEstimate(
            flops=2 * D * parts * (own * wq + rows * 2 * wk),
            bytes_accessed=2 * D * parts * (wq + 2 * wk) + 2 * rows * D,
            transcendentals=0,
        ),
        name="project_in",
    )(before, values, gain.reshape(1, D), weights)


def out_kernel(a_ref, w_ref, x_ref, o_ref):
    parts, _, width = w_ref.shape[1:]
    total = x_ref[...].astype(jnp.float32)
    for z in range(parts):
        total += contract_last(a_ref[:, z * width : (z + 1) * width], w_ref[0, z])
    o_ref[...] = total


def project_out(attended, weights, states, wo):
    size, parts, rows, columns = weights.shape
    own = states.shape[0]
    last = columns // wo - 1
    return pl.pallas_call(
        out_kernel,
        grid=(size,),
        out_shape=jax.ShapeDtypeStruct(states.shape, jnp.float32),
        in_specs=[
            pl.BlockSpec(attended.shape, lambda f: (0, 0)),
            pl.BlockSpec((1, parts, rows, wo), lambda f: (f, 0, 0, last)),
            pl.BlockSpec((own, rows), lambda f: (0, f)),
        ],
        out_specs=pl.BlockSpec((own, rows), lambda f: (0, f)),
        compiler_params=pltpu.CompilerParams(vmem_limit_bytes=VMEM),
        cost_estimate=pl.CostEstimate(
            flops=2 * own * D * parts * wo, bytes_accessed=24 * 1024 * 1024, transcendentals=0
        ),
        name="project_out",
    )(attended, weights, states)


def back_out_kernel(g_ref, w_ref, o_ref):
    size, _, rows, width = w_ref.shape
    o_ref[...] = dot(g_ref[...], w_ref[:, 0].reshape(size * rows, width)).astype(jnp.bfloat16)


def back_out(grad, weights, wo):
    size, parts, rows, columns = weights.shape
    own = grad.shape[0]
    last = columns // wo - 1
    return pl.pallas_call(
        back_out_kernel,
        grid=(parts,),
        out_shape=jax.ShapeDtypeStruct((own, parts * wo), jnp.bfloat16),
        in_specs=[
            pl.BlockSpec(grad.shape, lambda z: (0, 0)),
            pl.BlockSpec((size, 1, rows, wo), lambda z: (0, z, 0, last)),
        ],
        out_specs=pl.BlockSpec((own, wo), lambda z: (0, z)),
        compiler_params=pltpu.CompilerParams(vmem_limit_bytes=VMEM),
        cost_estimate=pl.CostEstimate(
            flops=2 * own * D * parts * wo, bytes_accessed=16 * 1024 * 1024, transcendentals=0
        ),
        name="back_out",
    )(grad, weights)


def turn(values, cosine, sine):
    return values * cosine + pltpu.roll(values, HD // 2, 1) * sine


def turn_back(grad, cosine, sine):
    return grad * cosine - pltpu.roll(grad, HD // 2, 1) * sine


def split_heads(block, group):
    return jnp.concatenate([block[:, i * HD : (i + 1) * HD] for i in range(group)], axis=0)


def join_heads(stacked, group):
    rows = stacked.shape[0] // group
    return jnp.concatenate([stacked[i * rows : (i + 1) * rows] for i in range(group)], axis=1)


def head_probs(query, keys, bias, group, scale):
    scores = contract_last(query, keys) * (scale * LOG2E)
    rows, span = scores.shape
    scores = (scores.reshape(group, rows // group, span) + bias[None]).reshape(rows, span)
    weights = jnp.exp2(scores)
    return weights * (1.0 / jnp.sum(weights, axis=-1, keepdims=True))


def attend_kernel(
    group, step, lead, q_ref, k_ref, v_ref, bias_ref, cos_ref, sin_ref, nq_ref, nk_ref, o_ref, keys
):
    tile, span = bias_ref.shape
    scale = HD ** (-0.5)
    index = pl.program_id(1)

    @pl.when(index == 0)
    def _():
        normed = normalize_rows(k_ref[...])[0] * nk_ref[...]
        keys[...] = turn(normed, cos_ref[...], sin_ref[...]).astype(jnp.bfloat16)

    here = pl.ds(pl.multiple_of(lead + index * tile, tile), tile)
    cosine, sine = (cos_ref[here, :], sin_ref[here, :])
    normed = normalize_rows(split_heads(q_ref[...], group))[0] * nq_ref[...]
    cosine, sine = (jnp.concatenate([cosine] * group, 0), jnp.concatenate([sine] * group, 0))
    query = turn(normed, cosine, sine).astype(jnp.bfloat16)
    window = pl.ds(pl.multiple_of(index * step, tile), span)
    probs = head_probs(query, keys[window, :], bias_ref[...], group, scale)
    mixed = dot(probs.astype(jnp.bfloat16), v_ref[window, :])
    o_ref[...] = join_heads(mixed.astype(jnp.bfloat16), group)


def attend_back_kernel(
    group,
    step,
    lead,
    size,
    lanes,
    q_ref,
    k_ref,
    v_ref,
    bias_ref,
    cos_ref,
    sin_ref,
    nq_ref,
    nk_ref,
    do_ref,
    left_ref,
    right_ref,
    dq_ref,
    pair_ref,
    gq_ref,
    gk_ref,
    out_ref,
    keys,
    dk,
    dv,
    mixed,
    got,
    own_sum,
    left,
    right,
    loads,
    hop_send,
    hop_recv,
    *refs,
):
    made, held, sent, came, *sems = refs
    tile, span = bias_ref.shape
    scale = HD ** (-0.5)
    head, index = (pl.program_id(0), pl.program_id(1))
    heads, tiles = (mixed.shape[0], (k_ref.shape[0] - lead) // tile)
    back, own = (mixed.shape[1], mixed.shape[3])
    me, z = (lax.axis_index("fsdp"), lax.axis_index("tp"))
    width = out_ref.shape[-1]
    rows = left.shape[1] // size

    def hop_copy(at, number):
        return pltpu.make_async_remote_copy(
            src_ref=mixed.at[at, number],
            dst_ref=got.at[at, number],
            send_sem=hop_send.at[at, number],
            recv_sem=hop_recv.at[at, number],
            device_id={"tp": lax.rem(z + lanes - 1, lanes)},
            device_id_type=MESH,
        )

    def relay(at, number):
        @pl.when(z + 1 < lanes)
        def _():
            hop_copy(at, number - 1).wait_recv()
            total = mixed[at, number].astype(jnp.float32)
            total = total + got[at, number - 1].astype(jnp.float32)
            mixed[at, number] = total.astype(jnp.bfloat16)

        @pl.when(z > 0)
        def _():
            hop_copy(at, number).start()

    loads_of = lambda: [pltpu.make_async_copy(left_ref, left, loads.at[PARTS])] + [
        pltpu.make_async_copy(
            right_ref.at[:, pl.ds(part * width, width)], right.at[part], loads.at[part]
        )
        for part in range(PARTS)
    ]

    @pl.when((head == 0) & (index == 0))
    def _():
        for copy in loads_of():
            copy.start()
        barrier = pltpu.get_barrier_semaphore()
        peers = [{"fsdp": flip(me, bit)} for bit in [1] + chip_bits(size)]
        peers += [{"tp": lax.rem(z + 1, lanes)}, {"tp": lax.rem(z + lanes - 1, lanes)}]
        for peer in peers:
            pl.semaphore_signal(barrier, inc=1, device_id=peer, device_id_type=MESH)
        pl.semaphore_wait(barrier, len(peers))
        for copy in loads_of():
            copy.wait()
        gq_ref[...] = jnp.zeros_like(gq_ref)
        gk_ref[...] = jnp.zeros_like(gk_ref)

    def partial(part, slot, columns):
        block = left[:, pl.ds(pl.multiple_of(slot * rows, rows), rows)]
        return contract_first(block, right[part, :, columns])

    calls, finish = scatter_steps(size, me, made, held, sent, came, sems, partial, out_ref)
    at_step = {}
    for number, call in enumerate(calls):
        at_step.setdefault(number * heads * tiles // len(calls), []).append(call)
    for number, some in at_step.items():

        @pl.when(head * tiles + index == number)
        def _():
            for call in some:
                call()

    @pl.when(index == 0)
    def _():
        normed = normalize_rows(k_ref[...])[0] * nk_ref[...]
        keys[...] = turn(normed, cos_ref[...], sin_ref[...]).astype(jnp.bfloat16)
        dk[...] = jnp.zeros_like(dk)
        dv[...] = jnp.zeros_like(dv)

    here = pl.ds(pl.multiple_of(lead + index * tile, tile), tile)
    cosine, sine = (cos_ref[here, :], sin_ref[here, :])
    cosine, sine = (jnp.concatenate([cosine] * group, 0), jnp.concatenate([sine] * group, 0))
    normed, factor = normalize_rows(split_heads(q_ref[...], group))
    query = turn(normed * nq_ref[...], cosine, sine).astype(jnp.bfloat16)
    window = pl.ds(pl.multiple_of(index * step, tile), span)
    probs = head_probs(query, keys[window, :], bias_ref[...], group, scale)
    grad_out = split_heads(do_ref[...], group)
    dv[window, :] += contract_first(probs.astype(jnp.bfloat16), grad_out)
    grad_probs = contract_last(grad_out, v_ref[window, :])
    centre = jnp.sum(probs * grad_probs, axis=-1, keepdims=True)
    grad_scores = (probs * (grad_probs - centre)).astype(jnp.bfloat16)
    dk[window, :] += contract_first(grad_scores, query) * scale
    grad_query = turn_back(dot(grad_scores, keys[window, :]) * scale, cosine, sine)
    gq_ref[...] += jnp.sum(grad_query * normed, axis=0, keepdims=True)
    grad_raw = norm_back(grad_query, normed, factor, nq_ref[...])
    dq_ref[...] = join_heads(grad_raw.astype(jnp.bfloat16), group)

    @pl.when(index == tiles - 1)
    def _():
        normed_key, key_factor = normalize_rows(k_ref[...])
        grad_key = turn_back(dk[...], cos_ref[...], sin_ref[...])
        gk_ref[...] += jnp.sum(grad_key * normed_key, axis=0, keepdims=True)
        grad_key = norm_back(grad_key, normed_key, key_factor, nk_ref[...])
        for number in range(back):
            block = slice(number * own, (number + 1) * own)
            mixed[head, number, 0] = grad_key[block].astype(jnp.bfloat16)
            mixed[head, number, 1] = dv[block, :].astype(jnp.bfloat16)
        own_sum[head, 0] = grad_key[lead:]
        own_sum[head, 1] = dv[lead:, :]

        @pl.when(z > 0)
        def _():
            hop_copy(head, 0).start()

        for number in range(1, back):

            @pl.when(head >= number)
            def _():
                relay(head - number, number)

    @pl.when((head == heads - 1) & (index == tiles - 1))
    def _():
        for number in range(1, back):
            for at in range(heads - number, heads):
                relay(at, number)
        for at in range(heads):
            columns = slice(at * HD, (at + 1) * HD)

            @pl.when(z + 1 < lanes)
            def _():
                hop_copy(at, back - 1).wait_recv()
                total = own_sum[at] + got[at, back - 1].astype(jnp.float32)
                pair_ref[:, :, columns] = total.astype(jnp.bfloat16)

            @pl.when(z + 1 == lanes)
            def _():
                pair_ref[:, :, columns] = own_sum[at].astype(jnp.bfloat16)

            @pl.when(z > 0)
            def _():
                for number in range(back):
                    hop_copy(at, number).wait_send()

        finish()


def attention_specs(own, rows, group, tile, span):
    whole = lambda g, t: (0, 0)
    return [
        pl.BlockSpec((tile, group * HD), lambda g, t: (t, g)),
        pl.BlockSpec((rows, HD), lambda g, t: (0, g)),
        pl.BlockSpec((rows, HD), lambda g, t: (0, g)),
        pl.BlockSpec((tile, span), lambda g, t: (t, 0)),
        pl.BlockSpec((rows, HD), whole),
        pl.BlockSpec((rows, HD), whole),
        pl.BlockSpec((1, HD), whole),
        pl.BlockSpec((1, HD), whole),
    ]


def attend(queries, keys, values, bias, cosine, sine, norm_query, norm_key, tile, step):
    own, rows = (queries.shape[0], keys.shape[0])
    heads = keys.shape[1] // HD
    group = queries.shape[1] // keys.shape[1]
    span = bias.shape[1]
    return pl.pallas_call(
        functools.partial(attend_kernel, group, step, rows - own),
        grid=(heads, own // tile),
        out_shape=jax.ShapeDtypeStruct(queries.shape, jnp.bfloat16),
        in_specs=attention_specs(own, rows, group, tile, span),
        out_specs=pl.BlockSpec((tile, group * HD), lambda g, t: (t, g)),
        scratch_shapes=[pltpu.VMEM((rows, HD), jnp.bfloat16)],
        compiler_params=pltpu.CompilerParams(vmem_limit_bytes=VMEM),
        cost_estimate=pl.CostEstimate(
            flops=16 * own * span * queries.shape[1],
            bytes_accessed=4 * queries.size + 6 * keys.size,
            transcendentals=own * span * heads * group,
        ),
        name="attend",
    )(queries, keys, values, bias, cosine, sine, norm_query, norm_key)


def attend_back(
    queries,
    keys,
    values,
    bias,
    cosine,
    sine,
    norm_query,
    norm_key,
    grad,
    tile,
    step,
    left,
    right,
    size,
    lanes,
):
    own, rows = (queries.shape[0], keys.shape[0])
    heads = keys.shape[1] // HD
    group = queries.shape[1] // keys.shape[1]
    span = bias.shape[1]
    lead = rows - own
    back = lead // own
    tokens, depth = left.shape
    width = right.shape[1] // PARTS
    whole = lambda g, t: (0, 0)
    any_space = pl.BlockSpec(memory_space=pl.ANY)
    return pl.pallas_call(
        functools.partial(attend_back_kernel, group, step, lead, size, lanes),
        grid=(heads, own // tile),
        out_shape=(
            jax.ShapeDtypeStruct(queries.shape, jnp.bfloat16),
            jax.ShapeDtypeStruct((2, own, heads * HD), jnp.bfloat16),
            jax.ShapeDtypeStruct((1, HD), jnp.float32),
            jax.ShapeDtypeStruct((1, HD), jnp.float32),
            jax.ShapeDtypeStruct((PARTS, depth // size, width), jnp.float32),
        ),
        in_specs=attention_specs(own, rows, group, tile, span)
        + [pl.BlockSpec((tile, group * HD), lambda g, t: (t, g)), any_space, any_space],
        out_specs=(
            pl.BlockSpec((tile, group * HD), lambda g, t: (t, g)),
            pl.BlockSpec((2, own, heads * HD), lambda g, t: (0, 0, 0)),
            pl.BlockSpec((1, HD), whole),
            pl.BlockSpec((1, HD), whole),
            pl.BlockSpec((PARTS, depth // size, width), lambda g, t: (0, 0, 0)),
        ),
        scratch_shapes=[
            pltpu.VMEM((rows, HD), jnp.bfloat16),
            pltpu.VMEM((rows, HD), jnp.float32),
            pltpu.VMEM((rows, HD), jnp.float32),
            pltpu.VMEM((heads, back, 2, own, HD), jnp.bfloat16),
            pltpu.VMEM((heads, back, 2, own, HD), jnp.bfloat16),
            pltpu.VMEM((heads, 2, own, HD), jnp.float32),
            pltpu.VMEM((tokens, depth), jnp.bfloat16),
            pltpu.VMEM((PARTS, tokens, width), jnp.bfloat16),
            pltpu.SemaphoreType.DMA((PARTS + 1,)),
            pltpu.SemaphoreType.DMA((heads, back)),
            pltpu.SemaphoreType.DMA((heads, back)),
            *scatter_scratch(size, depth // size, width),
        ],
        compiler_params=pltpu.CompilerParams(
            collective_id=9, has_side_effects=True, vmem_limit_bytes=60 * 1024 * 1024
        ),
        cost_estimate=pl.CostEstimate(
            flops=40 * own * span * queries.shape[1],
            bytes_accessed=8 * queries.size + 16 * keys.size,
            transcendentals=own * span * heads * group,
        ),
        name="attend_back",
    )(queries, keys, values, bias, cosine, sine, norm_query, norm_key, grad, left, right)


def window_tables(length_row, pad_row, first, own, lead, tile, span):
    places = first - lead + jnp.arange(lead + own, dtype=jnp.int32)
    ends = jnp.cumsum(length_row)
    passed = places[:, None] >= ends[None, :]
    docs = jnp.sum(passed.astype(jnp.int32), axis=1)
    starts = jnp.sum(jnp.where(passed, length_row[None, :], 0), axis=1)
    freqs = THETA ** (-(jnp.arange(HD // 2).astype(jnp.float32) * 2.0 / HD))
    angles = (places - starts).astype(jnp.float32)[:, None] * freqs[None, :]
    cosine, sine = (jnp.cos(angles), jnp.sin(angles))
    padded = jnp.concatenate((jnp.zeros((lead,), pad_row.dtype), pad_row))
    live = lax.dynamic_slice_in_dim(padded, first, lead + own, 0)
    step = tile if lead + own > span else 0
    masks = []
    for index in range(own // tile):
        at = lead + index * tile
        query, key = (places[at : at + tile, None], places[None, index * step : index * step + span])
        same = docs[at : at + tile, None] == docs[None, index * step : index * step + span]
        seen = (live[None, index * step : index * step + span] == 1) | (key == query)
        masks.append((key >= 0) & (key <= query) & (query - key < WINDOW) & same & seen)
    bias = jnp.where(jnp.concatenate(masks, axis=0), 0.0, NEG).astype(jnp.float32)
    cosine = jnp.concatenate((cosine, cosine), axis=1)
    sine = jnp.concatenate((-sine, sine), axis=1)
    return (bias, cosine, sine, step, live[lead:].astype(jnp.float32))


def shards(
    states,
    lengths,
    padding,
    teacher,
    norm_attn,
    w_query,
    w_key,
    w_value,
    norm_query,
    norm_key,
    w_out,
    norm_mlp,
    w_gate,
    w_up,
    w_down,
):
    own = states.shape[0]
    n_tp, n_fsdp = (lax.axis_size("tp"), lax.axis_size("fsdp"))
    first = lax.axis_index("tp") * own
    back = min(n_tp - 1, -(-WINDOW // own))
    lead = back * own
    tile = min(256, own)
    span = WINDOW + tile if lead >= WINDOW else lead + own
    wq, wk = (w_query.shape[1], w_key.shape[1])
    bias, cosine, sine, step, live = window_tables(
        lengths[0], padding[0], first, own, lead, tile, span
    )
    joined = jnp.concatenate((w_query, w_key, w_value, w_out.T), axis=1)
    wo = w_out.shape[0]
    units = [
        part.reshape(n_fsdp, -1, part.shape[1]) for part in (w_gate.T, w_up.T, w_down)
    ]
    live_here = jnp.full((8, 128), jnp.sum(padding).astype(jnp.float32))
    before, weights_attn, mine_pair, mine_down, counts = enter(
        n_fsdp, n_tp, back, states, joined, jnp.stack(units, axis=1), live_here
    )
    count = counts[0, 0]
    units_pair = lax.all_gather(mine_pair, "tp", axis=0)
    units_down = lax.all_gather(mine_down, "tp", axis=0)
    normed_in, query_raw, key_raw, value = project(
        before, states, norm_attn, weights_attn, wq, wk
    )
    gains = (norm_query.reshape(1, HD), norm_key.reshape(1, HD))
    attended = attend(query_raw, key_raw, value, bias, cosine, sine, *gains, tile, step)
    inputs = states.astype(jnp.float32)
    hidden_one = project_out(attended, weights_attn, states, wo)
    normed_two, factor_two = normalize_rows(hidden_one)
    whole_two, gate, up, product = gate_up(
        n_fsdp, (normed_two * norm_mlp).astype(jnp.bfloat16), units_pair
    )
    outputs = hidden_one + sum_products(n_fsdp, 2, (product,), ((units_down, 0),))
    errors = (outputs - teacher.astype(jnp.float32)) * live[:, None]
    squares = jnp.sum(errors * errors)
    grad_out = errors * (2.0 / (count * D))

    grad_gate, grad_up, units_early = grad_hidden_units(
        n_fsdp, grad_out.astype(jnp.bfloat16), units_down, gate, up, product, whole_two
    )
    units_early = lax.psum_scatter(units_early, "tp", scatter_dimension=0)
    grad_mid, units_late = sum_gradients(n_fsdp, grad_gate, grad_up, whole_two, units_pair)
    grad_norm_mlp = jnp.sum(grad_mid * normed_two, axis=0)
    grad_hidden = grad_out + norm_back(grad_mid, normed_two, factor_two, norm_mlp)

    grad_low_out = grad_hidden.astype(jnp.bfloat16)
    grad_attended = back_out(grad_low_out, weights_attn, wo)
    grad_query, grad_pair, grad_norm_query, grad_norm_key, sums_out = attend_back(
        query_raw,
        key_raw,
        value,
        bias,
        cosine,
        sine,
        *gains,
        grad_attended,
        tile,
        step,
        grad_low_out,
        attended,
        n_fsdp,
        n_tp,
    )
    units_late, grad_query = lax.optimization_barrier((units_late, grad_query))
    units_late = lax.psum_scatter(units_late, "tp", scatter_dimension=0)
    sums_query, back_early = sum_query(n_fsdp, normed_in, grad_query, units_early)
    sums_pair, grad_low, back_late, grad_w_out, grad_w_query = sum_key(
        n_fsdp,
        n_tp,
        normed_in,
        grad_query,
        grad_pair,
        weights_attn,
        units_late,
        sums_out,
        sums_query,
    )
    grad_w_down, grad_w_gate, grad_w_up = [
        part.reshape(-1, part.shape[2]).astype(jnp.float32)
        for part in (back_early[:, 0], back_early[:, 1], back_late[:, 0])
    ]
    normed_one, factor_one = normalize_rows(inputs)
    grad_norm_attn = jnp.sum(grad_low * normed_one, axis=0)
    grad_input = grad_hidden + norm_back(grad_low, normed_one, factor_one, norm_attn)
    lines = D // HD
    small = [
        grad_norm_attn.reshape(lines, HD),
        grad_norm_mlp.reshape(lines, HD),
        grad_norm_query,
        grad_norm_key,
        jnp.full((6, HD), squares),
    ]
    small, grad_input, grad_w_down, grad_w_gate, grad_w_up = lax.optimization_barrier(
        (jnp.concatenate(small, axis=0), grad_input, grad_w_down, grad_w_gate.T, grad_w_up.T)
    )
    grad_norm_attn, grad_norm_mlp, rest = sum_small(n_fsdp, n_tp, small, (lines, lines, 8))
    grad_norm_attn, grad_norm_mlp = (grad_norm_attn.reshape(D), grad_norm_mlp.reshape(D))
    grad_norm_query, grad_norm_key, squares = (rest[0], rest[1], rest[2, 0])
    grad_w_pair = lax.psum_scatter(sums_pair, "tp", scatter_dimension=2, tiled=True)
    grad_w_pair = grad_w_pair.astype(jnp.float32)
    return (
        outputs,
        squares / (count * D),
        grad_input,
        grad_norm_attn,
        grad_w_query,
        grad_w_pair[0],
        grad_w_pair[1],
        grad_norm_query,
        grad_norm_key,
        grad_w_out.T,
        grad_norm_mlp,
        grad_w_gate,
        grad_w_up,
        grad_w_down,
    )


def solution(mesh):
    tokens = P(("fsdp", "tp"), None)
    rows, columns, sequences = (P("fsdp", "tp"), P("tp", "fsdp"), P("fsdp", None))
    in_specs = (
        tokens,
        sequences,
        sequences,
        tokens,
        P(),
        rows,
        rows,
        rows,
        P(),
        P(),
        columns,
        P(),
        rows,
        rows,
        columns,
    )
    out_specs = (
        tokens,
        P(),
        tokens,
        P(),
        rows,
        rows,
        rows,
        P(),
        P(),
        columns,
        P(),
        rows,
        rows,
        columns,
    )
    return jax.shard_map(shards, mesh=mesh, in_specs=in_specs, out_specs=out_specs, check_vma=False)
```
